32 devices in a mesh: head: 4 (over x, core), blk: 8 (over z, y).
Axes of the slice: x: 2, y: 2, z: 4, core: 2. Of those that a mesh axis runs over, the one named last changes fastest.
Arguments:
- tokens: bfloat16 [2048, 4, 768], P('blk', 'head'), may hold values from -6 to 6
- attn_gain: bfloat16 [768], P(('head', 'blk')), may hold values from 0.5 to 1.5
- w_query: bfloat16 [768, 768], P(('head', 'blk')), may hold values from -0.109375 to 0.109375
- w_key: bfloat16 [768, 768], P(('head', 'blk')), may hold values from -0.109375 to 0.109375
- w_value: bfloat16 [768, 768], P(('head', 'blk')), may hold values from -0.21875 to 0.21875
- w_out: bfloat16 [768, 768], P(None, ('head', 'blk')), may hold values from -0.875 to 0.875
- bias_table: bfloat16 [384], P(('head', 'blk')), may hold values from -3 to 3
- moe_gain: bfloat16 [768], P(('head', 'blk')), may hold values from 0.5 to 1.5
- w_router: bfloat16 [768, 8], P(('head', 'blk')), may hold values from -0.15625 to 0.15625
- expert_in: bfloat16 [8, 768, 3072], P('blk', None, 'head'), may hold values from -0.21875 to 0.21875
- expert_out: bfloat16 [8, 3072, 768], P('blk', 'head'), may hold values from -0.875 to 0.875
- seq_lengths: int32 [4], replicated, may hold values from 1024 to 2048, as said below
- rel_buckets: int32 [2048], replicated, may hold values from 0 to 31, as said below
- routes: int32 [4, 2048, 1, 1], P('head', 'blk'), may hold values from 0 to 7; in each aligned block of 256 rows (0 to 255, 256 to 511, ..., all dimensions but the last counted through in order) at most 48 rows name the same one
- cotangent: bfloat16 [2048, 4, 768], P('blk', 'head'), may hold values from -6 to 6
Outputs:
- result: bfloat16 [2048, 4, 768], P('blk', 'head')
- grad_tokens: float32 [2048, 4, 768], P('blk', 'head')
- grad_attn_gain: float32 [768], P(('head', 'blk'))
- grad_query: float32 [768, 768], P(('head', 'blk'))
- grad_key: float32 [768, 768], P(('head', 'blk'))
- grad_value: float32 [768, 768], P(('head', 'blk'))
- grad_out: float32 [768, 768], P(None, ('head', 'blk'))
- grad_table: float32 [384], P(('head', 'blk'))
- grad_moe_gain: float32 [768], P(('head', 'blk'))
- grad_router: float32 [768, 8], P(('head', 'blk'))
- grad_expert_in: float32 [8, 768, 3072], P('blk', None, 'head')
- grad_expert_out: float32 [8, 3072, 768], P('blk', 'head')
The draws below stay inside these ranges and needn't reach their ends.
Inputs may be any that keep to these rules, and one draw needn't show every extreme that they name: `seq_lengths`: one sequence, which one drawn from the seed, has exactly 2048 tokens. `rel_buckets`: entry j is the bucket of distance j: j itself for j below half of 32, never falling, and 31 at the last entry. `routes`: in each aligned block of 256 rows (the rows of one device, in the array's order) no expert is named more than 48 times; in some blocks one expert is named exactly 48 times.
All inputs are finite; a program needn't handle non-finite values.
Results may differ from the reference program's by a relative error of at most 0.02.
Values may be sent and summed in bfloat16 or wider, within the bound.
No kernel may reach another device: no remote copies, remote signals or barrier semaphores. Data moves between devices by JAX's collectives and lax.ppermute only.
A program may use at most 256 MiB of HBM per device.

```python
import math
import jax
import jax.numpy as jnp
import numpy as np
from jax import lax

D = 768
HEADS = 12
HEAD_DIM = 64
FF = 3072
NUM_BUCKETS = 32
SEQLEN = 2048
MINLEN = 1024
INNER = 768
SEQS = 4
EXPERTS = 8
TOK_DEV = 256
BLOCK = 256
CAP = 48
N_HEAD = 4
N_BLK = 8
DEVICES = 32


def draw_seq_lengths(key, part):
    key = jax.random.fold_in(key, 11)
    first_key, second_key = jax.random.split(key)
    lengths = jax.random.randint(first_key, (SEQS,), MINLEN, SEQLEN + 1)
    longest_one = jax.random.randint(second_key, (), 0, SEQS)
    return jnp.where(jnp.arange(SEQS) == longest_one, SEQLEN, lengths).astype(jnp.int32)


def draw_rel_buckets(key, part):
    key = jax.random.fold_in(key, 23)
    near_count = NUM_BUCKETS // 2
    picks = jax.random.randint(key, (SEQLEN - near_count,), near_count, NUM_BUCKETS)
    ordered = jnp.sort(picks).astype(jnp.int32)
    ordered = ordered.at[SEQLEN - near_count - 1].set(NUM_BUCKETS - 1)
    return jnp.concatenate([jnp.arange(near_count, dtype=jnp.int32), ordered])


def block_levels(stream_key, shape, shards, least, largest):
    def one(position, shards_of):
        steps = jax.random.uniform(jax.random.fold_in(jax.random.fold_in(stream_key, 6), position), (shards_of,), jnp.float32, least / len(shards), largest / len(shards))
        return jnp.repeat(jnp.exp(steps), shape[position] // shards_of).reshape((-1,) + (1,) * (len(shape) - position - 1))

    level = one(*shards[0])
    for cut in shards[1:]:
        level = level * one(*cut)
    return level


def shared_out(rng, own, number, rows, count, top, reach, lean):
    order = jax.random.permutation(rng, count)
    heavy_load, ordinary = portions_of(count, rows * top, reach, lean, True), portions_of(count, rows * top, reach, lean, False)
    places = jnp.arange(count)

    def named(sizes, turn):
        used = int((sizes > 0).sum())
        fixed = max(1, used // 4)
        moved = fixed + (places - fixed + turn * (used - fixed)) % max(1, count - fixed)
        return jnp.zeros((count,), jnp.int32).at[order[jnp.where(places < fixed, places, moved)]].set(jnp.asarray(sizes, jnp.int32))

    sizes = jnp.where(number % 4 == 0, named(heavy_load, number // 4), named(ordinary, number - number // 4 - 1))
    mixed = jax.random.permutation(jax.random.fold_in(own, 3), count)
    donor, taker = mixed[0:count // 2 * 2:2], mixed[1:count // 2 * 2:2]
    margin = jnp.minimum(sizes[donor] - 1, reach - sizes[taker]) // 2
    margin = jnp.where((donor == order[0]) | (taker == order[0]) | (sizes[taker] == 0), 0, jnp.maximum(margin, 0))
    moved = jax.random.randint(jax.random.fold_in(own, 4), (count // 2,), 0, 1 << 20) % (margin + 1)
    sizes = sizes.at[donor].add(-moved).at[taker].add(moved)
    members = jnp.searchsorted(jnp.cumsum(sizes), jnp.arange(rows * top), side="right").astype(jnp.int32)
    table = members.reshape(top, rows).T
    table = table[jax.random.permutation(jax.random.fold_in(own, 1), rows)]
    turn = jax.random.randint(jax.random.fold_in(own, 2), (rows, 1), 0, top)
    return jnp.take_along_axis(table, (jnp.arange(top)[None, :] + turn) % top, axis=1)


def portions_of(amount, total, most, slope, full):
    loads = [(1 << 20) // math.isqrt(rank ** slope) + 1 for rank in range(1, amount + 1)]
    largest = most if full else min(most, max(-(-total // amount), total * loads[0] // sum(loads)))
    least = 1 if total - largest >= amount - 1 else 0
    holding, rest = [largest] + [least] * (amount - 1), total - largest - least * (amount - 1)
    while rest > 0:
        candidates = [i for i in range(1, amount) if holding[i] < largest] or [i for i in range(1, amount) if holding[i] < most]
        pool, budget = sum([loads[i] for i in candidates]), rest
        for i in candidates:
            addition = min(most - holding[i], max(1, budget * loads[i] // pool), rest)
            holding[i] = holding[i] + addition
            rest = rest - addition
    return np.array(holding)


def scatter_about(own_key, shape, width, bound, shards=(), kind=jnp.bfloat16):
    level = block_levels(own_key, shape, shards, -0.22, 0.18) if shards else 1.0
    result = jax.random.normal(own_key, shape, jnp.float32) * width * level
    return jnp.minimum(jnp.maximum(result, -bound), bound).astype(kind)


def setup_inputs(seed: int = 0) -> dict:
    seeds = jax.random.split(jax.random.key(seed), 16)
    tokens = scatter_about(seeds[0], (SEQLEN, SEQS, D), 1.0, 6.0, ((0, 8), (1, 4)))
    attn_gain = jnp.clip(1.0 + 0.1 * jax.random.normal(seeds[1], (D,), jnp.float32), 0.5, 1.5).astype(jnp.bfloat16)
    w_query = scatter_about(seeds[2], (D, INNER), (4 * D) ** -0.5, 0.109375, ((0, 32),))
    w_key = scatter_about(seeds[3], (D, INNER), (4 * D) ** -0.5, 0.109375, ((0, 32),))
    w_value = scatter_about(seeds[4], (D, INNER), D ** -0.5, 0.21875, ((0, 32),))
    w_out = scatter_about(seeds[5], (INNER, D), (INNER // 16) ** -0.5, 0.875, ((1, 32),))
    bias_table = scatter_about(seeds[6], (NUM_BUCKETS * HEADS,), 0.5, 3.0, ((0, 32),))
    moe_gain = jnp.clip(1.0 + 0.1 * jax.random.normal(seeds[7], (D,), jnp.float32), 0.5, 1.5).astype(jnp.bfloat16)
    w_router = scatter_about(seeds[8], (D, EXPERTS), (2 * D) ** -0.5, 0.15625, ((0, 32),))
    expert_in = scatter_about(seeds[9], (EXPERTS, D, FF), D ** -0.5, 0.21875, ((0, 8), (2, 4)))
    expert_out = scatter_about(seeds[10], (EXPERTS, FF, D), (max(1, FF // (EXPERTS * EXPERTS))) ** -0.5, 0.875, ((0, 8), (1, 4)))
    seq_lengths = draw_seq_lengths(jax.random.fold_in(seeds[15], 71), 0)
    rel_buckets = draw_rel_buckets(jax.random.fold_in(seeds[15], 71), 0)
    routes_keys = jax.random.split(jax.random.fold_in(seeds[13], 1), N_HEAD * SEQLEN * (SEQS // N_HEAD) // TOK_DEV)
    routes_turns = jax.random.permutation(jax.random.fold_in(seeds[13], 3), N_HEAD * SEQLEN * (SEQS // N_HEAD) // TOK_DEV)
    routes = jax.vmap(lambda own, number: shared_out(jax.random.fold_in(seeds[13], 2), own, number, TOK_DEV, EXPERTS, 1, CAP, 1))(routes_keys, routes_turns).reshape((N_HEAD, SEQLEN, SEQS // N_HEAD, 1))
    cotangent = scatter_about(seeds[14], (SEQLEN, SEQS, D), 1.0, 6.0, ((0, 8), (1, 4)))
    return {"tokens": tokens, "attn_gain": attn_gain, "w_query": w_query, "w_key": w_key, "w_value": w_value, "w_out": w_out, "bias_table": bias_table, "moe_gain": moe_gain, "w_router": w_router, "expert_in": expert_in, "expert_out": expert_out, "seq_lengths": seq_lengths, "rel_buckets": rel_buckets, "routes": routes, "cotangent": cotangent}


@jax.custom_vjp
def low(v):
    return lax.optimization_barrier(v.astype(jnp.bfloat16)).astype(jnp.float32)

@jax.custom_vjp
def low_back(v):
    return v

def low_keep(v):
    return (low(v), None)

def low_pass(kept, grad):
    return (grad,)

def back_keep(v):
    return (v, None)

def back_low(kept, grad):
    return (low(grad),)
low.defvjp(low_keep, low_pass)
low_back.defvjp(back_keep, back_low)
norm_eps = 1e-06
masked_score = -1e+30

def rms_norm(values, gain):
    return values * lax.rsqrt(lax.optimization_barrier(jnp.mean(values * values, axis=-1, keepdims=True)) + norm_eps) * gain

def attend_block(inputs, keys, values, length, table, rel_buckets):
    queries, query_positions = inputs
    key_positions = jnp.arange(SEQLEN, dtype=jnp.int32)
    raw = low_back(jnp.einsum('qhd,khd->hqk', queries, keys, precision=lax.Precision.HIGHEST))
    distance = jnp.clip(query_positions[:, None] - key_positions[None, :], 0, SEQLEN - 1).astype(jnp.int32)
    bias = jnp.take(table, jnp.take(rel_buckets, distance, axis=0), axis=0)
    scores = raw + jnp.transpose(bias, (2, 0, 1))
    valid = ((key_positions[None, :] <= query_positions[:, None]) & (key_positions[None, :] < length))[None]
    scores = jnp.where(valid, scores, masked_score)
    row_top = lax.optimization_barrier(jnp.max(scores, axis=-1, keepdims=True))
    weights = jnp.where(valid, jnp.exp(scores - row_top), 0.0)
    probs = weights / lax.optimization_barrier(jnp.sum(weights, axis=-1, keepdims=True))
    return jnp.einsum('hqk,khd->qhd', low(probs), values, precision=lax.Precision.HIGHEST)

def attend_sequence(queries, keys, values, length, table, rel_buckets):
    block_len = min(512, SEQLEN)
    query_blocks = queries.reshape(SEQLEN // block_len, block_len, HEADS, HEAD_DIM)
    position_blocks = jnp.arange(SEQLEN, dtype=jnp.int32).reshape(SEQLEN // block_len, block_len)

    def one_block(inputs):
        return attend_block(inputs, keys, values, length, table, rel_buckets)
    mixed = lax.map(jax.checkpoint(one_block), (query_blocks, position_blocks))
    return mixed.reshape(SEQLEN, HEADS, HEAD_DIM)

def one_expert(inputs):
    expert_rows, weight_in, weight_back = inputs
    pre = low_back(jnp.dot(expert_rows, weight_in, precision=lax.Precision.HIGHEST))
    activated = low(jax.nn.gelu(pre))
    return low_back(low(jnp.dot(activated, weight_back, precision=lax.Precision.HIGHEST)))

def forward(tokens, attn_gain, w_query, w_key, w_value, w_out, bias_table, moe_gain, w_router, expert_in, expert_out, seq_lengths, rel_buckets, routes):
    table = bias_table.reshape(NUM_BUCKETS, HEADS)
    attn_in = low(rms_norm(tokens, attn_gain))

    def project(weight):
        made = jnp.einsum('lsd,de->sle', attn_in, weight, precision=lax.Precision.HIGHEST)
        return low_back(low(made)).reshape(SEQS, SEQLEN, HEADS, HEAD_DIM)
    queries = project(w_query)
    keys = project(w_key)
    values = project(w_value)

    def one_sequence(inputs):
        seq_queries, seq_keys, seq_values, length = inputs
        return attend_sequence(seq_queries, seq_keys, seq_values, length, table, rel_buckets)
    heads = lax.map(one_sequence, (queries, keys, values, seq_lengths))
    attn_heads = low_back(low(jnp.transpose(heads, (1, 0, 2, 3)).reshape(SEQLEN, SEQS, HEADS * HEAD_DIM)))
    hidden = tokens + low_back(jnp.einsum('lse,ed->lsd', attn_heads, w_out, precision=lax.Precision.HIGHEST))
    group_seqs = SEQS // N_HEAD
    hidden_dev = jnp.transpose(hidden.reshape(N_BLK, BLOCK, N_HEAD, group_seqs, D), (2, 0, 1, 3, 4)).reshape(DEVICES, TOK_DEV, D)
    moe_in = low(rms_norm(hidden_dev, moe_gain))
    logits = low_back(jnp.einsum('ntd,de->nte', moe_in, w_router, precision=lax.Precision.HIGHEST))
    router_probs = jax.nn.softmax(logits, axis=-1)
    route = routes.reshape(DEVICES, TOK_DEV).astype(jnp.int32)
    chosen = route[..., None] == jnp.arange(EXPERTS, dtype=jnp.int32)
    gate = lax.optimization_barrier(jnp.sum(jnp.where(chosen, router_probs, 0.0), axis=-1))
    filled = jnp.cumsum(chosen.astype(jnp.int32), axis=1).astype(jnp.int32)
    slot = lax.optimization_barrier(jnp.sum(jnp.where(chosen, filled - 1, 0), axis=-1)).astype(jnp.int32)
    target = (route * CAP + slot).astype(jnp.int32)
    device_rows = jnp.broadcast_to(jnp.arange(DEVICES, dtype=jnp.int32)[:, None], (DEVICES, TOK_DEV))
    sent = low_back(moe_in)
    buffer = jnp.zeros((DEVICES, EXPERTS * CAP, D), jnp.float32).at[device_rows, target].set(sent)
    grouped = jnp.transpose(buffer.reshape(DEVICES, EXPERTS, CAP, D), (1, 0, 2, 3)).reshape(EXPERTS, DEVICES * CAP, D)
    done = lax.map(jax.checkpoint(one_expert), (grouped, expert_in, expert_out))
    back = jnp.transpose(done.reshape(EXPERTS, DEVICES, CAP, D), (1, 0, 2, 3)).reshape(DEVICES, EXPERTS * CAP, D)
    expert_tok = back[device_rows, target]
    mixed = hidden_dev + gate[..., None] * expert_tok
    return jnp.transpose(mixed.reshape(N_HEAD, N_BLK, BLOCK, group_seqs, D), (1, 2, 0, 3, 4)).reshape(SEQLEN, SEQS, D)

def reference(tokens, attn_gain, w_query, w_key, w_value, w_out, bias_table, moe_gain, w_router, expert_in, expert_out, seq_lengths, rel_buckets, routes, cotangent):
    weight_arrays = (tokens, attn_gain, w_query, w_key, w_value, w_out, bias_table, moe_gain, w_router, expert_in, expert_out)
    floats = tuple((array.astype(jnp.float32) for array in weight_arrays))

    def apply(tokens_f, attn_gain_f, query_f, key_f, value_f, out_f, table_f, moe_gain_f, router_f, expert_in_f, expert_out_f):
        return forward(tokens_f, attn_gain_f, query_f, key_f, value_f, out_f, table_f, moe_gain_f, router_f, expert_in_f, expert_out_f, seq_lengths, rel_buckets, routes)
    output, pull = jax.vjp(apply, *floats)
    grads = pull(cotangent.astype(jnp.float32))
    return (output.astype(jnp.bfloat16), grads[0], grads[1], grads[2], grads[3], grads[4], grads[5], grads[6], grads[7], grads[8], grads[9], grads[10])
```

```python
import functools
import math

import jax
import jax.numpy as jnp
from jax import lax
from jax.experimental import pallas as pl
from jax.experimental.pallas import tpu as pltpu
from jax.sharding import PartitionSpec as P

HEADS = 12
HEAD_DIM = 64
NUM_BUCKETS = 32


norm_eps = 1e-06
masked_score = -1e30


def inverse_rms(values):
    return lax.rsqrt(jnp.mean(values * values, axis=-1, keepdims=True) + norm_eps)


def norm_backward(grad_normed, source, inv_scale, gain):
    weighted = grad_normed * gain
    inner_mean = jnp.mean(weighted * source, axis=-1, keepdims=True)
    grad_source = inv_scale * weighted - source * (inv_scale * inv_scale * inv_scale) * inner_mean
    grad_gain = jnp.sum(grad_normed * source * inv_scale, axis=0)
    return (grad_source, grad_gain)


def same_state(running):
    return running


def bucket_bounds(rel_buckets):
    bucket_count = NUM_BUCKETS
    labels = jnp.arange(bucket_count, dtype=jnp.int32)
    starts = jnp.sum((rel_buckets[:, None] < labels[None, :]).astype(jnp.int32), axis=0)
    ends = jnp.concatenate([starts[1:], jnp.full((1,), rel_buckets.shape[0] + 1, jnp.int32)])
    return (starts, ends)


def bias_terms(query_positions, key_positions, bounds, table32):
    starts, ends = bounds
    distance = jnp.maximum(query_positions[:, None] - key_positions[None, :], 0)[:, :, None]
    inside = (distance >= starts[None, None, :]) & (distance < ends[None, None, :])
    onehot = inside.astype(jnp.bfloat16)
    bias = jnp.einsum(
        "qkb,bh->hqk", onehot, table32.astype(jnp.bfloat16), preferred_element_type=jnp.float32
    )
    return (onehot, bias)


def block_scores(queries, keys, query_positions, key_positions, seq_lengths, bounds, table32):
    onehot, bias = bias_terms(query_positions, key_positions, bounds, table32)
    raw = jnp.einsum("qshd,kshd->hsqk", queries, keys, preferred_element_type=jnp.float32)
    causal = key_positions[None, :] <= query_positions[:, None]
    present = key_positions[None, :] < seq_lengths[:, None]
    valid = causal[None, :, :] & present[:, None, :]
    return (raw + bias[:, None, :, :], valid[None], onehot)


def attend_step(
    running, queries, keys, values, query_positions, key_positions, seq_lengths, bounds, table32
):
    row_top, row_total, weighted = running
    scores, valid, unused = block_scores(
        queries, keys, query_positions, key_positions, seq_lengths, bounds, table32
    )
    scores = jnp.where(valid, scores, masked_score)
    new_top = jnp.maximum(row_top, jnp.max(scores, axis=-1))
    weights = jnp.where(valid, jnp.exp(scores - new_top[..., None]), 0.0)
    decay = jnp.exp(row_top - new_top)
    row_total = row_total * decay + jnp.sum(weights, axis=-1)
    mixed = jnp.einsum(
        "hsqk,kshd->qshd", weights.astype(jnp.bfloat16), values, preferred_element_type=jnp.float32
    )
    weighted = weighted * jnp.transpose(decay, (2, 1, 0))[..., None] + mixed
    return (new_top, row_total, weighted)


def grad_step(
    queries,
    grad_heads,
    log_total,
    delta,
    query_positions,
    keys,
    values,
    key_positions,
    seq_lengths,
    bounds,
    table32,
):
    scores, valid, onehot = block_scores(
        queries, keys, query_positions, key_positions, seq_lengths, bounds, table32
    )
    probs = jnp.where(valid, jnp.exp(scores - jnp.transpose(log_total, (2, 1, 0))[..., None]), 0.0)
    grad_probs = jnp.einsum(
        "qshd,kshd->hsqk", grad_heads, values, preferred_element_type=jnp.float32
    )
    grad_scores = probs * (grad_probs - jnp.transpose(delta, (2, 1, 0))[..., None])
    grad_table = jnp.einsum(
        "hqk,qkb->bh",
        jnp.sum(grad_scores, axis=1),
        onehot.astype(jnp.float32),
        precision=lax.Precision.HIGHEST,
    )
    low_scores = grad_scores.astype(jnp.bfloat16)
    grad_queries = jnp.einsum(
        "hsqk,kshd->qshd", low_scores, keys, preferred_element_type=jnp.float32
    )
    grad_keys = jnp.einsum(
        "hsqk,qshd->kshd", low_scores, queries, preferred_element_type=jnp.float32
    )
    grad_values = jnp.einsum(
        "hsqk,qshd->kshd",
        probs.astype(jnp.bfloat16),
        grad_heads,
        preferred_element_type=jnp.float32,
    )
    return (grad_queries, grad_keys, grad_values, grad_table)


def on_device(
    tokens,
    attn_gain,
    w_query,
    w_key,
    w_value,
    w_out,
    bias_table,
    moe_gain,
    w_router,
    expert_in,
    expert_out,
    seq_lengths,
    rel_buckets,
    routes,
    cotangent,
):
    head_count = lax.axis_size("head")
    blk_count = lax.axis_size("blk")
    head_index = lax.axis_index("head")
    blk_index = lax.axis_index("blk")
    block_rows, group_seqs, width = tokens.shape
    seq_count = group_seqs * head_count
    tok_rows = block_rows * group_seqs
    local_heads = HEADS // head_count
    head_width = local_heads * HEAD_DIM
    group_rows = block_rows * max(1, blk_count // 8)
    longest = jnp.max(seq_lengths)
    query_first = blk_index * block_rows
    query_last = query_first + block_rows - 1
    query_positions = query_first + jnp.arange(block_rows, dtype=jnp.int32)
    bounds = bucket_bounds(rel_buckets)
    fetched = (
        lax.all_gather(w_query, ("head", "blk"), axis=0, tiled=True),
        lax.all_gather(w_key, ("head", "blk"), axis=0, tiled=True),
        lax.all_gather(w_value, ("head", "blk"), axis=0, tiled=True),
        lax.all_gather(w_out, ("head", "blk"), axis=1, tiled=True),
        lax.all_gather(attn_gain, ("head", "blk"), axis=0, tiled=True),
        lax.all_gather(bias_table, ("head", "blk"), axis=0, tiled=True),
        lax.all_gather(moe_gain, ("head", "blk"), axis=0, tiled=True),
        lax.all_gather(w_router, ("head", "blk"), axis=0, tiled=True),
    )
    full_query, full_key, full_value, full_out, gain_attn, table_flat, gain_moe, full_router = (
        fetched
    )
    inner_width = full_query.shape[1]
    table_all = table_flat.astype(jnp.float32).reshape(NUM_BUCKETS, HEADS)
    table32 = lax.dynamic_slice_in_dim(table_all, head_index * local_heads, local_heads, 1)
    gain_attn32 = gain_attn.astype(jnp.float32)
    gain_moe32 = gain_moe.astype(jnp.float32)

    def to_heads(values):
        parts = values.shape[1]
        shaped = values.reshape(block_rows, group_seqs, parts, head_count, head_width)
        moved = lax.all_to_all(shaped, "head", split_axis=3, concat_axis=1, tiled=True)
        return moved.reshape(block_rows, seq_count, parts, local_heads, HEAD_DIM)

    def to_tokens(values):
        parts = values.shape[2]
        shaped = values.reshape(block_rows, seq_count, parts, 1, head_width)
        moved = lax.all_to_all(shaped, "head", split_axis=1, concat_axis=3, tiled=True)
        return moved.reshape(tok_rows, parts, inner_width)

    source = tokens.astype(jnp.float32).reshape(tok_rows, width)
    inv_attn = inverse_rms(source)
    attn_in = (source * inv_attn * gain_attn32).astype(jnp.bfloat16)
    stacked_weights = jnp.stack((full_query, full_key, full_value))
    projected = jnp.einsum(
        "td,cde->tce", attn_in, stacked_weights, preferred_element_type=jnp.float32
    ).astype(jnp.bfloat16)
    heads_in = to_heads(projected)
    queries = heads_in[:, :, 0]
    keys = heads_in[:, :, 1]
    values = heads_in[:, :, 2]
    start_state = (
        jnp.full((local_heads, seq_count, block_rows), masked_score, jnp.float32),
        jnp.zeros((local_heads, seq_count, block_rows), jnp.float32),
        jnp.zeros((block_rows, seq_count, local_heads, HEAD_DIM), jnp.float32),
    )
    key_piece = lax.all_gather(keys, "blk", axis=0, tiled=True)
    value_piece = lax.all_gather(values, "blk", axis=0, tiled=True)
    piece_rows = key_piece.shape[0]
    part_rows = math.gcd(piece_rows, group_rows)

    def forward_one_part(step_index, inner_state):
        offset = step_index * part_rows
        key_part = lax.dynamic_slice_in_dim(key_piece, offset, part_rows, 0)
        value_part = lax.dynamic_slice_in_dim(value_piece, offset, part_rows, 0)
        key_positions = offset + jnp.arange(part_rows, dtype=jnp.int32)

        def attend_now(current):
            return attend_step(
                current,
                queries,
                key_part,
                value_part,
                query_positions,
                key_positions,
                seq_lengths,
                bounds,
                table32,
            )

        skipped = (offset > query_last) | (offset >= longest)
        return lax.cond(skipped, same_state, attend_now, inner_state)

    row_top, row_total, weighted = lax.fori_loop(
        0, piece_rows // part_rows, forward_one_part, start_state
    )
    attn_heads = (weighted / jnp.transpose(row_total, (2, 1, 0))[..., None]).astype(jnp.bfloat16)
    log_total = jnp.transpose(row_top + jnp.log(row_total), (2, 1, 0))
    attn_tok = to_tokens(attn_heads[:, :, None])[:, 0]
    branch = jnp.dot(attn_tok, full_out, preferred_element_type=jnp.float32)
    hidden = source + branch
    expert_count = full_router.shape[1]
    local_experts = expert_in.shape[0]
    capacity = max(2, 3 * tok_rows // (2 * expert_count))
    inv_moe = inverse_rms(hidden)
    moe_in = (hidden * inv_moe * gain_moe32).astype(jnp.bfloat16)
    logits = jnp.dot(moe_in, full_router, preferred_element_type=jnp.float32)
    router_probs = jax.nn.softmax(logits, axis=-1)
    route_flat = routes.reshape(tok_rows)
    chosen = route_flat[:, None] == jnp.arange(expert_count, dtype=jnp.int32)[None, :]
    gate = jnp.sum(jnp.where(chosen, router_probs, 0.0), axis=-1)
    filled = jnp.cumsum(chosen.astype(jnp.int32), axis=0)
    slot = jnp.sum(jnp.where(chosen, filled - 1, 0), axis=-1)
    target = route_flat * capacity + slot
    dispatch = (
        target[:, None] == jnp.arange(expert_count * capacity, dtype=jnp.int32)[None, :]
    ).astype(jnp.bfloat16)

    def to_buffer(token_rows):
        packed = jnp.einsum(
            "tj,td->jd", dispatch, token_rows, preferred_element_type=jnp.float32
        ).astype(jnp.bfloat16)
        return packed.reshape(blk_count, local_experts, capacity, width)

    def from_buffer(buffer):
        return jnp.dot(
            dispatch,
            buffer.reshape(expert_count * capacity, width),
            preferred_element_type=jnp.float32,
        )

    def to_experts(buffer):
        return lax.all_to_all(buffer, "blk", split_axis=0, concat_axis=0, tiled=True)

    def all_rows(buffer):
        return lax.all_gather(buffer, "head", axis=0, tiled=True)

    def summed_rows(partial_terms):
        return lax.psum_scatter(
            partial_terms.astype(jnp.bfloat16), "head", scatter_dimension=0, tiled=True
        ).astype(jnp.float32)

    def to_owners(buffer):
        return lax.all_to_all(buffer, "blk", split_axis=0, concat_axis=0, tiled=True)

    expert_rows_in = all_rows(to_experts(to_buffer(moe_in)))
    expert_pre = jnp.einsum(
        "necd,edf->necf", expert_rows_in, expert_in, preferred_element_type=jnp.float32
    )
    expert_act, gelu_pull = jax.vjp(jax.nn.gelu, expert_pre)
    expert_low = expert_act.astype(jnp.bfloat16)
    expert_terms = jnp.einsum(
        "necf,efd->necd", expert_low, expert_out, preferred_element_type=jnp.float32
    )
    expert_tok = from_buffer(to_owners(summed_rows(expert_terms).astype(jnp.bfloat16)))
    result = hidden + gate[:, None] * expert_tok
    grad_result = cotangent.astype(jnp.float32).reshape(tok_rows, width)
    grad_expert_tok = (gate[:, None] * grad_result).astype(jnp.bfloat16)
    grad_gate = jnp.sum(grad_result * expert_tok, axis=-1)
    grad_logits = (
        router_probs * (jnp.where(chosen, grad_gate[:, None], 0.0) - (gate * grad_gate)[:, None])
    ).astype(jnp.bfloat16)
    grad_router = jnp.einsum("td,te->de", moe_in, grad_logits, preferred_element_type=jnp.float32)
    grad_rows = all_rows(to_experts(to_buffer(grad_expert_tok)))
    grad_act = jnp.einsum(
        "necd,efd->necf", grad_rows, expert_out, preferred_element_type=jnp.float32
    )
    grad_pre = gelu_pull(grad_act)[0].astype(jnp.bfloat16)
    grad_expert_out = jnp.einsum(
        "necf,necd->efd", expert_low, grad_rows, preferred_element_type=jnp.float32
    )
    grad_expert_in = jnp.einsum(
        "necd,necf->edf", expert_rows_in, grad_pre, preferred_element_type=jnp.float32
    )
    grad_back = jnp.einsum(
        "necf,edf->necd", grad_pre, expert_in, preferred_element_type=jnp.float32
    )
    grad_moe_in = from_buffer(to_owners(summed_rows(grad_back).astype(jnp.bfloat16)))
    grad_moe_in = grad_moe_in + jnp.einsum(
        "te,de->td", grad_logits, full_router, preferred_element_type=jnp.float32
    )
    grad_norm_moe, grad_gain_moe = norm_backward(grad_moe_in, hidden, inv_moe, gain_moe32)
    grad_hidden = grad_result + grad_norm_moe
    grad_branch = grad_hidden.astype(jnp.bfloat16)
    grad_out_w = jnp.einsum("te,td->ed", attn_tok, grad_branch, preferred_element_type=jnp.float32)
    grad_attn_tok = jnp.einsum(
        "td,ed->te", grad_branch, full_out, preferred_element_type=jnp.float32
    ).astype(jnp.bfloat16)
    grad_heads = to_heads(grad_attn_tok[:, None])[:, :, 0]
    delta = jnp.sum(grad_heads.astype(jnp.float32) * attn_heads.astype(jnp.float32), axis=-1)
    all_keys = lax.all_gather(keys, "blk", axis=0, tiled=True)
    all_values = lax.all_gather(values, "blk", axis=0, tiled=True)
    total_rows = all_keys.shape[0]
    step_rows = math.gcd(total_rows, group_rows)
    zero_heads = jnp.zeros((block_rows, seq_count, local_heads, HEAD_DIM), jnp.float32)
    zero_table = jnp.zeros(table32.shape, jnp.float32)

    def query_side(step_index, running):
        offset = step_index * step_rows
        key_block = lax.dynamic_slice_in_dim(all_keys, offset, step_rows, 0)
        value_block = lax.dynamic_slice_in_dim(all_values, offset, step_rows, 0)
        key_positions = offset + jnp.arange(step_rows, dtype=jnp.int32)

        def query_compute(current):
            grads = grad_step(
                queries,
                grad_heads,
                log_total,
                delta,
                query_positions,
                key_block,
                value_block,
                key_positions,
                seq_lengths,
                bounds,
                table32,
            )
            return (current[0] + grads[0], current[1] + grads[3])

        skipped = (offset > query_last) | (offset >= longest)
        return lax.cond(skipped, same_state, query_compute, running)

    grad_queries, grad_table = lax.fori_loop(
        0, total_rows // step_rows, query_side, (zero_heads, zero_table)
    )
    all_totals, all_deltas = (
        lax.all_gather(log_total, "blk", axis=0, tiled=True),
        lax.all_gather(delta, "blk", axis=0, tiled=True),
    )
    query_piece = lax.all_gather(queries, "blk", axis=0, tiled=True)
    grad_piece = lax.all_gather(grad_heads, "blk", axis=0, tiled=True)
    piece_rows = query_piece.shape[0]
    key_part_rows = math.gcd(piece_rows, group_rows)

    def key_one_part(step_index, inner_state):
        offset = step_index * key_part_rows
        query_part = lax.dynamic_slice_in_dim(query_piece, offset, key_part_rows, 0)
        grad_part = lax.dynamic_slice_in_dim(grad_piece, offset, key_part_rows, 0)
        total_part = lax.dynamic_slice_in_dim(all_totals, offset, key_part_rows, 0)
        delta_part = lax.dynamic_slice_in_dim(all_deltas, offset, key_part_rows, 0)
        part_positions = offset + jnp.arange(key_part_rows, dtype=jnp.int32)

        def key_compute(current):
            grads = grad_step(
                query_part,
                grad_part,
                total_part,
                delta_part,
                part_positions,
                keys,
                values,
                query_positions,
                seq_lengths,
                bounds,
                table32,
            )
            return (current[0] + grads[1], current[1] + grads[2])

        skipped = (offset + key_part_rows - 1 < query_first) | (query_first >= longest)
        return lax.cond(skipped, same_state, key_compute, inner_state)

    grad_keys, grad_values = lax.fori_loop(
        0, piece_rows // key_part_rows, key_one_part, (zero_heads, zero_heads)
    )
    grad_stack = jnp.stack((grad_queries, grad_keys, grad_values), axis=2).astype(jnp.bfloat16)
    grad_projected = to_tokens(grad_stack)
    grad_weights = jnp.einsum(
        "td,tce->cde", attn_in, grad_projected, preferred_element_type=jnp.float32
    )
    grad_attn_in = jnp.einsum(
        "tce,cde->td", grad_projected, stacked_weights, preferred_element_type=jnp.float32
    )
    grad_norm_attn, grad_gain_attn = norm_backward(grad_attn_in, source, inv_attn, gain_attn32)
    grad_tokens = grad_hidden + grad_norm_attn
    table_terms = lax.dynamic_update_slice_in_dim(
        jnp.zeros((NUM_BUCKETS, HEADS), jnp.float32), grad_table, head_index * local_heads, 1
    ).reshape(NUM_BUCKETS * HEADS)
    reduced = (
        lax.psum_scatter(grad_weights[0], ("head", "blk"), scatter_dimension=0, tiled=True),
        lax.psum_scatter(grad_weights[1], ("head", "blk"), scatter_dimension=0, tiled=True),
        lax.psum_scatter(grad_weights[2], ("head", "blk"), scatter_dimension=0, tiled=True),
        lax.psum_scatter(grad_out_w, ("head", "blk"), scatter_dimension=1, tiled=True),
        lax.psum_scatter(grad_gain_attn, ("head", "blk"), scatter_dimension=0, tiled=True),
        lax.psum_scatter(table_terms, ("head", "blk"), scatter_dimension=0, tiled=True),
        lax.psum_scatter(grad_gain_moe, ("head", "blk"), scatter_dimension=0, tiled=True),
        lax.psum_scatter(grad_router, ("head", "blk"), scatter_dimension=0, tiled=True),
    )
    return (
        result.astype(jnp.bfloat16).reshape(tokens.shape),
        grad_tokens.reshape(tokens.shape),
        reduced[4],
        reduced[0],
        reduced[1],
        reduced[2],
        reduced[3],
        reduced[5],
        reduced[6],
        reduced[7],
        grad_expert_in,
        grad_expert_out,
    )


BF = jnp.bfloat16
F4 = jnp.float32
NEG = -1e30
QB = 256
TILE = 512
LANES = 128


def dot(left, right, left_dim=1, right_dim=0):
    dims = (((left_dim,), (right_dim,)), ((), ()))
    return lax.dot_general(left, right, dims, preferred_element_type=F4)


def iota(shape, dim):
    return lax.broadcasted_iota(jnp.int32, shape, dim)


def vmem_call(body, scalars, args, outs, scratch=(), mem=40, flops=0):
    nbytes = sum(math.prod(a.shape) * a.dtype.itemsize for a in tuple(args) + tuple(outs))
    return pl.pallas_call(
        body,
        out_shape=tuple(outs),
        in_specs=[pl.BlockSpec(memory_space=pltpu.SMEM)]
        + [pl.BlockSpec(memory_space=pltpu.VMEM)] * len(args),
        out_specs=tuple(pl.BlockSpec(memory_space=pltpu.VMEM) for _ in outs),
        scratch_shapes=list(scratch),
        compiler_params=pltpu.CompilerParams(vmem_limit_bytes=mem * 1024 * 1024),
        cost_estimate=pl.CostEstimate(flops=flops, bytes_accessed=nbytes, transcendentals=0),
    )(scalars, *args)


def shaped(shape, dtype):
    return jax.ShapeDtypeStruct(shape, dtype)


def ring_block(step, own_blk, ring_len):
    half = ring_len // 2
    place = jnp.where((own_blk & 1) == 0, own_blk >> 1, ring_len - 1 - (own_blk >> 1))
    place = (place + step) & (ring_len - 1)
    return jnp.where(place < half, 2 * place, 2 * ring_len - 1 - 2 * place)


def ring_steps(ring_len):
    steps = [0]
    for hop in range(1, ring_len // 2):
        steps += [-hop, hop]
    return steps + [ring_len // 2]


def shared_turn(position_block):
    return ((position_block & 1) + (position_block >> 1)) & 1


def norm_scale(values):
    return lax.rsqrt(jnp.mean(values * values, axis=-1, keepdims=True) + norm_eps)


def head_tile(block, head, place):
    tile = block[:, LANES * (head // 2) : LANES * (head // 2) + LANES].astype(F4)
    return tile if head % 2 == place else pltpu.roll(tile, HEAD_DIM, 1)


def pack_units(n, sc, wq, wk, wv, misc, *rest):
    outs, buf = rest[:n], rest[n]
    rows = wq.shape[0]
    lane = iota((rows, LANES), 1)
    buf[...] = jnp.zeros(buf.shape, F4)
    for j in range(n):
        pair, turn = j // 2, j % 2
        for c, weight in enumerate((wq, wk, wv)):
            own = head_tile(weight, 3 * pair + turn, 0)
            both = head_tile(weight, 3 * pair + 2, 1)
            buf[j, 0:rows, LANES * c : LANES * c + LANES] = jnp.where(lane < HEAD_DIM, own, both)
        buf[j, 0:rows, 3 * LANES : 4 * LANES] = misc[...].astype(F4)
    for k in range(n):
        outs[k][...] = buf[sc[0] ^ k].astype(BF)


def place_rows(sc, n, rows, parts, dest):
    for kk, part in enumerate(parts):
        for k in range(n):
            first = pl.multiple_of(((sc[1] ^ kk) * n + (sc[0] ^ k)) * rows, 8)
            dest[pl.ds(first, rows), :] = part[k].astype(F4)[0:rows]


def unpack_units(n, rows, sc, p0, p1, p2, p3, unit_w, misc, misc_t, buf):
    place_rows(sc, n, rows, (p0, p1, p2, p3), buf)
    unit_w[...] = buf[:, 0 : 3 * LANES].astype(BF)
    tail = buf[:, 3 * LANES : 4 * LANES]
    misc[...] = tail.astype(BF)
    misc_t[...] = jnp.transpose(tail)


def unpack_rows(n, rows, sc, p0, p1, p2, p3, out, buf):
    place_rows(sc, n, rows, (p0, p1, p2, p3), buf)
    out[...] = buf[...].astype(BF)


def unpack_stack(n, rows, sc, p0, p1, p2, p3, out, buf):
    parts = (p0, p1, p2, p3)
    width = p0.shape[-1]
    for kk, part in enumerate(parts):
        for k in range(n):
            first = pl.multiple_of(((sc[1] ^ kk) * n + (sc[0] ^ k)) * rows, 8)
            block = part[k].astype(F4)
            for c in range(3):
                buf[pl.ds(first, rows), c * width : (c + 1) * width] = block[c * rows : (c + 1) * rows]
    out[...] = buf[...].astype(BF)


def bias_strips(sc, windows, out):
    row = iota((8, TILE), 0)
    for unit in range(2):
        out[unit, 0] = jnp.full((QB, QB), NEG, F4)
        for far in range(windows.shape[1]):
            flat = jnp.broadcast_to(windows[unit, far : far + 1, :], (8, TILE))
            turned = flat
            for c in range(1, 8):
                turned = jnp.where(row == c, pltpu.roll(flat, c, 1), turned)
            for group in range(QB // 8):
                moved = turned if group == 0 else pltpu.roll(turned, 8 * group, 1)
                strip = moved[:, QB:]
                if far == 0:
                    after = iota((8, QB), 1) >= iota((8, QB), 0) + 8 * group
                    strip = jnp.where(after, strip, NEG)
                out[unit, far + 1, 8 * group : 8 * group + 8, :] = strip


def project_blocks(layout, sc, *refs):
    count = sum(layout)
    blocks, (misc_t, unit_w), outs = refs[:count], refs[count : count + 2], refs[count + 2 :]
    gain = misc_t[0:1, :]
    at = 0
    for i, parts in enumerate(layout):
        block = jnp.concatenate([blocks[at + q][...].astype(F4) for q in range(parts)], axis=0)
        at += parts
        normed = (block * norm_scale(block) * gain).astype(BF)
        made = dot(normed, unit_w[...])
        outs[3 * i][...] = normed
        outs[3 * i + 1][...] = made.astype(BF)
        outs[3 * i + 2][...] = jnp.transpose(made).astype(BF)


def unit_operands(n, sc, rows_refs, cols_refs, key_own, key_both, query_t, key_t, value_t, value_r):
    lane = iota((QB, LANES), 1)
    row = iota((QB, LANES), 0)
    for i, step in enumerate(ring_steps(n)):
        first = pl.multiple_of(ring_block(step, sc[0], n) * QB, QB)
        keys = rows_refs[i][:, LANES : 2 * LANES].astype(F4)
        hidden_key = jnp.where(first + row < sc[2], 0.0, NEG)
        own = jnp.where(lane < HEAD_DIM, keys, jnp.where(lane == HEAD_DIM, hidden_key, 0.0))
        both = jnp.where(lane >= HEAD_DIM, keys, jnp.where(lane == 0, hidden_key, 0.0))
        key_own[pl.ds(first, QB), :] = own.astype(BF)
        key_both[pl.ds(first, QB), :] = both.astype(BF)
        query_t[:, pl.ds(first, QB)] = cols_refs[i][0:LANES, :]
        if key_t is not None:
            key_t[:, pl.ds(first, QB)] = cols_refs[i][LANES : 2 * LANES, :]
        if value_t is not None:
            value_t[:, pl.ds(first, QB)] = cols_refs[i][2 * LANES : 3 * LANES, :]
        if value_r is not None:
            value_r[pl.ds(first, QB), :] = rows_refs[i][:, 2 * LANES : 3 * LANES]


def unit_half(unit, half, other):
    return jnp.concatenate([half, other] if unit == 0 else [other, half], axis=0)


def ones_row(cols):
    return jnp.where(iota((HEAD_DIM, cols), 0) == 0, 1.0, 0.0).astype(BF)


def strip_tile(bias, unit, far, cols):
    def piece(key_half, query_half):
        return bias[unit, jnp.maximum(far + query_half - key_half, -1) + 1]

    if cols == TILE:
        return jnp.concatenate(
            [
                jnp.concatenate([piece(0, 0), piece(0, 1)], axis=1),
                jnp.concatenate([piece(1, 0), piece(1, 1)], axis=1),
            ],
            axis=0,
        )
    return jnp.concatenate([piece(0, 0), piece(1, 0)], axis=0)


def attend_units(n, sc, *refs):
    rows_refs, cols_refs, bias = refs[0:n], refs[n : 2 * n], refs[2 * n]
    outs = refs[2 * n + 1 : 3 * n + 1]
    logs = refs[3 * n + 1]
    key_own, key_both, query_t, value_t, heads = refs[3 * n + 2 :]
    turn = sc[0] & 1
    unit_operands(n, sc, rows_refs, cols_refs, key_own, key_both, query_t, None, value_t, None)
    heads[...] = jnp.zeros(heads.shape, F4)
    logs[...] = jnp.zeros(logs.shape, F4)

    def one_tile(unit, first_block, cols, last):
        key_ref = key_own if unit == 0 else key_both
        lo = HEAD_DIM * unit
        start = pl.multiple_of(first_block * QB, QB)
        queries = unit_half(
            unit, query_t[lo : lo + HEAD_DIM, pl.ds(start, cols)], ones_row(cols)
        )

        def step(part, state):
            top, total, mixed = state
            key_at = pl.multiple_of(part * TILE, TILE)
            scores = dot(key_ref[pl.ds(key_at, TILE), :], queries)
            scores = scores + strip_tile(bias, unit, first_block - 2 * part, cols)
            new_top = jnp.maximum(top, jnp.max(scores, axis=0, keepdims=True))
            weights = jnp.exp(scores - new_top)
            decay = jnp.exp(top - new_top)
            total = total * decay + jnp.sum(weights, axis=0, keepdims=True)
            added = dot(value_t[lo : lo + HEAD_DIM, pl.ds(key_at, TILE)], weights.astype(BF))
            return (new_top, total, mixed * decay + added)

        zero = jnp.zeros((1, cols), F4)
        top, total, mixed = lax.fori_loop(
            0, last + 1, step, (zero + NEG, zero, jnp.zeros((HEAD_DIM, cols), F4))
        )
        made = mixed / total
        log_total = top + jnp.log(total)
        for q in range(cols // QB):
            heads[first_block + q, lo : lo + HEAD_DIM, :] = made[:, q * QB : (q + 1) * QB]
            logs[unit * n + first_block + q] = log_total[:, q * QB : (q + 1) * QB]

    def own_tile(i, carry):
        one_tile(0, 2 * i, TILE, i)
        return carry

    def both_tile(i, carry):
        one_tile(1, 2 * i + ((i + turn) & 1), QB, i)
        return carry

    lax.fori_loop(0, n // 2, own_tile, 0)
    lax.fori_loop(0, n // 2, both_tile, 0)
    for k in range(n):
        outs[k][...] = heads[sc[0] ^ k].astype(BF)


def unit_grads(n, sc, *refs):
    rows_refs, cols_refs, bias = refs[0:n], refs[n : 2 * n], refs[2 * n]
    head_refs, grad_refs = refs[2 * n + 1 : 3 * n + 1], refs[3 * n + 1 : 4 * n + 1]
    logs = refs[4 * n + 1]
    outs = refs[4 * n + 2 : 5 * n + 2]
    stacked, table = refs[5 * n + 2 : 5 * n + 4]
    (key_own, key_both, query_t, key_t, value_r, grad_t, delta, grad_k, grad_v, strips) = refs[
        5 * n + 4 :
    ]
    turn = sc[0] & 1
    unit_operands(n, sc, rows_refs, cols_refs, key_own, key_both, query_t, key_t, None, value_r)
    for k in range(n):
        block = sc[0] ^ k
        grads = grad_refs[k][...]
        grad_t[:, pl.ds(pl.multiple_of(block * QB, QB), QB)] = grads
        product = grads.astype(F4) * head_refs[k][...].astype(F4)
        delta[block] = jnp.sum(product[0:HEAD_DIM], axis=0, keepdims=True)
        delta[n + block] = jnp.sum(product[HEAD_DIM:], axis=0, keepdims=True)
    grad_k[...] = jnp.zeros(grad_k.shape, F4)
    grad_v[...] = jnp.zeros(grad_v.shape, F4)
    strips[...] = jnp.zeros(strips.shape, F4)
    stacked[...] = jnp.zeros(stacked.shape, BF)

    def one_tile(unit, first_block, cols, last):
        key_ref = key_own if unit == 0 else key_both
        lo = HEAD_DIM * unit
        start = pl.multiple_of(first_block * QB, QB)
        nothing = jnp.zeros((HEAD_DIM, cols), BF)
        raw_queries = query_t[lo : lo + HEAD_DIM, pl.ds(start, cols)]
        queries = unit_half(unit, raw_queries, ones_row(cols))
        plain = unit_half(unit, raw_queries, nothing)
        grads = unit_half(unit, grad_t[lo : lo + HEAD_DIM, pl.ds(start, cols)], nothing)
        parts = cols // QB
        log_total = jnp.concatenate([logs[unit * n + first_block + q] for q in range(parts)], axis=1)
        inner = jnp.concatenate([delta[unit * n + first_block + q] for q in range(parts)], axis=1)

        def step(part, grad_q):
            key_at = pl.multiple_of(part * TILE, TILE)
            far = first_block - 2 * part
            scores = dot(key_ref[pl.ds(key_at, TILE), :], queries)
            scores = scores + strip_tile(bias, unit, far, cols)
            probs = jnp.exp(scores - log_total)
            grad_probs = dot(value_r[pl.ds(key_at, TILE), :], grads)
            grad_scores = probs * (grad_probs - inner)
            for key_half in range(2):
                for q in range(parts):
                    at = jnp.maximum(far + q - key_half, -1) + 1
                    strips[unit, at] += grad_scores[
                        key_half * QB : (key_half + 1) * QB, q * QB : (q + 1) * QB
                    ]
            low = grad_scores.astype(BF)
            grad_v[pl.ds(key_at, TILE), :] += dot(probs.astype(BF), grads, 1, 1)
            grad_k[pl.ds(key_at, TILE), :] += dot(low, plain, 1, 1)
            return grad_q + dot(key_t[lo : lo + HEAD_DIM, pl.ds(key_at, TILE)], low)

        grad_q = lax.fori_loop(0, last + 1, step, jnp.zeros((HEAD_DIM, cols), F4))
        for q in range(parts):
            stacked[first_block + q, lo : lo + HEAD_DIM, :] = grad_q[
                :, q * QB : (q + 1) * QB
            ].astype(BF)

    def own_tile(i, carry):
        one_tile(0, 2 * i, TILE, i)
        return carry

    def both_tile(i, carry):
        one_tile(1, 2 * i + ((i + turn) & 1), QB, i)
        return carry

    lax.fori_loop(0, n // 2, both_tile, 0)
    lax.fori_loop(0, n // 2, own_tile, 0)
    for j in range(n):
        stacked[j, LANES : 2 * LANES, :] = jnp.transpose(grad_k[QB * j : QB * j + QB, :]).astype(BF)
        stacked[j, 2 * LANES :, :] = jnp.transpose(grad_v[QB * j : QB * j + QB, :]).astype(BF)
    for k in range(n):
        outs[k][...] = stacked[sc[0] ^ k]
    row = iota((8, TILE), 0)
    empty = jnp.zeros((8, QB), F4)
    for unit in range(2):
        for far in range(n):
            total = jnp.zeros((8, TILE), F4)
            for group in range(QB // 8):
                rows8 = strips[unit, far + 1, 8 * group : 8 * group + 8, :]
                wide = jnp.concatenate([empty, rows8], axis=1)
                total = total + (wide if group == 0 else pltpu.roll(wide, TILE - 8 * group, 1))
            lined = jnp.where(row == 0, total, 0.0)
            for c in range(1, 8):
                lined = lined + jnp.where(row == c, pltpu.roll(total, TILE - c, 1), 0.0)
            table[unit * n + far] = jnp.sum(lined, axis=0, keepdims=True)


def dispatch_rows(n, cap, sc, route_ref, cot, wo_t, *rest):
    outs, target = rest[:n], rest[n]
    tok = cot.shape[0]
    rows = wo_t.shape[0]
    route = route_ref[...]
    chosen = iota((n, tok), 0) == route
    upto = jnp.where(iota((tok, tok), 0) <= iota((tok, tok), 1), 1.0, 0.0).astype(BF)
    filled = dot(jnp.where(chosen, 1.0, 0.0).astype(BF), upto)
    slot = jnp.sum(jnp.where(chosen, filled - 1.0, 0.0), axis=0, keepdims=True)
    place = (route ^ sc[0]) * cap + slot.astype(jnp.int32)
    target[...] = jnp.broadcast_to(place, target.shape)
    spread = jnp.where(iota((n * cap, tok), 0) == place, 1.0, 0.0).astype(BF)
    packed = dot(spread, cot[...])
    rest_rows = outs[0].shape[0] - cap - rows
    tail = [wo_t[...].astype(F4), jnp.zeros((rest_rows, packed.shape[1]), F4)]
    for k in range(n):
        outs[k][...] = jnp.concatenate([packed[k * cap : (k + 1) * cap]] + tail, axis=0).astype(BF)


def pair_rows(sc, n, refs, dest, place_own):
    turn = sc[0] & 1
    wanted = shared_turn(sc[0])
    for m in range(n // 2):
        pair = (sc[0] >> 1) ^ m
        for k in (2 * m, 2 * m + 1):
            head = 3 * pair + (turn ^ (k & 1))
            place_own(pl.multiple_of(head * HEAD_DIM, HEAD_DIM), refs[k])
        first = jnp.broadcast_to(turn == wanted, (HEAD_DIM, QB))
        both = jnp.where(
            first,
            refs[2 * m][HEAD_DIM:LANES, :].astype(F4),
            refs[2 * m + 1][HEAD_DIM:LANES, :].astype(F4),
        )
        dest[pl.ds(pl.multiple_of((3 * pair + 2) * HEAD_DIM, HEAD_DIM), HEAD_DIM), :] = both.astype(
            dest.dtype
        )


def spread_matrix(target, rows):
    place = target[0:1, :]
    return jnp.where(iota((rows, place.shape[1]), 0) == place, 1.0, 0.0)


def hidden_rows(n, cap, sc, *refs):
    heads, (wo_t, tokens, misc_t, target) = refs[:n], refs[n : n + 4]
    attn, hidden_out = refs[n + 4 : n + 6]
    outs, buf = refs[n + 6 : 2 * n + 6], refs[2 * n + 6]

    def place_own(at, ref):
        buf[pl.ds(at, HEAD_DIM), :] = ref[0:HEAD_DIM, :].astype(F4)

    pair_rows(sc, n, heads, buf, place_own)
    rows = jnp.transpose(buf[...]).astype(BF)
    attn[...] = rows
    hidden = tokens[...].astype(F4) + dot(rows, wo_t[...], 1, 1)
    hidden_out[...] = hidden
    moe_in = (hidden * norm_scale(hidden) * misc_t[1:2, :]).astype(BF)
    packed = dot(spread_matrix(target, n * cap).astype(BF), moe_in).astype(BF)
    for k in range(n):
        outs[k][...] = packed[k * cap : (k + 1) * cap]


def gelu_pair(values):
    scale = math.sqrt(2.0 / math.pi)
    square = values * values
    bend = jnp.tanh(scale * (values + 0.044715 * values * square))
    act = 0.5 * values * (1.0 + bend)
    slope = 0.5 * (1.0 + bend) + 0.5 * values * (1.0 - bend * bend) * scale * (
        1.0 + 3.0 * 0.044715 * square
    )
    return (act, slope)


def route_probs(experts, sc, rows, misc):
    logits = dot(rows, misc[...])
    lane = iota(logits.shape, 1)
    real = (lane >= 2) & (lane < 2 + experts)
    logits = jnp.where(real, logits, NEG)
    powers = jnp.where(real, jnp.exp(logits - jnp.max(logits, axis=-1, keepdims=True)), 0.0)
    probs = powers / jnp.sum(powers, axis=-1, keepdims=True)
    chosen = lane == sc[0] + 2
    gate = jnp.sum(jnp.where(chosen, probs, 0.0), axis=-1, keepdims=True)
    return (probs, chosen, gate)


def expert_back(experts, sc, rows_ref, cot_ref, in_a, in_b, out_a, out_b, misc, back, act_out, log_out, gate_out):
    rows, cots = rows_ref[...], cot_ref[...]
    probs, chosen, gate = route_probs(experts, sc, rows, misc)
    gate_out[...] = jnp.broadcast_to(gate, gate_out.shape)
    inner = jnp.zeros(gate.shape, F4)
    width = in_a.shape[1]
    total = jnp.zeros(rows.shape, F4)
    for half, (w_in, w_out) in enumerate(((in_a, out_a), (in_b, out_b))):
        act, slope = gelu_pair(dot(rows, w_in[...]))
        low = act.astype(BF)
        act_out[:, half * width : (half + 1) * width] = low
        grad_act = dot(cots, w_out[...], 1, 1)
        inner = inner + jnp.sum(low.astype(F4) * grad_act, axis=-1, keepdims=True)
        total = total + dot((gate * grad_act * slope).astype(BF), w_in[...], 1, 1)
    grad_logits = (inner * probs * (jnp.where(chosen, 1.0, 0.0) - gate)).astype(BF)
    log_out[...] = grad_logits
    back[...] = (total + dot(grad_logits, misc[...], 1, 1)).astype(back.dtype)


def expert_forward(sc, act, gate, out_a, out_b, made):
    width = out_a.shape[0]
    total = dot(act[:, :width], out_a[...]) + dot(act[:, width:], out_b[...])
    made[...] = (gate[:, 0:1] * total).astype(made.dtype)


def expert_weights(experts, count, sc, *refs):
    rows_refs, cot_refs = refs[:count], refs[count : 2 * count]
    w_in, w_out, misc, grad_in, grad_out = refs[2 * count :]
    for i in range(count):
        rows, cots = rows_refs[i][...], cot_refs[i][...]
        gate = route_probs(experts, sc, rows, misc)[2]
        act, slope = gelu_pair(dot(rows, w_in[...]))
        grads = (gate * cots.astype(F4)).astype(BF)
        grad_pre = (dot(grads, w_out[...], 1, 1) * slope).astype(BF)
        in_part = dot(rows, grad_pre, 0, 0)
        out_part = dot(act.astype(BF), grads, 0, 0)
        if i == 0:
            grad_in[...] = in_part
            grad_out[...] = out_part
        else:
            grad_in[...] += in_part
            grad_out[...] += out_part


def add_split(n, cap, extra, sc, own, other, *rest):
    tails, outs = rest[:extra], rest[extra:]
    total = own[...] + other[...].astype(F4)
    tail = [t[...].astype(F4) for t in tails]
    used = cap + sum(t.shape[0] for t in tail)
    if outs[0].shape[0] > used:
        tail.append(jnp.zeros((outs[0].shape[0] - used, total.shape[1]), F4))
    for k in range(n):
        outs[k][...] = jnp.concatenate([total[k * cap : (k + 1) * cap]] + tail, axis=0).astype(BF)


def result_rows(n, cap, sc, *refs):
    made, (target, hidden, out) = refs[:n], refs[n:]
    rows = jnp.concatenate([made[k][0:cap, :] for k in range(n)], axis=0)
    spread = jnp.transpose(spread_matrix(target, n * cap)).astype(BF)
    out[...] = (hidden[...] + dot(spread, rows)).astype(BF)


def norm_back(grads, source, gain):
    scale = norm_scale(source)
    weighted = grads * gain
    inner = jnp.mean(weighted * source, axis=-1, keepdims=True)
    return (scale * weighted - source * (scale * scale * scale) * inner, scale)


def hidden_grads(n, cap, sc, *refs):
    back, (target, hidden_ref, misc_t, cot, wo_t) = refs[:n], refs[n : n + 5]
    grad_out, low_out, gain_out = refs[n + 5 : n + 8]
    outs, buf = refs[n + 8 : 2 * n + 8], refs[2 * n + 8]
    rows = jnp.concatenate([back[k][...] for k in range(n)], axis=0)
    spread = jnp.transpose(spread_matrix(target, n * cap)).astype(BF)
    grads = dot(spread, rows)
    hidden = hidden_ref[...]
    normed, scale = norm_back(grads, hidden, misc_t[1:2, :])
    gain_out[...] = jnp.broadcast_to(
        jnp.sum(grads * hidden * scale, axis=0, keepdims=True), gain_out.shape
    )
    total = cot[...].astype(F4) + normed
    grad_out[...] = total
    low = total.astype(BF)
    low_out[...] = low
    buf[...] = jnp.transpose(dot(low, wo_t[...])).astype(BF)
    turn = sc[0] & 1
    for k in range(n):
        pair = (sc[0] >> 1) ^ (k >> 1)
        own = pl.multiple_of((3 * pair + (turn ^ (k & 1))) * HEAD_DIM, HEAD_DIM)
        both = pl.multiple_of((3 * pair + 2) * HEAD_DIM, HEAD_DIM)
        outs[k][0:HEAD_DIM, :] = buf[pl.ds(own, HEAD_DIM), :]
        outs[k][HEAD_DIM:, :] = buf[pl.ds(both, HEAD_DIM), :]


def token_grads(n, sc, *refs):
    grads, (weights, tokens, hidden_grad, misc_t, out, buf) = refs[:n], refs[n:]
    inner = weights.shape[1] // 3

    def place_own(at, ref):
        buf[pl.ds(at, HEAD_DIM), :] = ref[0:HEAD_DIM, :].astype(F4)
        for c in (1, 2):
            buf[pl.ds(c * inner + at, HEAD_DIM), :] = ref[
                c * LANES : c * LANES + HEAD_DIM, :
            ].astype(F4)

    pair_rows(sc, n, grads, buf, place_own)
    for m in range(n // 2):
        at = pl.multiple_of((3 * ((sc[0] >> 1) ^ m) + 2) * HEAD_DIM, HEAD_DIM)
        for c in (1, 2):
            lo = c * LANES + HEAD_DIM
            buf[pl.ds(c * inner + at, HEAD_DIM), :] = grads[2 * m][lo : lo + HEAD_DIM, :].astype(
                F4
            ) + grads[2 * m + 1][lo : lo + HEAD_DIM, :].astype(F4)
    made = jnp.transpose(dot(weights[...], buf[...].astype(BF)))
    normed, unused = norm_back(made, tokens[...].astype(F4), misc_t[0:1, :])
    out[...] = hidden_grad[...] + normed


def unit_weight_grads(n, heads, sc, *refs):
    normed, (stacked, table) = refs[:n], refs[n : n + 2]
    outs, buf = refs[n + 2 : n + 2 + heads], refs[n + 2 + heads]
    total = None
    for i, step in enumerate(ring_steps(n)):
        part = dot(stacked[ring_block(step, sc[0], n)], normed[i][...])
        total = part if total is None else total + part
    buf[...] = jnp.transpose(total)
    rows = buf.shape[0] // heads
    width = buf.shape[1]
    for kk in range(heads):
        to = sc[1] ^ kk
        outs[kk][...] = jnp.concatenate(
            [
                buf[pl.ds(pl.multiple_of(to * rows, 8), rows), :],
                table[pl.ds(pl.multiple_of(to * n, 8), n), :],
                jnp.zeros((8, width), F4),
            ],
            axis=0,
        ).astype(BF)


def two_parts(values, gap):
    high = values.astype(BF).astype(F4)
    lane = iota(values.shape, 1)
    low = pltpu.roll(jnp.where(lane < gap, values - high, 0.0), gap, 1)
    return jnp.where(lane < gap, high, low)


def one_part(values, gap):
    return values + pltpu.roll(values, values.shape[1] - gap, 1)


def unit_weight_sums(n, rows, sc, p0, p1, p2, p3, *rest):
    outs, buf = rest[:n], rest[n]
    buf[...] = (
        (p0[...].astype(F4) + p1[...].astype(F4)) + (p2[...].astype(F4) + p3[...].astype(F4))
    )
    base = n * rows
    for k in range(n):
        to = sc[0] ^ k
        entry = buf[pl.ds(base + to, 1), :]
        entry = two_parts(jnp.broadcast_to(one_part(entry, 2), (8, entry.shape[1])), 2)
        outs[k][...] = jnp.concatenate(
            [buf[pl.ds(pl.multiple_of(to * rows, 8), rows), :], entry], axis=0
        ).astype(BF)


def unit_weight_final(n, sc, *refs):
    parts, (wq, wk, wv, misc) = refs[:n], refs[n : n + 4]
    grads, gain, table, buf = refs[n + 4 : n + 7], refs[n + 7], refs[n + 8], refs[n + 9]
    rows = wq.shape[0]
    for k in range(n):
        buf[sc[0] ^ k] = parts[k][...].astype(F4)
    lane = iota((rows, LANES), 1)
    inner = jnp.zeros((rows, 1), F4)
    for c, weight in enumerate((wq, wk, wv)):
        lo = LANES * c

        def piece(head, place):
            pair, turn = head // 3, head % 3
            if turn < 2:
                tile, half = buf[2 * pair + turn, 0:rows, lo : lo + LANES], 0
            else:
                tile = (
                    buf[2 * pair, 0:rows, lo : lo + LANES]
                    + buf[2 * pair + 1, 0:rows, lo : lo + LANES]
                )
                half = 1
            return tile if half == place else pltpu.roll(tile, HEAD_DIM, 1)

        for m in range(weight.shape[1] // LANES):
            tile = jnp.where(lane < HEAD_DIM, piece(2 * m, 0), piece(2 * m + 1, 1))
            cols = slice(LANES * m, LANES * m + LANES)
            grads[c][:, cols] = tile
            inner = inner + jnp.sum(weight[:, cols].astype(F4) * tile, axis=-1, keepdims=True)
    gain[...] = jnp.broadcast_to(inner / misc[:, 0:1].astype(F4), gain.shape)
    for j in range(n):
        table[j : j + 1, :] = one_part(buf[j, rows : rows + 1, 0:LANES], 2)


def out_weight_grads(heads, sc, low, attn, rows_a, rows_b, logs_a, logs_b, gain, *rest):
    outs, buf = rest[:heads], rest[heads]
    width = attn.shape[1]
    buf[:, 0:width] = dot(low[...], attn[...], 0, 0)
    router = dot(rows_a[...], logs_a[...], 0, 0) + dot(rows_b[...], logs_b[...], 0, 0)
    wide = jnp.where(iota((LANES, gain.shape[1]), 0) == 1, gain[0:1, :], 0.0)
    buf[:, width : width + LANES] = two_parts(router + jnp.transpose(wide), 16)
    rows = buf.shape[0] // heads
    for kk in range(heads):
        first = pl.multiple_of((sc[1] ^ kk) * rows, 8)
        outs[kk][...] = buf[pl.ds(first, rows), :].astype(BF)


def out_weight_sums(n, rows, sc, p0, p1, p2, p3, *rest):
    outs, buf = rest[:n], rest[n]
    width = buf.shape[1] - LANES
    total = (p0[...].astype(F4) + p1[...].astype(F4)) + (p2[...].astype(F4) + p3[...].astype(F4))
    buf[:, 0:width] = total[:, 0:width]
    buf[:, width:] = two_parts(one_part(total[:, width:], 16), 16)
    for k in range(n):
        first = pl.multiple_of((sc[0] ^ k) * rows, 8)
        outs[k][...] = jnp.concatenate(
            [buf[pl.ds(first, rows), :], jnp.zeros((8, buf.shape[1]), F4)], axis=0
        ).astype(BF)


def out_weight_final(n, sc, *refs):
    parts, (grad, extra) = refs[:n], refs[n:]
    total = parts[0][...].astype(F4)
    for k in range(1, n):
        total = total + parts[k][...].astype(F4)
    width = grad.shape[1]
    grad[...] = total[0 : grad.shape[0], 0:width]
    extra[...] = one_part(total[0 : grad.shape[0], width:], 16)


def swap(values, axis, flip):
    if flip == 0:
        return values
    size = lax.axis_size(axis)
    return lax.ppermute(values, axis, [(i, i ^ flip) for i in range(size)])


def exchange(messages, axis):
    return [swap(message, axis, k) for k, message in enumerate(messages)]


def after(values, earlier):
    return lax.optimization_barrier((values, earlier))[0]


def over_heads(stack):
    across = swap(stack, "head", 2)
    return (stack, swap(stack, "head", 1), across, swap(across, "head", 1))


def on_plane(
    tokens,
    attn_gain,
    w_query,
    w_key,
    w_value,
    w_out,
    bias_table,
    moe_gain,
    w_router,
    expert_in,
    expert_out,
    seq_lengths,
    rel_buckets,
    routes,
    cotangent,
):
    heads = lax.axis_size("head")
    n = lax.axis_size("blk")
    head_index = lax.axis_index("head")
    blk = lax.axis_index("blk")
    tok, width = tokens.shape[0], tokens.shape[2]
    rows = w_query.shape[0]
    total_rows = n * tok
    experts = w_router.shape[1]
    cap = 3 * tok // (2 * experts)
    slots = n * cap
    x = tokens.reshape(tok, width)
    cot = cotangent.reshape(tok, width)
    length = lax.dynamic_index_in_dim(seq_lengths, head_index, 0, False)
    sc = jnp.stack([blk, head_index, length]).astype(jnp.int32)

    def call(body, args, outs, scratch=(), mem=40, flops=0):
        return vmem_call(body, sc, args, outs, scratch, mem, flops)

    table_row = jnp.zeros((rows, HEADS), BF).at[0].set(bias_table)
    misc_own = jnp.concatenate(
        [
            attn_gain[:, None],
            moe_gain[:, None],
            w_router,
            jnp.zeros((rows, 16 - 2 - experts), BF),
            table_row,
            jnp.zeros((rows, LANES - 16 - HEADS), BF),
        ],
        axis=1,
    )
    unit_cols = 4 * LANES
    packed = call(
        functools.partial(pack_units, n),
        (w_query, w_key, w_value, misc_own),
        [shaped((rows + 8, unit_cols), BF)] * n,
        [pltpu.VMEM((n, rows + 8, unit_cols), F4)],
    )
    unit_parts = over_heads(jnp.stack(exchange(packed, "blk")))
    unit_w, misc, misc_t = call(
        functools.partial(unpack_units, n, rows),
        unit_parts,
        [shaped((width, 3 * LANES), BF), shaped((width, LANES), BF), shaped((LANES, width), F4)],
        [pltpu.VMEM((width, unit_cols), F4)],
    )

    order = [ring_of(i, n) for i in range(n)]
    ahead = [(order[i], order[(i + 1) % n]) for i in range(n)]
    astern = [(b, a) for a, b in ahead]
    front = back = x
    blocks = [(x,)]
    for _ in range(n // 2 - 1):
        front = lax.ppermute(front, "blk", ahead)
        back = lax.ppermute(back, "blk", astern)
        blocks += [(front,), (back,)]
    half = tok // 2
    blocks.append(
        (
            lax.ppermute(front[:half], "blk", ahead),
            lax.ppermute(back[half:], "blk", astern),
        )
    )
    normed, unit_rows, unit_cols_t = [], [], []
    groups = [blocks[0:3], blocks[3:5], blocks[5:7], blocks[7:8]]
    for group in groups:
        made = call(
            functools.partial(project_blocks, [len(g) for g in group]),
            [part for g in group for part in g] + [misc_t, unit_w],
            [
                shaped((tok, width), BF),
                shaped((tok, 3 * LANES), BF),
                shaped((3 * LANES, tok), BF),
            ]
            * len(group),
            flops=2 * len(group) * tok * width * 3 * LANES,
        )
        normed += made[0::3]
        unit_rows += made[1::3]
        unit_cols_t += made[2::3]

    table_all = misc.reshape(heads * n, rows, LANES)[:, 0, 16 : 16 + HEADS].astype(F4)
    pair, turn = blk // 2, blk % 2
    own_col = lax.dynamic_index_in_dim(table_all, 3 * pair + turn, 1, False)
    both_col = lax.dynamic_index_in_dim(table_all, 3 * pair + 2, 1, False)
    labels = jnp.arange(NUM_BUCKETS, dtype=jnp.int32)
    by_bucket = rel_buckets[None, :] == labels[:, None]
    by_distance = jnp.stack(
        [jnp.sum(jnp.where(by_bucket, col[:, None], 0.0), axis=0) for col in (own_col, both_col)]
    )
    shifted = jnp.pad(by_distance, ((0, 0), (QB, 0)))
    windows = jnp.stack([shifted[:, QB * i : QB * i + TILE] for i in range(n)], axis=1)
    (strips,) = call(bias_strips, (windows,), [shaped((2, n + 1, QB, QB), F4)])

    wo_t = jnp.transpose(w_out)
    extra = 80 if cap == 48 else -(-(cap + rows) // 16) * 16
    cot_out = call(
        functools.partial(dispatch_rows, n, cap),
        (routes.reshape(1, tok), cot, wo_t),
        [shaped((extra, width), BF)] * n + [shaped((8, tok), jnp.int32)],
    )
    target = cot_out[n]
    cot_in = exchange([after(m, back) for m in cot_out[:n]], "blk")
    cot_rows = jnp.concatenate([m[:cap] for m in cot_in])
    (out_t,) = call(
        functools.partial(unpack_rows, n, rows),
        over_heads(jnp.stack([m[cap:] for m in cot_in])),
        [shaped((width, width), BF)],
        [pltpu.VMEM((width, width), F4)],
    )
    in_own, out_own = expert_in.reshape(expert_in.shape[1:]), expert_out.reshape(expert_out.shape[1:])
    in_other = swap(after(in_own, unit_parts[2]), "head", 2)
    out_other = swap(after(out_own, unit_parts[2]), "head", 2)

    made = call(
        functools.partial(attend_units, n),
        list(unit_rows) + list(unit_cols_t) + [strips],
        [shaped((LANES, tok), BF)] * n + [shaped((2 * n, 1, tok), F4)],
        [
            pltpu.VMEM((total_rows, LANES), BF),
            pltpu.VMEM((total_rows, LANES), BF),
            pltpu.VMEM((LANES, total_rows), BF),
            pltpu.VMEM((LANES, total_rows), BF),
            pltpu.VMEM((n, LANES, tok), F4),
        ],
        mem=48,
        flops=10**9,
    )
    head_out, logs = made[:n], made[n]
    head_in = exchange(head_out, "blk")
    made = call(
        functools.partial(hidden_rows, n, cap),
        list(head_in) + [out_t, x, misc_t, target],
        [shaped((tok, width), BF), shaped((tok, width), F4)] + [shaped((cap, width), BF)] * n,
        [pltpu.VMEM((width, tok), F4)],
        flops=4 * tok * width * width,
    )
    attn, hidden, moe_out = made[0], made[1], made[2:]

    moe_rows = jnp.concatenate(exchange(moe_out, "blk"))
    moe_pair = swap(moe_rows, "head", 1)
    cot_pair = swap(cot_rows, "head", 1)

    def backward_rows(rows_in, cots_in, kind):
        return call(
            functools.partial(expert_back, experts),
            (rows_in, cots_in, in_own, in_other, out_own, out_other, misc),
            [
                shaped((slots, width), kind),
                shaped((slots, 2 * width), BF),
                shaped((slots, LANES), BF),
                shaped((slots, LANES), F4),
            ],
            flops=12 * slots * width * width,
        )

    def forward_rows(act, gate, kind):
        return call(
            expert_forward,
            (act, gate, out_own, out_other),
            [shaped((slots, width), kind)],
            flops=4 * slots * width * width,
        )[0]

    back_pair, act_pair, logs_pair, gate_pair = backward_rows(moe_pair, cot_pair, BF)
    back_other = swap(back_pair, "head", 1)
    back_own, act_own, logs_own, gate_own = backward_rows(moe_rows, cot_rows, F4)
    back_out = call(
        functools.partial(add_split, n, cap, 0),
        (back_own, back_other),
        [shaped((cap, width), BF)] * n,
    )
    back_in = exchange(back_out, "blk")
    made = call(
        functools.partial(hidden_grads, n, cap),
        list(back_in) + [target, hidden, misc_t, cot, out_t],
        [shaped((tok, width), F4), shaped((tok, width), BF), shaped((8, width), F4)]
        + [shaped((LANES, tok), BF)] * n,
        [pltpu.VMEM((width, tok), BF)],
        flops=4 * tok * width * width,
    )
    grad_hidden, grad_low, gain_moe_part, grad_out_heads = made[0], made[1], made[2], made[3:]
    grad_heads = exchange(grad_out_heads, "blk")

    made = call(
        functools.partial(unit_grads, n),
        list(unit_rows) + list(unit_cols_t) + [strips] + list(head_out) + list(grad_heads) + [logs],
        [shaped((3 * LANES, tok), BF)] * n
        + [shaped((n, 3 * LANES, tok), BF), shaped((2 * n, 1, TILE), F4)],
        [
            pltpu.VMEM((total_rows, LANES), BF),
            pltpu.VMEM((total_rows, LANES), BF),
            pltpu.VMEM((LANES, total_rows), BF),
            pltpu.VMEM((LANES, total_rows), BF),
            pltpu.VMEM((total_rows, LANES), BF),
            pltpu.VMEM((LANES, total_rows), BF),
            pltpu.VMEM((2 * n, 1, tok), F4),
            pltpu.VMEM((total_rows, LANES), F4),
            pltpu.VMEM((total_rows, LANES), F4),
            pltpu.VMEM((2, n + 1, QB, QB), F4),
        ],
        mem=56,
        flops=3 * 10**9,
    )
    unit_out, stacked, lines = made[:n], made[n], made[n + 1]
    unit_in = exchange(unit_out, "blk")

    made_pair = forward_rows(act_pair, gate_pair, BF)
    made_own = forward_rows(act_own, gate_own, F4)
    tails = 3 * rows
    res_out = call(
        functools.partial(add_split, n, cap, 3),
        (made_own, swap(made_pair, "head", 1), w_query, w_key, w_value),
        [shaped((cap + tails + 8, width), BF)] * n,
    )
    res_out = [after(m, grad_heads[n - 1]) for m in res_out]
    res_in = exchange(res_out, "blk")
    (result,) = call(
        functools.partial(result_rows, n, cap),
        list(res_in) + [target, hidden],
        [shaped((tok, width), BF)],
    )
    (full_w,) = call(
        functools.partial(unpack_stack, n, rows),
        over_heads(jnp.stack([m[cap:] for m in res_in])),
        [shaped((width, 3 * width), BF)],
        [pltpu.VMEM((width, 3 * width), F4)],
    )
    (grad_tokens,) = call(
        functools.partial(token_grads, n),
        list(unit_in) + [full_w, x, grad_hidden, misc_t],
        [shaped((tok, width), F4)],
        [pltpu.VMEM((3 * width, tok), F4)],
    )

    moe_far = swap(moe_rows, "head", 2)
    cot_far = swap(after(cot_rows, out_other), "head", 2)
    all_moe = (moe_rows, moe_pair, moe_far, swap(moe_far, "head", 1))
    all_cot = (cot_rows, cot_pair, cot_far, swap(cot_far, "head", 1))
    grad_in, grad_out = call(
        functools.partial(expert_weights, experts, heads),
        all_moe + all_cot + (in_own, out_own, misc),
        [shaped(in_own.shape, F4), shaped(out_own.shape, F4)],
        flops=8 * heads * slots * width * width,
    )

    wide = width + LANES
    parts = call(
        functools.partial(out_weight_grads, heads),
        (grad_low, attn, moe_rows, moe_pair, logs_own, logs_pair, gain_moe_part),
        [shaped((width // heads, wide), BF)] * heads,
        [pltpu.VMEM((width, wide), F4)],
        flops=2 * tok * width * width,
    )
    sums = call(
        functools.partial(out_weight_sums, n, rows),
        exchange(parts, "head"),
        [shaped((rows + 8, wide), BF)] * n,
        [pltpu.VMEM((width // heads, wide), F4)],
    )
    grad_out_t, small = call(
        functools.partial(out_weight_final, n),
        exchange(sums, "blk"),
        [shaped((rows, width), F4), shaped((rows, LANES), F4)],
    )

    lines = lines.reshape(2, n, TILE)
    near, far = lines[:, :, QB:], lines[:, :, :QB]
    by_distance = near + jnp.pad(far[:, 1:], ((0, 0), (0, 1), (0, 0)))
    by_distance = by_distance.reshape(2, total_rows)
    table_part = jnp.sum(jnp.where(by_bucket[None], by_distance[:, None, :], 0.0), axis=2)
    high = table_part.astype(BF).astype(F4)
    table_part = jnp.concatenate([high, table_part - high]).T
    table_part = jnp.pad(table_part, ((0, 0), (0, 3 * LANES - 4)))
    parts = call(
        functools.partial(unit_weight_grads, n, heads),
        list(normed) + [stacked, table_part],
        [shaped((width // heads + n + 8, 3 * LANES), BF)] * heads,
        [pltpu.VMEM((width, 3 * LANES), F4)],
        flops=2 * total_rows * width * 3 * LANES,
    )
    sums = call(
        functools.partial(unit_weight_sums, n, rows),
        exchange(parts, "head"),
        [shaped((rows + 8, 3 * LANES), BF)] * n,
        [pltpu.VMEM((width // heads + n + 8, 3 * LANES), F4)],
    )
    made = call(
        functools.partial(unit_weight_final, n),
        exchange(sums, "blk") + [w_query, w_key, w_value, misc_own],
        [shaped((rows, width), F4)] * 3 + [shaped((rows, LANES), F4), shaped((n, LANES), F4)],
        [pltpu.VMEM((n, rows + 8, 3 * LANES), F4)],
    )
    grad_q, grad_k, grad_v, gain_attn_grad, table_sum = made
    own_sum, both_sum = table_sum[:, 0], table_sum[:, 1]
    both_sum = both_sum.reshape(n // 2, 2).sum(axis=1, keepdims=True)
    grad_table = jnp.concatenate([own_sum.reshape(n // 2, 2), both_sum], axis=1).reshape(HEADS)
    return (
        result.reshape(tokens.shape),
        grad_tokens.reshape(tokens.shape),
        gain_attn_grad[:, 0],
        grad_q,
        grad_k,
        grad_v,
        jnp.transpose(grad_out_t),
        grad_table,
        small[:, 1],
        small[:, 2 : 2 + experts],
        grad_in.reshape(expert_in.shape),
        grad_out.reshape(expert_out.shape),
    )


def ring_of(place, ring_len):
    return 2 * place if place < ring_len // 2 else 2 * ring_len - 1 - 2 * place


def solution(mesh):
    in_specs = (
        P("blk", "head", None),
        P(("head", "blk")),
        P(("head", "blk"), None),
        P(("head", "blk"), None),
        P(("head", "blk"), None),
        P(None, ("head", "blk")),
        P(("head", "blk")),
        P(("head", "blk")),
        P(("head", "blk"), None),
        P("blk", None, "head"),
        P("blk", "head", None),
        P(),
        P(),
        P("head", "blk", None, None),
        P("blk", "head", None),
    )
    out_specs = (
        P("blk", "head", None),
        P("blk", "head", None),
        P(("head", "blk")),
        P(("head", "blk"), None),
        P(("head", "blk"), None),
        P(("head", "blk"), None),
        P(None, ("head", "blk")),
        P(("head", "blk")),
        P(("head", "blk")),
        P(("head", "blk"), None),
        P("blk", None, "head"),
        P("blk", "head", None),
    )
    one_each = mesh.shape["head"] == 4 and mesh.shape["blk"] == 8
    return jax.shard_map(
        on_plane if one_each else on_device, mesh=mesh, in_specs=in_specs, out_specs=out_specs, check_vma=False
    )
```

```python
import functools
import math

import jax
import jax.numpy as jnp
from jax import lax
from jax.experimental import pallas as pl
from jax.experimental.pallas import tpu as pltpu
from jax.sharding import PartitionSpec as P

HEADS = 12
HEAD_DIM = 64
NUM_BUCKETS = 32


norm_eps = 1e-06
masked_score = -1e30


def inverse_rms(values):
    return lax.rsqrt(jnp.mean(values * values, axis=-1, keepdims=True) + norm_eps)


def norm_backward(grad_normed, source, inv_scale, gain):
    weighted = grad_normed * gain
    inner_mean = jnp.mean(weighted * source, axis=-1, keepdims=True)
    grad_source = inv_scale * weighted - source * (inv_scale * inv_scale * inv_scale) * inner_mean
    grad_gain = jnp.sum(grad_normed * source * inv_scale, axis=0)
    return (grad_source, grad_gain)


def same_state(running):
    return running


def bucket_bounds(rel_buckets):
    bucket_count = NUM_BUCKETS
    labels = jnp.arange(bucket_count, dtype=jnp.int32)
    starts = jnp.sum((rel_buckets[:, None] < labels[None, :]).astype(jnp.int32), axis=0)
    ends = jnp.concatenate([starts[1:], jnp.full((1,), rel_buckets.shape[0] + 1, jnp.int32)])
    return (starts, ends)


def bias_terms(query_positions, key_positions, bounds, table32):
    starts, ends = bounds
    distance = jnp.maximum(query_positions[:, None] - key_positions[None, :], 0)[:, :, None]
    inside = (distance >= starts[None, None, :]) & (distance < ends[None, None, :])
    onehot = inside.astype(jnp.bfloat16)
    bias = jnp.einsum(
        "qkb,bh->hqk", onehot, table32.astype(jnp.bfloat16), preferred_element_type=jnp.float32
    )
    return (onehot, bias)


def block_scores(queries, keys, query_positions, key_positions, seq_lengths, bounds, table32):
    onehot, bias = bias_terms(query_positions, key_positions, bounds, table32)
    raw = jnp.einsum("qshd,kshd->hsqk", queries, keys, preferred_element_type=jnp.float32)
    causal = key_positions[None, :] <= query_positions[:, None]
    present = key_positions[None, :] < seq_lengths[:, None]
    valid = causal[None, :, :] & present[:, None, :]
    return (raw + bias[:, None, :, :], valid[None], onehot)


def attend_step(
    running, queries, keys, values, query_positions, key_positions, seq_lengths, bounds, table32
):
    row_top, row_total, weighted = running
    scores, valid, unused = block_scores(
        queries, keys, query_positions, key_positions, seq_lengths, bounds, table32
    )
    scores = jnp.where(valid, scores, masked_score)
    new_top = jnp.maximum(row_top, jnp.max(scores, axis=-1))
    weights = jnp.where(valid, jnp.exp(scores - new_top[..., None]), 0.0)
    decay = jnp.exp(row_top - new_top)
    row_total = row_total * decay + jnp.sum(weights, axis=-1)
    mixed = jnp.einsum(
        "hsqk,kshd->qshd", weights.astype(jnp.bfloat16), values, preferred_element_type=jnp.float32
    )
    weighted = weighted * jnp.transpose(decay, (2, 1, 0))[..., None] + mixed
    return (new_top, row_total, weighted)


def grad_step(
    queries,
    grad_heads,
    log_total,
    delta,
    query_positions,
    keys,
    values,
    key_positions,
    seq_lengths,
    bounds,
    table32,
):
    scores, valid, onehot = block_scores(
        queries, keys, query_positions, key_positions, seq_lengths, bounds, table32
    )
    probs = jnp.where(valid, jnp.exp(scores - jnp.transpose(log_total, (2, 1, 0))[..., None]), 0.0)
    grad_probs = jnp.einsum(
        "qshd,kshd->hsqk", grad_heads, values, preferred_element_type=jnp.float32
    )
    grad_scores = probs * (grad_probs - jnp.transpose(delta, (2, 1, 0))[..., None])
    grad_table = jnp.einsum(
        "hqk,qkb->bh",
        jnp.sum(grad_scores, axis=1),
        onehot.astype(jnp.float32),
        precision=lax.Precision.HIGHEST,
    )
    low_scores = grad_scores.astype(jnp.bfloat16)
    grad_queries = jnp.einsum(
        "hsqk,kshd->qshd", low_scores, keys, preferred_element_type=jnp.float32
    )
    grad_keys = jnp.einsum(
        "hsqk,qshd->kshd", low_scores, queries, preferred_element_type=jnp.float32
    )
    grad_values = jnp.einsum(
        "hsqk,qshd->kshd",
        probs.astype(jnp.bfloat16),
        grad_heads,
        preferred_element_type=jnp.float32,
    )
    return (grad_queries, grad_keys, grad_values, grad_table)


def on_device(
    tokens,
    attn_gain,
    w_query,
    w_key,
    w_value,
    w_out,
    bias_table,
    moe_gain,
    w_router,
    expert_in,
    expert_out,
    seq_lengths,
    rel_buckets,
    routes,
    cotangent,
):
    head_count = lax.axis_size("head")
    blk_count = lax.axis_size("blk")
    head_index = lax.axis_index("head")
    blk_index = lax.axis_index("blk")
    block_rows, group_seqs, width = tokens.shape
    seq_count = group_seqs * head_count
    tok_rows = block_rows * group_seqs
    local_heads = HEADS // head_count
    head_width = local_heads * HEAD_DIM
    group_rows = block_rows * max(1, blk_count // 8)
    longest = jnp.max(seq_lengths)
    query_first = blk_index * block_rows
    query_last = query_first + block_rows - 1
    query_positions = query_first + jnp.arange(block_rows, dtype=jnp.int32)
    bounds = bucket_bounds(rel_buckets)
    fetched = (
        lax.all_gather(w_query, ("head", "blk"), axis=0, tiled=True),
        lax.all_gather(w_key, ("head", "blk"), axis=0, tiled=True),
        lax.all_gather(w_value, ("head", "blk"), axis=0, tiled=True),
        lax.all_gather(w_out, ("head", "blk"), axis=1, tiled=True),
        lax.all_gather(attn_gain, ("head", "blk"), axis=0, tiled=True),
        lax.all_gather(bias_table, ("head", "blk"), axis=0, tiled=True),
        lax.all_gather(moe_gain, ("head", "blk"), axis=0, tiled=True),
        lax.all_gather(w_router, ("head", "blk"), axis=0, tiled=True),
    )
    full_query, full_key, full_value, full_out, gain_attn, table_flat, gain_moe, full_router = (
        fetched
    )
    inner_width = full_query.shape[1]
    table_all = table_flat.astype(jnp.float32).reshape(NUM_BUCKETS, HEADS)
    table32 = lax.dynamic_slice_in_dim(table_all, head_index * local_heads, local_heads, 1)
    gain_attn32 = gain_attn.astype(jnp.float32)
    gain_moe32 = gain_moe.astype(jnp.float32)

    def to_heads(values):
        parts = values.shape[1]
        shaped = values.reshape(block_rows, group_seqs, parts, head_count, head_width)
        moved = lax.all_to_all(shaped, "head", split_axis=3, concat_axis=1, tiled=True)
        return moved.reshape(block_rows, seq_count, parts, local_heads, HEAD_DIM)

    def to_tokens(values):
        parts = values.shape[2]
        shaped = values.reshape(block_rows, seq_count, parts, 1, head_width)
        moved = lax.all_to_all(shaped, "head", split_axis=1, concat_axis=3, tiled=True)
        return moved.reshape(tok_rows, parts, inner_width)

    source = tokens.astype(jnp.float32).reshape(tok_rows, width)
    inv_attn = inverse_rms(source)
    attn_in = (source * inv_attn * gain_attn32).astype(jnp.bfloat16)
    stacked_weights = jnp.stack((full_query, full_key, full_value))
    projected = jnp.einsum(
        "td,cde->tce", attn_in, stacked_weights, preferred_element_type=jnp.float32
    ).astype(jnp.bfloat16)
    heads_in = to_heads(projected)
    queries = heads_in[:, :, 0]
    keys = heads_in[:, :, 1]
    values = heads_in[:, :, 2]
    start_state = (
        jnp.full((local_heads, seq_count, block_rows), masked_score, jnp.float32),
        jnp.zeros((local_heads, seq_count, block_rows), jnp.float32),
        jnp.zeros((block_rows, seq_count, local_heads, HEAD_DIM), jnp.float32),
    )
    key_piece = lax.all_gather(keys, "blk", axis=0, tiled=True)
    value_piece = lax.all_gather(values, "blk", axis=0, tiled=True)
    piece_rows = key_piece.shape[0]
    part_rows = math.gcd(piece_rows, group_rows)

    def forward_one_part(step_index, inner_state):
        offset = step_index * part_rows
        key_part = lax.dynamic_slice_in_dim(key_piece, offset, part_rows, 0)
        value_part = lax.dynamic_slice_in_dim(value_piece, offset, part_rows, 0)
        key_positions = offset + jnp.arange(part_rows, dtype=jnp.int32)

        def attend_now(current):
            return attend_step(
                current,
                queries,
                key_part,
                value_part,
                query_positions,
                key_positions,
                seq_lengths,
                bounds,
                table32,
            )

        skipped = (offset > query_last) | (offset >= longest)
        return lax.cond(skipped, same_state, attend_now, inner_state)

    row_top, row_total, weighted = lax.fori_loop(
        0, piece_rows // part_rows, forward_one_part, start_state
    )
    attn_heads = (weighted / jnp.transpose(row_total, (2, 1, 0))[..., None]).astype(jnp.bfloat16)
    log_total = jnp.transpose(row_top + jnp.log(row_total), (2, 1, 0))
    attn_tok = to_tokens(attn_heads[:, :, None])[:, 0]
    branch = jnp.dot(attn_tok, full_out, preferred_element_type=jnp.float32)
    hidden = source + branch
    expert_count = full_router.shape[1]
    local_experts = expert_in.shape[0]
    capacity = max(2, 3 * tok_rows // (2 * expert_count))
    inv_moe = inverse_rms(hidden)
    moe_in = (hidden * inv_moe * gain_moe32).astype(jnp.bfloat16)
    logits = jnp.dot(moe_in, full_router, preferred_element_type=jnp.float32)
    router_probs = jax.nn.softmax(logits, axis=-1)
    route_flat = routes.reshape(tok_rows)
    chosen = route_flat[:, None] == jnp.arange(expert_count, dtype=jnp.int32)[None, :]
    gate = jnp.sum(jnp.where(chosen, router_probs, 0.0), axis=-1)
    filled = jnp.cumsum(chosen.astype(jnp.int32), axis=0)
    slot = jnp.sum(jnp.where(chosen, filled - 1, 0), axis=-1)
    target = route_flat * capacity + slot
    dispatch = (
        target[:, None] == jnp.arange(expert_count * capacity, dtype=jnp.int32)[None, :]
    ).astype(jnp.bfloat16)

    def to_buffer(token_rows):
        packed = jnp.einsum(
            "tj,td->jd", dispatch, token_rows, preferred_element_type=jnp.float32
        ).astype(jnp.bfloat16)
        return packed.reshape(blk_count, local_experts, capacity, width)

    def from_buffer(buffer):
        return jnp.dot(
            dispatch,
            buffer.reshape(expert_count * capacity, width),
            preferred_element_type=jnp.float32,
        )

    def to_experts(buffer):
        return lax.all_to_all(buffer, "blk", split_axis=0, concat_axis=0, tiled=True)

    def all_rows(buffer):
        return lax.all_gather(buffer, "head", axis=0, tiled=True)

    def summed_rows(partial_terms):
        return lax.psum_scatter(
            partial_terms.astype(jnp.bfloat16), "head", scatter_dimension=0, tiled=True
        ).astype(jnp.float32)

    def to_owners(buffer):
        return lax.all_to_all(buffer, "blk", split_axis=0, concat_axis=0, tiled=True)

    expert_rows_in = all_rows(to_experts(to_buffer(moe_in)))
    expert_pre = jnp.einsum(
        "necd,edf->necf", expert_rows_in, expert_in, preferred_element_type=jnp.float32
    )
    expert_act, gelu_pull = jax.vjp(jax.nn.gelu, expert_pre)
    expert_low = expert_act.astype(jnp.bfloat16)
    expert_terms = jnp.einsum(
        "necf,efd->necd", expert_low, expert_out, preferred_element_type=jnp.float32
    )
    expert_tok = from_buffer(to_owners(summed_rows(expert_terms).astype(jnp.bfloat16)))
    result = hidden + gate[:, None] * expert_tok
    grad_result = cotangent.astype(jnp.float32).reshape(tok_rows, width)
    grad_expert_tok = (gate[:, None] * grad_result).astype(jnp.bfloat16)
    grad_gate = jnp.sum(grad_result * expert_tok, axis=-1)
    grad_logits = (
        router_probs * (jnp.where(chosen, grad_gate[:, None], 0.0) - (gate * grad_gate)[:, None])
    ).astype(jnp.bfloat16)
    grad_router = jnp.einsum("td,te->de", moe_in, grad_logits, preferred_element_type=jnp.float32)
    grad_rows = all_rows(to_experts(to_buffer(grad_expert_tok)))
    grad_act = jnp.einsum(
        "necd,efd->necf", grad_rows, expert_out, preferred_element_type=jnp.float32
    )
    grad_pre = gelu_pull(grad_act)[0].astype(jnp.bfloat16)
    grad_expert_out = jnp.einsum(
        "necf,necd->efd", expert_low, grad_rows, preferred_element_type=jnp.float32
    )
    grad_expert_in = jnp.einsum(
        "necd,necf->edf", expert_rows_in, grad_pre, preferred_element_type=jnp.float32
    )
    grad_back = jnp.einsum(
        "necf,edf->necd", grad_pre, expert_in, preferred_element_type=jnp.float32
    )
    grad_moe_in = from_buffer(to_owners(summed_rows(grad_back).astype(jnp.bfloat16)))
    grad_moe_in = grad_moe_in + jnp.einsum(
        "te,de->td", grad_logits, full_router, preferred_element_type=jnp.float32
    )
    grad_norm_moe, grad_gain_moe = norm_backward(grad_moe_in, hidden, inv_moe, gain_moe32)
    grad_hidden = grad_result + grad_norm_moe
    grad_branch = grad_hidden.astype(jnp.bfloat16)
    grad_out_w = jnp.einsum("te,td->ed", attn_tok, grad_branch, preferred_element_type=jnp.float32)
    grad_attn_tok = jnp.einsum(
        "td,ed->te", grad_branch, full_out, preferred_element_type=jnp.float32
    ).astype(jnp.bfloat16)
    grad_heads = to_heads(grad_attn_tok[:, None])[:, :, 0]
    delta = jnp.sum(grad_heads.astype(jnp.float32) * attn_heads.astype(jnp.float32), axis=-1)
    all_keys = lax.all_gather(keys, "blk", axis=0, tiled=True)
    all_values = lax.all_gather(values, "blk", axis=0, tiled=True)
    total_rows = all_keys.shape[0]
    step_rows = math.gcd(total_rows, group_rows)
    zero_heads = jnp.zeros((block_rows, seq_count, local_heads, HEAD_DIM), jnp.float32)
    zero_table = jnp.zeros(table32.shape, jnp.float32)

    def query_side(step_index, running):
        offset = step_index * step_rows
        key_block = lax.dynamic_slice_in_dim(all_keys, offset, step_rows, 0)
        value_block = lax.dynamic_slice_in_dim(all_values, offset, step_rows, 0)
        key_positions = offset + jnp.arange(step_rows, dtype=jnp.int32)

        def query_compute(current):
            grads = grad_step(
                queries,
                grad_heads,
                log_total,
                delta,
                query_positions,
                key_block,
                value_block,
                key_positions,
                seq_lengths,
                bounds,
                table32,
            )
            return (current[0] + grads[0], current[1] + grads[3])

        skipped = (offset > query_last) | (offset >= longest)
        return lax.cond(skipped, same_state, query_compute, running)

    grad_queries, grad_table = lax.fori_loop(
        0, total_rows // step_rows, query_side, (zero_heads, zero_table)
    )
    all_totals, all_deltas = (
        lax.all_gather(log_total, "blk", axis=0, tiled=True),
        lax.all_gather(delta, "blk", axis=0, tiled=True),
    )
    query_piece = lax.all_gather(queries, "blk", axis=0, tiled=True)
    grad_piece = lax.all_gather(grad_heads, "blk", axis=0, tiled=True)
    piece_rows = query_piece.shape[0]
    key_part_rows = math.gcd(piece_rows, group_rows)

    def key_one_part(step_index, inner_state):
        offset = step_index * key_part_rows
        query_part = lax.dynamic_slice_in_dim(query_piece, offset, key_part_rows, 0)
        grad_part = lax.dynamic_slice_in_dim(grad_piece, offset, key_part_rows, 0)
        total_part = lax.dynamic_slice_in_dim(all_totals, offset, key_part_rows, 0)
        delta_part = lax.dynamic_slice_in_dim(all_deltas, offset, key_part_rows, 0)
        part_positions = offset + jnp.arange(key_part_rows, dtype=jnp.int32)

        def key_compute(current):
            grads = grad_step(
                query_part,
                grad_part,
                total_part,
                delta_part,
                part_positions,
                keys,
                values,
                query_positions,
                seq_lengths,
                bounds,
                table32,
            )
            return (current[0] + grads[1], current[1] + grads[2])

        skipped = (offset + key_part_rows - 1 < query_first) | (query_first >= longest)
        return lax.cond(skipped, same_state, key_compute, inner_state)

    grad_keys, grad_values = lax.fori_loop(
        0, piece_rows // key_part_rows, key_one_part, (zero_heads, zero_heads)
    )
    grad_stack = jnp.stack((grad_queries, grad_keys, grad_values), axis=2).astype(jnp.bfloat16)
    grad_projected = to_tokens(grad_stack)
    grad_weights = jnp.einsum(
        "td,tce->cde", attn_in, grad_projected, preferred_element_type=jnp.float32
    )
    grad_attn_in = jnp.einsum(
        "tce,cde->td", grad_projected, stacked_weights, preferred_element_type=jnp.float32
    )
    grad_norm_attn, grad_gain_attn = norm_backward(grad_attn_in, source, inv_attn, gain_attn32)
    grad_tokens = grad_hidden + grad_norm_attn
    table_terms = lax.dynamic_update_slice_in_dim(
        jnp.zeros((NUM_BUCKETS, HEADS), jnp.float32), grad_table, head_index * local_heads, 1
    ).reshape(NUM_BUCKETS * HEADS)
    reduced = (
        lax.psum_scatter(grad_weights[0], ("head", "blk"), scatter_dimension=0, tiled=True),
        lax.psum_scatter(grad_weights[1], ("head", "blk"), scatter_dimension=0, tiled=True),
        lax.psum_scatter(grad_weights[2], ("head", "blk"), scatter_dimension=0, tiled=True),
        lax.psum_scatter(grad_out_w, ("head", "blk"), scatter_dimension=1, tiled=True),
        lax.psum_scatter(grad_gain_attn, ("head", "blk"), scatter_dimension=0, tiled=True),
        lax.psum_scatter(table_terms, ("head", "blk"), scatter_dimension=0, tiled=True),
        lax.psum_scatter(grad_gain_moe, ("head", "blk"), scatter_dimension=0, tiled=True),
        lax.psum_scatter(grad_router, ("head", "blk"), scatter_dimension=0, tiled=True),
    )
    return (
        result.astype(jnp.bfloat16).reshape(tokens.shape),
        grad_tokens.reshape(tokens.shape),
        reduced[4],
        reduced[0],
        reduced[1],
        reduced[2],
        reduced[3],
        reduced[5],
        reduced[6],
        reduced[7],
        grad_expert_in,
        grad_expert_out,
    )


BF = jnp.bfloat16
F4 = jnp.float32
NEG = -1e30
QB = 256
TILE = 512
LANES = 128


def dot(left, right, left_dim=1, right_dim=0):
    dims = (((left_dim,), (right_dim,)), ((), ()))
    return lax.dot_general(left, right, dims, preferred_element_type=F4)


def iota(shape, dim):
    return lax.broadcasted_iota(jnp.int32, shape, dim)


class Place:
    def __init__(self, lengths):
        self.lengths = lengths

    def __getitem__(self, item):
        if item == 0:
            return lax.axis_index("blk")
        if item == 1:
            return lax.axis_index("head")
        return self.lengths[lax.axis_index("head")]


class Made(tuple):
    @property
    def token(self):
        return self[-1]


def vmem_call(body, lengths, args, outs, scratch=(), mem=60, ties=()):
    count, tied, made = len(args), len(ties), len(outs)

    def kernel(length_ref, *refs):
        inputs, rest = refs[:count], refs[count + tied :]
        body(Place(length_ref), *inputs, *rest[:made], *rest[made + 1 :])
        rest[made][...] = jnp.zeros((8, LANES), F4)

    vmem = pl.BlockSpec(memory_space=pltpu.VMEM)
    return Made(
        pl.pallas_call(
            kernel,
            out_shape=tuple(outs) + (shaped((8, LANES), F4),),
            in_specs=[pl.BlockSpec(memory_space=pltpu.SMEM)] + [vmem] * (count + tied),
            out_specs=(vmem,) * (made + 1),
            scratch_shapes=list(scratch),
            compiler_params=pltpu.CompilerParams(vmem_limit_bytes=mem * 1024 * 1024),
            cost_estimate=pl.CostEstimate(flops=1, bytes_accessed=1, transcendentals=0),
        )(lengths, *args, *ties)
    )


def shaped(shape, dtype):
    return jax.ShapeDtypeStruct(shape, dtype)


def ring_block(step, own_blk, ring_len):
    half = ring_len // 2
    place = jnp.where((own_blk & 1) == 0, own_blk >> 1, ring_len - 1 - (own_blk >> 1))
    place = (place + step) & (ring_len - 1)
    return jnp.where(place < half, 2 * place, 2 * ring_len - 1 - 2 * place)


def ring_steps(ring_len):
    steps = [0]
    for hop in range(1, ring_len // 2):
        steps += [-hop, hop]
    return steps + [ring_len // 2]


def norm_scale(values):
    return lax.rsqrt(jnp.mean(values * values, axis=-1, keepdims=True) + norm_eps)


def head_tile(block, head, place):
    tile = block[:, LANES * (head // 2) : LANES * (head // 2) + LANES].astype(F4)
    return tile if head % 2 == place else pltpu.roll(tile, HEAD_DIM, 1)


def column(row, size):
    square = jnp.where(iota((size, size), 0) == iota((size, size), 1), row.astype(F4), 0.0)
    return jnp.sum(square, axis=1, keepdims=True)


def pack_units(n, sc, wq, wk, wv, wo_t, gain_a, gain_m, router, table, out):
    rows = wq.shape[0]
    lane = iota((rows, LANES), 1)
    row = iota((rows, LANES), 0)

    def widen(values, at):
        blank = jnp.zeros((values.shape[0], LANES - values.shape[1]), F4)
        return pltpu.roll(jnp.concatenate([values.astype(F4), blank], axis=1), at, 1)

    misc = widen(router[...], 2)
    misc = jnp.where(lane == 0, column(gain_a[...], rows), misc)
    misc = jnp.where(lane == 1, column(gain_m[...], rows), misc)
    listed = jnp.broadcast_to(widen(table[...], 16), (rows, LANES))
    misc = (misc + jnp.where(row == 0, listed, 0.0)).astype(BF)
    for j in range(n):
        pair, turn = j // 2, j % 2
        for c, weight in enumerate((wq, wk, wv)):
            own = head_tile(weight, 3 * pair + turn, 0)
            both = head_tile(weight, 3 * pair + 2, 1)
            out[j, :, LANES * c : LANES * c + LANES] = jnp.where(
                lane < HEAD_DIM, own, both
            ).astype(BF)
        out[j, :, 3 * LANES : 4 * LANES] = misc
        out[j, :, 4 * LANES :] = wo_t[...]


def place_rows(sc, n, rows, parts, dest):
    for kk, part in enumerate(parts):
        for j in range(n):
            first = pl.multiple_of(((sc[1] ^ kk) * n + j) * rows, 8)
            dest[pl.ds(first, rows), :] = part[j].astype(F4)


def unpack_units(n, rows, sc, p0, p1, p2, p3, unit_w, out_t, misc, misc_t, table, buf):
    place_rows(sc, n, rows, (p0, p1, p2, p3), buf)
    unit_w[...] = buf[:, 0 : 3 * LANES].astype(BF)
    out_t[...] = buf[:, 4 * LANES :].astype(BF)
    for b in range(NUM_BUCKETS):
        table[b : b + 1, :] = buf[rows * b : rows * b + 1, 3 * LANES : 4 * LANES]
    tail = buf[:, 3 * LANES : 4 * LANES]
    misc[...] = tail.astype(BF)
    misc_t[...] = jnp.transpose(tail)


def copy_rows(n, sc, *refs):
    parts, out = refs[:-1], refs[-1]
    rows = jnp.concatenate([part[...].astype(F4) for part in parts], axis=0).astype(BF)
    for j in range(n):
        out[j] = rows


def unpack_stack(n, rows, columns, sc, p0, p1, p2, p3, out, buf):
    width = p0.shape[-1]
    for kk, part in enumerate((p0, p1, p2, p3)):
        for j in range(n):
            first = pl.multiple_of(((sc[1] ^ kk) * n + j) * rows, 8)
            block = part[j].astype(F4)
            for c in range(columns):
                buf[pl.ds(first, rows), c * width : (c + 1) * width] = block[c * rows : (c + 1) * rows]
    out[...] = buf[...].astype(BF)


def bias_strips(n, sc, table, buckets, out, line):
    row = iota((8, TILE), 0)
    pair, turn = sc[0] >> 1, sc[0] & 1
    listed = table[...]
    lane = iota(listed.shape, 1)
    reach = buckets.shape[1]
    inside = iota((NUM_BUCKETS, reach), 0) == buckets[...]
    for unit, head in enumerate((3 * pair + turn, 3 * pair + 2)):
        entry = jnp.sum(jnp.where(lane == 16 + head, listed, 0.0), axis=1, keepdims=True)
        line[:, 0:QB] = jnp.zeros((1, QB), F4)
        line[:, QB:] = jnp.sum(jnp.where(inside, entry, 0.0), axis=0, keepdims=True)
        out[unit, 0] = jnp.full((QB, QB), NEG, F4)
        for far in range(n):
            flat = jnp.broadcast_to(line[:, far * QB : far * QB + TILE], (8, TILE))
            turned = flat
            for c in range(1, 8):
                turned = jnp.where(row == c, pltpu.roll(flat, c, 1), turned)
            for group in range(QB // 8):
                moved = turned if group == 0 else pltpu.roll(turned, 8 * group, 1)
                strip = moved[:, QB:]
                if far == 0:
                    after = iota((8, QB), 1) >= iota((8, QB), 0) + 8 * group
                    strip = jnp.where(after, strip, NEG)
                out[unit, far + 1, 8 * group : 8 * group + 8, :] = strip


def ones_row(cols):
    return jnp.where(iota((HEAD_DIM, cols), 0) == 0, 1.0, 0.0).astype(BF)


def unit_operands(n, sc, blocks, misc_t, unit_w, normed, outs):
    key_own, key_both, query_t, key_t, value_t, value_r = outs
    lane = iota((QB, LANES), 1)
    row = iota((QB, LANES), 0)
    gain = misc_t[0:1, :]
    for i, step in enumerate(ring_steps(n)):
        place = ring_block(step, sc[0], n)
        first = pl.multiple_of(place * QB, QB)
        block = jnp.concatenate([part[...].astype(F4) for part in blocks[i]], axis=0)
        rows = (block * norm_scale(block) * gain).astype(BF)
        normed[place] = rows
        made = dot(rows, unit_w[...])
        low = made.astype(BF)
        turned = jnp.transpose(made).astype(BF)
        keys = made[:, LANES : 2 * LANES]
        hidden_key = jnp.where(first + row < sc[2], 0.0, NEG)
        own = jnp.where(lane < HEAD_DIM, keys, jnp.where(lane == HEAD_DIM, hidden_key, 0.0))
        both = jnp.where(lane >= HEAD_DIM, keys, jnp.where(lane == 0, hidden_key, 0.0))
        key_own[pl.ds(first, QB), :] = own.astype(BF)
        key_both[pl.ds(first, QB), :] = both.astype(BF)
        query_t[:, pl.ds(first, QB)] = turned[0:LANES]
        key_t[:, pl.ds(first, QB)] = turned[LANES : 2 * LANES]
        value_t[:, pl.ds(first, QB)] = turned[2 * LANES :]
        value_r[pl.ds(first, QB), :] = low[:, 2 * LANES :]


class Unit:
    def __init__(self, shared, sc):
        self.shared = shared
        self.lo = HEAD_DIM if shared else 0
        self.part = LANES if shared else QB
        self.shift = pl.multiple_of((sc[0] & 1) * LANES, LANES) if shared else 0

    def lanes(self, block):
        return pl.ds(pl.multiple_of(block * QB, QB) + self.shift, self.part)

    def columns(self, ref, pair):
        rows = pl.ds(self.lo, HEAD_DIM)
        return jnp.concatenate([ref[rows, self.lanes(2 * pair + q)] for q in range(2)], axis=1)

    def padded(self, half, other):
        return jnp.concatenate([other, half] if self.shared else [half, other], axis=0)

    def strip(self, bias, far):
        def piece(key_half, query_half):
            at = jnp.maximum(far + query_half - key_half, -1) + 1
            return bias[int(self.shared), at, :, pl.ds(self.shift, self.part)]

        return jnp.concatenate(
            [jnp.concatenate([piece(k, 0), piece(k, 1)], axis=1) for k in range(2)], axis=0
        )


def attend_unit(n, unit, key_ref, query_t, value_t, bias, heads, logs):
    cols = 2 * unit.part

    def one_tile(pair, carry):
        queries = unit.padded(unit.columns(query_t, pair), ones_row(cols))

        def step(part, state):
            top, total, mixed = state
            key_at = pl.multiple_of(part * TILE, TILE)
            scores = dot(key_ref[pl.ds(key_at, TILE), :], queries)
            scores = scores + unit.strip(bias, 2 * (pair - part))
            new_top = jnp.maximum(top, jnp.max(scores, axis=0, keepdims=True))
            weights = jnp.exp(scores - new_top)
            decay = jnp.exp(top - new_top)
            total = total * decay + jnp.sum(weights, axis=0, keepdims=True)
            values = value_t[pl.ds(unit.lo, HEAD_DIM), pl.ds(key_at, TILE)]
            return (new_top, total, mixed * decay + dot(values, weights.astype(BF)))

        zero = jnp.zeros((1, cols), F4)
        top, total, mixed = lax.fori_loop(
            0, pair + 1, step, (zero + NEG, zero, jnp.zeros((HEAD_DIM, cols), F4))
        )
        made = (mixed / total).astype(BF)
        log_total = top + jnp.log(total)
        at = slice(QB, QB + LANES) if unit.shared else slice(0, QB)
        for q in range(2):
            cut = slice(q * unit.part, (q + 1) * unit.part)
            heads[2 * pair + q, :, at] = made[:, cut]
            logs[2 * pair + q] = log_total[:, cut]
        return carry

    lax.fori_loop(0, n // 2, one_tile, 0)


def attend_own(n, sc, *refs):
    blocks = [(ref,) for ref in refs[: n - 1]] + [refs[n - 1 : n + 1]]
    misc_t, unit_w, bias, heads, logs, normed = refs[n + 1 : n + 7]
    outs = refs[n + 7 :]
    unit_operands(n, sc, blocks, misc_t, unit_w, normed, outs)
    attend_unit(n, Unit(False, sc), outs[0], outs[2], outs[4], bias, heads, logs)


def attend_both(n, sc, key_both, query_t, value_t, bias, begun, heads, logs):
    for j in range(n):
        heads[j, :, 0:QB] = begun[j]
    attend_unit(n, Unit(True, sc), key_both, query_t, value_t, bias, heads, logs)


def unit_grads(n, sc, *refs):
    key_own, key_both, query_t, key_t, value_r, bias, heads, grads_in, logs_own, logs_both = refs[:10]
    stacked, table = refs[10:12]
    grad_t, delta_own, delta_both, grad_q, grad_k, grad_v, strips = refs[12:]
    units = (Unit(True, sc), Unit(False, sc))
    for j in range(n):
        grads = grads_in[j]
        grad_t[0:HEAD_DIM, j * QB : (j + 1) * QB] = grads[:, 0:QB]
        grad_t[HEAD_DIM:, units[0].lanes(j)] = grads[:, QB:]
        product = jnp.sum(grads.astype(F4) * heads[j].astype(F4), axis=0, keepdims=True)
        delta_own[j] = product[:, 0:QB]
        delta_both[j] = product[:, QB:]
    grad_k[...] = jnp.zeros(grad_k.shape, F4)
    grad_v[...] = jnp.zeros(grad_v.shape, F4)
    strips[...] = jnp.zeros(strips.shape, F4)

    for unit in units:
        key_ref = key_both if unit.shared else key_own
        logs, delta = (logs_both, delta_both) if unit.shared else (logs_own, delta_own)
        cols = 2 * unit.part

        def one_tile(pair, carry):
            nothing = jnp.zeros((HEAD_DIM, cols), BF)
            raw_queries = unit.columns(query_t, pair)
            queries = unit.padded(raw_queries, ones_row(cols))
            plain = unit.padded(raw_queries, nothing)
            grads = unit.padded(unit.columns(grad_t, pair), nothing)
            log_total = jnp.concatenate([logs[2 * pair + q] for q in range(2)], axis=1)
            inner = jnp.concatenate([delta[2 * pair + q] for q in range(2)], axis=1)

            def step(part, made):
                key_at = pl.multiple_of(part * TILE, TILE)
                far = 2 * (pair - part)
                scores = dot(key_ref[pl.ds(key_at, TILE), :], queries)
                scores = scores + unit.strip(bias, far)
                probs = jnp.exp(scores - log_total)
                grad_probs = dot(value_r[pl.ds(key_at, TILE), :], grads)
                grad_scores = probs * (grad_probs - inner)
                for key_half in range(2):
                    for q in range(2):
                        at = jnp.maximum(far + q - key_half, -1) + 1
                        strips[int(unit.shared), at, :, pl.ds(unit.shift, unit.part)] += grad_scores[
                            key_half * QB : (key_half + 1) * QB,
                            q * unit.part : (q + 1) * unit.part,
                        ]
                low = grad_scores.astype(BF)
                grad_v[pl.ds(key_at, TILE), :] += dot(probs.astype(BF), grads, 1, 1)
                grad_k[pl.ds(key_at, TILE), :] += dot(low, plain, 1, 1)
                return made + dot(key_t[pl.ds(unit.lo, HEAD_DIM), pl.ds(key_at, TILE)], low)

            made = lax.fori_loop(0, pair + 1, step, jnp.zeros((HEAD_DIM, cols), F4))
            for q in range(2):
                cut = made[:, q * unit.part : (q + 1) * unit.part]
                if unit.shared:
                    half = HEAD_DIM // 2
                    cut = jnp.concatenate([cut[0:half], cut[half:]], axis=1)
                    stacked[2 * pair + q, 5 * HEAD_DIM :, :] = cut.astype(BF)
                else:
                    stacked[2 * pair + q, 0:HEAD_DIM, :] = cut.astype(BF)
            return carry

        lax.fori_loop(0, n // 2, one_tile, 0)
    for j in range(n):
        keys = jnp.transpose(grad_k[QB * j : QB * j + QB, :]).astype(BF)
        values = jnp.transpose(grad_v[QB * j : QB * j + QB, :]).astype(BF)
        for at, piece in ((1, keys[0:HEAD_DIM]), (2, values[0:HEAD_DIM])):
            stacked[j, at * HEAD_DIM : (at + 1) * HEAD_DIM, :] = piece
        for at, piece in ((3, keys[HEAD_DIM:]), (4, values[HEAD_DIM:])):
            stacked[j, at * HEAD_DIM : (at + 1) * HEAD_DIM, :] = piece
    row = iota((8, TILE), 0)
    empty = jnp.zeros((8, QB), F4)
    for unit in range(2):
        for far in range(n):
            total = jnp.zeros((8, TILE), F4)
            for group in range(QB // 8):
                rows8 = strips[unit, far + 1, 8 * group : 8 * group + 8, :]
                wide = jnp.concatenate([empty, rows8], axis=1)
                total = total + (wide if group == 0 else pltpu.roll(wide, TILE - 8 * group, 1))
            lined = jnp.where(row == 0, total, 0.0)
            for c in range(1, 8):
                lined = lined + jnp.where(row == c, pltpu.roll(total, TILE - c, 1), 0.0)
            table[unit * n + far] = jnp.sum(lined, axis=0, keepdims=True)


def dispatch_rows(n, cap, sc, route_ref, cot, out, target):
    tok = cot.shape[0]
    route = route_ref[...]
    chosen = iota((n, tok), 0) == route
    upto = jnp.where(iota((tok, tok), 0) <= iota((tok, tok), 1), 1.0, 0.0).astype(BF)
    filled = dot(jnp.where(chosen, 1.0, 0.0).astype(BF), upto)
    slot = jnp.sum(jnp.where(chosen, filled - 1.0, 0.0), axis=0, keepdims=True)
    slot = slot.astype(jnp.int32)
    place = route * cap + slot
    target[...] = jnp.broadcast_to(place, target.shape)
    spread = jnp.where(iota((n * cap, tok), 0) == place, 1.0, 0.0).astype(BF)
    packed = dot(spread, cot[...]).astype(BF)
    for j in range(n):
        out[j] = packed[j * cap : (j + 1) * cap]


def spread_matrix(target, rows):
    place = target[0:1, :]
    return jnp.where(iota((rows, place.shape[1]), 0) == place, 1.0, 0.0)


def hidden_rows(n, cap, sc, heads, wo_t, tokens, misc_t, target, attn, hidden_out, out, buf):
    for pair in range(n // 2):
        at = 3 * pair * HEAD_DIM
        for turn in range(2):
            made = heads[2 * pair + turn].astype(F4)
            buf[at + turn * HEAD_DIM : at + (turn + 1) * HEAD_DIM, :] = made[:, 0:QB]
            both = slice(turn * LANES, (turn + 1) * LANES)
            buf[at + 2 * HEAD_DIM : at + 3 * HEAD_DIM, both] = made[:, QB:]
    rows = jnp.transpose(buf[...]).astype(BF)
    attn[...] = rows
    hidden = tokens[...].astype(F4) + dot(rows, wo_t[...], 1, 1)
    hidden_out[...] = hidden
    moe_in = (hidden * norm_scale(hidden) * misc_t[1:2, :]).astype(BF)
    packed = dot(spread_matrix(target, n * cap).astype(BF), moe_in).astype(BF)
    for j in range(n):
        out[j] = packed[j * cap : (j + 1) * cap]


def gelu_pair(values):
    scale = math.sqrt(2.0 / math.pi)
    square = values * values
    bend = jnp.tanh(scale * (values + 0.044715 * values * square))
    act = 0.5 * values * (1.0 + bend)
    slope = 0.5 * (1.0 + bend) + 0.5 * values * (1.0 - bend * bend) * scale * (
        1.0 + 3.0 * 0.044715 * square
    )
    return (act, slope)


def route_probs(experts, sc, rows, misc):
    logits = dot(rows, misc[...])
    lane = iota(logits.shape, 1)
    real = (lane >= 2) & (lane < 2 + experts)
    logits = jnp.where(real, logits, NEG)
    powers = jnp.where(real, jnp.exp(logits - jnp.max(logits, axis=-1, keepdims=True)), 0.0)
    probs = powers / jnp.sum(powers, axis=-1, keepdims=True)
    chosen = lane == sc[0] + 2
    gate = jnp.sum(jnp.where(chosen, probs, 0.0), axis=-1, keepdims=True)
    return (probs, chosen, gate)


def flat_rows(ref):
    return jnp.concatenate([ref[j] for j in range(ref.shape[0])], axis=0)


def expert_back(
    experts, sc, rows_ref, cot_ref, in_a, out_a, in_b, out_b, misc, back, act_out, log_out, gate_out
):
    rows, cots = flat_rows(rows_ref), flat_rows(cot_ref)
    probs, chosen, gate = route_probs(experts, sc, rows, misc)
    gate_out[...] = jnp.broadcast_to(gate, gate_out.shape)
    inner = jnp.zeros(gate.shape, F4)
    width = in_a.shape[1]
    total = jnp.zeros(rows.shape, F4)
    for half, (w_in, w_out) in enumerate(((in_a, out_a), (in_b, out_b))):
        act, slope = gelu_pair(dot(rows, w_in[...]))
        low = act.astype(BF)
        act_out[:, half * width : (half + 1) * width] = low
        grad_act = dot(cots, w_out[...], 1, 1)
        inner = inner + jnp.sum(low.astype(F4) * grad_act, axis=-1, keepdims=True)
        total = total + dot((gate * grad_act * slope).astype(BF), w_in[...], 1, 1)
    grad_logits = (inner * probs * (jnp.where(chosen, 1.0, 0.0) - gate)).astype(BF)
    log_out[...] = grad_logits
    back[...] = (total + dot(grad_logits, misc[...], 1, 1)).astype(back.dtype)


def expert_forward(sc, act, gate, out_a, out_b, made):
    width = out_a.shape[0]
    total = dot(act[:, :width], out_a[...]) + dot(act[:, width:], out_b[...])
    made[...] = (gate[:, 0:1] * total).astype(made.dtype)


def expert_weights(experts, count, sc, *refs):
    rows_refs, cot_refs = refs[:count], refs[count : 2 * count]
    w_in, w_out, misc, grad_in, grad_out, token, all_rows, all_grads = refs[2 * count :]
    token[...] = jnp.zeros(token.shape, F4)
    size = rows_refs[0].shape[0] * rows_refs[0].shape[1]

    @pl.when(pl.program_id(0) == 0)
    def _():
        for i in range(count):
            at = slice(i * size, (i + 1) * size)
            rows, cots = flat_rows(rows_refs[i]), flat_rows(cot_refs[i])
            gate = route_probs(experts, sc, rows, misc)[2]
            all_rows[at, :] = rows
            all_grads[at, :] = (gate * cots.astype(F4)).astype(BF)

    rows, grads = all_rows[...], all_grads[...]
    act, slope = gelu_pair(dot(rows, w_in[...]))
    grad_pre = (dot(grads, w_out[...], 1, 1) * slope).astype(BF)
    grad_in[...] = dot(rows, grad_pre, 0, 0)
    grad_out[...] = dot(act.astype(BF), grads, 0, 0)


def expert_weights_call(experts, lengths, rows_in, cots_in, w_in, w_out, misc, ties, begun, start, steps):
    count, (depth, hidden) = len(rows_in), w_in.shape
    size = rows_in[0].shape[0] * rows_in[0].shape[1]
    body = functools.partial(expert_weights, experts, count)
    args = tuple(rows_in) + tuple(cots_in) + (w_in, w_out, misc)
    unread = len(ties) + len(begun)

    def kernel(length_ref, *refs):
        body(Place(length_ref), *refs[: len(args)], *refs[len(args) + unread :])

    whole = pl.BlockSpec(memory_space=pltpu.VMEM)
    chunk = 2 * LANES
    columns = pl.BlockSpec((depth, chunk), lambda i: (0, i + start))
    lines = pl.BlockSpec((chunk, depth), lambda i: (i + start, 0))
    first = 1 + len(args) + len(ties)
    return pl.pallas_call(
        kernel,
        grid=(steps,),
        out_shape=(
            shaped((depth, hidden), F4),
            shaped((hidden, depth), F4),
            shaped((8, LANES), F4),
        ),
        in_specs=[pl.BlockSpec(memory_space=pltpu.SMEM)]
        + [whole] * (2 * count)
        + [columns, lines, whole]
        + [whole] * len(ties)
        + [pl.BlockSpec(memory_space=pl.ANY)] * len(begun),
        out_specs=(columns, lines, whole),
        input_output_aliases={first: 0, first + 1: 1} if begun else {},
        scratch_shapes=[
            pltpu.VMEM((count * size, depth), BF),
            pltpu.VMEM((count * size, depth), BF),
        ],
        compiler_params=pltpu.CompilerParams(vmem_limit_bytes=36 * 1024 * 1024),
        cost_estimate=pl.CostEstimate(flops=1, bytes_accessed=1, transcendentals=0),
    )(lengths, *args, *ties, *begun)


def add_stack(n, cap, sc, own, other, out):
    total = (own[...] + other[...].astype(F4)).astype(BF)
    for j in range(n):
        out[j] = total[j * cap : (j + 1) * cap]


def result_rows(n, cap, sc, made, target, hidden, out):
    rows = flat_rows(made)
    spread = jnp.transpose(spread_matrix(target, n * cap)).astype(BF)
    out[...] = (hidden[...] + dot(spread, rows)).astype(BF)


def norm_back(grads, source, gain):
    scale = norm_scale(source)
    weighted = grads * gain
    inner = jnp.mean(weighted * source, axis=-1, keepdims=True)
    return (scale * weighted - source * (scale * scale * scale) * inner, scale)


def hidden_grads(
    n, cap, sc, back, target, hidden_ref, misc_t, cot, wo_t, grad_out, low_out, gain_out, out, buf
):
    spread = jnp.transpose(spread_matrix(target, n * cap)).astype(BF)
    grads = dot(spread, flat_rows(back))
    hidden = hidden_ref[...]
    normed, scale = norm_back(grads, hidden, misc_t[1:2, :])
    gain_out[...] = jnp.broadcast_to(
        jnp.sum(grads * hidden * scale, axis=0, keepdims=True), gain_out.shape
    )
    total = cot[...].astype(F4) + normed
    grad_out[...] = total
    low = total.astype(BF)
    low_out[...] = low
    buf[...] = jnp.transpose(dot(low, wo_t[...])).astype(BF)
    for pair in range(n // 2):
        at = 3 * pair * HEAD_DIM
        for turn in range(2):
            out[2 * pair + turn, :, 0:QB] = buf[at + turn * HEAD_DIM : at + (turn + 1) * HEAD_DIM, :]
            both = slice(turn * LANES, (turn + 1) * LANES)
            out[2 * pair + turn, :, QB:] = buf[at + 2 * HEAD_DIM : at + 3 * HEAD_DIM, both]


def unfolded(piece):
    return jnp.concatenate([piece[:, 0:LANES], piece[:, LANES:]], axis=0)


def token_grads(n, sc, grads, weights, tokens, hidden_grad, misc_t, out, buf):
    inner = weights.shape[1] // 3
    for pair in range(n // 2):
        at = 3 * pair * HEAD_DIM
        last = at + 2 * HEAD_DIM
        for turn in range(2):
            j = 2 * pair + turn
            for c in range(3):
                lo = c * inner + at + turn * HEAD_DIM
                buf[lo : lo + HEAD_DIM, :] = grads[j, c * HEAD_DIM : (c + 1) * HEAD_DIM, :]
            both = slice(turn * LANES, (turn + 1) * LANES)
            buf[last : last + HEAD_DIM, both] = unfolded(grads[j, 5 * HEAD_DIM :, :])
        for c in (1, 2):
            rows = slice((c + 2) * HEAD_DIM, (c + 3) * HEAD_DIM)
            both = grads[2 * pair, rows, :].astype(F4) + grads[2 * pair + 1, rows, :].astype(F4)
            buf[c * inner + last : c * inner + last + HEAD_DIM, :] = both.astype(BF)
    made = jnp.transpose(dot(weights[...], buf[...]))
    normed, unused = norm_back(made, tokens[...].astype(F4), misc_t[0:1, :])
    out[...] = hidden_grad[...] + normed


def unit_weight_grads(n, heads, sc, normed, stacked, lines, buckets, *rest):
    outs, (buf, table) = rest[:heads], rest[heads:]
    width = buf.shape[1]
    sums = []
    for unit in range(2):
        made = jnp.zeros((NUM_BUCKETS, 1), F4)
        for far in range(n):
            line = lines[unit * n + far][:, QB:]
            if far + 1 < n:
                line = line + lines[unit * n + far + 1][:, :QB]
            inside = iota((NUM_BUCKETS, QB), 0) == buckets[:, far * QB : (far + 1) * QB]
            made = made + jnp.sum(jnp.where(inside, line, 0.0), axis=1, keepdims=True)
        sums.append(made)
    lane = iota((NUM_BUCKETS, width), 1)
    high = [value.astype(BF).astype(F4) for value in sums]
    listed = jnp.zeros((NUM_BUCKETS, width), F4)
    for at, value in enumerate(high + [sums[0] - high[0], sums[1] - high[1]]):
        listed = jnp.where(lane == at, value, listed)
    table[...] = listed
    total = None
    for j in range(n):
        grads = stacked[j]
        shared = unfolded(grads[5 * HEAD_DIM :]).astype(F4)
        blank = jnp.zeros(shared.shape, F4)
        turn = jnp.broadcast_to((sc[0] & 1) == 0, shared.shape)
        shared = jnp.concatenate(
            [jnp.where(turn, shared, blank), jnp.where(turn, blank, shared)], axis=1
        )
        pieces = [grads[c * HEAD_DIM : (c + 1) * HEAD_DIM] for c in range(5)]
        own_first = [pieces[0], shared.astype(BF), pieces[1], pieces[3], pieces[2], pieces[4]]
        part = dot(jnp.concatenate(own_first, axis=0), normed[j])
        total = part if total is None else total + part
    buf[...] = jnp.transpose(total)
    rows = buf.shape[0] // heads
    for kk in range(heads):
        to = sc[1] ^ kk
        outs[kk][...] = jnp.concatenate(
            [
                buf[pl.ds(pl.multiple_of(to * rows, 8), rows), :],
                table[pl.ds(pl.multiple_of(to * n, 8), n), :],
                jnp.zeros((8, width), F4),
            ],
            axis=0,
        ).astype(BF)


def two_parts(values, gap):
    high = values.astype(BF).astype(F4)
    lane = iota(values.shape, 1)
    low = pltpu.roll(jnp.where(lane < gap, values - high, 0.0), gap, 1)
    return jnp.where(lane < gap, high, low)


def one_part(values, gap):
    return values + pltpu.roll(values, values.shape[1] - gap, 1)


def weight_sums(n, rows, heads, sc, *refs):
    units, outer = refs[:heads], refs[heads : 2 * heads]
    outs, buf = refs[2 * heads : -1], refs[-1]
    total = (units[0][...].astype(F4) + units[1][...].astype(F4)) + (
        units[2][...].astype(F4) + units[3][...].astype(F4)
    )
    base = n * rows
    entries = two_parts(one_part(total[base : base + n], 2), 2)
    wide = (outer[0][...].astype(F4) + outer[1][...].astype(F4)) + (
        outer[2][...].astype(F4) + outer[3][...].astype(F4)
    )
    width = wide.shape[1] - LANES
    extra = two_parts(one_part(wide[:, width:], 16), 16)
    for to in range(n):
        at = slice(to * rows, (to + 1) * rows)
        entry = jnp.broadcast_to(entries[to : to + 1], (8, entries.shape[1]))
        top = jnp.concatenate([total[at], wide[at, 0:width], extra[at]], axis=1)
        low = jnp.concatenate([entry, jnp.zeros((8, wide.shape[1]), F4)], axis=1)
        buf[to] = jnp.concatenate([top, low], axis=0)
    for k in range(n):
        outs[k][...] = buf[sc[0] ^ k].astype(BF)


def as_row(values):
    size = values.shape[0]
    square = jnp.where(iota((size, size), 0) == iota((size, size), 1), values, 0.0)
    return jnp.sum(square, axis=0, keepdims=True)


def weight_final(n, experts, sc, *refs):
    parts, (wq, wk, wv, gain_a) = refs[:n], refs[n : n + 4]
    grads = refs[n + 4 : n + 7]
    gain, table, grad_out, gain_out, router, buf = refs[n + 7 :]
    rows = wq.shape[0]
    units = 3 * LANES
    for j in range(n):
        buf[sc[0] ^ j] = parts[j][:, 0:units].astype(F4)
    lane = iota((rows, LANES), 1)
    inner = jnp.zeros((rows, 1), F4)
    for c, weight in enumerate((wq, wk, wv)):
        lo = LANES * c

        def piece(head, place):
            pair, turn = head // 3, head % 3
            if turn < 2:
                tile, half = buf[2 * pair + turn, 0:rows, lo : lo + LANES], 0
            else:
                tile = (
                    buf[2 * pair, 0:rows, lo : lo + LANES]
                    + buf[2 * pair + 1, 0:rows, lo : lo + LANES]
                )
                half = 1
            return tile if half == place else pltpu.roll(tile, HEAD_DIM, 1)

        for m in range(weight.shape[1] // LANES):
            tile = jnp.where(lane < HEAD_DIM, piece(2 * m, 0), piece(2 * m + 1, 1))
            cols = slice(LANES * m, LANES * m + LANES)
            grads[c][:, cols] = tile
            inner = inner + jnp.sum(weight[:, cols].astype(F4) * tile, axis=-1, keepdims=True)
    gain[...] = as_row(inner / column(gain_a[...], rows))
    lane = iota((1, HEADS), 1)
    listed = jnp.zeros((1, HEADS), F4)
    for j in range(n):
        entry = one_part(buf[j, rows : rows + 1, 0:LANES], 2)
        listed = listed + jnp.where(lane == 3 * (j // 2) + j % 2, entry[:, 0:1], 0.0)
        listed = listed + jnp.where(lane == 3 * (j // 2) + 2, entry[:, 1:2], 0.0)
    table[...] = listed
    total = parts[0][:, units:].astype(F4)
    for j in range(1, n):
        total = total + parts[j][:, units:].astype(F4)
    width = grad_out.shape[0]
    grad_out[...] = jnp.transpose(total[:, 0:width])[:, 0:rows]
    extra = one_part(total[0:rows, width:], 16)
    gain_out[...] = as_row(extra[:, 1:2])
    router[...] = pltpu.roll(extra, LANES - 2, 1)[:, 0:experts]


def out_weight_grads(heads, sc, low, attn, rows_a, rows_b, logs_a, logs_b, gain, *rest):
    outs, buf = rest[:heads], rest[heads]
    width = attn.shape[1]
    buf[:, 0:width] = dot(low[...], attn[...], 0, 0)
    router = dot(flat_rows(rows_a), logs_a[...], 0, 0) + dot(flat_rows(rows_b), logs_b[...], 0, 0)
    wide = jnp.where(iota((LANES, gain.shape[1]), 0) == 1, gain[0:1, :], 0.0)
    buf[:, width : width + LANES] = two_parts(router + jnp.transpose(wide), 16)
    rows = buf.shape[0] // heads
    for kk in range(heads):
        first = pl.multiple_of((sc[1] ^ kk) * rows, 8)
        outs[kk][...] = buf[pl.ds(first, rows), :].astype(BF)


def swap(values, axis, flip):
    if flip == 0:
        return values
    size = lax.axis_size(axis)
    return lax.ppermute(values, axis, [(i, i ^ flip) for i in range(size)])


def exchange(messages, axis):
    return [swap(message, axis, k) for k, message in enumerate(messages)]


def hold(values, *earlier):
    return lax.optimization_barrier((values, earlier))[0]


def over_heads(stack):
    across = swap(stack, "head", 2)
    return (stack, swap(stack, "head", 1), across, swap(across, "head", 1))


def on_plane(
    tokens,
    attn_gain,
    w_query,
    w_key,
    w_value,
    w_out,
    bias_table,
    moe_gain,
    w_router,
    expert_in,
    expert_out,
    seq_lengths,
    rel_buckets,
    routes,
    cotangent,
):
    heads = lax.axis_size("head")
    n = lax.axis_size("blk")
    tok, width = tokens.shape[0], tokens.shape[2]
    rows = w_query.shape[0]
    total_rows = n * tok
    experts = w_router.shape[1]
    cap = 3 * tok // (2 * experts)
    slots = n * cap
    scope = jax.named_scope
    x = tokens.reshape(tok, width)
    cot = cotangent.reshape(tok, width)
    gain_a = attn_gain.reshape(1, rows)
    gain_m = moe_gain.reshape(1, rows)
    in_own, out_own = expert_in.reshape(expert_in.shape[1:]), expert_out.reshape(expert_out.shape[1:])

    def call(body, args, outs, scratch=(), ties=(), mem=16):
        return vmem_call(body, seq_lengths, args, outs, scratch, mem, ties)

    def all_to_all(stack, axis="blk"):
        return lax.all_to_all(stack, axis, split_axis=0, concat_axis=0, tiled=True)

    order = [ring_of(i, n) for i in range(n)]
    ahead = [(order[i], order[(i + 1) % n]) for i in range(n)]
    astern = [(b, a) for a, b in ahead]
    unit_cols = 4 * LANES + width

    def hop(front, back):
        with scope("ring"):
            front = lax.ppermute(front, "blk", ahead)
            back = lax.ppermute(back, "blk", astern)
            return lax.optimization_barrier((front, back))

    first = hop(x, x)
    with scope("unit_weights"):
        packed, unused = call(
            functools.partial(pack_units, n),
            hold((w_query, w_key, w_value, jnp.transpose(w_out)), first[0])
            + (gain_a, gain_m, w_router, bias_table.reshape(1, -1)),
            [shaped((n, rows, unit_cols), BF)],
            mem=60,
        )
        unit_in = all_to_all(packed)
    second = hop(*first)
    with scope("unit_weights"):
        unit_parts = over_heads(hold(unit_in, second[0]))
        unit_w, out_t, misc, misc_t, table, unused = call(
            functools.partial(unpack_units, n, rows),
            unit_parts,
            [
                shaped((width, 3 * LANES), BF),
                shaped((width, width), BF),
                shaped((width, LANES), BF),
                shaped((LANES, width), F4),
                shaped((NUM_BUCKETS, LANES), F4),
            ],
            [pltpu.VMEM((width, unit_cols), F4)],
        )
    third = hop(*second)
    half = tok // 2
    with scope("ring"):
        front, back = hold((third[0][:half], third[1][half:]), table)
        front, back = lax.ppermute(front, "blk", ahead), lax.ppermute(back, "blk", astern)
    with scope("expert_swap"):
        in_other = swap(hold(in_own, unit_parts[2]), "head", 2)
        out_other = swap(hold(out_own, in_other), "head", 2)

    buckets = rel_buckets.reshape(1, -1)
    with scope("bias"):
        strips, strips_token = call(
            functools.partial(bias_strips, n),
            (table, buckets),
            [shaped((2, n + 1, QB, QB), F4)],
            [pltpu.VMEM((1, QB + total_rows), F4)],
        )

    with scope("cot_rows"):
        cot_out, target, cot_token = call(
            functools.partial(dispatch_rows, n, cap),
            (routes.reshape(1, tok), hold(cot, third[0])),
            [shaped((n, cap, width), BF), shaped((8, tok), jnp.int32)],
        )
        cot_rows = all_to_all(cot_out)

    with scope("attend"):
        (
            heads_own,
            logs_own,
            normed,
            key_own,
            key_both,
            query_t,
            key_t,
            value_t,
            value_r,
            unused,
        ) = call(
            functools.partial(attend_own, n),
            (x,) + first + second + third + (front, back, misc_t, unit_w, strips),
            [
                shaped((n, HEAD_DIM, QB), BF),
                shaped((n, 1, QB), F4),
                shaped((n, tok, width), BF),
                shaped((total_rows, LANES), BF),
                shaped((total_rows, LANES), BF),
                shaped((LANES, total_rows), BF),
                shaped((LANES, total_rows), BF),
                shaped((LANES, total_rows), BF),
                shaped((total_rows, LANES), BF),
            ],
            ties=(cot_token, hold(strips_token, in_other)),
            mem=60,
        )
        head_out, logs_both, unused = call(
            functools.partial(attend_both, n),
            (key_both, query_t, value_t, strips, heads_own),
            [shaped((n, HEAD_DIM, QB + LANES), BF), shaped((n, 1, LANES), F4)],
            ties=(hold(strips_token, cot_rows),),
            mem=20,
        )
        head_in = all_to_all(head_out)
    with scope("cot_pair"):
        cot_pair = swap(cot_rows, "head", 1)
        cot_far = swap(cot_rows, "head", 2)
        cot_far_pair = swap(cot_far, "head", 1)
    with scope("hidden"):
        attn, hidden, moe_out, unused = call(
            functools.partial(hidden_rows, n, cap),
            (head_in, out_t, x, misc_t, target),
            [shaped((tok, width), BF), shaped((tok, width), F4), shaped((n, cap, width), BF)],
            [pltpu.VMEM((width, tok), F4)],
            ties=(hold(strips_token, out_other, cot_pair),),
        )

    with scope("moe_rows"):
        moe_rows = all_to_all(moe_out)
        moe_pair = swap(moe_rows, "head", 1)
    with scope("moe_far"):
        moe_far = swap(moe_rows, "head", 2)
        far_pair = swap(moe_far, "head", 1)

    def backward_rows(rows_in, cots_in, kind, ties=()):
        return call(
            functools.partial(expert_back, experts),
            (rows_in, cots_in, in_own, out_own, in_other, out_other, misc),
            [
                shaped((slots, width), kind),
                shaped((slots, 2 * width), BF),
                shaped((slots, LANES), BF),
                shaped((slots, LANES), F4),
            ],
            ties=ties,
            mem=24,
        )

    def forward_rows(act, gate, kind, ties=()):
        return call(
            expert_forward,
            (act, gate, out_own, out_other),
            [shaped((slots, width), kind)],
            ties=ties,
        )

    with scope("full_weights"):
        w_stack, unused = call(
            functools.partial(copy_rows, n),
            hold((w_query, w_key, w_value), moe_pair),
            [shaped((n, 3 * rows, width), BF)],
        )
        w_in = all_to_all(w_stack)
    with scope("expert_back"):
        back_pair, act_pair, logs_pair, gate_pair, token = backward_rows(moe_pair, cot_pair, BF)
        back_other = swap(back_pair, "head", 1)
        back_own, act_own, logs_own2, gate_own, unused = backward_rows(
            moe_rows, cot_rows, F4, (token,)
        )
        back_out, back_token = call(
            functools.partial(add_stack, n, cap),
            (back_own, back_other),
            [shaped((n, cap, width), BF)],
            ties=(hold(token, w_in),),
        )
        back_in = all_to_all(back_out)
    with scope("full_weights"):
        w_parts = over_heads(hold(w_in, back_token))
    with scope("result_rows"):
        made_pair, token = forward_rows(act_pair, gate_pair, BF, (back_token,))
        made_own, token = forward_rows(act_own, gate_own, F4, (token,))
        res_out, token = call(
            functools.partial(add_stack, n, cap),
            (made_own, swap(made_pair, "head", 1)),
            [shaped((n, cap, width), BF)],
        )
    with scope("expert_weight_grads"):
        expert_args = (
            experts,
            seq_lengths,
            (moe_rows, moe_pair, moe_far, far_pair),
            (cot_rows, cot_pair, cot_far, cot_far_pair),
            in_own,
            out_own,
            misc,
        )
        *begun, expert_token = expert_weights_call(*expert_args, (token,), (), 0, 1)
    with scope("hidden_grads"):
        grad_hidden, grad_low, gain_moe_part, grad_heads_out, hidden_token = call(
            functools.partial(hidden_grads, n, cap),
            (back_in, target, hidden, misc_t, cot, out_t),
            [
                shaped((tok, width), F4),
                shaped((tok, width), BF),
                shaped((8, width), F4),
                shaped((n, HEAD_DIM, QB + LANES), BF),
            ],
            [pltpu.VMEM((width, tok), BF)],
            ties=(expert_token,),
        )
        grad_heads = all_to_all(grad_heads_out)
    wide = width + LANES
    with scope("out_weight_grads"):
        *out_parts, out_token = call(
            functools.partial(out_weight_grads, heads),
            (grad_low, attn, moe_rows, moe_pair, logs_own2, logs_pair, gain_moe_part),
            [shaped((width // heads, wide), BF)] * heads,
            [pltpu.VMEM((width, wide), F4)],
        )
        out_parts_in = exchange(out_parts, "head")
    with scope("expert_weight_grads"):
        steps = in_own.shape[1] // (2 * LANES) - 1
        grad_in, grad_out, expert_token = expert_weights_call(
            *expert_args, (out_token,), begun, 1, steps
        )
    with scope("result_rows"):
        res_in = all_to_all(hold(res_out, grad_heads, expert_token))

    with scope("attend_grads"):
        stacked, lines, unused = call(
            functools.partial(unit_grads, n),
            (
                key_own,
                key_both,
                query_t,
                key_t,
                value_r,
                strips,
                head_out,
                grad_heads,
                logs_own,
                logs_both,
            ),
            [shaped((n, 5 * HEAD_DIM + HEAD_DIM // 2, tok), BF), shaped((2 * n, 1, TILE), F4)],
            [
                pltpu.VMEM((LANES, total_rows), BF),
                pltpu.VMEM((n, 1, QB), F4),
                pltpu.VMEM((n, 1, LANES), F4),
                pltpu.VMEM((8, LANES), F4),
                pltpu.VMEM((total_rows, LANES), F4),
                pltpu.VMEM((total_rows, LANES), F4),
                pltpu.VMEM((2, n + 1, QB, QB), F4),
            ],
            ties=(hold(expert_token, w_parts),),
            mem=32,
        )
        unit_in = all_to_all(hold(stacked, res_in))

    with scope("weight_grads"):
        *unit_grad_parts, parts_token = call(
            functools.partial(unit_weight_grads, n, heads),
            (normed, stacked, lines, buckets),
            [shaped((width // heads + n + 8, 3 * LANES), BF)] * heads,
            [pltpu.VMEM((width, 3 * LANES), F4), pltpu.VMEM((NUM_BUCKETS, 3 * LANES), F4)],
            mem=60,
        )
        *sums, unused = call(
            functools.partial(weight_sums, n, rows, heads),
            exchange(unit_grad_parts, "head") + out_parts_in,
            [shaped((rows + 8, 3 * LANES + wide), BF)] * n,
            [pltpu.VMEM((n, rows + 8, 3 * LANES + wide), F4)],
        )
        sums_in = exchange(sums, "blk")
    with scope("result"):
        result, result_token = call(
            functools.partial(result_rows, n, cap),
            (res_in, target, hidden),
            [shaped((tok, width), BF)],
            ties=(parts_token,),
        )
    with scope("full_weights"):
        full_w, unused = call(
            functools.partial(unpack_stack, n, rows, 3),
            w_parts,
            [shaped((width, 3 * width), BF)],
            [pltpu.VMEM((width, 3 * width), F4)],
            ties=(parts_token,),
            mem=24,
        )
    with scope("weight_final"):
        (
            grad_q,
            grad_k,
            grad_v,
            grad_gain_attn,
            grad_table,
            grad_out_w,
            grad_gain_moe,
            grad_router,
            final_token,
        ) = call(
            functools.partial(weight_final, n, experts),
            sums_in + [w_query, w_key, w_value, gain_a],
            [shaped((rows, width), F4)] * 3
            + [
                shaped((1, rows), F4),
                shaped((1, HEADS), F4),
                shaped((width, rows), F4),
                shaped((1, rows), F4),
                shaped((rows, experts), F4),
            ],
            [pltpu.VMEM((n, rows + 8, 3 * LANES), F4)],
        )
    with scope("token_grads"):
        grad_tokens, unused = call(
            functools.partial(token_grads, n),
            (unit_in, full_w, x, grad_hidden, misc_t),
            [shaped((tok, width), F4)],
            [pltpu.VMEM((3 * width, tok), BF)],
            ties=(result_token, final_token),
            mem=24,
        )
    return (
        result.reshape(tokens.shape),
        grad_tokens.reshape(tokens.shape),
        grad_gain_attn.reshape(-1),
        grad_q,
        grad_k,
        grad_v,
        grad_out_w,
        grad_table.reshape(-1),
        grad_gain_moe.reshape(-1),
        grad_router,
        grad_in.reshape(expert_in.shape),
        grad_out.reshape(expert_out.shape),
    )


def ring_of(place, ring_len):
    return 2 * place if place < ring_len // 2 else 2 * ring_len - 1 - 2 * place


def solution(mesh):
    in_specs = (
        P("blk", "head", None),
        P(("head", "blk")),
        P(("head", "blk"), None),
        P(("head", "blk"), None),
        P(("head", "blk"), None),
        P(None, ("head", "blk")),
        P(("head", "blk")),
        P(("head", "blk")),
        P(("head", "blk"), None),
        P("blk", None, "head"),
        P("blk", "head", None),
        P(),
        P(),
        P("head", "blk", None, None),
        P("blk", "head", None),
    )
    out_specs = (
        P("blk", "head", None),
        P("blk", "head", None),
        P(("head", "blk")),
        P(("head", "blk"), None),
        P(("head", "blk"), None),
        P(("head", "blk"), None),
        P(None, ("head", "blk")),
        P(("head", "blk")),
        P(("head", "blk")),
        P(("head", "blk"), None),
        P("blk", None, "head"),
        P("blk", "head", None),
    )
    one_each = mesh.shape["head"] == 4 and mesh.shape["blk"] == 8
    return jax.shard_map(
        on_plane if one_each else on_device, mesh=mesh, in_specs=in_specs, out_specs=out_specs, check_vma=False
    )
```

```python
import functools
import math

import jax
import jax.numpy as jnp
from jax import lax
from jax.experimental import pallas as pl
from jax.experimental.pallas import tpu as pltpu
from jax.sharding import PartitionSpec as P

HEADS = 12
HEAD_DIM = 64
NUM_BUCKETS = 32


norm_eps = 1e-06
masked_score = -1e30


def inverse_rms(values):
    return lax.rsqrt(jnp.mean(values * values, axis=-1, keepdims=True) + norm_eps)


def norm_backward(grad_normed, source, inv_scale, gain):
    weighted = grad_normed * gain
    inner_mean = jnp.mean(weighted * source, axis=-1, keepdims=True)
    grad_source = inv_scale * weighted - source * (inv_scale * inv_scale * inv_scale) * inner_mean
    grad_gain = jnp.sum(grad_normed * source * inv_scale, axis=0)
    return (grad_source, grad_gain)


def same_state(running):
    return running


def bucket_bounds(rel_buckets):
    bucket_count = NUM_BUCKETS
    labels = jnp.arange(bucket_count, dtype=jnp.int32)
    starts = jnp.sum((rel_buckets[:, None] < labels[None, :]).astype(jnp.int32), axis=0)
    ends = jnp.concatenate([starts[1:], jnp.full((1,), rel_buckets.shape[0] + 1, jnp.int32)])
    return (starts, ends)


def bias_terms(query_positions, key_positions, bounds, table32):
    starts, ends = bounds
    distance = jnp.maximum(query_positions[:, None] - key_positions[None, :], 0)[:, :, None]
    inside = (distance >= starts[None, None, :]) & (distance < ends[None, None, :])
    onehot = inside.astype(jnp.bfloat16)
    bias = jnp.einsum(
        "qkb,bh->hqk", onehot, table32.astype(jnp.bfloat16), preferred_element_type=jnp.float32
    )
    return (onehot, bias)


def block_scores(queries, keys, query_positions, key_positions, seq_lengths, bounds, table32):
    onehot, bias = bias_terms(query_positions, key_positions, bounds, table32)
    raw = jnp.einsum("qshd,kshd->hsqk", queries, keys, preferred_element_type=jnp.float32)
    causal = key_positions[None, :] <= query_positions[:, None]
    present = key_positions[None, :] < seq_lengths[:, None]
    valid = causal[None, :, :] & present[:, None, :]
    return (raw + bias[:, None, :, :], valid[None], onehot)


def attend_step(
    running, queries, keys, values, query_positions, key_positions, seq_lengths, bounds, table32
):
    row_top, row_total, weighted = running
    scores, valid, unused = block_scores(
        queries, keys, query_positions, key_positions, seq_lengths, bounds, table32
    )
    scores = jnp.where(valid, scores, masked_score)
    new_top = jnp.maximum(row_top, jnp.max(scores, axis=-1))
    weights = jnp.where(valid, jnp.exp(scores - new_top[..., None]), 0.0)
    decay = jnp.exp(row_top - new_top)
    row_total = row_total * decay + jnp.sum(weights, axis=-1)
    mixed = jnp.einsum(
        "hsqk,kshd->qshd", weights.astype(jnp.bfloat16), values, preferred_element_type=jnp.float32
    )
    weighted = weighted * jnp.transpose(decay, (2, 1, 0))[..., None] + mixed
    return (new_top, row_total, weighted)


def grad_step(
    queries,
    grad_heads,
    log_total,
    delta,
    query_positions,
    keys,
    values,
    key_positions,
    seq_lengths,
    bounds,
    table32,
):
    scores, valid, onehot = block_scores(
        queries, keys, query_positions, key_positions, seq_lengths, bounds, table32
    )
    probs = jnp.where(valid, jnp.exp(scores - jnp.transpose(log_total, (2, 1, 0))[..., None]), 0.0)
    grad_probs = jnp.einsum(
        "qshd,kshd->hsqk", grad_heads, values, preferred_element_type=jnp.float32
    )
    grad_scores = probs * (grad_probs - jnp.transpose(delta, (2, 1, 0))[..., None])
    grad_table = jnp.einsum(
        "hqk,qkb->bh",
        jnp.sum(grad_scores, axis=1),
        onehot.astype(jnp.float32),
        precision=lax.Precision.HIGHEST,
    )
    low_scores = grad_scores.astype(jnp.bfloat16)
    grad_queries = jnp.einsum(
        "hsqk,kshd->qshd", low_scores, keys, preferred_element_type=jnp.float32
    )
    grad_keys = jnp.einsum(
        "hsqk,qshd->kshd", low_scores, queries, preferred_element_type=jnp.float32
    )
    grad_values = jnp.einsum(
        "hsqk,qshd->kshd",
        probs.astype(jnp.bfloat16),
        grad_heads,
        preferred_element_type=jnp.float32,
    )
    return (grad_queries, grad_keys, grad_values, grad_table)


def on_device(
    tokens,
    attn_gain,
    w_query,
    w_key,
    w_value,
    w_out,
    bias_table,
    moe_gain,
    w_router,
    expert_in,
    expert_out,
    seq_lengths,
    rel_buckets,
    routes,
    cotangent,
):
    head_count = lax.axis_size("head")
    blk_count = lax.axis_size("blk")
    head_index = lax.axis_index("head")
    blk_index = lax.axis_index("blk")
    block_rows, group_seqs, width = tokens.shape
    seq_count = group_seqs * head_count
    tok_rows = block_rows * group_seqs
    local_heads = HEADS // head_count
    head_width = local_heads * HEAD_DIM
    group_rows = block_rows * max(1, blk_count // 8)
    longest = jnp.max(seq_lengths)
    query_first = blk_index * block_rows
    query_last = query_first + block_rows - 1
    query_positions = query_first + jnp.arange(block_rows, dtype=jnp.int32)
    bounds = bucket_bounds(rel_buckets)
    fetched = (
        lax.all_gather(w_query, ("head", "blk"), axis=0, tiled=True),
        lax.all_gather(w_key, ("head", "blk"), axis=0, tiled=True),
        lax.all_gather(w_value, ("head", "blk"), axis=0, tiled=True),
        lax.all_gather(w_out, ("head", "blk"), axis=1, tiled=True),
        lax.all_gather(attn_gain, ("head", "blk"), axis=0, tiled=True),
        lax.all_gather(bias_table, ("head", "blk"), axis=0, tiled=True),
        lax.all_gather(moe_gain, ("head", "blk"), axis=0, tiled=True),
        lax.all_gather(w_router, ("head", "blk"), axis=0, tiled=True),
    )
    full_query, full_key, full_value, full_out, gain_attn, table_flat, gain_moe, full_router = (
        fetched
    )
    inner_width = full_query.shape[1]
    table_all = table_flat.astype(jnp.float32).reshape(NUM_BUCKETS, HEADS)
    table32 = lax.dynamic_slice_in_dim(table_all, head_index * local_heads, local_heads, 1)
    gain_attn32 = gain_attn.astype(jnp.float32)
    gain_moe32 = gain_moe.astype(jnp.float32)

    def to_heads(values):
        parts = values.shape[1]
        shaped = values.reshape(block_rows, group_seqs, parts, head_count, head_width)
        moved = lax.all_to_all(shaped, "head", split_axis=3, concat_axis=1, tiled=True)
        return moved.reshape(block_rows, seq_count, parts, local_heads, HEAD_DIM)

    def to_tokens(values):
        parts = values.shape[2]
        shaped = values.reshape(block_rows, seq_count, parts, 1, head_width)
        moved = lax.all_to_all(shaped, "head", split_axis=1, concat_axis=3, tiled=True)
        return moved.reshape(tok_rows, parts, inner_width)

    source = tokens.astype(jnp.float32).reshape(tok_rows, width)
    inv_attn = inverse_rms(source)
    attn_in = (source * inv_attn * gain_attn32).astype(jnp.bfloat16)
    stacked_weights = jnp.stack((full_query, full_key, full_value))
    projected = jnp.einsum(
        "td,cde->tce", attn_in, stacked_weights, preferred_element_type=jnp.float32
    ).astype(jnp.bfloat16)
    heads_in = to_heads(projected)
    queries = heads_in[:, :, 0]
    keys = heads_in[:, :, 1]
    values = heads_in[:, :, 2]
    start_state = (
        jnp.full((local_heads, seq_count, block_rows), masked_score, jnp.float32),
        jnp.zeros((local_heads, seq_count, block_rows), jnp.float32),
        jnp.zeros((block_rows, seq_count, local_heads, HEAD_DIM), jnp.float32),
    )
    key_piece = lax.all_gather(keys, "blk", axis=0, tiled=True)
    value_piece = lax.all_gather(values, "blk", axis=0, tiled=True)
    piece_rows = key_piece.shape[0]
    part_rows = math.gcd(piece_rows, group_rows)

    def forward_one_part(step_index, inner_state):
        offset = step_index * part_rows
        key_part = lax.dynamic_slice_in_dim(key_piece, offset, part_rows, 0)
        value_part = lax.dynamic_slice_in_dim(value_piece, offset, part_rows, 0)
        key_positions = offset + jnp.arange(part_rows, dtype=jnp.int32)

        def attend_now(current):
            return attend_step(
                current,
                queries,
                key_part,
                value_part,
                query_positions,
                key_positions,
                seq_lengths,
                bounds,
                table32,
            )

        skipped = (offset > query_last) | (offset >= longest)
        return lax.cond(skipped, same_state, attend_now, inner_state)

    row_top, row_total, weighted = lax.fori_loop(
        0, piece_rows // part_rows, forward_one_part, start_state
    )
    attn_heads = (weighted / jnp.transpose(row_total, (2, 1, 0))[..., None]).astype(jnp.bfloat16)
    log_total = jnp.transpose(row_top + jnp.log(row_total), (2, 1, 0))
    attn_tok = to_tokens(attn_heads[:, :, None])[:, 0]
    branch = jnp.dot(attn_tok, full_out, preferred_element_type=jnp.float32)
    hidden = source + branch
    expert_count = full_router.shape[1]
    local_experts = expert_in.shape[0]
    capacity = max(2, 3 * tok_rows // (2 * expert_count))
    inv_moe = inverse_rms(hidden)
    moe_in = (hidden * inv_moe * gain_moe32).astype(jnp.bfloat16)
    logits = jnp.dot(moe_in, full_router, preferred_element_type=jnp.float32)
    router_probs = jax.nn.softmax(logits, axis=-1)
    route_flat = routes.reshape(tok_rows)
    chosen = route_flat[:, None] == jnp.arange(expert_count, dtype=jnp.int32)[None, :]
    gate = jnp.sum(jnp.where(chosen, router_probs, 0.0), axis=-1)
    filled = jnp.cumsum(chosen.astype(jnp.int32), axis=0)
    slot = jnp.sum(jnp.where(chosen, filled - 1, 0), axis=-1)
    target = route_flat * capacity + slot
    dispatch = (
        target[:, None] == jnp.arange(expert_count * capacity, dtype=jnp.int32)[None, :]
    ).astype(jnp.bfloat16)

    def to_buffer(token_rows):
        packed = jnp.einsum(
            "tj,td->jd", dispatch, token_rows, preferred_element_type=jnp.float32
        ).astype(jnp.bfloat16)
        return packed.reshape(blk_count, local_experts, capacity, width)

    def from_buffer(buffer):
        return jnp.dot(
            dispatch,
            buffer.reshape(expert_count * capacity, width),
            preferred_element_type=jnp.float32,
        )

    def to_experts(buffer):
        return lax.all_to_all(buffer, "blk", split_axis=0, concat_axis=0, tiled=True)

    def all_rows(buffer):
        return lax.all_gather(buffer, "head", axis=0, tiled=True)

    def summed_rows(partial_terms):
        return lax.psum_scatter(
            partial_terms.astype(jnp.bfloat16), "head", scatter_dimension=0, tiled=True
        ).astype(jnp.float32)

    def to_owners(buffer):
        return lax.all_to_all(buffer, "blk", split_axis=0, concat_axis=0, tiled=True)

    expert_rows_in = all_rows(to_experts(to_buffer(moe_in)))
    expert_pre = jnp.einsum(
        "necd,edf->necf", expert_rows_in, expert_in, preferred_element_type=jnp.float32
    )
    expert_act, gelu_pull = jax.vjp(jax.nn.gelu, expert_pre)
    expert_low = expert_act.astype(jnp.bfloat16)
    expert_terms = jnp.einsum(
        "necf,efd->necd", expert_low, expert_out, preferred_element_type=jnp.float32
    )
    expert_tok = from_buffer(to_owners(summed_rows(expert_terms).astype(jnp.bfloat16)))
    result = hidden + gate[:, None] * expert_tok
    grad_result = cotangent.astype(jnp.float32).reshape(tok_rows, width)
    grad_expert_tok = (gate[:, None] * grad_result).astype(jnp.bfloat16)
    grad_gate = jnp.sum(grad_result * expert_tok, axis=-1)
    grad_logits = (
        router_probs * (jnp.where(chosen, grad_gate[:, None], 0.0) - (gate * grad_gate)[:, None])
    ).astype(jnp.bfloat16)
    grad_router = jnp.einsum("td,te->de", moe_in, grad_logits, preferred_element_type=jnp.float32)
    grad_rows = all_rows(to_experts(to_buffer(grad_expert_tok)))
    grad_act = jnp.einsum(
        "necd,efd->necf", grad_rows, expert_out, preferred_element_type=jnp.float32
    )
    grad_pre = gelu_pull(grad_act)[0].astype(jnp.bfloat16)
    grad_expert_out = jnp.einsum(
        "necf,necd->efd", expert_low, grad_rows, preferred_element_type=jnp.float32
    )
    grad_expert_in = jnp.einsum(
        "necd,necf->edf", expert_rows_in, grad_pre, preferred_element_type=jnp.float32
    )
    grad_back = jnp.einsum(
        "necf,edf->necd", grad_pre, expert_in, preferred_element_type=jnp.float32
    )
    grad_moe_in = from_buffer(to_owners(summed_rows(grad_back).astype(jnp.bfloat16)))
    grad_moe_in = grad_moe_in + jnp.einsum(
        "te,de->td", grad_logits, full_router, preferred_element_type=jnp.float32
    )
    grad_norm_moe, grad_gain_moe = norm_backward(grad_moe_in, hidden, inv_moe, gain_moe32)
    grad_hidden = grad_result + grad_norm_moe
    grad_branch = grad_hidden.astype(jnp.bfloat16)
    grad_out_w = jnp.einsum("te,td->ed", attn_tok, grad_branch, preferred_element_type=jnp.float32)
    grad_attn_tok = jnp.einsum(
        "td,ed->te", grad_branch, full_out, preferred_element_type=jnp.float32
    ).astype(jnp.bfloat16)
    grad_heads = to_heads(grad_attn_tok[:, None])[:, :, 0]
    delta = jnp.sum(grad_heads.astype(jnp.float32) * attn_heads.astype(jnp.float32), axis=-1)
    all_keys = lax.all_gather(keys, "blk", axis=0, tiled=True)
    all_values = lax.all_gather(values, "blk", axis=0, tiled=True)
    total_rows = all_keys.shape[0]
    step_rows = math.gcd(total_rows, group_rows)
    zero_heads = jnp.zeros((block_rows, seq_count, local_heads, HEAD_DIM), jnp.float32)
    zero_table = jnp.zeros(table32.shape, jnp.float32)

    def query_side(step_index, running):
        offset = step_index * step_rows
        key_block = lax.dynamic_slice_in_dim(all_keys, offset, step_rows, 0)
        value_block = lax.dynamic_slice_in_dim(all_values, offset, step_rows, 0)
        key_positions = offset + jnp.arange(step_rows, dtype=jnp.int32)

        def query_compute(current):
            grads = grad_step(
                queries,
                grad_heads,
                log_total,
                delta,
                query_positions,
                key_block,
                value_block,
                key_positions,
                seq_lengths,
                bounds,
                table32,
            )
            return (current[0] + grads[0], current[1] + grads[3])

        skipped = (offset > query_last) | (offset >= longest)
        return lax.cond(skipped, same_state, query_compute, running)

    grad_queries, grad_table = lax.fori_loop(
        0, total_rows // step_rows, query_side, (zero_heads, zero_table)
    )
    all_totals, all_deltas = (
        lax.all_gather(log_total, "blk", axis=0, tiled=True),
        lax.all_gather(delta, "blk", axis=0, tiled=True),
    )
    query_piece = lax.all_gather(queries, "blk", axis=0, tiled=True)
    grad_piece = lax.all_gather(grad_heads, "blk", axis=0, tiled=True)
    piece_rows = query_piece.shape[0]
    key_part_rows = math.gcd(piece_rows, group_rows)

    def key_one_part(step_index, inner_state):
        offset = step_index * key_part_rows
        query_part = lax.dynamic_slice_in_dim(query_piece, offset, key_part_rows, 0)
        grad_part = lax.dynamic_slice_in_dim(grad_piece, offset, key_part_rows, 0)
        total_part = lax.dynamic_slice_in_dim(all_totals, offset, key_part_rows, 0)
        delta_part = lax.dynamic_slice_in_dim(all_deltas, offset, key_part_rows, 0)
        part_positions = offset + jnp.arange(key_part_rows, dtype=jnp.int32)

        def key_compute(current):
            grads = grad_step(
                query_part,
                grad_part,
                total_part,
                delta_part,
                part_positions,
                keys,
                values,
                query_positions,
                seq_lengths,
                bounds,
                table32,
            )
            return (current[0] + grads[1], current[1] + grads[2])

        skipped = (offset + key_part_rows - 1 < query_first) | (query_first >= longest)
        return lax.cond(skipped, same_state, key_compute, inner_state)

    grad_keys, grad_values = lax.fori_loop(
        0, piece_rows // key_part_rows, key_one_part, (zero_heads, zero_heads)
    )
    grad_stack = jnp.stack((grad_queries, grad_keys, grad_values), axis=2).astype(jnp.bfloat16)
    grad_projected = to_tokens(grad_stack)
    grad_weights = jnp.einsum(
        "td,tce->cde", attn_in, grad_projected, preferred_element_type=jnp.float32
    )
    grad_attn_in = jnp.einsum(
        "tce,cde->td", grad_projected, stacked_weights, preferred_element_type=jnp.float32
    )
    grad_norm_attn, grad_gain_attn = norm_backward(grad_attn_in, source, inv_attn, gain_attn32)
    grad_tokens = grad_hidden + grad_norm_attn
    table_terms = lax.dynamic_update_slice_in_dim(
        jnp.zeros((NUM_BUCKETS, HEADS), jnp.float32), grad_table, head_index * local_heads, 1
    ).reshape(NUM_BUCKETS * HEADS)
    reduced = (
        lax.psum_scatter(grad_weights[0], ("head", "blk"), scatter_dimension=0, tiled=True),
        lax.psum_scatter(grad_weights[1], ("head", "blk"), scatter_dimension=0, tiled=True),
        lax.psum_scatter(grad_weights[2], ("head", "blk"), scatter_dimension=0, tiled=True),
        lax.psum_scatter(grad_out_w, ("head", "blk"), scatter_dimension=1, tiled=True),
        lax.psum_scatter(grad_gain_attn, ("head", "blk"), scatter_dimension=0, tiled=True),
        lax.psum_scatter(table_terms, ("head", "blk"), scatter_dimension=0, tiled=True),
        lax.psum_scatter(grad_gain_moe, ("head", "blk"), scatter_dimension=0, tiled=True),
        lax.psum_scatter(grad_router, ("head", "blk"), scatter_dimension=0, tiled=True),
    )
    return (
        result.astype(jnp.bfloat16).reshape(tokens.shape),
        grad_tokens.reshape(tokens.shape),
        reduced[4],
        reduced[0],
        reduced[1],
        reduced[2],
        reduced[3],
        reduced[5],
        reduced[6],
        reduced[7],
        grad_expert_in,
        grad_expert_out,
    )


BF = jnp.bfloat16
F4 = jnp.float32
NEG = -1e30
QB = 256
TILE = 512
LANES = 128


def dot(left, right, left_dim=1, right_dim=0):
    dims = (((left_dim,), (right_dim,)), ((), ()))
    return lax.dot_general(left, right, dims, preferred_element_type=F4)


def iota(shape, dim):
    return lax.broadcasted_iota(jnp.int32, shape, dim)


class Place:
    def __init__(self, lengths):
        self.lengths = lengths

    def __getitem__(self, item):
        if item == 0:
            return lax.axis_index("blk")
        if item == 1:
            return lax.axis_index("head")
        return self.lengths[lax.axis_index("head")]


class Made(tuple):
    @property
    def token(self):
        return self[-1]


def vmem_call(body, lengths, args, outs, scratch=(), ties=(), loose=(), away=()):
    count, tied, made = len(args), len(ties), len(outs)

    def kernel(length_ref, *refs):
        inputs, rest = refs[:count], refs[count + tied :]
        body(Place(length_ref), *inputs, *rest[:made], *rest[made + 1 :])
        rest[made][...] = jnp.zeros((8, LANES), F4)

    vmem = pl.BlockSpec(memory_space=pltpu.VMEM)
    place = pl.BlockSpec(memory_space=pl.ANY)
    return Made(
        pl.pallas_call(
            kernel,
            out_shape=tuple(outs) + (shaped((8, LANES), F4),),
            in_specs=[pl.BlockSpec(memory_space=pltpu.SMEM)]
            + [place if i in loose else vmem for i in range(count)]
            + [vmem] * tied,
            out_specs=tuple(place if i in away else vmem for i in range(made)) + (vmem,),
            scratch_shapes=list(scratch),
            compiler_params=pltpu.CompilerParams(vmem_limit_bytes=60 * 1024 * 1024),
            cost_estimate=pl.CostEstimate(flops=1, bytes_accessed=1, transcendentals=0),
        )(lengths, *args, *ties)
    )


def shaped(shape, dtype):
    return jax.ShapeDtypeStruct(shape, dtype)


def ring_block(step, own_blk, ring_len):
    half = ring_len // 2
    place = jnp.where((own_blk & 1) == 0, own_blk >> 1, ring_len - 1 - (own_blk >> 1))
    place = (place + step) & (ring_len - 1)
    return jnp.where(place < half, 2 * place, 2 * ring_len - 1 - 2 * place)


def ring_steps(ring_len):
    steps = [0]
    for hop in range(1, ring_len // 2):
        steps += [-hop, hop]
    return steps + [ring_len // 2]


def norm_scale(values):
    return lax.rsqrt(jnp.mean(values * values, axis=-1, keepdims=True) + norm_eps)


def head_tile(block, head, place):
    tile = block[:, LANES * (head // 2) : LANES * (head // 2) + LANES].astype(F4)
    return tile if head % 2 == place else pltpu.roll(tile, HEAD_DIM, 1)


def column(row, size):
    square = jnp.where(iota((size, size), 0) == iota((size, size), 1), row.astype(F4), 0.0)
    return jnp.sum(square, axis=1, keepdims=True)


def pack_units(n, sc, wq, wk, wv, gain_a, gain_m, router, table, out):
    rows = wq.shape[0]
    lane = iota((rows, LANES), 1)
    row = iota((rows, LANES), 0)

    def widen(values, at):
        blank = jnp.zeros((values.shape[0], LANES - values.shape[1]), F4)
        return pltpu.roll(jnp.concatenate([values.astype(F4), blank], axis=1), at, 1)

    misc = widen(jnp.transpose(router[...].astype(F4)), 2)
    misc = jnp.where(lane == 0, column(gain_a[...], rows), misc)
    misc = jnp.where(lane == 1, column(gain_m[...], rows), misc)
    listed = jnp.broadcast_to(widen(table[...], 16), (rows, LANES))
    misc = (misc + jnp.where(row == 0, listed, 0.0)).astype(BF)
    for j in range(n):
        pair, turn = j // 2, j % 2
        for c, weight in enumerate((wq, wk, wv)):
            own = head_tile(weight, 3 * pair + turn, 0)
            both = head_tile(weight, 3 * pair + 2, 1)
            out[j, :, LANES * c : LANES * c + LANES] = jnp.where(
                lane < HEAD_DIM, own, both
            ).astype(BF)
        out[j, :, 3 * LANES : 4 * LANES] = misc


def place_rows(sc, n, rows, parts, dest):
    for kk, part in enumerate(parts):
        for j in range(n):
            first = pl.multiple_of(((sc[1] ^ kk) * n + j) * rows, 8)
            dest[pl.ds(first, rows), :] = part[j].astype(F4)


def unpack_units(n, rows, sc, p0, p1, p2, p3, unit_w, misc, misc_t, table, buf):
    place_rows(sc, n, rows, (p0, p1, p2, p3), buf)
    unit_w[...] = buf[:, 0 : 3 * LANES].astype(BF)
    for b in range(NUM_BUCKETS):
        table[b : b + 1, :] = buf[rows * b : rows * b + 1, 3 * LANES : 4 * LANES]
    tail = buf[:, 3 * LANES : 4 * LANES]
    misc[...] = tail.astype(BF)
    misc_t[...] = jnp.transpose(tail)


def bias_strips(n, sc, table, buckets, out, line):
    row = iota((8, TILE), 0)
    pair, turn = sc[0] >> 1, sc[0] & 1
    listed = table[...]
    lane = iota(listed.shape, 1)
    reach = buckets.shape[1]
    inside = iota((NUM_BUCKETS, reach), 0) == buckets[...]
    for unit, head in enumerate((3 * pair + turn, 3 * pair + 2)):
        entry = jnp.sum(jnp.where(lane == 16 + head, listed, 0.0), axis=1, keepdims=True)
        line[:, 0:QB] = jnp.zeros((1, QB), F4)
        line[:, QB:] = jnp.sum(jnp.where(inside, entry, 0.0), axis=0, keepdims=True)
        out[unit, 0] = jnp.full((QB, QB), NEG, F4)
        for far in range(n):
            flat = jnp.broadcast_to(line[:, far * QB : far * QB + TILE], (8, TILE))
            turned = flat
            for c in range(1, 8):
                turned = jnp.where(row == c, pltpu.roll(flat, c, 1), turned)
            for group in range(QB // 8):
                moved = turned if group == 0 else pltpu.roll(turned, 8 * group, 1)
                strip = moved[:, QB:]
                if far == 0:
                    after = iota((8, QB), 1) >= iota((8, QB), 0) + 8 * group
                    strip = jnp.where(after, strip, NEG)
                out[unit, far + 1, 8 * group : 8 * group + 8, :] = strip


def ones_row(cols):
    return jnp.where(iota((HEAD_DIM, cols), 0) == 0, 1.0, 0.0).astype(BF)


def unit_operands(n, sc, blocks, misc_t, unit_w, normed, outs):
    key_own, key_both, query_t, key_t, value_t, value_r = outs
    lane = iota((QB, LANES), 1)
    row = iota((QB, LANES), 0)
    gain = misc_t[0:1, :]
    for i, step in enumerate(ring_steps(n)):
        place = ring_block(step, sc[0], n)
        first = pl.multiple_of(place * QB, QB)
        block = jnp.concatenate([part[...].astype(F4) for part in blocks[i]], axis=0)
        rows = (block * norm_scale(block) * gain).astype(BF)
        normed[place] = rows
        made = dot(rows, unit_w[...])
        low = made.astype(BF)
        turned = jnp.transpose(made).astype(BF)
        keys = made[:, LANES : 2 * LANES]
        hidden_key = jnp.where(first + row < sc[2], 0.0, NEG)
        own = jnp.where(lane < HEAD_DIM, keys, jnp.where(lane == HEAD_DIM, hidden_key, 0.0))
        both = jnp.where(lane >= HEAD_DIM, keys, jnp.where(lane == 0, hidden_key, 0.0))
        key_own[pl.ds(first, QB), :] = own.astype(BF)
        key_both[pl.ds(first, QB), :] = both.astype(BF)
        query_t[:, pl.ds(first, QB)] = turned[0:LANES]
        key_t[:, pl.ds(first, QB)] = turned[LANES : 2 * LANES]
        value_t[:, pl.ds(first, QB)] = turned[2 * LANES :]
        value_r[pl.ds(first, QB), :] = low[:, 2 * LANES :]


class Unit:
    def __init__(self, shared, sc):
        self.shared = shared
        self.lo = HEAD_DIM if shared else 0
        self.part = LANES if shared else QB
        self.shift = pl.multiple_of((sc[0] & 1) * LANES, LANES) if shared else 0

    def lanes(self, block):
        return pl.ds(pl.multiple_of(block * QB, QB) + self.shift, self.part)

    def columns(self, ref, pair):
        rows = pl.ds(self.lo, HEAD_DIM)
        return jnp.concatenate([ref[rows, self.lanes(2 * pair + q)] for q in range(2)], axis=1)

    def padded(self, half, other):
        return jnp.concatenate([other, half] if self.shared else [half, other], axis=0)

    def strip(self, bias, far):
        def piece(key_half, query_half):
            at = jnp.maximum(far + query_half - key_half, -1) + 1
            return bias[int(self.shared), at, :, pl.ds(self.shift, self.part)]

        return jnp.concatenate(
            [jnp.concatenate([piece(k, 0), piece(k, 1)], axis=1) for k in range(2)], axis=0
        )


def attend_unit(n, unit, key_ref, query_t, value_t, bias, heads, logs):
    cols = 2 * unit.part

    def one_tile(pair, carry):
        queries = unit.padded(unit.columns(query_t, pair), ones_row(cols))

        def step(part, state):
            top, total, mixed = state
            key_at = pl.multiple_of(part * TILE, TILE)
            scores = dot(key_ref[pl.ds(key_at, TILE), :], queries)
            scores = scores + unit.strip(bias, 2 * (pair - part))
            new_top = jnp.maximum(top, jnp.max(scores, axis=0, keepdims=True))
            weights = jnp.exp(scores - new_top)
            decay = jnp.exp(top - new_top)
            total = total * decay + jnp.sum(weights, axis=0, keepdims=True)
            values = value_t[pl.ds(unit.lo, HEAD_DIM), pl.ds(key_at, TILE)]
            return (new_top, total, mixed * decay + dot(values, weights.astype(BF)))

        zero = jnp.zeros((1, cols), F4)
        top, total, mixed = lax.fori_loop(
            0, pair + 1, step, (zero + NEG, zero, jnp.zeros((HEAD_DIM, cols), F4))
        )
        made = (mixed / total).astype(BF)
        log_total = top + jnp.log(total)
        at = slice(QB, QB + LANES) if unit.shared else slice(0, QB)
        for q in range(2):
            cut = slice(q * unit.part, (q + 1) * unit.part)
            heads[2 * pair + q, :, at] = made[:, cut]
            logs[2 * pair + q] = log_total[:, cut]
        return carry

    lax.fori_loop(0, n // 2, one_tile, 0)


def copies_of(pairs, sems):
    return [
        pltpu.make_async_copy(source, dest, sems.at[i]) for i, (source, dest) in enumerate(pairs)
    ]


def attend_units(n, sc, *refs):
    blocks = [(ref,) for ref in refs[: n - 1]] + [refs[n - 1 : n + 1]]
    misc_t, unit_w, table, buckets, heads, logs_own, logs_both = refs[n + 1 : n + 8]
    outs = refs[n + 8 : n + 15]
    kept, (value_t, line, sems) = refs[n + 15 : n + 22], refs[n + 22 :]
    normed, key_own, key_both, query_t, key_t, value_r, bias = kept
    copies = copies_of(list(zip(kept, outs)), sems)
    placed = (key_own, key_both, query_t, key_t, value_t, value_r)
    unit_operands(n, sc, blocks, misc_t, unit_w, normed, placed)
    for copy in copies[:-1]:
        copy.start()
    bias_strips(n, sc, table, buckets, bias, line)
    copies[-1].start()
    attend_unit(n, Unit(False, sc), key_own, query_t, value_t, bias, heads, logs_own)
    attend_unit(n, Unit(True, sc), key_both, query_t, value_t, bias, heads, logs_both)
    for copy in copies:
        copy.wait()


def unit_grads(n, sc, *refs):
    key_own, key_both, query_t, key_t, value_r, bias, heads, grads_in, logs_own, logs_both = refs[:10]
    stacked, table = refs[10:12]
    grad_t, delta_own, delta_both, grad_k, grad_v, strips, held, sems = refs[12:]
    units = (Unit(True, sc), Unit(False, sc))
    copies = copies_of([(bias.at[i], held.at[i]) for i in (1, 0)], sems)
    for copy in copies:
        copy.start()
    bias = held
    for j in range(n):
        grads = grads_in[j]
        grad_t[0:HEAD_DIM, j * QB : (j + 1) * QB] = grads[:, 0:QB]
        grad_t[HEAD_DIM:, units[0].lanes(j)] = grads[:, QB:]
        product = jnp.sum(grads.astype(F4) * heads[j].astype(F4), axis=0, keepdims=True)
        delta_own[j] = product[:, 0:QB]
        delta_both[j] = product[:, QB:]
    grad_k[...] = jnp.zeros(grad_k.shape, F4)
    grad_v[...] = jnp.zeros(grad_v.shape, F4)
    strips[...] = jnp.zeros(strips.shape, F4)

    for unit, copy in zip(units, copies):
        copy.wait()
        key_ref = key_both if unit.shared else key_own
        logs, delta = (logs_both, delta_both) if unit.shared else (logs_own, delta_own)
        cols = 2 * unit.part

        def one_tile(pair, carry):
            nothing = jnp.zeros((HEAD_DIM, cols), BF)
            raw_queries = unit.columns(query_t, pair)
            queries = unit.padded(raw_queries, ones_row(cols))
            plain = unit.padded(raw_queries, nothing)
            grads = unit.padded(unit.columns(grad_t, pair), nothing)
            log_total = jnp.concatenate([logs[2 * pair + q] for q in range(2)], axis=1)
            inner = jnp.concatenate([delta[2 * pair + q] for q in range(2)], axis=1)

            def step(part, made):
                key_at = pl.multiple_of(part * TILE, TILE)
                far = 2 * (pair - part)
                scores = dot(key_ref[pl.ds(key_at, TILE), :], queries)
                scores = scores + unit.strip(bias, far)
                probs = jnp.exp(scores - log_total)
                grad_probs = dot(value_r[pl.ds(key_at, TILE), :], grads)
                grad_scores = probs * (grad_probs - inner)
                for key_half in range(2):
                    for q in range(2):
                        at = jnp.maximum(far + q - key_half, -1) + 1
                        strips[int(unit.shared), at, :, pl.ds(unit.shift, unit.part)] += grad_scores[
                            key_half * QB : (key_half + 1) * QB,
                            q * unit.part : (q + 1) * unit.part,
                        ]
                low = grad_scores.astype(BF)
                grad_v[pl.ds(key_at, TILE), :] += dot(probs.astype(BF), grads, 1, 1)
                grad_k[pl.ds(key_at, TILE), :] += dot(low, plain, 1, 1)
                return made + dot(key_t[pl.ds(unit.lo, HEAD_DIM), pl.ds(key_at, TILE)], low)

            made = lax.fori_loop(0, pair + 1, step, jnp.zeros((HEAD_DIM, cols), F4))
            for q in range(2):
                cut = made[:, q * unit.part : (q + 1) * unit.part]
                if unit.shared:
                    half = HEAD_DIM // 2
                    cut = jnp.concatenate([cut[0:half], cut[half:]], axis=1)
                    stacked[2 * pair + q, 5 * HEAD_DIM :, :] = cut.astype(BF)
                else:
                    stacked[2 * pair + q, 0:HEAD_DIM, :] = cut.astype(BF)
            return carry

        lax.fori_loop(0, n // 2, one_tile, 0)
    for j in range(n):
        keys = jnp.transpose(grad_k[QB * j : QB * j + QB, :]).astype(BF)
        values = jnp.transpose(grad_v[QB * j : QB * j + QB, :]).astype(BF)
        for at, piece in ((1, keys[0:HEAD_DIM]), (2, values[0:HEAD_DIM])):
            stacked[j, at * HEAD_DIM : (at + 1) * HEAD_DIM, :] = piece
        for at, piece in ((3, keys[HEAD_DIM:]), (4, values[HEAD_DIM:])):
            stacked[j, at * HEAD_DIM : (at + 1) * HEAD_DIM, :] = piece
    row = iota((8, TILE), 0)
    empty = jnp.zeros((8, QB), F4)
    for unit in range(2):
        for far in range(n):
            total = jnp.zeros((8, TILE), F4)
            for group in range(QB // 8):
                rows8 = strips[unit, far + 1, 8 * group : 8 * group + 8, :]
                wide = jnp.concatenate([empty, rows8], axis=1)
                total = total + (wide if group == 0 else pltpu.roll(wide, TILE - 8 * group, 1))
            lined = jnp.where(row == 0, total, 0.0)
            for c in range(1, 8):
                lined = lined + jnp.where(row == c, pltpu.roll(total, TILE - c, 1), 0.0)
            table[unit * n + far] = jnp.sum(lined, axis=0, keepdims=True)


def dispatch_rows(n, cap, sc, route_ref, cot, wo_t, wq, wk, wv, out, target, w_out):
    tok = cot.shape[0]
    route = route_ref[...]
    chosen = iota((n, tok), 0) == route
    upto = jnp.where(iota((tok, tok), 0) <= iota((tok, tok), 1), 1.0, 0.0).astype(BF)
    filled = dot(jnp.where(chosen, 1.0, 0.0).astype(BF), upto)
    slot = jnp.sum(jnp.where(chosen, filled - 1.0, 0.0), axis=0, keepdims=True)
    slot = slot.astype(jnp.int32)
    place = route * cap + slot
    target[...] = jnp.broadcast_to(place, target.shape)
    spread = jnp.where(iota((n * cap, tok), 0) == place, 1.0, 0.0).astype(BF)
    packed = dot(spread, cot[...]).astype(BF)
    weights = jnp.concatenate([w[...].astype(F4) for w in (wq, wk, wv)], axis=0).astype(BF)
    for j in range(n):
        out[j, 0:cap, :] = packed[j * cap : (j + 1) * cap]
        out[j, cap:, :] = wo_t[...]
        w_out[j] = weights


def spread_matrix(target, rows):
    place = target[0:1, :]
    return jnp.where(iota((rows, place.shape[1]), 0) == place, 1.0, 0.0)


def hidden_rows(
    n, cap, sc, heads, p0, p1, p2, p3, tokens, misc_t, target, attn, hidden_out, out, wo_t, buf, wide
):
    place_rows(sc, n, p0.shape[1], (p0, p1, p2, p3), wide)
    wo_t[...] = wide[...].astype(BF)
    for pair in range(n // 2):
        at = 3 * pair * HEAD_DIM
        for turn in range(2):
            made = heads[2 * pair + turn].astype(F4)
            buf[at + turn * HEAD_DIM : at + (turn + 1) * HEAD_DIM, :] = made[:, 0:QB]
            both = slice(turn * LANES, (turn + 1) * LANES)
            buf[at + 2 * HEAD_DIM : at + 3 * HEAD_DIM, both] = made[:, QB:]
    rows = jnp.transpose(buf[...]).astype(BF)
    attn[...] = rows
    hidden = tokens[...].astype(F4) + dot(rows, wo_t[...], 1, 1)
    hidden_out[...] = hidden
    moe_in = (hidden * norm_scale(hidden) * misc_t[1:2, :]).astype(BF)
    packed = dot(spread_matrix(target, n * cap).astype(BF), moe_in).astype(BF)
    for j in range(n):
        out[j] = packed[j * cap : (j + 1) * cap]


def gelu_pair(values):
    scale = math.sqrt(2.0 / math.pi)
    square = values * values
    bend = jnp.tanh(scale * (values + 0.044715 * values * square))
    act = 0.5 * values * (1.0 + bend)
    slope = 0.5 * (1.0 + bend) + 0.5 * values * (1.0 - bend * bend) * scale * (
        1.0 + 3.0 * 0.044715 * square
    )
    return (act, slope)


def route_probs(experts, sc, rows, misc):
    logits = dot(rows, misc[...])
    lane = iota(logits.shape, 1)
    real = (lane >= 2) & (lane < 2 + experts)
    logits = jnp.where(real, logits, NEG)
    powers = jnp.where(real, jnp.exp(logits - jnp.max(logits, axis=-1, keepdims=True)), 0.0)
    probs = powers / jnp.sum(powers, axis=-1, keepdims=True)
    chosen = lane == sc[0] + 2
    gate = jnp.sum(jnp.where(chosen, probs, 0.0), axis=-1, keepdims=True)
    return (probs, chosen, gate)


def flat_rows(ref, cap=None):
    return jnp.concatenate([ref[j][0:cap] for j in range(ref.shape[0])], axis=0)


def expert_back(
    experts,
    sc,
    rows_ref,
    cot_ref,
    in_a,
    out_a,
    in_b,
    out_b,
    misc,
    back,
    made,
    log_out,
    weights,
    sems,
):
    copies = copies_of(
        [(ref, weights.at[i]) for i, ref in enumerate((in_a, out_a, in_b, out_b))], sems
    )
    for copy in copies:
        copy.start()
    rows, cots = flat_rows(rows_ref), flat_rows(cot_ref, rows_ref.shape[1])
    probs, chosen, gate = route_probs(experts, sc, rows, misc)
    inner = jnp.zeros(gate.shape, F4)
    total = jnp.zeros(rows.shape, F4)
    result = jnp.zeros(rows.shape, F4)
    for half in range(2):
        copies[2 * half].wait()
        w_in, w_out = weights.at[2 * half], weights.at[2 * half + 1]
        act, slope = gelu_pair(dot(rows, w_in[...]))
        copies[2 * half + 1].wait()
        low = act.astype(BF)
        result = result + dot(low, w_out[...])
        grad_act = dot(cots, w_out[...], 1, 1)
        inner = inner + jnp.sum(low.astype(F4) * grad_act, axis=-1, keepdims=True)
        total = total + dot((gate * grad_act * slope).astype(BF), w_in[...], 1, 1)
    grad_logits = (inner * probs * (jnp.where(chosen, 1.0, 0.0) - gate)).astype(BF)
    log_out[...] = grad_logits
    made[...] = (gate * result).astype(made.dtype)
    back[...] = (total + dot(grad_logits, misc[...], 1, 1)).astype(back.dtype)


def expert_weights(experts, count, more, sc, *refs):
    rows_refs, cot_refs = refs[:count], refs[count : 2 * count]
    w_in, w_out, misc = refs[2 * count : 2 * count + 3]
    begun = refs[2 * count + 3 : 2 * count + 5] if more else None
    grad_in, grad_out, token, all_rows, all_grads = refs[2 * count + (5 if more else 3) :]
    token[...] = jnp.zeros(token.shape, F4)
    size = rows_refs[0].shape[0] * rows_refs[0].shape[1]

    @pl.when(pl.program_id(0) == 0)
    def _():
        for i in range(count):
            at = slice(i * size, (i + 1) * size)
            rows, cots = flat_rows(rows_refs[i]), flat_rows(cot_refs[i], rows_refs[i].shape[1])
            gate = route_probs(experts, sc, rows, misc)[2]
            all_rows[at, :] = rows
            all_grads[at, :] = (gate * cots.astype(F4)).astype(BF)

    rows, grads = all_rows[...], all_grads[...]
    act, slope = gelu_pair(dot(rows, w_in[...]))
    grad_pre = (dot(grads, w_out[...], 1, 1) * slope).astype(BF)
    in_part = dot(rows, grad_pre, 0, 0)
    out_part = dot(act.astype(BF), grads, 0, 0)
    grad_in[...] = begun[0][...] + in_part if more else in_part
    grad_out[...] = begun[1][...] + out_part if more else out_part


def chunked_specs(w_in):
    depth, hidden = w_in.shape
    chunk = 2 * LANES
    columns = pl.BlockSpec((depth, chunk), lambda i: (0, i))
    lines = pl.BlockSpec((chunk, depth), lambda i: (i, 0))
    return hidden // chunk, columns, lines


def expert_weights_call(experts, lengths, rows_in, cots_in, w_in, w_out, misc, ties, begun=()):
    count, (depth, hidden) = len(rows_in), w_in.shape
    size = rows_in[0].shape[0] * rows_in[0].shape[1]
    body = functools.partial(expert_weights, experts, count, bool(begun))
    args = tuple(rows_in) + tuple(cots_in) + (w_in, w_out, misc) + tuple(begun)

    def kernel(length_ref, *refs):
        body(Place(length_ref), *refs[: len(args)], *refs[len(args) + len(ties) :])

    whole = pl.BlockSpec(memory_space=pltpu.VMEM)
    steps, columns, lines = chunked_specs(w_in)
    return pl.pallas_call(
        kernel,
        grid=(steps,),
        out_shape=(
            shaped((depth, hidden), F4),
            shaped((hidden, depth), F4),
            shaped((8, LANES), F4),
        ),
        in_specs=[pl.BlockSpec(memory_space=pltpu.SMEM)]
        + [whole] * (2 * count)
        + [columns, lines, whole]
        + ([columns, lines] if begun else [])
        + [whole] * len(ties),
        out_specs=(columns, lines, whole),
        scratch_shapes=[
            pltpu.VMEM((count * size, depth), BF),
            pltpu.VMEM((count * size, depth), BF),
        ],
        compiler_params=pltpu.CompilerParams(vmem_limit_bytes=60 * 1024 * 1024),
        cost_estimate=pl.CostEstimate(flops=1, bytes_accessed=1, transcendentals=0),
    )(lengths, *args, *ties)


def result_rows(n, cap, sc, made, target, hidden, out):
    rows = flat_rows(made)
    spread = jnp.transpose(spread_matrix(target, n * cap)).astype(BF)
    out[...] = (hidden[...] + dot(spread, rows)).astype(BF)


def norm_back(grads, source, gain):
    scale = norm_scale(source)
    weighted = grads * gain
    inner = jnp.mean(weighted * source, axis=-1, keepdims=True)
    return (scale * weighted - source * (scale * scale * scale) * inner, scale)


def hidden_grads(
    n, cap, sc, back, target, hidden_ref, misc_t, cot, wo_t, grad_out, low_out, gain_out, out, buf
):
    spread = jnp.transpose(spread_matrix(target, n * cap)).astype(BF)
    grads = dot(spread, flat_rows(back))
    hidden = hidden_ref[...]
    normed, scale = norm_back(grads, hidden, misc_t[1:2, :])
    gain_out[...] = jnp.broadcast_to(
        jnp.sum(grads * hidden * scale, axis=0, keepdims=True), gain_out.shape
    )
    total = cot[...].astype(F4) + normed
    grad_out[...] = total
    low = total.astype(BF)
    low_out[...] = low
    buf[...] = jnp.transpose(dot(low, wo_t[...])).astype(BF)
    for pair in range(n // 2):
        at = 3 * pair * HEAD_DIM
        for turn in range(2):
            out[2 * pair + turn, :, 0:QB] = buf[at + turn * HEAD_DIM : at + (turn + 1) * HEAD_DIM, :]
            both = slice(turn * LANES, (turn + 1) * LANES)
            out[2 * pair + turn, :, QB:] = buf[at + 2 * HEAD_DIM : at + 3 * HEAD_DIM, both]


def unfolded(piece):
    return jnp.concatenate([piece[:, 0:LANES], piece[:, LANES:]], axis=0)


def unpack_full(n, rows, sc, p0, p1, p2, p3, out, wide):
    inner = wide.shape[1] // 3
    for kk, part in enumerate((p0, p1, p2, p3)):
        for j in range(n):
            first = pl.multiple_of(((sc[1] ^ kk) * n + j) * rows, 8)
            block = part[j].astype(F4)
            for c in range(3):
                wide[pl.ds(first, rows), c * inner : (c + 1) * inner] = block[
                    c * rows : (c + 1) * rows
                ]
    out[...] = wide[...].astype(BF)


def token_grads(n, sc, grads, weights, tokens, hidden_grad, misc_t, out, buf):
    inner = weights.shape[1] // 3
    for pair in range(n // 2):
        at = 3 * pair * HEAD_DIM
        last = at + 2 * HEAD_DIM
        for turn in range(2):
            j = 2 * pair + turn
            for c in range(3):
                lo = c * inner + at + turn * HEAD_DIM
                buf[lo : lo + HEAD_DIM, :] = grads[j, c * HEAD_DIM : (c + 1) * HEAD_DIM, :]
            both = slice(turn * LANES, (turn + 1) * LANES)
            buf[last : last + HEAD_DIM, both] = unfolded(grads[j, 5 * HEAD_DIM :, :])
        for c in (1, 2):
            rows = slice((c + 2) * HEAD_DIM, (c + 3) * HEAD_DIM)
            both = grads[2 * pair, rows, :].astype(F4) + grads[2 * pair + 1, rows, :].astype(F4)
            buf[c * inner + last : c * inner + last + HEAD_DIM, :] = both.astype(BF)
    made = jnp.transpose(dot(weights[...], buf[...]))
    normed, unused = norm_back(made, tokens[...].astype(F4), misc_t[0:1, :])
    out[...] = (hidden_grad[...] + normed).reshape(out.shape)


def unit_weight_grads(n, heads, sc, normed, stacked, lines, buckets, *rest):
    outs, (buf, table) = rest[:heads], rest[heads:]
    width = buf.shape[1]
    sums = []
    for unit in range(2):
        made = jnp.zeros((NUM_BUCKETS, 1), F4)
        for far in range(n):
            line = lines[unit * n + far][:, QB:]
            if far + 1 < n:
                line = line + lines[unit * n + far + 1][:, :QB]
            inside = iota((NUM_BUCKETS, QB), 0) == buckets[:, far * QB : (far + 1) * QB]
            made = made + jnp.sum(jnp.where(inside, line, 0.0), axis=1, keepdims=True)
        sums.append(made)
    lane = iota((NUM_BUCKETS, width), 1)
    high = [value.astype(BF).astype(F4) for value in sums]
    listed = jnp.zeros((NUM_BUCKETS, width), F4)
    for at, value in enumerate(high + [sums[0] - high[0], sums[1] - high[1]]):
        listed = jnp.where(lane == at, value, listed)
    table[...] = listed
    total = None
    for j in range(n):
        grads = stacked[j]
        shared = unfolded(grads[5 * HEAD_DIM :]).astype(F4)
        blank = jnp.zeros(shared.shape, F4)
        turn = jnp.broadcast_to((sc[0] & 1) == 0, shared.shape)
        shared = jnp.concatenate(
            [jnp.where(turn, shared, blank), jnp.where(turn, blank, shared)], axis=1
        )
        pieces = [grads[c * HEAD_DIM : (c + 1) * HEAD_DIM] for c in range(5)]
        own_first = [pieces[0], shared.astype(BF), pieces[1], pieces[3], pieces[2], pieces[4]]
        part = dot(jnp.concatenate(own_first, axis=0), normed[j])
        total = part if total is None else total + part
    buf[...] = jnp.transpose(total)
    rows = buf.shape[0] // heads
    for kk in range(heads):
        to = sc[1] ^ kk
        outs[kk][...] = jnp.concatenate(
            [
                buf[pl.ds(pl.multiple_of(to * rows, 8), rows), :],
                table[pl.ds(pl.multiple_of(to * n, 8), n), :],
                jnp.zeros((8, width), F4),
            ],
            axis=0,
        ).astype(BF)


def two_parts(values, gap):
    high = values.astype(BF).astype(F4)
    lane = iota(values.shape, 1)
    low = pltpu.roll(jnp.where(lane < gap, values - high, 0.0), gap, 1)
    return jnp.where(lane < gap, high, low)


def one_part(values, gap):
    return values + pltpu.roll(values, values.shape[1] - gap, 1)


def weight_sums(n, rows, heads, sc, *refs):
    units, outer = refs[:heads], refs[heads : 2 * heads]
    outs, buf = refs[2 * heads : -1], refs[-1]
    total = (units[0][...].astype(F4) + units[1][...].astype(F4)) + (
        units[2][...].astype(F4) + units[3][...].astype(F4)
    )
    base = n * rows
    entries = two_parts(one_part(total[base : base + n], 2), 2)
    wide = (outer[0][...].astype(F4) + outer[1][...].astype(F4)) + (
        outer[2][...].astype(F4) + outer[3][...].astype(F4)
    )
    width = wide.shape[1] - LANES
    extra = two_parts(one_part(wide[:, width:], 16), 16)
    for to in range(n):
        at = slice(to * rows, (to + 1) * rows)
        entry = pltpu.roll(entries[to : to + 1, 0:LANES], 64, 1)
        entry = jnp.where(iota((rows, LANES), 0) == 0, entry, 0.0)
        buf[to] = jnp.concatenate([total[at], wide[at, 0:width], extra[at] + entry], axis=1)
    for k in range(n):
        outs[k][...] = buf[sc[0] ^ k].astype(BF)


def as_row(values):
    size = values.shape[0]
    square = jnp.where(iota((size, size), 0) == iota((size, size), 1), values, 0.0)
    return jnp.sum(square, axis=0, keepdims=True)


def weight_final(n, experts, sc, *refs):
    parts, (wq, wk, wv, gain_a) = refs[:n], refs[n : n + 4]
    grads = refs[n + 4 : n + 7]
    gain, table, grad_out, gain_out, router, buf, tables = refs[n + 7 :]
    rows = wq.shape[0]
    units = 3 * LANES
    small = slice(parts[0].shape[1] - LANES, parts[0].shape[1])
    total = None
    for j in range(n):
        part = parts[j][...].astype(F4)
        buf[sc[0] ^ j] = part[:, 0:units]
        tables[sc[0] ^ j] = part[0:1, small]
        total = part[:, units:] if total is None else total + part[:, units:]
    lane = iota((rows, LANES), 1)
    inner = jnp.zeros((rows, 1), F4)
    for c, weight in enumerate((wq, wk, wv)):
        lo = LANES * c

        def piece(head, place):
            pair, turn = head // 3, head % 3
            if turn < 2:
                tile, half = buf[2 * pair + turn, 0:rows, lo : lo + LANES], 0
            else:
                tile = (
                    buf[2 * pair, 0:rows, lo : lo + LANES]
                    + buf[2 * pair + 1, 0:rows, lo : lo + LANES]
                )
                half = 1
            return tile if half == place else pltpu.roll(tile, HEAD_DIM, 1)

        for m in range(weight.shape[1] // LANES):
            tile = jnp.where(lane < HEAD_DIM, piece(2 * m, 0), piece(2 * m + 1, 1))
            cols = slice(LANES * m, LANES * m + LANES)
            grads[c][:, cols] = tile
            inner = inner + jnp.sum(weight[:, cols].astype(F4) * tile, axis=-1, keepdims=True)
    gain[...] = as_row(inner / column(gain_a[...], rows))
    lane = iota((1, HEADS), 1)
    listed = jnp.zeros((1, HEADS), F4)
    for j in range(n):
        entry = one_part(pltpu.roll(tables[j], 64, 1), 2)
        listed = listed + jnp.where(lane == 3 * (j // 2) + j % 2, entry[:, 0:1], 0.0)
        listed = listed + jnp.where(lane == 3 * (j // 2) + 2, entry[:, 1:2], 0.0)
    table[...] = listed
    width = grad_out.shape[1]
    grad_out[...] = total[:, 0:width]
    extra = total[0:rows, width:]
    extra = one_part(jnp.where(iota(extra.shape, 1) < 32, extra, 0.0), 16)
    gain_out[...] = as_row(extra[:, 1:2])
    router[...] = jnp.transpose(pltpu.roll(extra, LANES - 2, 1))[0:experts]


def out_weight_grads(heads, sc, low, attn, rows_a, rows_b, logs_a, logs_b, gain, *rest):
    outs, buf = rest[:heads], rest[heads]
    width = attn.shape[1]
    buf[:, 0:width] = dot(low[...], attn[...], 0, 0)
    router = dot(flat_rows(rows_a), logs_a[...], 0, 0) + dot(flat_rows(rows_b), logs_b[...], 0, 0)
    wide = jnp.where(iota((LANES, gain.shape[1]), 0) == 1, gain[0:1, :], 0.0)
    buf[:, width : width + LANES] = two_parts(router + jnp.transpose(wide), 16)
    rows = buf.shape[0] // heads
    for kk in range(heads):
        first = pl.multiple_of((sc[1] ^ kk) * rows, 8)
        outs[kk][...] = buf[pl.ds(first, rows), :].astype(BF)


def swap(values, axis, flip):
    if flip == 0:
        return values
    size = lax.axis_size(axis)
    return lax.ppermute(values, axis, [(i, i ^ flip) for i in range(size)])


def exchange(messages, axis):
    return [swap(message, axis, k) for k, message in enumerate(messages)]


def hold(values, *earlier):
    return lax.optimization_barrier((values, earlier))[0]


def over_heads(stack):
    across = swap(stack, "head", 2)
    return (stack, swap(stack, "head", 1), across, swap(across, "head", 1))


def on_plane(
    tokens,
    attn_gain,
    w_query,
    w_key,
    w_value,
    w_out,
    bias_table,
    moe_gain,
    w_router,
    expert_in,
    expert_out,
    seq_lengths,
    rel_buckets,
    routes,
    cotangent,
):
    heads = lax.axis_size("head")
    n = lax.axis_size("blk")
    tok, width = tokens.shape[0], tokens.shape[2]
    rows = w_query.shape[0]
    total_rows = n * tok
    experts = w_router.shape[1]
    cap = 3 * tok // (2 * experts)
    slots = n * cap
    scope = jax.named_scope
    x = tokens.reshape(tok, width)
    cot = cotangent.reshape(tok, width)
    gain_a = attn_gain.reshape(1, rows)
    gain_m = moe_gain.reshape(1, rows)
    in_own, out_own = expert_in.reshape(expert_in.shape[1:]), expert_out.reshape(expert_out.shape[1:])

    def call(body, args, outs, scratch=(), ties=(), loose=(), away=()):
        return vmem_call(body, seq_lengths, args, outs, scratch, ties, loose, away)

    def all_to_all(stack, axis="blk"):
        return lax.all_to_all(stack, axis, split_axis=0, concat_axis=0, tiled=True)

    order = [ring_of(i, n) for i in range(n)]
    ahead = [(order[i], order[(i + 1) % n]) for i in range(n)]
    astern = [(b, a) for a, b in ahead]
    unit_cols = 4 * LANES

    def hop(front, back):
        with scope("ring"):
            front = lax.ppermute(front, "blk", ahead)
            back = lax.ppermute(back, "blk", astern)
            return lax.optimization_barrier((front, back))

    first = hop(x, x)
    with scope("cot_rows"):
        cot_out, target, w_stack, cot_token = call(
            functools.partial(dispatch_rows, n, cap),
            (routes.reshape(1, tok), cot, jnp.transpose(w_out), w_query, w_key, w_value),
            [
                shaped((n, cap + rows, width), BF),
                shaped((8, tok), jnp.int32),
                shaped((n, 3 * rows, width), BF),
            ],
        )
    with scope("unit_weights"):
        packed, packed_token = call(
            functools.partial(pack_units, n),
            (w_query, w_key, w_value)
            + (gain_a, gain_m, jnp.transpose(w_router), bias_table.reshape(1, -1)),
            [shaped((n, rows, unit_cols), BF)],
            ties=(cot_token,),
        )
        unit_in = all_to_all(hold(packed, first[0]))
    with scope("expert_swap"):
        in_other = swap(in_own, "head", 2)
    second = hop(*first)
    with scope("unit_weights"):
        unit_parts = exchange([hold(unit_in, second[0])] * heads, "head")
    third = hop(*hold(second, unit_in, in_other))
    half = tok // 2
    with scope("ring"):
        front_half, back_half = (third[0][:half], third[1][half:])
        front, back = lax.ppermute(front_half, "blk", ahead), lax.ppermute(back_half, "blk", astern)
    with scope("unit_weights"):
        unit_w, misc, misc_t, table, unused = call(
            functools.partial(unpack_units, n, rows),
            unit_parts,
            [
                shaped((width, 3 * LANES), BF),
                shaped((width, LANES), BF),
                shaped((LANES, width), F4),
                shaped((NUM_BUCKETS, LANES), F4),
            ],
            [pltpu.VMEM((width, unit_cols), F4)],
        )
    with scope("expert_swap"):
        out_other = swap(hold(out_own, unit_parts[2], unit_parts[3]), "head", 2)

    buckets = rel_buckets.reshape(1, -1)

    with scope("cot_rows"):
        cot_in = all_to_all(hold(cot_out, front, back, table))
        cot_rows, wo_rows = cot_in[:, :cap], cot_in[:, cap:]

    kept = [
        shaped((n, tok, width), BF),
        shaped((total_rows, LANES), BF),
        shaped((total_rows, LANES), BF),
        shaped((LANES, total_rows), BF),
        shaped((LANES, total_rows), BF),
        shaped((total_rows, LANES), BF),
        shaped((2, n + 1, QB, QB), F4),
    ]
    with scope("attend"):
        (
            head_out,
            logs_own,
            logs_both,
            normed,
            key_own,
            key_both,
            query_t,
            key_t,
            value_r,
            strips,
            attend_token,
        ) = call(
            functools.partial(attend_units, n),
            (x,) + first + second + third + (front, back, misc_t, unit_w, table, buckets),
            [
                shaped((n, HEAD_DIM, QB + LANES), BF),
                shaped((n, 1, QB), F4),
                shaped((n, 1, LANES), F4),
            ]
            + kept,
            [pltpu.VMEM(k.shape, k.dtype) for k in kept]
            + [
                pltpu.VMEM((LANES, total_rows), BF),
                pltpu.VMEM((1, QB + total_rows), F4),
                pltpu.SemaphoreType.DMA((len(kept),)),
            ],
            ties=(cot_token,),
            away=range(3, 3 + len(kept)),
        )
        head_in = all_to_all(head_out)
    with scope("out_weights"):
        wo_parts = over_heads(hold(wo_rows, out_other, logs_both))
    with scope("cot_pair"):
        all_cot = over_heads(hold(cot_rows, wo_parts[2]))
        cot_pair = all_cot[1]
    with scope("hidden"):
        attn, hidden, moe_out, out_t, hidden_token = call(
            functools.partial(hidden_rows, n, cap),
            (head_in,) + wo_parts + (x, misc_t, target),
            [
                shaped((tok, width), BF),
                shaped((tok, width), F4),
                shaped((n, cap, width), BF),
                shaped((width, width), BF),
            ],
            [pltpu.VMEM((width, tok), F4), pltpu.VMEM((width, width), F4)],
            ties=(hold(attend_token, cot_pair),),

        )

    with scope("moe_rows"):
        moe_rows = all_to_all(moe_out)
        moe_pair = swap(hold(moe_rows, all_cot[2]), "head", 1)
    def backward_rows(rows_in, cots_in, kind, ties=()):
        return call(
            functools.partial(expert_back, experts),
            (rows_in, cots_in, in_own, out_own, in_other, out_other, misc),
            [
                shaped((slots, width), kind),
                shaped((slots, width), BF),
                shaped((slots, LANES), BF),
            ],
            [pltpu.VMEM((4,) + in_own.shape, BF), pltpu.SemaphoreType.DMA((4,))],
            ties=ties,
            loose=range(2, 6),
        )

    with scope("full_weights"):
        w_in = all_to_all(hold(w_stack, moe_pair))
    with scope("moe_far"):
        moe_far = swap(moe_rows, "head", 2)
        far_pair = swap(moe_far, "head", 1)

    with scope("expert_back"):
        back_pair, made_pair, logs_pair, token = backward_rows(moe_pair, cot_pair, BF)
        back_other = swap(back_pair, "head", 1)
        back_own, made_own, logs_own2, token = backward_rows(
            moe_rows, cot_rows, F4, (token,)
        )
        back_out = (back_own + back_other.astype(F4)).astype(BF).reshape(n, cap, width)
        back_out, back_token = hold((back_out, token), w_in)
        back_in = all_to_all(back_out)
    with scope("full_weights"):
        w_parts = over_heads(hold(w_in, back_token))
    with scope("expert_weight_grads"):
        expert_ends = (in_own, out_own, misc)
        *begun, expert_token = expert_weights_call(
            experts,
            seq_lengths,
            (moe_rows, moe_pair),
            all_cot[:2],
            *expert_ends,
            (back_token,),
        )
    with scope("hidden_grads"):
        grad_hidden, grad_low, gain_moe_part, grad_heads_out, unused = call(
            functools.partial(hidden_grads, n, cap),
            (back_in, target, hidden, misc_t, cot, out_t),
            [
                shaped((tok, width), F4),
                shaped((tok, width), BF),
                shaped((8, width), F4),
                shaped((n, HEAD_DIM, QB + LANES), BF),
            ],
            [pltpu.VMEM((width, tok), BF)],
            ties=(hold(expert_token, far_pair, all_cot[3]),),
        )
        grad_heads = all_to_all(grad_heads_out)
    wide = width + LANES
    with scope("out_weight_grads"):
        *out_parts, out_token = call(
            functools.partial(out_weight_grads, heads),
            (grad_low, attn, moe_rows, moe_pair, logs_own2, logs_pair, gain_moe_part),
            [shaped((width // heads, wide), BF)] * heads,
            [pltpu.VMEM((width, wide), F4)],
        )
        out_parts_in = exchange(out_parts, "head")
    with scope("result_rows"):
        res_out = made_own.astype(F4) + swap(made_pair, "head", 1).astype(F4)
        res_out = res_out.astype(BF).reshape(n, cap, width)
        res_in = all_to_all(hold(res_out, grad_heads, out_token))

    with scope("attend_grads"):
        stacked, lines, unused = call(
            functools.partial(unit_grads, n),
            (
                key_own,
                key_both,
                query_t,
                key_t,
                value_r,
                strips,
                head_out,
                grad_heads,
                logs_own,
                logs_both,
            ),
            [shaped((n, 5 * HEAD_DIM + HEAD_DIM // 2, tok), BF), shaped((2 * n, 1, TILE), F4)],
            [
                pltpu.VMEM((LANES, total_rows), BF),
                pltpu.VMEM((n, 1, QB), F4),
                pltpu.VMEM((n, 1, LANES), F4),
                pltpu.VMEM((total_rows, LANES), F4),
                pltpu.VMEM((total_rows, LANES), F4),
                pltpu.VMEM((2, n + 1, QB, QB), F4),
                pltpu.VMEM((2, n + 1, QB, QB), F4),
                pltpu.SemaphoreType.DMA((2,)),
            ],
            loose=(5,),
            ties=(hold(out_token, w_parts),),
        )
        unit_in = all_to_all(hold(stacked, res_in, out_parts_in))

    with scope("weight_grads"):
        *unit_grad_parts, parts_token = call(
            functools.partial(unit_weight_grads, n, heads),
            (normed, stacked, lines, buckets),
            [shaped((width // heads + n + 8, 3 * LANES), BF)] * heads,
            [pltpu.VMEM((width, 3 * LANES), F4), pltpu.VMEM((NUM_BUCKETS, 3 * LANES), F4)],
        )
        unit_parts_in = exchange(unit_grad_parts, "head")
    with scope("expert_weight_grads"):
        grad_in, grad_out, expert_token = expert_weights_call(
            experts,
            seq_lengths,
            (moe_far, far_pair),
            all_cot[2:],
            *expert_ends,
            (parts_token,),
            begun,
        )
    with scope("weight_grads"):
        *sums, sums_token = call(
            functools.partial(weight_sums, n, rows, heads),
            unit_parts_in + out_parts_in,
            [shaped((rows, 3 * LANES + wide), BF)] * n,
            [pltpu.VMEM((n, rows, 3 * LANES + wide), F4)],
            ties=(expert_token,),
        )
        sums_in = exchange(sums, "blk")
    with scope("result"):
        result, result_token = call(
            functools.partial(result_rows, n, cap),
            (res_in, target, hidden),
            [shaped((tok, width), BF)],
            ties=(sums_token,),
        )
    with scope("full_weights"):
        full_w, full_token = call(
            functools.partial(unpack_full, n, rows),
            w_parts,
            [shaped((width, 3 * width), BF)],
            [pltpu.VMEM((width, 3 * width), F4)],
            ties=(sums_token,),
        )
    with scope("weight_final"):
        (
            grad_q,
            grad_k,
            grad_v,
            grad_gain_attn,
            grad_table,
            grad_out_w,
            grad_gain_moe,
            grad_router,
            final_token,
        ) = call(
            functools.partial(weight_final, n, experts),
            sums_in + [w_query, w_key, w_value, gain_a],
            [shaped((rows, width), F4)] * 3
            + [
                shaped((1, rows), F4),
                shaped((1, HEADS), F4),
                shaped((rows, width), F4),
                shaped((1, rows), F4),
                shaped((experts, rows), F4),
            ],
            [pltpu.VMEM((n, rows, 3 * LANES), F4), pltpu.VMEM((n, 1, LANES), F4)],
            ties=(result_token, full_token),
        )
    with scope("token_grads"):
        grad_tokens, unused = call(
            functools.partial(token_grads, n),
            (unit_in, full_w, x, grad_hidden, misc_t),
            [shaped(tokens.shape, F4)],
            [pltpu.VMEM((3 * width, tok), BF)],
            ties=(final_token,),
        )
    return (
        result.reshape(tokens.shape),
        grad_tokens,
        grad_gain_attn.reshape(-1),
        grad_q,
        grad_k,
        grad_v,
        jnp.transpose(grad_out_w),
        grad_table.reshape(-1),
        grad_gain_moe.reshape(-1),
        jnp.transpose(grad_router),
        grad_in.reshape(expert_in.shape),
        grad_out.reshape(expert_out.shape),
    )


def ring_of(place, ring_len):
    return 2 * place if place < ring_len // 2 else 2 * ring_len - 1 - 2 * place


def solution(mesh):
    in_specs = (
        P("blk", "head", None),
        P(("head", "blk")),
        P(("head", "blk"), None),
        P(("head", "blk"), None),
        P(("head", "blk"), None),
        P(None, ("head", "blk")),
        P(("head", "blk")),
        P(("head", "blk")),
        P(("head", "blk"), None),
        P("blk", None, "head"),
        P("blk", "head", None),
        P(),
        P(),
        P("head", "blk", None, None),
        P("blk", "head", None),
    )
    out_specs = (
        P("blk", "head", None),
        P("blk", "head", None),
        P(("head", "blk")),
        P(("head", "blk"), None),
        P(("head", "blk"), None),
        P(("head", "blk"), None),
        P(None, ("head", "blk")),
        P(("head", "blk")),
        P(("head", "blk")),
        P(("head", "blk"), None),
        P("blk", None, "head"),
        P("blk", "head", None),
    )
    one_each = mesh.shape["head"] == 4 and mesh.shape["blk"] == 8
    return jax.shard_map(
        on_plane if one_each else on_device, mesh=mesh, in_specs=in_specs, out_specs=out_specs, check_vma=False
    )
```

```python
import functools
import math

import jax
import jax.numpy as jnp
from jax import lax
from jax.experimental import pallas as pl
from jax.experimental.pallas import tpu as pltpu
from jax.sharding import PartitionSpec as P

HEADS = 12
HEAD_DIM = 64
NUM_BUCKETS = 32
HEAD, BLK = "head", "blk"


norm_eps = 1e-06
masked_score = -1e30


def inverse_rms(values):
    return lax.rsqrt(jnp.mean(values * values, axis=-1, keepdims=True) + norm_eps)


def norm_backward(grad_normed, source, inv_scale, gain):
    weighted = grad_normed * gain
    inner_mean = jnp.mean(weighted * source, axis=-1, keepdims=True)
    grad_source = inv_scale * weighted - source * (inv_scale * inv_scale * inv_scale) * inner_mean
    grad_gain = jnp.sum(grad_normed * source * inv_scale, axis=0)
    return (grad_source, grad_gain)


def same_state(running):
    return running


def bucket_bounds(rel_buckets):
    bucket_count = NUM_BUCKETS
    labels = jnp.arange(bucket_count, dtype=jnp.int32)
    starts = jnp.sum((rel_buckets[:, None] < labels[None, :]).astype(jnp.int32), axis=0)
    ends = jnp.concatenate([starts[1:], jnp.full((1,), rel_buckets.shape[0] + 1, jnp.int32)])
    return (starts, ends)


def bias_terms(query_positions, key_positions, bounds, table32):
    starts, ends = bounds
    distance = jnp.maximum(query_positions[:, None] - key_positions[None, :], 0)[:, :, None]
    inside = (distance >= starts[None, None, :]) & (distance < ends[None, None, :])
    onehot = inside.astype(jnp.bfloat16)
    bias = jnp.einsum(
        "qkb,bh->hqk", onehot, table32.astype(jnp.bfloat16), preferred_element_type=jnp.float32
    )
    return (onehot, bias)


def block_scores(queries, keys, query_positions, key_positions, seq_lengths, bounds, table32):
    onehot, bias = bias_terms(query_positions, key_positions, bounds, table32)
    raw = jnp.einsum("qshd,kshd->hsqk", queries, keys, preferred_element_type=jnp.float32)
    causal = key_positions[None, :] <= query_positions[:, None]
    present = key_positions[None, :] < seq_lengths[:, None]
    valid = causal[None, :, :] & present[:, None, :]
    return (raw + bias[:, None, :, :], valid[None], onehot)


def attend_step(
    running, queries, keys, values, query_positions, key_positions, seq_lengths, bounds, table32
):
    row_top, row_total, weighted = running
    scores, valid, unused = block_scores(
        queries, keys, query_positions, key_positions, seq_lengths, bounds, table32
    )
    scores = jnp.where(valid, scores, masked_score)
    new_top = jnp.maximum(row_top, jnp.max(scores, axis=-1))
    weights = jnp.where(valid, jnp.exp(scores - new_top[..., None]), 0.0)
    decay = jnp.exp(row_top - new_top)
    row_total = row_total * decay + jnp.sum(weights, axis=-1)
    mixed = jnp.einsum(
        "hsqk,kshd->qshd", weights.astype(jnp.bfloat16), values, preferred_element_type=jnp.float32
    )
    weighted = weighted * jnp.transpose(decay, (2, 1, 0))[..., None] + mixed
    return (new_top, row_total, weighted)


def grad_step(
    queries,
    grad_heads,
    log_total,
    delta,
    query_positions,
    keys,
    values,
    key_positions,
    seq_lengths,
    bounds,
    table32,
):
    scores, valid, onehot = block_scores(
        queries, keys, query_positions, key_positions, seq_lengths, bounds, table32
    )
    probs = jnp.where(valid, jnp.exp(scores - jnp.transpose(log_total, (2, 1, 0))[..., None]), 0.0)
    grad_probs = jnp.einsum(
        "qshd,kshd->hsqk", grad_heads, values, preferred_element_type=jnp.float32
    )
    grad_scores = probs * (grad_probs - jnp.transpose(delta, (2, 1, 0))[..., None])
    grad_table = jnp.einsum(
        "hqk,qkb->bh",
        jnp.sum(grad_scores, axis=1),
        onehot.astype(jnp.float32),
        precision=lax.Precision.HIGHEST,
    )
    low_scores = grad_scores.astype(jnp.bfloat16)
    grad_queries = jnp.einsum(
        "hsqk,kshd->qshd", low_scores, keys, preferred_element_type=jnp.float32
    )
    grad_keys = jnp.einsum(
        "hsqk,qshd->kshd", low_scores, queries, preferred_element_type=jnp.float32
    )
    grad_values = jnp.einsum(
        "hsqk,qshd->kshd",
        probs.astype(jnp.bfloat16),
        grad_heads,
        preferred_element_type=jnp.float32,
    )
    return (grad_queries, grad_keys, grad_values, grad_table)


def on_device(
    tokens,
    attn_gain,
    w_query,
    w_key,
    w_value,
    w_out,
    bias_table,
    moe_gain,
    w_router,
    expert_in,
    expert_out,
    seq_lengths,
    rel_buckets,
    routes,
    cotangent,
):
    head_count = lax.axis_size(HEAD)
    blk_count = lax.axis_size(BLK)
    head_index = lax.axis_index(HEAD)
    blk_index = lax.axis_index(BLK)
    block_rows, group_seqs, width = tokens.shape
    seq_count = group_seqs * head_count
    tok_rows = block_rows * group_seqs
    local_heads = HEADS // head_count
    head_width = local_heads * HEAD_DIM
    group_rows = block_rows * max(1, blk_count // 8)
    longest = jnp.max(seq_lengths)
    query_first = blk_index * block_rows
    query_last = query_first + block_rows - 1
    query_positions = query_first + jnp.arange(block_rows, dtype=jnp.int32)
    bounds = bucket_bounds(rel_buckets)
    fetched = (
        lax.all_gather(w_query, (HEAD, BLK), axis=0, tiled=True),
        lax.all_gather(w_key, (HEAD, BLK), axis=0, tiled=True),
        lax.all_gather(w_value, (HEAD, BLK), axis=0, tiled=True),
        lax.all_gather(w_out, (HEAD, BLK), axis=1, tiled=True),
        lax.all_gather(attn_gain, (HEAD, BLK), axis=0, tiled=True),
        lax.all_gather(bias_table, (HEAD, BLK), axis=0, tiled=True),
        lax.all_gather(moe_gain, (HEAD, BLK), axis=0, tiled=True),
        lax.all_gather(w_router, (HEAD, BLK), axis=0, tiled=True),
    )
    full_query, full_key, full_value, full_out, gain_attn, table_flat, gain_moe, full_router = (
        fetched
    )
    inner_width = full_query.shape[1]
    table_all = table_flat.astype(jnp.float32).reshape(NUM_BUCKETS, HEADS)
    table32 = lax.dynamic_slice_in_dim(table_all, head_index * local_heads, local_heads, 1)
    gain_attn32 = gain_attn.astype(jnp.float32)
    gain_moe32 = gain_moe.astype(jnp.float32)

    def to_heads(values):
        parts = values.shape[1]
        shaped = values.reshape(block_rows, group_seqs, parts, head_count, head_width)
        moved = lax.all_to_all(shaped, HEAD, split_axis=3, concat_axis=1, tiled=True)
        return moved.reshape(block_rows, seq_count, parts, local_heads, HEAD_DIM)

    def to_tokens(values):
        parts = values.shape[2]
        shaped = values.reshape(block_rows, seq_count, parts, 1, head_width)
        moved = lax.all_to_all(shaped, HEAD, split_axis=1, concat_axis=3, tiled=True)
        return moved.reshape(tok_rows, parts, inner_width)

    source = tokens.astype(jnp.float32).reshape(tok_rows, width)
    inv_attn = inverse_rms(source)
    attn_in = (source * inv_attn * gain_attn32).astype(jnp.bfloat16)
    stacked_weights = jnp.stack((full_query, full_key, full_value))
    projected = jnp.einsum(
        "td,cde->tce", attn_in, stacked_weights, preferred_element_type=jnp.float32
    ).astype(jnp.bfloat16)
    heads_in = to_heads(projected)
    queries = heads_in[:, :, 0]
    keys = heads_in[:, :, 1]
    values = heads_in[:, :, 2]
    start_state = (
        jnp.full((local_heads, seq_count, block_rows), masked_score, jnp.float32),
        jnp.zeros((local_heads, seq_count, block_rows), jnp.float32),
        jnp.zeros((block_rows, seq_count, local_heads, HEAD_DIM), jnp.float32),
    )
    key_piece = lax.all_gather(keys, BLK, axis=0, tiled=True)
    value_piece = lax.all_gather(values, BLK, axis=0, tiled=True)
    piece_rows = key_piece.shape[0]
    part_rows = math.gcd(piece_rows, group_rows)

    def forward_one_part(step_index, inner_state):
        offset = step_index * part_rows
        key_part = lax.dynamic_slice_in_dim(key_piece, offset, part_rows, 0)
        value_part = lax.dynamic_slice_in_dim(value_piece, offset, part_rows, 0)
        key_positions = offset + jnp.arange(part_rows, dtype=jnp.int32)

        def attend_now(current):
            return attend_step(
                current,
                queries,
                key_part,
                value_part,
                query_positions,
                key_positions,
                seq_lengths,
                bounds,
                table32,
            )

        skipped = (offset > query_last) | (offset >= longest)
        return lax.cond(skipped, same_state, attend_now, inner_state)

    row_top, row_total, weighted = lax.fori_loop(
        0, piece_rows // part_rows, forward_one_part, start_state
    )
    attn_heads = (weighted / jnp.transpose(row_total, (2, 1, 0))[..., None]).astype(jnp.bfloat16)
    log_total = jnp.transpose(row_top + jnp.log(row_total), (2, 1, 0))
    attn_tok = to_tokens(attn_heads[:, :, None])[:, 0]
    branch = jnp.dot(attn_tok, full_out, preferred_element_type=jnp.float32)
    hidden = source + branch
    expert_count = full_router.shape[1]
    local_experts = expert_in.shape[0]
    capacity = max(2, 3 * tok_rows // (2 * expert_count))
    inv_moe = inverse_rms(hidden)
    moe_in = (hidden * inv_moe * gain_moe32).astype(jnp.bfloat16)
    logits = jnp.dot(moe_in, full_router, preferred_element_type=jnp.float32)
    router_probs = jax.nn.softmax(logits, axis=-1)
    route_flat = routes.reshape(tok_rows)
    chosen = route_flat[:, None] == jnp.arange(expert_count, dtype=jnp.int32)[None, :]
    gate = jnp.sum(jnp.where(chosen, router_probs, 0.0), axis=-1)
    filled = jnp.cumsum(chosen.astype(jnp.int32), axis=0)
    slot = jnp.sum(jnp.where(chosen, filled - 1, 0), axis=-1)
    target = route_flat * capacity + slot
    dispatch = (
        target[:, None] == jnp.arange(expert_count * capacity, dtype=jnp.int32)[None, :]
    ).astype(jnp.bfloat16)

    def to_buffer(token_rows):
        packed = jnp.einsum(
            "tj,td->jd", dispatch, token_rows, preferred_element_type=jnp.float32
        ).astype(jnp.bfloat16)
        return packed.reshape(blk_count, local_experts, capacity, width)

    def from_buffer(buffer):
        return jnp.dot(
            dispatch,
            buffer.reshape(expert_count * capacity, width),
            preferred_element_type=jnp.float32,
        )

    def to_experts(buffer):
        return lax.all_to_all(buffer, BLK, split_axis=0, concat_axis=0, tiled=True)

    def all_rows(buffer):
        return lax.all_gather(buffer, HEAD, axis=0, tiled=True)

    def summed_rows(partial_terms):
        return lax.psum_scatter(
            partial_terms.astype(jnp.bfloat16), HEAD, scatter_dimension=0, tiled=True
        ).astype(jnp.float32)

    def to_owners(buffer):
        return lax.all_to_all(buffer, BLK, split_axis=0, concat_axis=0, tiled=True)

    expert_rows_in = all_rows(to_experts(to_buffer(moe_in)))
    expert_pre = jnp.einsum(
        "necd,edf->necf", expert_rows_in, expert_in, preferred_element_type=jnp.float32
    )
    expert_act, gelu_pull = jax.vjp(jax.nn.gelu, expert_pre)
    expert_low = expert_act.astype(jnp.bfloat16)
    expert_terms = jnp.einsum(
        "necf,efd->necd", expert_low, expert_out, preferred_element_type=jnp.float32
    )
    expert_tok = from_buffer(to_owners(summed_rows(expert_terms).astype(jnp.bfloat16)))
    result = hidden + gate[:, None] * expert_tok
    grad_result = cotangent.astype(jnp.float32).reshape(tok_rows, width)
    grad_expert_tok = (gate[:, None] * grad_result).astype(jnp.bfloat16)
    grad_gate = jnp.sum(grad_result * expert_tok, axis=-1)
    grad_logits = (
        router_probs * (jnp.where(chosen, grad_gate[:, None], 0.0) - (gate * grad_gate)[:, None])
    ).astype(jnp.bfloat16)
    grad_router = jnp.einsum("td,te->de", moe_in, grad_logits, preferred_element_type=jnp.float32)
    grad_rows = all_rows(to_experts(to_buffer(grad_expert_tok)))
    grad_act = jnp.einsum(
        "necd,efd->necf", grad_rows, expert_out, preferred_element_type=jnp.float32
    )
    grad_pre = gelu_pull(grad_act)[0].astype(jnp.bfloat16)
    grad_expert_out = jnp.einsum(
        "necf,necd->efd", expert_low, grad_rows, preferred_element_type=jnp.float32
    )
    grad_expert_in = jnp.einsum(
        "necd,necf->edf", expert_rows_in, grad_pre, preferred_element_type=jnp.float32
    )
    grad_back = jnp.einsum(
        "necf,edf->necd", grad_pre, expert_in, preferred_element_type=jnp.float32
    )
    grad_moe_in = from_buffer(to_owners(summed_rows(grad_back).astype(jnp.bfloat16)))
    grad_moe_in = grad_moe_in + jnp.einsum(
        "te,de->td", grad_logits, full_router, preferred_element_type=jnp.float32
    )
    grad_norm_moe, grad_gain_moe = norm_backward(grad_moe_in, hidden, inv_moe, gain_moe32)
    grad_hidden = grad_result + grad_norm_moe
    grad_branch = grad_hidden.astype(jnp.bfloat16)
    grad_out_w = jnp.einsum("te,td->ed", attn_tok, grad_branch, preferred_element_type=jnp.float32)
    grad_attn_tok = jnp.einsum(
        "td,ed->te", grad_branch, full_out, preferred_element_type=jnp.float32
    ).astype(jnp.bfloat16)
    grad_heads = to_heads(grad_attn_tok[:, None])[:, :, 0]
    delta = jnp.sum(grad_heads.astype(jnp.float32) * attn_heads.astype(jnp.float32), axis=-1)
    all_keys = lax.all_gather(keys, BLK, axis=0, tiled=True)
    all_values = lax.all_gather(values, BLK, axis=0, tiled=True)
    total_rows = all_keys.shape[0]
    step_rows = math.gcd(total_rows, group_rows)
    zero_heads = jnp.zeros((block_rows, seq_count, local_heads, HEAD_DIM), jnp.float32)
    zero_table = jnp.zeros(table32.shape, jnp.float32)

    def query_side(step_index, running):
        offset = step_index * step_rows
        key_block = lax.dynamic_slice_in_dim(all_keys, offset, step_rows, 0)
        value_block = lax.dynamic_slice_in_dim(all_values, offset, step_rows, 0)
        key_positions = offset + jnp.arange(step_rows, dtype=jnp.int32)

        def query_compute(current):
            grads = grad_step(
                queries,
                grad_heads,
                log_total,
                delta,
                query_positions,
                key_block,
                value_block,
                key_positions,
                seq_lengths,
                bounds,
                table32,
            )
            return (current[0] + grads[0], current[1] + grads[3])

        skipped = (offset > query_last) | (offset >= longest)
        return lax.cond(skipped, same_state, query_compute, running)

    grad_queries, grad_table = lax.fori_loop(
        0, total_rows // step_rows, query_side, (zero_heads, zero_table)
    )
    all_totals, all_deltas = (
        lax.all_gather(log_total, BLK, axis=0, tiled=True),
        lax.all_gather(delta, BLK, axis=0, tiled=True),
    )
    query_piece = lax.all_gather(queries, BLK, axis=0, tiled=True)
    grad_piece = lax.all_gather(grad_heads, BLK, axis=0, tiled=True)
    piece_rows = query_piece.shape[0]
    key_part_rows = math.gcd(piece_rows, group_rows)

    def key_one_part(step_index, inner_state):
        offset = step_index * key_part_rows
        query_part = lax.dynamic_slice_in_dim(query_piece, offset, key_part_rows, 0)
        grad_part = lax.dynamic_slice_in_dim(grad_piece, offset, key_part_rows, 0)
        total_part = lax.dynamic_slice_in_dim(all_totals, offset, key_part_rows, 0)
        delta_part = lax.dynamic_slice_in_dim(all_deltas, offset, key_part_rows, 0)
        part_positions = offset + jnp.arange(key_part_rows, dtype=jnp.int32)

        def key_compute(current):
            grads = grad_step(
                query_part,
                grad_part,
                total_part,
                delta_part,
                part_positions,
                keys,
                values,
                query_positions,
                seq_lengths,
                bounds,
                table32,
            )
            return (current[0] + grads[1], current[1] + grads[2])

        skipped = (offset + key_part_rows - 1 < query_first) | (query_first >= longest)
        return lax.cond(skipped, same_state, key_compute, inner_state)

    grad_keys, grad_values = lax.fori_loop(
        0, piece_rows // key_part_rows, key_one_part, (zero_heads, zero_heads)
    )
    grad_stack = jnp.stack((grad_queries, grad_keys, grad_values), axis=2).astype(jnp.bfloat16)
    grad_projected = to_tokens(grad_stack)
    grad_weights = jnp.einsum(
        "td,tce->cde", attn_in, grad_projected, preferred_element_type=jnp.float32
    )
    grad_attn_in = jnp.einsum(
        "tce,cde->td", grad_projected, stacked_weights, preferred_element_type=jnp.float32
    )
    grad_norm_attn, grad_gain_attn = norm_backward(grad_attn_in, source, inv_attn, gain_attn32)
    grad_tokens = grad_hidden + grad_norm_attn
    table_terms = lax.dynamic_update_slice_in_dim(
        jnp.zeros((NUM_BUCKETS, HEADS), jnp.float32), grad_table, head_index * local_heads, 1
    ).reshape(NUM_BUCKETS * HEADS)
    reduced = (
        lax.psum_scatter(grad_weights[0], (HEAD, BLK), scatter_dimension=0, tiled=True),
        lax.psum_scatter(grad_weights[1], (HEAD, BLK), scatter_dimension=0, tiled=True),
        lax.psum_scatter(grad_weights[2], (HEAD, BLK), scatter_dimension=0, tiled=True),
        lax.psum_scatter(grad_out_w, (HEAD, BLK), scatter_dimension=1, tiled=True),
        lax.psum_scatter(grad_gain_attn, (HEAD, BLK), scatter_dimension=0, tiled=True),
        lax.psum_scatter(table_terms, (HEAD, BLK), scatter_dimension=0, tiled=True),
        lax.psum_scatter(grad_gain_moe, (HEAD, BLK), scatter_dimension=0, tiled=True),
        lax.psum_scatter(grad_router, (HEAD, BLK), scatter_dimension=0, tiled=True),
    )
    return (
        result.astype(jnp.bfloat16).reshape(tokens.shape),
        grad_tokens.reshape(tokens.shape),
        reduced[4],
        reduced[0],
        reduced[1],
        reduced[2],
        reduced[3],
        reduced[5],
        reduced[6],
        reduced[7],
        grad_expert_in,
        grad_expert_out,
    )


BF = jnp.bfloat16
F4 = jnp.float32
NEG = -1e30
QB = 256
TILE = 512
LANES = 128


def dot(left, right, left_dim=1, right_dim=0):
    dims = (((left_dim,), (right_dim,)), ((), ()))
    return lax.dot_general(left, right, dims, preferred_element_type=F4)


def iota(shape, dim):
    return lax.broadcasted_iota(jnp.int32, shape, dim)


class Place:
    def __init__(self, lengths):
        self.lengths = lengths

    def __getitem__(self, item):
        if item == 0:
            return lax.axis_index(BLK)
        if item == 1:
            return lax.axis_index(HEAD)
        return self.lengths[lax.axis_index(HEAD)]


class Made(tuple):
    @property
    def token(self):
        return self[-1]


def vmem_call(body, lengths, args, outs, scratch=(), ties=(), loose=(), away=()):
    count, tied, made = len(args), len(ties), len(outs)

    def kernel(length_ref, *refs):
        inputs, rest = refs[:count], refs[count + tied :]
        body(Place(length_ref), *inputs, *rest[:made], *rest[made + 1 :])
        rest[made][...] = jnp.zeros((8, LANES), F4)

    vmem = pl.BlockSpec(memory_space=pltpu.VMEM)
    place = pl.BlockSpec(memory_space=pl.ANY)
    return Made(
        pl.pallas_call(
            kernel,
            out_shape=tuple(outs) + (shaped((8, LANES), F4),),
            in_specs=[pl.BlockSpec(memory_space=pltpu.SMEM)]
            + [place if i in loose else vmem for i in range(count)]
            + [vmem] * tied,
            out_specs=tuple(place if i in away else vmem for i in range(made)) + (vmem,),
            scratch_shapes=list(scratch),
            compiler_params=pltpu.CompilerParams(vmem_limit_bytes=60 * 1024 * 1024),
            cost_estimate=pl.CostEstimate(flops=1, bytes_accessed=1, transcendentals=0),
        )(lengths, *args, *ties)
    )


def shaped(shape, dtype):
    return jax.ShapeDtypeStruct(shape, dtype)


def ring_block(step, own_blk, ring_len):
    half = ring_len // 2
    place = jnp.where((own_blk & 1) == 0, own_blk >> 1, ring_len - 1 - (own_blk >> 1))
    place = (place + step) & (ring_len - 1)
    return jnp.where(place < half, 2 * place, 2 * ring_len - 1 - 2 * place)


def ring_steps(ring_len):
    steps = [0]
    for hop in range(1, ring_len // 2):
        steps += [-hop, hop]
    return steps + [ring_len // 2]


def norm_scale(values):
    return lax.rsqrt(jnp.mean(values * values, axis=-1, keepdims=True) + norm_eps)


def head_tile(block, head, place):
    tile = block[:, LANES * (head // 2) : LANES * (head // 2) + LANES].astype(F4)
    return tile if head % 2 == place else pltpu.roll(tile, HEAD_DIM, 1)


def column(row, size):
    square = jnp.where(iota((size, size), 0) == iota((size, size), 1), row.astype(F4), 0.0)
    return jnp.sum(square, axis=1, keepdims=True)


def pack_units(n, sc, wq, wk, wv, gain_a, gain_m, router, table, out):
    rows = wq.shape[0]
    lane = iota((rows, LANES), 1)
    row = iota((rows, LANES), 0)

    def widen(values, at):
        blank = jnp.zeros((values.shape[0], LANES - values.shape[1]), F4)
        return pltpu.roll(jnp.concatenate([values.astype(F4), blank], axis=1), at, 1)

    misc = widen(jnp.transpose(router[...].astype(F4)), 2)
    misc = jnp.where(lane == 0, column(gain_a[...], rows), misc)
    misc = jnp.where(lane == 1, column(gain_m[...], rows), misc)
    listed = jnp.broadcast_to(widen(table[...], 16), (rows, LANES))
    misc = (misc + jnp.where(row == 0, listed, 0.0)).astype(BF)
    for j in range(n):
        pair, turn = j // 2, j % 2
        for c, weight in enumerate((wq, wk, wv)):
            own = head_tile(weight, 3 * pair + turn, 0)
            both = head_tile(weight, 3 * pair + 2, 1)
            out[j, :, LANES * c : LANES * c + LANES] = jnp.where(
                lane < HEAD_DIM, own, both
            ).astype(BF)
        out[j, :, 3 * LANES : 4 * LANES] = misc


def place_rows(sc, n, rows, parts, dest):
    for kk, part in enumerate(parts):
        for j in range(n):
            first = pl.multiple_of(((sc[1] ^ kk) * n + j) * rows, 8)
            dest[pl.ds(first, rows), :] = part[j].astype(F4)


def unpack_units(n, rows, sc, p0, p1, p2, p3, unit_w, misc, misc_t, table, buf):
    place_rows(sc, n, rows, (p0, p1, p2, p3), buf)
    unit_w[...] = buf[:, 0 : 3 * LANES].astype(BF)
    for b in range(NUM_BUCKETS):
        table[b : b + 1, :] = buf[rows * b : rows * b + 1, 3 * LANES : 4 * LANES]
    tail = buf[:, 3 * LANES : 4 * LANES]
    misc[...] = tail.astype(BF)
    misc_t[...] = jnp.transpose(tail)


def bias_strips(n, sc, table, buckets, out, line):
    row = iota((8, TILE), 0)
    pair, turn = sc[0] >> 1, sc[0] & 1
    listed = table[...]
    lane = iota(listed.shape, 1)
    reach = buckets.shape[1]
    inside = iota((NUM_BUCKETS, reach), 0) == buckets[...]
    for unit, head in enumerate((3 * pair + turn, 3 * pair + 2)):
        entry = jnp.sum(jnp.where(lane == 16 + head, listed, 0.0), axis=1, keepdims=True)
        line[:, 0:QB] = jnp.zeros((1, QB), F4)
        line[:, QB:] = jnp.sum(jnp.where(inside, entry, 0.0), axis=0, keepdims=True)
        out[unit, 0] = jnp.full((QB, QB), NEG, F4)
        for far in range(n):
            flat = jnp.broadcast_to(line[:, far * QB : far * QB + TILE], (8, TILE))
            turned = flat
            for c in range(1, 8):
                turned = jnp.where(row == c, pltpu.roll(flat, c, 1), turned)
            for group in range(QB // 8):
                moved = turned if group == 0 else pltpu.roll(turned, 8 * group, 1)
                strip = moved[:, QB:]
                if far == 0:
                    after = iota((8, QB), 1) >= iota((8, QB), 0) + 8 * group
                    strip = jnp.where(after, strip, NEG)
                out[unit, far + 1, 8 * group : 8 * group + 8, :] = strip


def ones_row(cols):
    return jnp.where(iota((HEAD_DIM, cols), 0) == 0, 1.0, 0.0).astype(BF)


def unit_operands(n, sc, blocks, misc_t, unit_w, normed, outs):
    key_own, key_both, query_t, key_t, value_t, value_r = outs
    lane = iota((QB, LANES), 1)
    row = iota((QB, LANES), 0)
    gain = misc_t[0:1, :]
    for i, step in enumerate(ring_steps(n)):
        place = ring_block(step, sc[0], n)
        first = pl.multiple_of(place * QB, QB)
        block = jnp.concatenate([part[...].astype(F4) for part in blocks[i]], axis=0)
        rows = (block * norm_scale(block) * gain).astype(BF)
        normed[place] = rows
        made = dot(rows, unit_w[...])
        low = made.astype(BF)
        turned = jnp.transpose(made).astype(BF)
        keys = made[:, LANES : 2 * LANES]
        hidden_key = jnp.where(first + row < sc[2], 0.0, NEG)
        own = jnp.where(lane < HEAD_DIM, keys, jnp.where(lane == HEAD_DIM, hidden_key, 0.0))
        both = jnp.where(lane >= HEAD_DIM, keys, jnp.where(lane == 0, hidden_key, 0.0))
        key_own[pl.ds(first, QB), :] = own.astype(BF)
        key_both[pl.ds(first, QB), :] = both.astype(BF)
        query_t[:, pl.ds(first, QB)] = turned[0:LANES]
        key_t[:, pl.ds(first, QB)] = turned[LANES : 2 * LANES]
        value_t[:, pl.ds(first, QB)] = turned[2 * LANES :]
        value_r[pl.ds(first, QB), :] = low[:, 2 * LANES :]


class Unit:
    def __init__(self, shared, sc):
        self.shared = shared
        self.lo = HEAD_DIM if shared else 0
        self.part = LANES if shared else QB
        self.shift = pl.multiple_of((sc[0] & 1) * LANES, LANES) if shared else 0

    def lanes(self, block):
        start = block * QB if isinstance(block, int) else pl.multiple_of(block * QB, QB)
        return pl.ds(start + self.shift, self.part)

    def columns(self, ref, pair):
        rows = pl.ds(self.lo, HEAD_DIM)
        return jnp.concatenate([ref[rows, self.lanes(2 * pair + q)] for q in range(2)], axis=1)

    def padded(self, half, other):
        return jnp.concatenate([other, half] if self.shared else [half, other], axis=0)

    def strip(self, bias, far):
        def piece(key_half, query_half):
            at = max(far + query_half - key_half, -1) + 1 if isinstance(far, int) else (
                jnp.maximum(far + query_half - key_half, -1) + 1
            )
            return bias[at, :, pl.ds(self.shift, self.part)]

        return jnp.concatenate(
            [jnp.concatenate([piece(k, 0), piece(k, 1)], axis=1) for k in range(2)], axis=0
        )


def attend_tiles(n, unit, key_ref, query_t, value_t, bias, heads, log_ref):
    cols = 2 * unit.part
    for pair in range(n // 2):
        queries = unit.padded(unit.columns(query_t, pair), ones_row(cols))
        top = jnp.zeros((1, cols), F4) + NEG
        total = jnp.zeros((1, cols), F4)
        mixed = jnp.zeros((HEAD_DIM, cols), F4)
        for part in range(pair + 1):
            tile = dot(key_ref[part * TILE : (part + 1) * TILE, :], queries)
            tile = tile + unit.strip(bias, 2 * (pair - part))
            new_top = jnp.maximum(top, jnp.max(tile, axis=0, keepdims=True))
            weights = jnp.exp(tile - new_top)
            decay = jnp.exp(top - new_top)
            top = new_top
            total = total * decay + jnp.sum(weights, axis=0, keepdims=True)
            values = value_t[unit.lo : unit.lo + HEAD_DIM, part * TILE : (part + 1) * TILE]
            mixed = mixed * decay + dot(values, weights.astype(BF))
        made = (mixed / total).astype(BF)
        log_total = top + jnp.log(total)
        at = slice(QB, QB + LANES) if unit.shared else slice(0, QB)
        for q in range(2):
            cut = slice(q * unit.part, (q + 1) * unit.part)
            heads[2 * pair + q, :, at] = made[:, cut]
            log_ref[2 * pair + q] = log_total[:, cut]


def copies_of(pairs, sems):
    return [
        pltpu.make_async_copy(source, dest, sems.at[i]) for i, (source, dest) in enumerate(pairs)
    ]


def attend_units(n, sc, *refs):
    blocks = [(ref,) for ref in refs[: n - 1]] + [refs[n - 1 : n + 1]]
    misc_t, unit_w, table, buckets, heads, logs_own, logs_both = refs[n + 1 : n + 8]
    outs = refs[n + 8 : n + 15]
    kept, (value_t, line, sems) = refs[n + 15 : n + 22], refs[n + 22 :]
    normed, key_own, key_both, query_t, key_t, value_r, bias = kept
    copies = copies_of(list(zip(kept, outs)), sems)
    placed = (key_own, key_both, query_t, key_t, value_t, value_r)
    unit_operands(n, sc, blocks, misc_t, unit_w, normed, placed)
    for copy in copies[:-1]:
        copy.start()
    bias_strips(n, sc, table, buckets, bias, line)
    copies[-1].start()
    for shared, key_ref, log_ref in ((False, key_own, logs_own), (True, key_both, logs_both)):
        strips = bias.at[int(shared)]
        attend_tiles(n, Unit(shared, sc), key_ref, query_t, value_t, strips, heads, log_ref)
    for copy in copies:
        copy.wait()


def split_units(ref):
    return (ref.at[:, 0 : 3 * HEAD_DIM, :], ref.at[:, 3 * HEAD_DIM :, :])


def unit_grads(n, sc, *refs):
    key_own, key_both, query_t, key_t, value_r, strips_in, heads, grads_in = refs[:8]
    logs_own, logs_both, stacked, table = refs[8:12]
    grads_own, grads_both, delta_own, delta_both, grad_k, grad_v, strips, bias, sems = refs[12:]
    copies = copies_of([(strips_in.at[i], bias.at[i]) for i in (1, 0)], sems)
    for copy in copies:
        copy.start()
    own, both = split_units(stacked)
    common = (query_t, key_t, value_r, heads, grads_in)
    shared_only = (logs_both, both, table.at[n : 2 * n], grads_both, delta_both)
    own_only = (logs_own, own, table.at[0:n], grads_own, delta_own)
    sums = (grad_k, grad_v, strips)
    grads_of_unit(n, True, sc, copies[0], bias.at[1], key_both, *common, *shared_only, *sums)
    grads_of_unit(n, False, sc, copies[1], bias.at[0], key_own, *common, *own_only, *sums)


def grads_of_unit(
    n,
    shared,
    sc,
    copy,
    bias,
    key_ref,
    query_t,
    key_t,
    value_r,
    heads,
    grads_in,
    logs,
    stacked,
    table,
    grad_t,
    delta,
    grad_k,
    grad_v,
    strips,
):
    unit = Unit(shared, sc)
    cols = 2 * unit.part
    at = slice(QB, QB + LANES) if shared else slice(0, QB)
    rows = slice(unit.lo, unit.lo + HEAD_DIM)
    for j in range(n):
        grads = grads_in[j, :, at]
        grad_t[:, j * unit.part : (j + 1) * unit.part] = grads
        product = grads.astype(F4) * heads[j, :, at].astype(F4)
        delta[j] = jnp.sum(product, axis=0, keepdims=True)
    grad_k[...] = jnp.zeros(grad_k.shape, F4)
    grad_v[...] = jnp.zeros(grad_v.shape, F4)
    strips[...] = jnp.zeros(strips.shape, F4)
    copy.wait()

    def one_tile(pair, carry):
        nothing = jnp.zeros((HEAD_DIM, cols), BF)
        raw_queries = unit.columns(query_t, pair)
        queries = unit.padded(raw_queries, ones_row(cols))
        plain = unit.padded(raw_queries, nothing)
        start = pair * cols
        grads = unit.padded(grad_t[:, pl.ds(start, cols)], nothing)
        log_total = jnp.concatenate([logs[2 * pair + q] for q in range(2)], axis=1)
        inner = jnp.concatenate([delta[2 * pair + q] for q in range(2)], axis=1)

        def step(part, made):
            key_at = part * TILE
            far = 2 * (pair - part)
            scores = dot(key_ref[pl.ds(key_at, TILE), :], queries)
            scores = scores + unit.strip(bias, far)
            probs = jnp.exp(scores - log_total)
            grad_probs = dot(value_r[pl.ds(key_at, TILE), :], grads)
            grad_scores = probs * (grad_probs - inner)
            for key_half in range(2):
                for q in range(2):
                    place = max(far + q - key_half, -1) + 1
                    strips[place, :, pl.ds(unit.shift, unit.part)] += grad_scores[
                        key_half * QB : (key_half + 1) * QB, q * unit.part : (q + 1) * unit.part
                    ]
            low = grad_scores.astype(BF)
            grad_v[pl.ds(key_at, TILE), :] += dot(probs.astype(BF), grads, 1, 1)
            grad_k[pl.ds(key_at, TILE), :] += dot(low, plain, 1, 1)
            return made + dot(key_t[pl.ds(unit.lo, HEAD_DIM), pl.ds(key_at, TILE)], low)

        made = jnp.zeros((HEAD_DIM, cols), F4)
        for part in range(pair + 1):
            made = step(part, made)
        for q in range(2):
            cut = made[:, q * unit.part : (q + 1) * unit.part]
            if shared:
                half = HEAD_DIM // 2
                cut = jnp.concatenate([cut[0:half], cut[half:]], axis=1)
            stacked[2 * pair + q, 2 * HEAD_DIM :, :] = cut.astype(BF)
        return carry

    for pair in range(n // 2):
        one_tile(pair, 0)
    for j in range(n):
        block = slice(QB * j, QB * (j + 1))
        stacked[j, 0:HEAD_DIM, :] = jnp.transpose(grad_k[block, :])[rows].astype(BF)
        stacked[j, HEAD_DIM : 2 * HEAD_DIM, :] = jnp.transpose(grad_v[block, :])[rows].astype(BF)
    row = iota((8, TILE), 0)
    empty = jnp.zeros((8, QB), F4)
    for far in range(n):
        total = jnp.zeros((8, TILE), F4)
        for group in range(QB // 8):
            rows8 = strips[far + 1, 8 * group : 8 * group + 8, :]
            wide = jnp.concatenate([empty, rows8], axis=1)
            total = total + (wide if group == 0 else pltpu.roll(wide, TILE - 8 * group, 1))
        lined = jnp.where(row == 0, total, 0.0)
        for c in range(1, 8):
            lined = lined + jnp.where(row == c, pltpu.roll(total, TILE - c, 1), 0.0)
        table[far] = jnp.sum(lined, axis=0, keepdims=True)


def dispatch_rows(n, cap, sc, route_ref, cot, wo_t, wq, wk, wv, out, target, w_out):
    tok = cot.shape[0]
    route = route_ref[...]
    chosen = iota((n, tok), 0) == route
    upto = jnp.where(iota((tok, tok), 0) <= iota((tok, tok), 1), 1.0, 0.0).astype(BF)
    filled = dot(jnp.where(chosen, 1.0, 0.0).astype(BF), upto)
    slot = jnp.sum(jnp.where(chosen, filled - 1.0, 0.0), axis=0, keepdims=True)
    slot = slot.astype(jnp.int32)
    place = route * cap + slot
    target[...] = jnp.broadcast_to(place, target.shape)
    spread = jnp.where(iota((n * cap, tok), 0) == place, 1.0, 0.0).astype(BF)
    packed = dot(spread, cot[...]).astype(BF)
    weights = jnp.concatenate([w[...].astype(F4) for w in (wq, wk, wv)], axis=0).astype(BF)
    for j in range(n):
        out[j, 0:cap, :] = packed[j * cap : (j + 1) * cap]
        out[j, cap:, :] = wo_t[...]
        w_out[j] = weights


def spread_matrix(target, rows):
    place = target[0:1, :]
    return jnp.where(iota((rows, place.shape[1]), 0) == place, 1.0, 0.0)


def hidden_rows(
    n, cap, sc, heads, p0, p1, p2, p3, tokens, misc_t, target, attn, hidden_out, out, wo_t, buf, wide
):
    place_rows(sc, n, p0.shape[1], (p0, p1, p2, p3), wide)
    wo_t[...] = wide[...].astype(BF)
    for pair in range(n // 2):
        at = 3 * pair * HEAD_DIM
        for turn in range(2):
            made = heads[2 * pair + turn].astype(F4)
            buf[at + turn * HEAD_DIM : at + (turn + 1) * HEAD_DIM, :] = made[:, 0:QB]
            both = slice(turn * LANES, (turn + 1) * LANES)
            buf[at + 2 * HEAD_DIM : at + 3 * HEAD_DIM, both] = made[:, QB:]
    rows = jnp.transpose(buf[...]).astype(BF)
    attn[...] = rows
    hidden = tokens[...].astype(F4) + dot(rows, wo_t[...], 1, 1)
    hidden_out[...] = hidden
    moe_in = (hidden * norm_scale(hidden) * misc_t[1:2, :]).astype(BF)
    packed = dot(spread_matrix(target, n * cap).astype(BF), moe_in).astype(BF)
    for j in range(n):
        out[j] = packed[j * cap : (j + 1) * cap]


def gelu_pair(values):
    scale = math.sqrt(2.0 / math.pi)
    square = values * values
    bend = jnp.tanh(scale * (values + 0.044715 * values * square))
    act = 0.5 * values * (1.0 + bend)
    slope = 0.5 * (1.0 + bend) + 0.5 * values * (1.0 - bend * bend) * scale * (
        1.0 + 3.0 * 0.044715 * square
    )
    return (act, slope)


def route_probs(experts, sc, rows, misc):
    logits = dot(rows, misc[...])
    lane = iota(logits.shape, 1)
    real = (lane >= 2) & (lane < 2 + experts)
    logits = jnp.where(real, logits, NEG)
    powers = jnp.where(real, jnp.exp(logits - jnp.max(logits, axis=-1, keepdims=True)), 0.0)
    probs = powers / jnp.sum(powers, axis=-1, keepdims=True)
    chosen = lane == sc[0] + 2
    gate = jnp.sum(jnp.where(chosen, probs, 0.0), axis=-1, keepdims=True)
    return (probs, chosen, gate)


def flat_rows(ref, cap=None):
    return jnp.concatenate([ref[j][0:cap] for j in range(ref.shape[0])], axis=0)


def expert_back(
    experts, sc, rows_ref, cot_ref, in_a, out_a, in_b, out_b, misc, back, made, log_out
):
    rows, cots = flat_rows(rows_ref), flat_rows(cot_ref, rows_ref.shape[1])
    probs, chosen, gate = route_probs(experts, sc, rows, misc)
    inner = jnp.zeros(gate.shape, F4)
    total = jnp.zeros(rows.shape, F4)
    result = jnp.zeros(rows.shape, F4)
    for w_in, w_out in ((in_a, out_a), (in_b, out_b)):
        act, slope = gelu_pair(dot(rows, w_in[...]))
        low = act.astype(BF)
        result = result + dot(low, w_out[...])
        grad_act = dot(cots, w_out[...], 1, 1)
        inner = inner + jnp.sum(low.astype(F4) * grad_act, axis=-1, keepdims=True)
        total = total + dot((gate * grad_act * slope).astype(BF), w_in[...], 1, 1)
    grad_logits = (inner * probs * (jnp.where(chosen, 1.0, 0.0) - gate)).astype(BF)
    log_out[...] = grad_logits
    made[...] = (gate * result).astype(made.dtype)
    back[...] = (total + dot(grad_logits, misc[...], 1, 1)).astype(back.dtype)


def expert_weights(experts, count, more, sc, *refs):
    rows_refs, cot_refs = refs[:count], refs[count : 2 * count]
    w_in, w_out, misc = refs[2 * count : 2 * count + 3]
    begun = refs[2 * count + 3 : 2 * count + 5] if more else None
    grad_in, grad_out, token, all_rows, all_grads, turned = refs[2 * count + (5 if more else 3) :]
    token[...] = jnp.zeros(token.shape, F4)
    size = rows_refs[0].shape[0] * rows_refs[0].shape[1]

    @pl.when(pl.program_id(0) == 0)
    def _():
        for i in range(count):
            at = slice(i * size, (i + 1) * size)
            rows, cots = flat_rows(rows_refs[i]), flat_rows(cot_refs[i], rows_refs[i].shape[1])
            gate = route_probs(experts, sc, rows, misc)[2]
            all_rows[at, :] = rows
            turned[:, at] = jnp.transpose(rows.astype(F4)).astype(BF)
            all_grads[at, :] = (gate * cots.astype(F4)).astype(BF)

    rows, grads = all_rows[...], all_grads[...]
    act, slope = gelu_pair(dot(rows, w_in[...]))
    grad_pre = (dot(grads, w_out[...], 1, 1) * slope).astype(BF)
    in_part = dot(turned[...], grad_pre)
    out_part = dot(act.astype(BF), grads, 0, 0)
    grad_in[...] = begun[0][...] + in_part if more else in_part
    grad_out[...] = begun[1][...] + out_part if more else out_part


def chunked_specs(w_in):
    depth, hidden = w_in.shape
    chunk = 2 * LANES
    columns = pl.BlockSpec((depth, chunk), lambda i: (0, i))
    lines = pl.BlockSpec((chunk, depth), lambda i: (i, 0))
    return hidden // chunk, columns, lines


def expert_weights_call(experts, lengths, rows_in, cots_in, w_in, w_out, misc, ties, begun=()):
    count, (depth, hidden) = len(rows_in), w_in.shape
    size = rows_in[0].shape[0] * rows_in[0].shape[1]
    body = functools.partial(expert_weights, experts, count, bool(begun))
    args = tuple(rows_in) + tuple(cots_in) + (w_in, w_out, misc) + tuple(begun)

    def kernel(length_ref, *refs):
        body(Place(length_ref), *refs[: len(args)], *refs[len(args) + len(ties) :])

    whole = pl.BlockSpec(memory_space=pltpu.VMEM)
    steps, columns, lines = chunked_specs(w_in)
    return pl.pallas_call(
        kernel,
        grid=(steps,),
        out_shape=(
            shaped((depth, hidden), F4),
            shaped((hidden, depth), F4),
            shaped((8, LANES), F4),
        ),
        in_specs=[pl.BlockSpec(memory_space=pltpu.SMEM)]
        + [whole] * (2 * count)
        + [columns, lines, whole]
        + ([columns, lines] if begun else [])
        + [whole] * len(ties),
        out_specs=(columns, lines, whole),
        scratch_shapes=[
            pltpu.VMEM((count * size, depth), BF),
            pltpu.VMEM((count * size, depth), BF),
            pltpu.VMEM((depth, count * size), BF),
        ],
        compiler_params=pltpu.CompilerParams(vmem_limit_bytes=60 * 1024 * 1024),
        cost_estimate=pl.CostEstimate(flops=1, bytes_accessed=1, transcendentals=0),
    )(lengths, *args, *ties)


def result_rows(n, cap, sc, made, target, hidden, out):
    rows = flat_rows(made)
    spread = jnp.transpose(spread_matrix(target, n * cap)).astype(BF)
    out[...] = (hidden[...] + dot(spread, rows)).astype(BF)


def norm_back(grads, source, gain):
    scale = norm_scale(source)
    weighted = grads * gain
    inner = jnp.mean(weighted * source, axis=-1, keepdims=True)
    return (scale * weighted - source * (scale * scale * scale) * inner, scale)


def hidden_grads(
    n, cap, sc, back, target, hidden_ref, misc_t, cot, wo_t, grad_out, low_out, gain_out, out, buf
):
    spread = jnp.transpose(spread_matrix(target, n * cap)).astype(BF)
    grads = dot(spread, flat_rows(back))
    hidden = hidden_ref[...]
    normed, scale = norm_back(grads, hidden, misc_t[1:2, :])
    gain_out[...] = jnp.broadcast_to(
        jnp.sum(grads * hidden * scale, axis=0, keepdims=True), gain_out.shape
    )
    total = cot[...].astype(F4) + normed
    grad_out[...] = total
    low = total.astype(BF)
    low_out[...] = low
    buf[...] = jnp.transpose(dot(low, wo_t[...])).astype(BF)
    for pair in range(n // 2):
        at = 3 * pair * HEAD_DIM
        for turn in range(2):
            out[2 * pair + turn, :, 0:QB] = buf[at + turn * HEAD_DIM : at + (turn + 1) * HEAD_DIM, :]
            both = slice(turn * LANES, (turn + 1) * LANES)
            out[2 * pair + turn, :, QB:] = buf[at + 2 * HEAD_DIM : at + 3 * HEAD_DIM, both]


def unfolded(piece):
    return jnp.concatenate([piece[:, 0:LANES], piece[:, LANES:]], axis=0)


def unpack_full(n, rows, sc, p0, p1, p2, p3, out, wide):
    inner = wide.shape[1] // 3
    for kk, part in enumerate((p0, p1, p2, p3)):
        for j in range(n):
            first = pl.multiple_of(((sc[1] ^ kk) * n + j) * rows, 8)
            block = part[j].astype(F4)
            for c in range(3):
                wide[pl.ds(first, rows), c * inner : (c + 1) * inner] = block[
                    c * rows : (c + 1) * rows
                ]
    out[...] = wide[...].astype(BF)


def token_grads(n, sc, stacked, weights, tokens, hidden_grad, misc_t, out, buf):
    own, both = split_units(stacked)
    inner = weights.shape[1] // 3
    for pair in range(n // 2):
        at = 3 * pair * HEAD_DIM
        last = at + 2 * HEAD_DIM
        for turn in range(2):
            j = 2 * pair + turn
            for c, piece in enumerate((2, 0, 1)):
                lo = c * inner + at + turn * HEAD_DIM
                buf[lo : lo + HEAD_DIM, :] = own[j, piece * HEAD_DIM : (piece + 1) * HEAD_DIM, :]
            half = slice(turn * LANES, (turn + 1) * LANES)
            buf[last : last + HEAD_DIM, half] = unfolded(both[j, 2 * HEAD_DIM :, :])
        for c in (1, 2):
            rows = slice((c - 1) * HEAD_DIM, c * HEAD_DIM)
            total = both[2 * pair, rows, :].astype(F4) + both[2 * pair + 1, rows, :].astype(F4)
            buf[c * inner + last : c * inner + last + HEAD_DIM, :] = total.astype(BF)
    made = jnp.transpose(dot(weights[...], buf[...]))
    normed, unused = norm_back(made, tokens[...].astype(F4), misc_t[0:1, :])
    out[...] = (hidden_grad[...] + normed).reshape(out.shape)


def unit_weight_grads(n, heads, sc, normed, stacked, lines_ref, buckets, *rest):
    own, both = split_units(stacked)
    outs, (buf, table) = rest[:heads], rest[heads:]
    width = buf.shape[1]
    sums = []
    for unit in range(2):
        made = jnp.zeros((NUM_BUCKETS, 1), F4)
        for far in range(n):
            lines = lines_ref.at[unit * n : (unit + 1) * n]
            line = lines[far][:, QB:]
            if far + 1 < n:
                line = line + lines[far + 1][:, :QB]
            inside = iota((NUM_BUCKETS, QB), 0) == buckets[:, far * QB : (far + 1) * QB]
            made = made + jnp.sum(jnp.where(inside, line, 0.0), axis=1, keepdims=True)
        sums.append(made)
    lane = iota((NUM_BUCKETS, width), 1)
    high = [value.astype(BF).astype(F4) for value in sums]
    listed = jnp.zeros((NUM_BUCKETS, width), F4)
    for at, value in enumerate(high + [sums[0] - high[0], sums[1] - high[1]]):
        listed = jnp.where(lane == at, value, listed)
    table[...] = listed
    total = None
    for j in range(n):
        shared = unfolded(both[j, 2 * HEAD_DIM :, :]).astype(F4)
        blank = jnp.zeros(shared.shape, F4)
        turn = jnp.broadcast_to((sc[0] & 1) == 0, shared.shape)
        shared = jnp.concatenate(
            [jnp.where(turn, shared, blank), jnp.where(turn, blank, shared)], axis=1
        )
        pieces = [own[j, 2 * HEAD_DIM :, :], shared.astype(BF)]
        for c in range(2):
            rows = slice(c * HEAD_DIM, (c + 1) * HEAD_DIM)
            pieces += [own[j, rows, :], both[j, rows, :]]
        part = dot(jnp.concatenate(pieces, axis=0), normed[j])
        total = part if total is None else total + part
    buf[...] = jnp.transpose(total)
    rows = buf.shape[0] // heads
    for kk in range(heads):
        to = sc[1] ^ kk
        outs[kk][...] = jnp.concatenate(
            [
                buf[pl.ds(pl.multiple_of(to * rows, 8), rows), :],
                table[pl.ds(pl.multiple_of(to * n, 8), n), :],
                jnp.zeros((8, width), F4),
            ],
            axis=0,
        ).astype(BF)


def two_parts(values, gap):
    high = values.astype(BF).astype(F4)
    lane = iota(values.shape, 1)
    low = pltpu.roll(jnp.where(lane < gap, values - high, 0.0), gap, 1)
    return jnp.where(lane < gap, high, low)


def one_part(values, gap):
    return values + pltpu.roll(values, values.shape[1] - gap, 1)


def weight_sums(n, rows, heads, sc, *refs):
    units, outer = refs[:heads], refs[heads : 2 * heads]
    outs, buf = refs[2 * heads : -1], refs[-1]
    total = (units[0][...].astype(F4) + units[1][...].astype(F4)) + (
        units[2][...].astype(F4) + units[3][...].astype(F4)
    )
    base = n * rows
    entries = two_parts(one_part(total[base : base + n], 2), 2)
    wide = (outer[0][...].astype(F4) + outer[1][...].astype(F4)) + (
        outer[2][...].astype(F4) + outer[3][...].astype(F4)
    )
    width = wide.shape[1] - LANES
    extra = two_parts(one_part(wide[:, width:], 16), 16)
    for to in range(n):
        at = slice(to * rows, (to + 1) * rows)
        entry = pltpu.roll(entries[to : to + 1, 0:LANES], 64, 1)
        entry = jnp.where(iota((rows, LANES), 0) == 0, entry, 0.0)
        buf[to] = jnp.concatenate([total[at], wide[at, 0:width], extra[at] + entry], axis=1)
    for k in range(n):
        outs[k][...] = buf[sc[0] ^ k].astype(BF)


def as_row(values):
    size = values.shape[0]
    square = jnp.where(iota((size, size), 0) == iota((size, size), 1), values, 0.0)
    return jnp.sum(square, axis=0, keepdims=True)


def weight_final(n, experts, sc, *refs):
    parts, (wq, wk, wv, gain_a) = refs[:n], refs[n : n + 4]
    grads = refs[n + 4 : n + 7]
    gain, table, grad_out, gain_out, router, buf, tables = refs[n + 7 :]
    rows = wq.shape[0]
    units = 3 * LANES
    small = slice(parts[0].shape[1] - LANES, parts[0].shape[1])
    total = None
    for j in range(n):
        part = parts[j][...].astype(F4)
        buf[sc[0] ^ j] = part[:, 0:units]
        tables[sc[0] ^ j] = part[0:1, small]
        total = part[:, units:] if total is None else total + part[:, units:]
    lane = iota((rows, LANES), 1)
    inner = jnp.zeros((rows, 1), F4)
    for c, weight in enumerate((wq, wk, wv)):
        lo = LANES * c

        def piece(head, place):
            pair, turn = head // 3, head % 3
            if turn < 2:
                tile, half = buf[2 * pair + turn, 0:rows, lo : lo + LANES], 0
            else:
                tile = (
                    buf[2 * pair, 0:rows, lo : lo + LANES]
                    + buf[2 * pair + 1, 0:rows, lo : lo + LANES]
                )
                half = 1
            return tile if half == place else pltpu.roll(tile, HEAD_DIM, 1)

        for m in range(weight.shape[1] // LANES):
            tile = jnp.where(lane < HEAD_DIM, piece(2 * m, 0), piece(2 * m + 1, 1))
            cols = slice(LANES * m, LANES * m + LANES)
            grads[c][:, cols] = tile
            inner = inner + jnp.sum(weight[:, cols].astype(F4) * tile, axis=-1, keepdims=True)
    gain[...] = as_row(inner / column(gain_a[...], rows))
    lane = iota((1, HEADS), 1)
    listed = jnp.zeros((1, HEADS), F4)
    for j in range(n):
        entry = one_part(pltpu.roll(tables[j], 64, 1), 2)
        listed = listed + jnp.where(lane == 3 * (j // 2) + j % 2, entry[:, 0:1], 0.0)
        listed = listed + jnp.where(lane == 3 * (j // 2) + 2, entry[:, 1:2], 0.0)
    table[...] = listed
    width = grad_out.shape[1]
    grad_out[...] = total[:, 0:width]
    extra = total[0:rows, width:]
    extra = one_part(jnp.where(iota(extra.shape, 1) < 32, extra, 0.0), 16)
    gain_out[...] = as_row(extra[:, 1:2])
    router[...] = jnp.transpose(pltpu.roll(extra, LANES - 2, 1))[0:experts]


def out_weight_grads(heads, sc, low, attn, rows_a, rows_b, logs_a, logs_b, gain, *rest):
    outs, buf = rest[:heads], rest[heads]
    width = attn.shape[1]
    buf[:, 0:width] = dot(low[...], attn[...], 0, 0)
    router = dot(flat_rows(rows_a), logs_a[...], 0, 0) + dot(flat_rows(rows_b), logs_b[...], 0, 0)
    wide = jnp.where(iota((LANES, gain.shape[1]), 0) == 1, gain[0:1, :], 0.0)
    buf[:, width : width + LANES] = two_parts(router + jnp.transpose(wide), 16)
    rows = buf.shape[0] // heads
    for kk in range(heads):
        first = pl.multiple_of((sc[1] ^ kk) * rows, 8)
        outs[kk][...] = buf[pl.ds(first, rows), :].astype(BF)


def last_grads(n, experts, sc, *refs):
    parts, own, rest = refs[: n + 4], refs[n + 4 : n + 9], refs[n + 9 :]
    weight_final(n, experts, sc, *parts, *rest[:8], *rest[9:11])
    token_grads(n, sc, *own, rest[8], rest[11])


def swap(values, axis, flip):
    if flip == 0:
        return values
    size = lax.axis_size(axis)
    return lax.ppermute(values, axis, [(i, i ^ flip) for i in range(size)])


def exchange(messages, axis):
    return [swap(message, axis, k) for k, message in enumerate(messages)]


def hold(values, *earlier):
    return lax.optimization_barrier((values, earlier))[0]


def over_heads(stack):
    across = swap(stack, HEAD, 2)
    return (stack, swap(stack, HEAD, 1), across, swap(across, HEAD, 1))


def on_plane(
    tokens,
    attn_gain,
    w_query,
    w_key,
    w_value,
    w_out,
    bias_table,
    moe_gain,
    w_router,
    expert_in,
    expert_out,
    seq_lengths,
    rel_buckets,
    routes,
    cotangent,
):
    heads = lax.axis_size(HEAD)
    n = lax.axis_size(BLK)
    tok, width = tokens.shape[0], tokens.shape[2]
    rows = w_query.shape[0]
    total_rows = n * tok
    experts = w_router.shape[1]
    cap = 3 * tok // (2 * experts)
    slots = n * cap
    scope = jax.named_scope
    x = tokens.reshape(tok, width)
    cot = cotangent.reshape(tok, width)
    gain_a = attn_gain.reshape(1, rows)
    gain_m = moe_gain.reshape(1, rows)
    in_own, out_own = expert_in.reshape(expert_in.shape[1:]), expert_out.reshape(expert_out.shape[1:])

    def call(body, args, outs, scratch=(), ties=(), loose=(), away=()):
        return vmem_call(body, seq_lengths, args, outs, scratch, ties, loose, away)

    def all_to_all(stack, axis=BLK):
        return lax.all_to_all(stack, axis, split_axis=0, concat_axis=0, tiled=True)

    order = [ring_of(i, n) for i in range(n)]
    ahead = [(order[i], order[(i + 1) % n]) for i in range(n)]
    astern = [(b, a) for a, b in ahead]
    unit_cols = 4 * LANES

    def hop(front, back):
        with scope("rin"):
            front = lax.ppermute(front, BLK, ahead)
            back = lax.ppermute(back, BLK, astern)
            return lax.optimization_barrier((front, back))

    first = hop(x, x)
    with scope("uw"):
        packed, packed_token = call(
            functools.partial(pack_units, n),
            (w_query, w_key, w_value)
            + (gain_a, gain_m, jnp.transpose(w_router), bias_table.reshape(1, -1)),
            [shaped((n, rows, unit_cols), BF)],
        )
        unit_in = all_to_all(hold(packed, first[0]))
    with scope("cr"):
        cot_out, target, w_stack, cot_token = call(
            functools.partial(dispatch_rows, n, cap),
            (routes.reshape(1, tok), cot, jnp.transpose(w_out), w_query, w_key, w_value),
            [
                shaped((n, cap + rows, width), BF),
                shaped((8, tok), jnp.int32),
                shaped((n, 3 * rows, width), BF),
            ],
            ties=(packed_token,),
        )
    with scope("es"):
        in_other = swap(in_own, HEAD, 2)
    second = hop(*hold(first, packed_token))
    with scope("uw"):
        unit_parts = over_heads(hold(unit_in, second[0]))
    third = hop(*hold(second, unit_in, in_other, cot_token))
    half = tok // 2
    with scope("rin"):
        front_half, back_half = (third[0][:half], third[1][half:])
        front, back = lax.ppermute(front_half, BLK, ahead), lax.ppermute(back_half, BLK, astern)
    with scope("uw"):
        unit_w, misc, misc_t, table, unused = call(
            functools.partial(unpack_units, n, rows),
            unit_parts,
            [
                shaped((width, 3 * LANES), BF),
                shaped((width, LANES), BF),
                shaped((LANES, width), F4),
                shaped((NUM_BUCKETS, LANES), F4),
            ],
            [pltpu.VMEM((width, unit_cols), F4)],
        )
    with scope("es"):
        out_other = swap(hold(out_own, unit_parts[2], unit_parts[3]), HEAD, 2)

    buckets = rel_buckets.reshape(1, -1)

    with scope("cr"):
        cot_in = all_to_all(hold(cot_out, front, back, table))
        cot_rows, wo_rows = cot_in[:, :cap], cot_in[:, cap:]

    kept = [
        shaped((n, tok, width), BF),
        shaped((total_rows, LANES), BF),
        shaped((total_rows, LANES), BF),
        shaped((LANES, total_rows), BF),
        shaped((LANES, total_rows), BF),
        shaped((total_rows, LANES), BF),
        shaped((2, n + 1, QB, QB), F4),
    ]
    with scope("att"):
        (
            head_out,
            logs_own,
            logs_both,
            normed,
            key_own,
            key_both,
            query_t,
            key_t,
            value_r,
            strips,
            attend_token,
        ) = call(
            functools.partial(attend_units, n),
            (x,) + first + second + third + (front, back, misc_t, unit_w, table, buckets),
            [
                shaped((n, HEAD_DIM, QB + LANES), BF),
                shaped((n, 1, QB), F4),
                shaped((n, 1, LANES), F4),
            ]
            + kept,
            [pltpu.VMEM(k.shape, k.dtype) for k in kept]
            + [
                pltpu.VMEM((LANES, total_rows), BF),
                pltpu.VMEM((1, QB + total_rows), F4),
                pltpu.SemaphoreType.DMA((len(kept),)),
            ],
            ties=(cot_token,),
            away=range(3, 3 + len(kept)),
        )
        head_in = all_to_all(head_out)
    with scope("ow"):
        wo_parts = over_heads(hold(wo_rows, logs_both))
    with scope("cp"):
        all_cot = over_heads(hold(cot_rows, wo_parts[2]))
        cot_pair = all_cot[1]
    with scope("hid"):
        attn, hidden, moe_out, out_t, hidden_token = call(
            functools.partial(hidden_rows, n, cap),
            (head_in,) + wo_parts + (x, misc_t, target),
            [
                shaped((tok, width), BF),
                shaped((tok, width), F4),
                shaped((n, cap, width), BF),
                shaped((width, width), BF),
            ],
            [pltpu.VMEM((width, tok), F4), pltpu.VMEM((width, width), F4)],
            ties=(hold(attend_token, out_other),),

        )

    with scope("mr"):
        moe_rows = all_to_all(moe_out)
        moe_pair = swap(hold(moe_rows, all_cot[2], cot_pair), HEAD, 1)
    def backward_rows(rows_in, cots_in, kind, ties=()):
        return call(
            functools.partial(expert_back, experts),
            (rows_in, cots_in, in_own, out_own, in_other, out_other, misc),
            [
                shaped((slots, width), kind),
                shaped((slots, width), BF),
                shaped((slots, LANES), BF),
            ],
            ties=ties,
        )

    with scope("fw"):
        w_in = all_to_all(hold(w_stack, moe_pair))
    with scope("mf"):
        moe_far = swap(moe_rows, HEAD, 2)
        far_pair = swap(moe_far, HEAD, 1)

    with scope("eb"):
        back_pair, made_pair, logs_pair, token = backward_rows(moe_pair, cot_pair, BF)
        back_other = swap(back_pair, HEAD, 1)
        back_own, made_own, logs_own2, token = backward_rows(
            moe_rows, cot_rows, F4, (token,)
        )
        back_out = (back_own + back_other.astype(F4)).astype(BF).reshape(n, cap, width)
        back_out, back_token = hold((back_out, token), w_in)
        back_in = all_to_all(back_out)
    with scope("fw"):
        w_parts = over_heads(hold(w_in, back_token))
    with scope("ewg"):
        expert_ends = (in_own, out_own, misc)
        *begun, expert_token = expert_weights_call(
            experts,
            seq_lengths,
            (moe_rows, moe_pair),
            all_cot[:2],
            *expert_ends,
            (back_token,),
        )
    with scope("hg"):
        grad_hidden, grad_low, gain_moe_part, grad_heads_out, unused = call(
            functools.partial(hidden_grads, n, cap),
            (back_in, target, hidden, misc_t, cot, out_t),
            [
                shaped((tok, width), F4),
                shaped((tok, width), BF),
                shaped((8, width), F4),
                shaped((n, HEAD_DIM, QB + LANES), BF),
            ],
            [pltpu.VMEM((width, tok), BF)],
            ties=(hold(expert_token, far_pair, all_cot[3]),),
        )
        grad_heads = all_to_all(grad_heads_out)
    wide = width + LANES
    with scope("owg"):
        *out_parts, out_token = call(
            functools.partial(out_weight_grads, heads),
            (grad_low, attn, moe_rows, moe_pair, logs_own2, logs_pair, gain_moe_part),
            [shaped((width // heads, wide), BF)] * heads,
            [pltpu.VMEM((width, wide), F4)],
        )
        out_parts_in = exchange(out_parts, HEAD)
    with scope("rr"):
        res_out = made_own.astype(F4) + swap(made_pair, HEAD, 1).astype(F4)
        res_out = res_out.astype(BF).reshape(n, cap, width)
        res_in = all_to_all(hold(res_out, grad_heads, out_token))

    with scope("ag"):
        stacked, lines, unused = call(
            functools.partial(unit_grads, n),
            (
                key_own,
                key_both,
                query_t,
                key_t,
                value_r,
                strips,
                head_out,
                grad_heads,
                logs_own,
                logs_both,
            ),
            [shaped((n, 5 * HEAD_DIM + HEAD_DIM // 2, tok), BF), shaped((2 * n, 1, TILE), F4)],
            [
                pltpu.VMEM((HEAD_DIM, total_rows), BF),
                pltpu.VMEM((HEAD_DIM, total_rows // 2), BF),
                pltpu.VMEM((n, 1, QB), F4),
                pltpu.VMEM((n, 1, LANES), F4),
                pltpu.VMEM((total_rows, LANES), F4),
                pltpu.VMEM((total_rows, LANES), F4),
                pltpu.VMEM((n + 1, QB, QB), F4),
                pltpu.VMEM((2, n + 1, QB, QB), F4),
                pltpu.SemaphoreType.DMA((2,)),
            ],
            loose=(5,),
            ties=(hold(out_token, w_parts),),
        )
        unit_in = all_to_all(hold(stacked, res_in, out_parts_in))

    with scope("wg"):
        *unit_grad_parts, parts_token = call(
            functools.partial(unit_weight_grads, n, heads),
            (normed, stacked, lines, buckets),
            [shaped((width // heads + n + 8, 3 * LANES), BF)] * heads,
            [pltpu.VMEM((width, 3 * LANES), F4), pltpu.VMEM((NUM_BUCKETS, 3 * LANES), F4)],
        )
        unit_parts_in = exchange(unit_grad_parts, HEAD)
    with scope("res"):
        result, result_token = call(
            functools.partial(result_rows, n, cap),
            (res_in, target, hidden),
            [shaped((tok, width), BF)],
            ties=(parts_token,),
        )
    with scope("fw"):
        full_w, full_token = call(
            functools.partial(unpack_full, n, rows),
            w_parts,
            [shaped((width, 3 * width), BF)],
            [pltpu.VMEM((width, 3 * width), F4)],
            ties=(parts_token,),
        )
    with scope("wg"):
        *sums, sums_token = call(
            functools.partial(weight_sums, n, rows, heads),
            unit_parts_in + out_parts_in,
            [shaped((rows, 3 * LANES + wide), BF)] * n,
            [pltpu.VMEM((n, rows, 3 * LANES + wide), F4)],
            ties=(full_token, result_token),
        )
        sums_in = exchange(sums, BLK)
    with scope("ewg"):
        grad_in, grad_out, expert_token = expert_weights_call(
            experts,
            seq_lengths,
            (moe_far, far_pair),
            all_cot[2:],
            *expert_ends,
            (sums_token,),
            begun,
        )
    with scope("fin"):
        (
            grad_q,
            grad_k,
            grad_v,
            grad_gain_attn,
            grad_table,
            grad_out_w,
            grad_gain_moe,
            grad_router,
            grad_tokens,
            unused,
        ) = call(
            functools.partial(last_grads, n, experts),
            sums_in
            + [w_query, w_key, w_value, gain_a]
            + [unit_in, full_w, x, grad_hidden, misc_t],
            [shaped((rows, width), F4)] * 3
            + [
                shaped((1, rows), F4),
                shaped((1, HEADS), F4),
                shaped((rows, width), F4),
                shaped((1, rows), F4),
                shaped((experts, rows), F4),
                shaped(tokens.shape, F4),
            ],
            [
                pltpu.VMEM((n, rows, 3 * LANES), F4),
                pltpu.VMEM((n, 1, LANES), F4),
                pltpu.VMEM((3 * width, tok), BF),
            ],
            ties=(expert_token,),
        )
    return (
        result.reshape(tokens.shape),
        grad_tokens,
        grad_gain_attn.reshape(-1),
        grad_q,
        grad_k,
        grad_v,
        jnp.transpose(grad_out_w),
        grad_table.reshape(-1),
        grad_gain_moe.reshape(-1),
        jnp.transpose(grad_router),
        grad_in.reshape(expert_in.shape),
        grad_out.reshape(expert_out.shape),
    )


def ring_of(place, ring_len):
    return 2 * place if place < ring_len // 2 else 2 * ring_len - 1 - 2 * place


def solution(mesh):
    in_specs = (
        P(BLK, HEAD, None),
        P((HEAD, BLK)),
        P((HEAD, BLK), None),
        P((HEAD, BLK), None),
        P((HEAD, BLK), None),
        P(None, (HEAD, BLK)),
        P((HEAD, BLK)),
        P((HEAD, BLK)),
        P((HEAD, BLK), None),
        P(BLK, None, HEAD),
        P(BLK, HEAD, None),
        P(),
        P(),
        P(HEAD, BLK, None, None),
        P(BLK, HEAD, None),
    )
    out_specs = (
        P(BLK, HEAD, None),
        P(BLK, HEAD, None),
        P((HEAD, BLK)),
        P((HEAD, BLK), None),
        P((HEAD, BLK), None),
        P((HEAD, BLK), None),
        P(None, (HEAD, BLK)),
        P((HEAD, BLK)),
        P((HEAD, BLK)),
        P((HEAD, BLK), None),
        P(BLK, None, HEAD),
        P(BLK, HEAD, None),
    )
    one_each = mesh.shape[HEAD] == 4 and mesh.shape[BLK] == 8
    return jax.shard_map(
        on_plane if one_each else on_device, mesh=mesh, in_specs=in_specs, out_specs=out_specs, check_vma=False
    )
```

```python
import functools
import math

import jax
import jax.numpy as jnp
from jax import lax
from jax.experimental import pallas as pl
from jax.experimental.pallas import tpu as pltpu
from jax.sharding import PartitionSpec as P

HEADS = 12
HEAD_DIM = 64
NUM_BUCKETS = 32
HEAD, BLK = "head", "blk"


norm_eps = 1e-06
masked_score = -1e30


def inverse_rms(values):
    return lax.rsqrt(jnp.mean(values * values, axis=-1, keepdims=True) + norm_eps)


def norm_backward(grad_normed, source, inv_scale, gain):
    weighted = grad_normed * gain
    inner_mean = jnp.mean(weighted * source, axis=-1, keepdims=True)
    grad_source = inv_scale * weighted - source * (inv_scale * inv_scale * inv_scale) * inner_mean
    grad_gain = jnp.sum(grad_normed * source * inv_scale, axis=0)
    return (grad_source, grad_gain)


def same_state(running):
    return running


def bucket_bounds(rel_buckets):
    bucket_count = NUM_BUCKETS
    labels = jnp.arange(bucket_count, dtype=jnp.int32)
    starts = jnp.sum((rel_buckets[:, None] < labels[None, :]).astype(jnp.int32), axis=0)
    ends = jnp.concatenate([starts[1:], jnp.full((1,), rel_buckets.shape[0] + 1, jnp.int32)])
    return (starts, ends)


def bias_terms(query_positions, key_positions, bounds, table32):
    starts, ends = bounds
    distance = jnp.maximum(query_positions[:, None] - key_positions[None, :], 0)[:, :, None]
    inside = (distance >= starts[None, None, :]) & (distance < ends[None, None, :])
    onehot = inside.astype(jnp.bfloat16)
    bias = jnp.einsum(
        "qkb,bh->hqk", onehot, table32.astype(jnp.bfloat16), preferred_element_type=jnp.float32
    )
    return (onehot, bias)


def block_scores(queries, keys, query_positions, key_positions, seq_lengths, bounds, table32):
    onehot, bias = bias_terms(query_positions, key_positions, bounds, table32)
    raw = jnp.einsum("qshd,kshd->hsqk", queries, keys, preferred_element_type=jnp.float32)
    causal = key_positions[None, :] <= query_positions[:, None]
    present = key_positions[None, :] < seq_lengths[:, None]
    valid = causal[None, :, :] & present[:, None, :]
    return (raw + bias[:, None, :, :], valid[None], onehot)


def attend_step(
    running, queries, keys, values, query_positions, key_positions, seq_lengths, bounds, table32
):
    row_top, row_total, weighted = running
    scores, valid, unused = block_scores(
        queries, keys, query_positions, key_positions, seq_lengths, bounds, table32
    )
    scores = jnp.where(valid, scores, masked_score)
    new_top = jnp.maximum(row_top, jnp.max(scores, axis=-1))
    weights = jnp.where(valid, jnp.exp(scores - new_top[..., None]), 0.0)
    decay = jnp.exp(row_top - new_top)
    row_total = row_total * decay + jnp.sum(weights, axis=-1)
    mixed = jnp.einsum(
        "hsqk,kshd->qshd", weights.astype(jnp.bfloat16), values, preferred_element_type=jnp.float32
    )
    weighted = weighted * jnp.transpose(decay, (2, 1, 0))[..., None] + mixed
    return (new_top, row_total, weighted)


def grad_step(
    queries,
    grad_heads,
    log_total,
    delta,
    query_positions,
    keys,
    values,
    key_positions,
    seq_lengths,
    bounds,
    table32,
):
    scores, valid, onehot = block_scores(
        queries, keys, query_positions, key_positions, seq_lengths, bounds, table32
    )
    probs = jnp.where(valid, jnp.exp(scores - jnp.transpose(log_total, (2, 1, 0))[..., None]), 0.0)
    grad_probs = jnp.einsum(
        "qshd,kshd->hsqk", grad_heads, values, preferred_element_type=jnp.float32
    )
    grad_scores = probs * (grad_probs - jnp.transpose(delta, (2, 1, 0))[..., None])
    grad_table = jnp.einsum(
        "hqk,qkb->bh",
        jnp.sum(grad_scores, axis=1),
        onehot.astype(jnp.float32),
        precision=lax.Precision.HIGHEST,
    )
    low_scores = grad_scores.astype(jnp.bfloat16)
    grad_queries = jnp.einsum(
        "hsqk,kshd->qshd", low_scores, keys, preferred_element_type=jnp.float32
    )
    grad_keys = jnp.einsum(
        "hsqk,qshd->kshd", low_scores, queries, preferred_element_type=jnp.float32
    )
    grad_values = jnp.einsum(
        "hsqk,qshd->kshd",
        probs.astype(jnp.bfloat16),
        grad_heads,
        preferred_element_type=jnp.float32,
    )
    return (grad_queries, grad_keys, grad_values, grad_table)


def on_device(
    tokens,
    attn_gain,
    w_query,
    w_key,
    w_value,
    w_out,
    bias_table,
    moe_gain,
    w_router,
    expert_in,
    expert_out,
    seq_lengths,
    rel_buckets,
    routes,
    cotangent,
):
    head_count = lax.axis_size(HEAD)
    blk_count = lax.axis_size(BLK)
    head_index = lax.axis_index(HEAD)
    blk_index = lax.axis_index(BLK)
    block_rows, group_seqs, width = tokens.shape
    seq_count = group_seqs * head_count
    tok_rows = block_rows * group_seqs
    local_heads = HEADS // head_count
    head_width = local_heads * HEAD_DIM
    group_rows = block_rows * max(1, blk_count // 8)
    longest = jnp.max(seq_lengths)
    query_first = blk_index * block_rows
    query_last = query_first + block_rows - 1
    query_positions = query_first + jnp.arange(block_rows, dtype=jnp.int32)
    bounds = bucket_bounds(rel_buckets)
    fetched = (
        lax.all_gather(w_query, (HEAD, BLK), axis=0, tiled=True),
        lax.all_gather(w_key, (HEAD, BLK), axis=0, tiled=True),
        lax.all_gather(w_value, (HEAD, BLK), axis=0, tiled=True),
        lax.all_gather(w_out, (HEAD, BLK), axis=1, tiled=True),
        lax.all_gather(attn_gain, (HEAD, BLK), axis=0, tiled=True),
        lax.all_gather(bias_table, (HEAD, BLK), axis=0, tiled=True),
        lax.all_gather(moe_gain, (HEAD, BLK), axis=0, tiled=True),
        lax.all_gather(w_router, (HEAD, BLK), axis=0, tiled=True),
    )
    full_query, full_key, full_value, full_out, gain_attn, table_flat, gain_moe, full_router = (
        fetched
    )
    inner_width = full_query.shape[1]
    table_all = table_flat.astype(jnp.float32).reshape(NUM_BUCKETS, HEADS)
    table32 = lax.dynamic_slice_in_dim(table_all, head_index * local_heads, local_heads, 1)
    gain_attn32 = gain_attn.astype(jnp.float32)
    gain_moe32 = gain_moe.astype(jnp.float32)

    def to_heads(values):
        parts = values.shape[1]
        shaped = values.reshape(block_rows, group_seqs, parts, head_count, head_width)
        moved = lax.all_to_all(shaped, HEAD, split_axis=3, concat_axis=1, tiled=True)
        return moved.reshape(block_rows, seq_count, parts, local_heads, HEAD_DIM)

    def to_tokens(values):
        parts = values.shape[2]
        shaped = values.reshape(block_rows, seq_count, parts, 1, head_width)
        moved = lax.all_to_all(shaped, HEAD, split_axis=1, concat_axis=3, tiled=True)
        return moved.reshape(tok_rows, parts, inner_width)

    source = tokens.astype(jnp.float32).reshape(tok_rows, width)
    inv_attn = inverse_rms(source)
    attn_in = (source * inv_attn * gain_attn32).astype(jnp.bfloat16)
    stacked_weights = jnp.stack((full_query, full_key, full_value))
    projected = jnp.einsum(
        "td,cde->tce", attn_in, stacked_weights, preferred_element_type=jnp.float32
    ).astype(jnp.bfloat16)
    heads_in = to_heads(projected)
    queries = heads_in[:, :, 0]
    keys = heads_in[:, :, 1]
    values = heads_in[:, :, 2]
    start_state = (
        jnp.full((local_heads, seq_count, block_rows), masked_score, jnp.float32),
        jnp.zeros((local_heads, seq_count, block_rows), jnp.float32),
        jnp.zeros((block_rows, seq_count, local_heads, HEAD_DIM), jnp.float32),
    )
    key_piece = lax.all_gather(keys, BLK, axis=0, tiled=True)
    value_piece = lax.all_gather(values, BLK, axis=0, tiled=True)
    piece_rows = key_piece.shape[0]
    part_rows = math.gcd(piece_rows, group_rows)

    def forward_one_part(step_index, inner_state):
        offset = step_index * part_rows
        key_part = lax.dynamic_slice_in_dim(key_piece, offset, part_rows, 0)
        value_part = lax.dynamic_slice_in_dim(value_piece, offset, part_rows, 0)
        key_positions = offset + jnp.arange(part_rows, dtype=jnp.int32)

        def attend_now(current):
            return attend_step(
                current,
                queries,
                key_part,
                value_part,
                query_positions,
                key_positions,
                seq_lengths,
                bounds,
                table32,
            )

        skipped = (offset > query_last) | (offset >= longest)
        return lax.cond(skipped, same_state, attend_now, inner_state)

    row_top, row_total, weighted = lax.fori_loop(
        0, piece_rows // part_rows, forward_one_part, start_state
    )
    attn_heads = (weighted / jnp.transpose(row_total, (2, 1, 0))[..., None]).astype(jnp.bfloat16)
    log_total = jnp.transpose(row_top + jnp.log(row_total), (2, 1, 0))
    attn_tok = to_tokens(attn_heads[:, :, None])[:, 0]
    branch = jnp.dot(attn_tok, full_out, preferred_element_type=jnp.float32)
    hidden = source + branch
    expert_count = full_router.shape[1]
    local_experts = expert_in.shape[0]
    capacity = max(2, 3 * tok_rows // (2 * expert_count))
    inv_moe = inverse_rms(hidden)
    moe_in = (hidden * inv_moe * gain_moe32).astype(jnp.bfloat16)
    logits = jnp.dot(moe_in, full_router, preferred_element_type=jnp.float32)
    router_probs = jax.nn.softmax(logits, axis=-1)
    route_flat = routes.reshape(tok_rows)
    chosen = route_flat[:, None] == jnp.arange(expert_count, dtype=jnp.int32)[None, :]
    gate = jnp.sum(jnp.where(chosen, router_probs, 0.0), axis=-1)
    filled = jnp.cumsum(chosen.astype(jnp.int32), axis=0)
    slot = jnp.sum(jnp.where(chosen, filled - 1, 0), axis=-1)
    target = route_flat * capacity + slot
    dispatch = (
        target[:, None] == jnp.arange(expert_count * capacity, dtype=jnp.int32)[None, :]
    ).astype(jnp.bfloat16)

    def to_buffer(token_rows):
        packed = jnp.einsum(
            "tj,td->jd", dispatch, token_rows, preferred_element_type=jnp.float32
        ).astype(jnp.bfloat16)
        return packed.reshape(blk_count, local_experts, capacity, width)

    def from_buffer(buffer):
        return jnp.dot(
            dispatch,
            buffer.reshape(expert_count * capacity, width),
            preferred_element_type=jnp.float32,
        )

    def to_experts(buffer):
        return lax.all_to_all(buffer, BLK, split_axis=0, concat_axis=0, tiled=True)

    def all_rows(buffer):
        return lax.all_gather(buffer, HEAD, axis=0, tiled=True)

    def summed_rows(partial_terms):
        return lax.psum_scatter(
            partial_terms.astype(jnp.bfloat16), HEAD, scatter_dimension=0, tiled=True
        ).astype(jnp.float32)

    def to_owners(buffer):
        return lax.all_to_all(buffer, BLK, split_axis=0, concat_axis=0, tiled=True)

    expert_rows_in = all_rows(to_experts(to_buffer(moe_in)))
    expert_pre = jnp.einsum(
        "necd,edf->necf", expert_rows_in, expert_in, preferred_element_type=jnp.float32
    )
    expert_act, gelu_pull = jax.vjp(jax.nn.gelu, expert_pre)
    expert_low = expert_act.astype(jnp.bfloat16)
    expert_terms = jnp.einsum(
        "necf,efd->necd", expert_low, expert_out, preferred_element_type=jnp.float32
    )
    expert_tok = from_buffer(to_owners(summed_rows(expert_terms).astype(jnp.bfloat16)))
    result = hidden + gate[:, None] * expert_tok
    grad_result = cotangent.astype(jnp.float32).reshape(tok_rows, width)
    grad_expert_tok = (gate[:, None] * grad_result).astype(jnp.bfloat16)
    grad_gate = jnp.sum(grad_result * expert_tok, axis=-1)
    grad_logits = (
        router_probs * (jnp.where(chosen, grad_gate[:, None], 0.0) - (gate * grad_gate)[:, None])
    ).astype(jnp.bfloat16)
    grad_router = jnp.einsum("td,te->de", moe_in, grad_logits, preferred_element_type=jnp.float32)
    grad_rows = all_rows(to_experts(to_buffer(grad_expert_tok)))
    grad_act = jnp.einsum(
        "necd,efd->necf", grad_rows, expert_out, preferred_element_type=jnp.float32
    )
    grad_pre = gelu_pull(grad_act)[0].astype(jnp.bfloat16)
    grad_expert_out = jnp.einsum(
        "necf,necd->efd", expert_low, grad_rows, preferred_element_type=jnp.float32
    )
    grad_expert_in = jnp.einsum(
        "necd,necf->edf", expert_rows_in, grad_pre, preferred_element_type=jnp.float32
    )
    grad_back = jnp.einsum(
        "necf,edf->necd", grad_pre, expert_in, preferred_element_type=jnp.float32
    )
    grad_moe_in = from_buffer(to_owners(summed_rows(grad_back).astype(jnp.bfloat16)))
    grad_moe_in = grad_moe_in + jnp.einsum(
        "te,de->td", grad_logits, full_router, preferred_element_type=jnp.float32
    )
    grad_norm_moe, grad_gain_moe = norm_backward(grad_moe_in, hidden, inv_moe, gain_moe32)
    grad_hidden = grad_result + grad_norm_moe
    grad_branch = grad_hidden.astype(jnp.bfloat16)
    grad_out_w = jnp.einsum("te,td->ed", attn_tok, grad_branch, preferred_element_type=jnp.float32)
    grad_attn_tok = jnp.einsum(
        "td,ed->te", grad_branch, full_out, preferred_element_type=jnp.float32
    ).astype(jnp.bfloat16)
    grad_heads = to_heads(grad_attn_tok[:, None])[:, :, 0]
    delta = jnp.sum(grad_heads.astype(jnp.float32) * attn_heads.astype(jnp.float32), axis=-1)
    all_keys = lax.all_gather(keys, BLK, axis=0, tiled=True)
    all_values = lax.all_gather(values, BLK, axis=0, tiled=True)
    total_rows = all_keys.shape[0]
    step_rows = math.gcd(total_rows, group_rows)
    zero_heads = jnp.zeros((block_rows, seq_count, local_heads, HEAD_DIM), jnp.float32)
    zero_table = jnp.zeros(table32.shape, jnp.float32)

    def query_side(step_index, running):
        offset = step_index * step_rows
        key_block = lax.dynamic_slice_in_dim(all_keys, offset, step_rows, 0)
        value_block = lax.dynamic_slice_in_dim(all_values, offset, step_rows, 0)
        key_positions = offset + jnp.arange(step_rows, dtype=jnp.int32)

        def query_compute(current):
            grads = grad_step(
                queries,
                grad_heads,
                log_total,
                delta,
                query_positions,
                key_block,
                value_block,
                key_positions,
                seq_lengths,
                bounds,
                table32,
            )
            return (current[0] + grads[0], current[1] + grads[3])

        skipped = (offset > query_last) | (offset >= longest)
        return lax.cond(skipped, same_state, query_compute, running)

    grad_queries, grad_table = lax.fori_loop(
        0, total_rows // step_rows, query_side, (zero_heads, zero_table)
    )
    all_totals, all_deltas = (
        lax.all_gather(log_total, BLK, axis=0, tiled=True),
        lax.all_gather(delta, BLK, axis=0, tiled=True),
    )
    query_piece = lax.all_gather(queries, BLK, axis=0, tiled=True)
    grad_piece = lax.all_gather(grad_heads, BLK, axis=0, tiled=True)
    piece_rows = query_piece.shape[0]
    key_part_rows = math.gcd(piece_rows, group_rows)

    def key_one_part(step_index, inner_state):
        offset = step_index * key_part_rows
        query_part = lax.dynamic_slice_in_dim(query_piece, offset, key_part_rows, 0)
        grad_part = lax.dynamic_slice_in_dim(grad_piece, offset, key_part_rows, 0)
        total_part = lax.dynamic_slice_in_dim(all_totals, offset, key_part_rows, 0)
        delta_part = lax.dynamic_slice_in_dim(all_deltas, offset, key_part_rows, 0)
        part_positions = offset + jnp.arange(key_part_rows, dtype=jnp.int32)

        def key_compute(current):
            grads = grad_step(
                query_part,
                grad_part,
                total_part,
                delta_part,
                part_positions,
                keys,
                values,
                query_positions,
                seq_lengths,
                bounds,
                table32,
            )
            return (current[0] + grads[1], current[1] + grads[2])

        skipped = (offset + key_part_rows - 1 < query_first) | (query_first >= longest)
        return lax.cond(skipped, same_state, key_compute, inner_state)

    grad_keys, grad_values = lax.fori_loop(
        0, piece_rows // key_part_rows, key_one_part, (zero_heads, zero_heads)
    )
    grad_stack = jnp.stack((grad_queries, grad_keys, grad_values), axis=2).astype(jnp.bfloat16)
    grad_projected = to_tokens(grad_stack)
    grad_weights = jnp.einsum(
        "td,tce->cde", attn_in, grad_projected, preferred_element_type=jnp.float32
    )
    grad_attn_in = jnp.einsum(
        "tce,cde->td", grad_projected, stacked_weights, preferred_element_type=jnp.float32
    )
    grad_norm_attn, grad_gain_attn = norm_backward(grad_attn_in, source, inv_attn, gain_attn32)
    grad_tokens = grad_hidden + grad_norm_attn
    table_terms = lax.dynamic_update_slice_in_dim(
        jnp.zeros((NUM_BUCKETS, HEADS), jnp.float32), grad_table, head_index * local_heads, 1
    ).reshape(NUM_BUCKETS * HEADS)
    reduced = (
        lax.psum_scatter(grad_weights[0], (HEAD, BLK), scatter_dimension=0, tiled=True),
        lax.psum_scatter(grad_weights[1], (HEAD, BLK), scatter_dimension=0, tiled=True),
        lax.psum_scatter(grad_weights[2], (HEAD, BLK), scatter_dimension=0, tiled=True),
        lax.psum_scatter(grad_out_w, (HEAD, BLK), scatter_dimension=1, tiled=True),
        lax.psum_scatter(grad_gain_attn, (HEAD, BLK), scatter_dimension=0, tiled=True),
        lax.psum_scatter(table_terms, (HEAD, BLK), scatter_dimension=0, tiled=True),
        lax.psum_scatter(grad_gain_moe, (HEAD, BLK), scatter_dimension=0, tiled=True),
        lax.psum_scatter(grad_router, (HEAD, BLK), scatter_dimension=0, tiled=True),
    )
    return (
        result.astype(jnp.bfloat16).reshape(tokens.shape),
        grad_tokens.reshape(tokens.shape),
        reduced[4],
        reduced[0],
        reduced[1],
        reduced[2],
        reduced[3],
        reduced[5],
        reduced[6],
        reduced[7],
        grad_expert_in,
        grad_expert_out,
    )


BF = jnp.bfloat16
F4 = jnp.float32
NEG = -1e30
QB = 256
TILE = 512
LANES = 128


def dot(left, right, left_dim=1, right_dim=0):
    dims = (((left_dim,), (right_dim,)), ((), ()))
    return lax.dot_general(left, right, dims, preferred_element_type=F4)


def iota(shape, dim):
    return lax.broadcasted_iota(jnp.int32, shape, dim)


class Place:
    def __init__(self, lengths):
        self.lengths = lengths

    def __getitem__(self, item):
        if item == 0:
            return lax.axis_index(BLK)
        if item == 1:
            return lax.axis_index(HEAD)
        return self.lengths[lax.axis_index(HEAD)]


class Made(tuple):
    @property
    def token(self):
        return self[-1]


def vmem_call(body, lengths, args, outs, scratch=(), ties=(), loose=(), away=()):
    count, tied, made = len(args), len(ties), len(outs)

    def kernel(length_ref, *refs):
        inputs, rest = refs[:count], refs[count + tied :]
        body(Place(length_ref), *inputs, *rest[:made], *rest[made + 1 :])
        rest[made][...] = jnp.zeros((8, LANES), F4)

    vmem = pl.BlockSpec(memory_space=pltpu.VMEM)
    place = pl.BlockSpec(memory_space=pl.ANY)
    return Made(
        pl.pallas_call(
            kernel,
            out_shape=tuple(outs) + (shaped((8, LANES), F4),),
            in_specs=[pl.BlockSpec(memory_space=pltpu.SMEM)]
            + [place if i in loose else vmem for i in range(count)]
            + [vmem] * tied,
            out_specs=tuple(place if i in away else vmem for i in range(made)) + (vmem,),
            scratch_shapes=list(scratch),
            compiler_params=pltpu.CompilerParams(vmem_limit_bytes=60 * 1024 * 1024),
            cost_estimate=pl.CostEstimate(flops=1, bytes_accessed=1, transcendentals=0),
        )(lengths, *args, *ties)
    )


def shaped(shape, dtype):
    return jax.ShapeDtypeStruct(shape, dtype)


def ring_block(step, own_blk, ring_len):
    half = ring_len // 2
    place = jnp.where((own_blk & 1) == 0, own_blk >> 1, ring_len - 1 - (own_blk >> 1))
    place = (place + step) & (ring_len - 1)
    return jnp.where(place < half, 2 * place, 2 * ring_len - 1 - 2 * place)


def ring_steps(ring_len):
    steps = [0]
    for hop in range(1, ring_len // 2):
        steps += [-hop, hop]
    return steps + [ring_len // 2]


def norm_scale(values):
    return lax.rsqrt(jnp.mean(values * values, axis=-1, keepdims=True) + norm_eps)


def head_tile(block, head, place):
    tile = block[:, LANES * (head // 2) : LANES * (head // 2) + LANES].astype(F4)
    return tile if head % 2 == place else pltpu.roll(tile, HEAD_DIM, 1)


def column(row, size):
    square = jnp.where(iota((size, size), 0) == iota((size, size), 1), row.astype(F4), 0.0)
    return jnp.sum(square, axis=1, keepdims=True)


def pack_units(n, sc, wq, wk, wv, gain_a, gain_m, router, table, out):
    rows = wq.shape[0]
    lane = iota((rows, LANES), 1)
    row = iota((rows, LANES), 0)

    def widen(values, at):
        blank = jnp.zeros((values.shape[0], LANES - values.shape[1]), F4)
        return pltpu.roll(jnp.concatenate([values.astype(F4), blank], axis=1), at, 1)

    misc = widen(jnp.transpose(router[...].astype(F4)), 2)
    misc = jnp.where(lane == 0, column(gain_a[...], rows), misc)
    misc = jnp.where(lane == 1, column(gain_m[...], rows), misc)
    listed = jnp.broadcast_to(widen(table[...], 16), (rows, LANES))
    misc = (misc + jnp.where(row == 0, listed, 0.0)).astype(BF)
    for j in range(n):
        pair, turn = j // 2, j % 2
        for c, weight in enumerate((wq, wk, wv)):
            own = head_tile(weight, 3 * pair + turn, 0)
            both = head_tile(weight, 3 * pair + 2, 1)
            out[j, :, LANES * c : LANES * c + LANES] = jnp.where(
                lane < HEAD_DIM, own, both
            ).astype(BF)
        out[j, :, 3 * LANES : 4 * LANES] = misc


def place_rows(sc, n, rows, parts, dest):
    for kk, part in enumerate(parts):
        for j in range(n):
            first = pl.multiple_of(((sc[1] ^ kk) * n + j) * rows, 8)
            dest[pl.ds(first, rows), :] = part[j].astype(F4)


def unpack_units(n, rows, sc, p0, p1, p2, p3, unit_w, misc, misc_t, table, buf):
    place_rows(sc, n, rows, (p0, p1, p2, p3), buf)
    unit_w[...] = buf[:, 0 : 3 * LANES].astype(BF)
    for b in range(NUM_BUCKETS):
        table[b : b + 1, :] = buf[rows * b : rows * b + 1, 3 * LANES : 4 * LANES]
    tail = buf[:, 3 * LANES : 4 * LANES]
    misc[...] = tail.astype(BF)
    misc_t[...] = jnp.transpose(tail)


def bias_strips(n, sc, table, buckets, out, line):
    row = iota((8, TILE), 0)
    pair, turn = sc[0] >> 1, sc[0] & 1
    listed = table[...]
    lane = iota(listed.shape, 1)
    reach = buckets.shape[1]
    inside = iota((NUM_BUCKETS, reach), 0) == buckets[...]
    for unit, head in enumerate((3 * pair + turn, 3 * pair + 2)):
        entry = jnp.sum(jnp.where(lane == 16 + head, listed, 0.0), axis=1, keepdims=True)
        line[:, 0:QB] = jnp.zeros((1, QB), F4)
        line[:, QB:] = jnp.sum(jnp.where(inside, entry, 0.0), axis=0, keepdims=True)
        out[unit, 0] = jnp.full((QB, QB), NEG, F4)
        for far in range(n):
            flat = jnp.broadcast_to(line[:, far * QB : far * QB + TILE], (8, TILE))
            turned = flat
            for c in range(1, 8):
                turned = jnp.where(row == c, pltpu.roll(flat, c, 1), turned)
            for group in range(QB // 8):
                moved = turned if group == 0 else pltpu.roll(turned, 8 * group, 1)
                strip = moved[:, QB:]
                if far == 0:
                    after = iota((8, QB), 1) >= iota((8, QB), 0) + 8 * group
                    strip = jnp.where(after, strip, NEG)
                out[unit, far + 1, 8 * group : 8 * group + 8, :] = strip


def ones_row(cols):
    return jnp.where(iota((HEAD_DIM, cols), 0) == 0, 1.0, 0.0).astype(BF)


def unit_operands(n, sc, blocks, misc_t, unit_w, normed, outs):
    key_own, key_both, query_t, key_t, value_t, value_r = outs
    lane = iota((QB, LANES), 1)
    row = iota((QB, LANES), 0)
    gain = misc_t[0:1, :]
    for i, step in enumerate(ring_steps(n)):
        place = ring_block(step, sc[0], n)
        first = pl.multiple_of(place * QB, QB)
        block = jnp.concatenate([part[...].astype(F4) for part in blocks[i]], axis=0)
        rows = (block * norm_scale(block) * gain).astype(BF)
        normed[place] = rows
        made = dot(rows, unit_w[...])
        low = made.astype(BF)
        turned = jnp.transpose(made).astype(BF)
        keys = made[:, LANES : 2 * LANES]
        hidden_key = jnp.where(first + row < sc[2], 0.0, NEG)
        own = jnp.where(lane < HEAD_DIM, keys, jnp.where(lane == HEAD_DIM, hidden_key, 0.0))
        both = jnp.where(lane >= HEAD_DIM, keys, jnp.where(lane == 0, hidden_key, 0.0))
        key_own[pl.ds(first, QB), :] = own.astype(BF)
        key_both[pl.ds(first, QB), :] = both.astype(BF)
        query_t[:, pl.ds(first, QB)] = turned[0:LANES]
        key_t[:, pl.ds(first, QB)] = turned[LANES : 2 * LANES]
        value_t[:, pl.ds(first, QB)] = turned[2 * LANES :]
        value_r[pl.ds(first, QB), :] = low[:, 2 * LANES :]


class Unit:
    def __init__(self, shared, sc):
        self.shared = shared
        self.lo = HEAD_DIM if shared else 0
        self.part = LANES if shared else QB
        self.shift = pl.multiple_of((sc[0] & 1) * LANES, LANES) if shared else 0

    def lanes(self, block):
        start = block * QB if isinstance(block, int) else pl.multiple_of(block * QB, QB)
        return pl.ds(start + self.shift, self.part)

    def columns(self, ref, pair):
        rows = pl.ds(self.lo, HEAD_DIM)
        return jnp.concatenate([ref[rows, self.lanes(2 * pair + q)] for q in range(2)], axis=1)

    def padded(self, half, other):
        return jnp.concatenate([other, half] if self.shared else [half, other], axis=0)

    def strip(self, bias, far):
        def piece(key_half, query_half):
            at = max(far + query_half - key_half, -1) + 1 if isinstance(far, int) else (
                jnp.maximum(far + query_half - key_half, -1) + 1
            )
            return bias[at, :, pl.ds(self.shift, self.part)]

        return jnp.concatenate(
            [jnp.concatenate([piece(k, 0), piece(k, 1)], axis=1) for k in range(2)], axis=0
        )


def attend_tiles(n, unit, key_ref, query_t, value_t, bias, heads, log_ref):
    cols = 2 * unit.part
    for pair in range(n // 2):
        queries = unit.padded(unit.columns(query_t, pair), ones_row(cols))
        top = jnp.zeros((1, cols), F4) + NEG
        total = jnp.zeros((1, cols), F4)
        mixed = jnp.zeros((HEAD_DIM, cols), F4)
        for part in range(pair + 1):
            tile = dot(key_ref[part * TILE : (part + 1) * TILE, :], queries)
            tile = tile + unit.strip(bias, 2 * (pair - part))
            new_top = jnp.maximum(top, jnp.max(tile, axis=0, keepdims=True))
            weights = jnp.exp(tile - new_top)
            decay = jnp.exp(top - new_top)
            top = new_top
            total = total * decay + jnp.sum(weights, axis=0, keepdims=True)
            values = value_t[unit.lo : unit.lo + HEAD_DIM, part * TILE : (part + 1) * TILE]
            mixed = mixed * decay + dot(values, weights.astype(BF))
        made = (mixed / total).astype(BF)
        log_total = top + jnp.log(total)
        at = slice(QB, QB + LANES) if unit.shared else slice(0, QB)
        for q in range(2):
            cut = slice(q * unit.part, (q + 1) * unit.part)
            heads[2 * pair + q, :, at] = made[:, cut]
            log_ref[2 * pair + q] = log_total[:, cut]


def copies_of(pairs, sems):
    return [
        pltpu.make_async_copy(source, dest, sems.at[i]) for i, (source, dest) in enumerate(pairs)
    ]


def attend_units(n, sc, *refs):
    blocks = [(ref,) for ref in refs[: n - 1]] + [refs[n - 1 : n + 1]]
    misc_t, unit_w, table, buckets, heads, logs_own, logs_both = refs[n + 1 : n + 8]
    outs = refs[n + 8 : n + 15]
    kept, (value_t, line, sems) = refs[n + 15 : n + 22], refs[n + 22 :]
    normed, key_own, key_both, query_t, key_t, value_r, bias = kept
    copies = copies_of(list(zip(kept, outs)), sems)
    placed = (key_own, key_both, query_t, key_t, value_t, value_r)
    unit_operands(n, sc, blocks, misc_t, unit_w, normed, placed)
    for copy in copies[:-1]:
        copy.start()
    bias_strips(n, sc, table, buckets, bias, line)
    copies[-1].start()
    for shared, key_ref, log_ref in ((False, key_own, logs_own), (True, key_both, logs_both)):
        strips = bias.at[int(shared)]
        attend_tiles(n, Unit(shared, sc), key_ref, query_t, value_t, strips, heads, log_ref)
    for copy in copies:
        copy.wait()


def split_units(ref):
    return (ref.at[:, 0 : 3 * HEAD_DIM, :], ref.at[:, 3 * HEAD_DIM :, :])


def unit_grads(n, sc, *refs):
    key_own, key_both, query_t, key_t, value_r, strips_in, heads, grads_in = refs[:8]
    logs_own, logs_both, stacked, table = refs[8:12]
    grads_own, grads_both, delta_own, delta_both, grad_k, grad_v, strips, bias, sems = refs[12:]
    copies = copies_of([(strips_in.at[i], bias.at[i]) for i in (1, 0)], sems)
    for copy in copies:
        copy.start()
    own, both = split_units(stacked)
    common = (query_t, key_t, value_r, heads, grads_in)
    shared_only = (logs_both, both, table.at[n : 2 * n], grads_both, delta_both)
    own_only = (logs_own, own, table.at[0:n], grads_own, delta_own)
    sums = (grad_k, grad_v, strips)
    grads_of_unit(n, True, sc, copies[0], bias.at[1], key_both, *common, *shared_only, *sums)
    grads_of_unit(n, False, sc, copies[1], bias.at[0], key_own, *common, *own_only, *sums)


def grads_of_unit(
    n,
    shared,
    sc,
    copy,
    bias,
    key_ref,
    query_t,
    key_t,
    value_r,
    heads,
    grads_in,
    logs,
    stacked,
    table,
    grad_t,
    delta,
    grad_k,
    grad_v,
    strips,
):
    unit = Unit(shared, sc)
    cols = 2 * unit.part
    at = slice(QB, QB + LANES) if shared else slice(0, QB)
    rows = slice(unit.lo, unit.lo + HEAD_DIM)
    for j in range(n):
        grads = grads_in[j, :, at]
        grad_t[:, j * unit.part : (j + 1) * unit.part] = grads
        product = grads.astype(F4) * heads[j, :, at].astype(F4)
        delta[j] = jnp.sum(product, axis=0, keepdims=True)
    grad_k[...] = jnp.zeros(grad_k.shape, F4)
    grad_v[...] = jnp.zeros(grad_v.shape, F4)
    strips[...] = jnp.zeros(strips.shape, F4)
    copy.wait()

    def one_tile(pair, carry):
        nothing = jnp.zeros((HEAD_DIM, cols), BF)
        raw_queries = unit.columns(query_t, pair)
        queries = unit.padded(raw_queries, ones_row(cols))
        plain = unit.padded(raw_queries, nothing)
        start = pair * cols
        grads = unit.padded(grad_t[:, pl.ds(start, cols)], nothing)
        log_total = jnp.concatenate([logs[2 * pair + q] for q in range(2)], axis=1)
        inner = jnp.concatenate([delta[2 * pair + q] for q in range(2)], axis=1)

        def step(part, made):
            key_at = part * TILE
            far = 2 * (pair - part)
            scores = dot(key_ref[pl.ds(key_at, TILE), :], queries)
            scores = scores + unit.strip(bias, far)
            probs = jnp.exp(scores - log_total)
            grad_probs = dot(value_r[pl.ds(key_at, TILE), :], grads)
            grad_scores = probs * (grad_probs - inner)
            for key_half in range(2):
                for q in range(2):
                    place = max(far + q - key_half, -1) + 1
                    strips[place, :, pl.ds(unit.shift, unit.part)] += grad_scores[
                        key_half * QB : (key_half + 1) * QB, q * unit.part : (q + 1) * unit.part
                    ]
            low = grad_scores.astype(BF)
            grad_v[pl.ds(key_at, TILE), :] += dot(probs.astype(BF), grads, 1, 1)
            grad_k[pl.ds(key_at, TILE), :] += dot(low, plain, 1, 1)
            return made + dot(key_t[pl.ds(unit.lo, HEAD_DIM), pl.ds(key_at, TILE)], low)

        made = jnp.zeros((HEAD_DIM, cols), F4)
        for part in range(pair + 1):
            made = step(part, made)
        for q in range(2):
            cut = made[:, q * unit.part : (q + 1) * unit.part]
            if shared:
                half = HEAD_DIM // 2
                cut = jnp.concatenate([cut[0:half], cut[half:]], axis=1)
            stacked[2 * pair + q, 2 * HEAD_DIM :, :] = cut.astype(BF)
        return carry

    for pair in range(n // 2):
        one_tile(pair, 0)
    for j in range(n):
        block = slice(QB * j, QB * (j + 1))
        stacked[j, 0:HEAD_DIM, :] = jnp.transpose(grad_k[block, :])[rows].astype(BF)
        stacked[j, HEAD_DIM : 2 * HEAD_DIM, :] = jnp.transpose(grad_v[block, :])[rows].astype(BF)
    row = iota((8, TILE), 0)
    empty = jnp.zeros((8, QB), F4)
    for far in range(n):
        total = jnp.zeros((8, TILE), F4)
        for group in range(QB // 8):
            rows8 = strips[far + 1, 8 * group : 8 * group + 8, :]
            wide = jnp.concatenate([empty, rows8], axis=1)
            total = total + (wide if group == 0 else pltpu.roll(wide, TILE - 8 * group, 1))
        lined = jnp.where(row == 0, total, 0.0)
        for c in range(1, 8):
            lined = lined + jnp.where(row == c, pltpu.roll(total, TILE - c, 1), 0.0)
        table[far] = jnp.sum(lined, axis=0, keepdims=True)


def dispatch_rows(n, cap, sc, route_ref, cot, wo_t, wq, wk, wv, out, target, w_out):
    tok = cot.shape[0]
    route = route_ref[...]
    chosen = iota((n, tok), 0) == route
    upto = jnp.where(iota((tok, tok), 0) <= iota((tok, tok), 1), 1.0, 0.0).astype(BF)
    filled = dot(jnp.where(chosen, 1.0, 0.0).astype(BF), upto)
    slot = jnp.sum(jnp.where(chosen, filled - 1.0, 0.0), axis=0, keepdims=True)
    slot = slot.astype(jnp.int32)
    place = route * cap + slot
    target[...] = jnp.broadcast_to(place, target.shape)
    spread = jnp.where(iota((n * cap, tok), 0) == place, 1.0, 0.0).astype(BF)
    packed = dot(spread, cot[...]).astype(BF)
    weights = jnp.concatenate([w[...].astype(F4) for w in (wq, wk, wv)], axis=0).astype(BF)
    for j in range(n):
        out[j, 0:cap, :] = packed[j * cap : (j + 1) * cap]
        out[j, cap:, :] = wo_t[...]
        w_out[j] = weights


def spread_matrix(target, rows):
    place = target[0:1, :]
    return jnp.where(iota((rows, place.shape[1]), 0) == place, 1.0, 0.0)


def hidden_rows(
    n, cap, sc, heads, p0, p1, p2, p3, tokens, misc_t, target, attn, hidden_out, out, wo_t, buf, wide
):
    place_rows(sc, n, p0.shape[1], (p0, p1, p2, p3), wide)
    wo_t[...] = wide[...].astype(BF)
    for pair in range(n // 2):
        at = 3 * pair * HEAD_DIM
        for turn in range(2):
            made = heads[2 * pair + turn].astype(F4)
            buf[at + turn * HEAD_DIM : at + (turn + 1) * HEAD_DIM, :] = made[:, 0:QB]
            both = slice(turn * LANES, (turn + 1) * LANES)
            buf[at + 2 * HEAD_DIM : at + 3 * HEAD_DIM, both] = made[:, QB:]
    rows = jnp.transpose(buf[...]).astype(BF)
    attn[...] = rows
    hidden = tokens[...].astype(F4) + dot(rows, wo_t[...], 1, 1)
    hidden_out[...] = hidden
    moe_in = (hidden * norm_scale(hidden) * misc_t[1:2, :]).astype(BF)
    packed = dot(spread_matrix(target, n * cap).astype(BF), moe_in).astype(BF)
    for j in range(n):
        out[j] = packed[j * cap : (j + 1) * cap]


def gelu_pair(values):
    scale = math.sqrt(2.0 / math.pi)
    square = values * values
    bend = jnp.tanh(scale * (values + 0.044715 * values * square))
    act = 0.5 * values * (1.0 + bend)
    slope = 0.5 * (1.0 + bend) + 0.5 * values * (1.0 - bend * bend) * scale * (
        1.0 + 3.0 * 0.044715 * square
    )
    return (act, slope)


def route_probs(experts, sc, rows, misc):
    logits = dot(rows, misc[...])
    lane = iota(logits.shape, 1)
    real = (lane >= 2) & (lane < 2 + experts)
    logits = jnp.where(real, logits, NEG)
    powers = jnp.where(real, jnp.exp(logits - jnp.max(logits, axis=-1, keepdims=True)), 0.0)
    probs = powers / jnp.sum(powers, axis=-1, keepdims=True)
    chosen = lane == sc[0] + 2
    gate = jnp.sum(jnp.where(chosen, probs, 0.0), axis=-1, keepdims=True)
    return (probs, chosen, gate)


def flat_rows(ref, cap=None):
    return jnp.concatenate([ref[j][0:cap] for j in range(ref.shape[0])], axis=0)


def expert_back(experts, sc, rows_ref, cot_ref, *refs):
    ins, outs, (misc, back, made, log_out) = refs[0:4], refs[4:8], refs[8:12]
    rows, cots = flat_rows(rows_ref), flat_rows(cot_ref, rows_ref.shape[1])
    probs, chosen, gate = route_probs(experts, sc, rows, misc)
    inner = jnp.zeros(gate.shape, F4)
    total = jnp.zeros(rows.shape, F4)
    result = jnp.zeros(rows.shape, F4)
    for w_in, w_out in zip(ins, outs):
        act, slope = gelu_pair(dot(rows, w_in[...]))
        low = act.astype(BF)
        result = result + dot(low, w_out[...])
        grad_act = dot(cots, w_out[...], 1, 1)
        inner = inner + jnp.sum(low.astype(F4) * grad_act, axis=-1, keepdims=True)
        total = total + dot((gate * grad_act * slope).astype(BF), w_in[...], 1, 1)
    grad_logits = (inner * probs * (jnp.where(chosen, 1.0, 0.0) - gate)).astype(BF)
    log_out[...] = grad_logits
    total = (total + dot(grad_logits, misc[...], 1, 1)).astype(BF)
    result = (gate * result).astype(BF)
    cap = made.shape[1]
    for j in range(made.shape[0]):
        back[j] = total[j * cap : (j + 1) * cap]
        made[j] = result[j * cap : (j + 1) * cap]


def expert_weights(experts, count, more, sc, *refs):
    rows_refs, cot_refs = refs[:count], refs[count : 2 * count]
    w_in, w_out, misc = refs[2 * count : 2 * count + 3]
    begun = refs[2 * count + 3 : 2 * count + 5] if more else None
    grad_in, grad_out, token, all_rows, all_grads, turned = refs[2 * count + (5 if more else 3) :]
    token[...] = jnp.zeros(token.shape, F4)
    size = rows_refs[0].shape[0] * rows_refs[0].shape[1]

    @pl.when(pl.program_id(0) == 0)
    def _():
        for i in range(count):
            at = slice(i * size, (i + 1) * size)
            rows, cots = flat_rows(rows_refs[i]), flat_rows(cot_refs[i], rows_refs[i].shape[1])
            gate = route_probs(experts, sc, rows, misc)[2]
            all_rows[at, :] = rows
            turned[:, at] = jnp.transpose(rows.astype(F4)).astype(BF)
            all_grads[at, :] = (gate * cots.astype(F4)).astype(BF)

    rows, grads = all_rows[...], all_grads[...]
    act, slope = gelu_pair(dot(rows, w_in[...]))
    grad_pre = (dot(grads, w_out[...], 1, 1) * slope).astype(BF)
    in_part = dot(turned[...], grad_pre)
    out_part = dot(act.astype(BF), grads, 0, 0)
    grad_in[...] = begun[0][...] + in_part if more else in_part
    grad_out[...] = begun[1][...] + out_part if more else out_part


def chunked_specs(w_in):
    depth, hidden = w_in.shape
    chunk = 2 * LANES
    columns = pl.BlockSpec((depth, chunk), lambda i: (0, i))
    lines = pl.BlockSpec((chunk, depth), lambda i: (i, 0))
    return hidden // chunk, columns, lines


def expert_weights_call(experts, lengths, rows_in, cots_in, w_in, w_out, misc, ties, begun=()):
    count, (depth, hidden) = len(rows_in), w_in.shape
    size = rows_in[0].shape[0] * rows_in[0].shape[1]
    body = functools.partial(expert_weights, experts, count, bool(begun))
    args = tuple(rows_in) + tuple(cots_in) + (w_in, w_out, misc) + tuple(begun)

    def kernel(length_ref, *refs):
        body(Place(length_ref), *refs[: len(args)], *refs[len(args) + len(ties) :])

    whole = pl.BlockSpec(memory_space=pltpu.VMEM)
    steps, columns, lines = chunked_specs(w_in)
    return pl.pallas_call(
        kernel,
        grid=(steps,),
        out_shape=(
            shaped((depth, hidden), F4),
            shaped((hidden, depth), F4),
            shaped((8, LANES), F4),
        ),
        in_specs=[pl.BlockSpec(memory_space=pltpu.SMEM)]
        + [whole] * (2 * count)
        + [columns, lines, whole]
        + ([columns, lines] if begun else [])
        + [whole] * len(ties),
        out_specs=(columns, lines, whole),
        scratch_shapes=[
            pltpu.VMEM((count * size, depth), BF),
            pltpu.VMEM((count * size, depth), BF),
            pltpu.VMEM((depth, count * size), BF),
        ],
        compiler_params=pltpu.CompilerParams(vmem_limit_bytes=60 * 1024 * 1024),
        cost_estimate=pl.CostEstimate(flops=1, bytes_accessed=1, transcendentals=0),
    )(lengths, *args, *ties)


def result_rows(n, cap, sc, made, target, hidden, out):
    rows = flat_rows(made)
    spread = jnp.transpose(spread_matrix(target, n * cap)).astype(BF)
    out[...] = (hidden[...] + dot(spread, rows)).astype(BF)


def norm_back(grads, source, gain):
    scale = norm_scale(source)
    weighted = grads * gain
    inner = jnp.mean(weighted * source, axis=-1, keepdims=True)
    return (scale * weighted - source * (scale * scale * scale) * inner, scale)


def hidden_grads(
    n, cap, sc, back, target, hidden_ref, misc_t, cot, wo_t, grad_out, low_out, gain_out, out, buf
):
    spread = jnp.transpose(spread_matrix(target, n * cap)).astype(BF)
    grads = dot(spread, flat_rows(back))
    hidden = hidden_ref[...]
    normed, scale = norm_back(grads, hidden, misc_t[1:2, :])
    gain_out[...] = jnp.broadcast_to(
        jnp.sum(grads * hidden * scale, axis=0, keepdims=True), gain_out.shape
    )
    total = cot[...].astype(F4) + normed
    grad_out[...] = total
    low = total.astype(BF)
    low_out[...] = low
    buf[...] = jnp.transpose(dot(low, wo_t[...])).astype(BF)
    for pair in range(n // 2):
        at = 3 * pair * HEAD_DIM
        for turn in range(2):
            out[2 * pair + turn, :, 0:QB] = buf[at + turn * HEAD_DIM : at + (turn + 1) * HEAD_DIM, :]
            both = slice(turn * LANES, (turn + 1) * LANES)
            out[2 * pair + turn, :, QB:] = buf[at + 2 * HEAD_DIM : at + 3 * HEAD_DIM, both]


def unfolded(piece):
    return jnp.concatenate([piece[:, 0:LANES], piece[:, LANES:]], axis=0)


def unpack_full(n, rows, sc, p0, p1, p2, p3, out, wide):
    inner = wide.shape[1] // 3
    for kk, part in enumerate((p0, p1, p2, p3)):
        for j in range(n):
            first = pl.multiple_of(((sc[1] ^ kk) * n + j) * rows, 8)
            block = part[j].astype(F4)
            for c in range(3):
                wide[pl.ds(first, rows), c * inner : (c + 1) * inner] = block[
                    c * rows : (c + 1) * rows
                ]
    out[...] = wide[...].astype(BF)


def token_grads(n, sc, stacked, weights, tokens, hidden_grad, misc_t, out, buf):
    own, both = split_units(stacked)
    inner = weights.shape[1] // 3
    for pair in range(n // 2):
        at = 3 * pair * HEAD_DIM
        last = at + 2 * HEAD_DIM
        for turn in range(2):
            j = 2 * pair + turn
            for c, piece in enumerate((2, 0, 1)):
                lo = c * inner + at + turn * HEAD_DIM
                buf[lo : lo + HEAD_DIM, :] = own[j, piece * HEAD_DIM : (piece + 1) * HEAD_DIM, :]
            half = slice(turn * LANES, (turn + 1) * LANES)
            buf[last : last + HEAD_DIM, half] = unfolded(both[j, 2 * HEAD_DIM :, :])
        for c in (1, 2):
            rows = slice((c - 1) * HEAD_DIM, c * HEAD_DIM)
            total = both[2 * pair, rows, :].astype(F4) + both[2 * pair + 1, rows, :].astype(F4)
            buf[c * inner + last : c * inner + last + HEAD_DIM, :] = total.astype(BF)
    made = jnp.transpose(dot(weights[...], buf[...]))
    normed, unused = norm_back(made, tokens[...].astype(F4), misc_t[0:1, :])
    out[...] = (hidden_grad[...] + normed).reshape(out.shape)


def unit_weight_grads(n, heads, sc, normed, stacked, lines_ref, buckets, *rest):
    own, both = split_units(stacked)
    outs, (buf, table) = rest[:heads], rest[heads:]
    width = buf.shape[1]
    sums = []
    for unit in range(2):
        made = jnp.zeros((NUM_BUCKETS, 1), F4)
        for far in range(n):
            lines = lines_ref.at[unit * n : (unit + 1) * n]
            line = lines[far][:, QB:]
            if far + 1 < n:
                line = line + lines[far + 1][:, :QB]
            inside = iota((NUM_BUCKETS, QB), 0) == buckets[:, far * QB : (far + 1) * QB]
            made = made + jnp.sum(jnp.where(inside, line, 0.0), axis=1, keepdims=True)
        sums.append(made)
    lane = iota((NUM_BUCKETS, width), 1)
    high = [value.astype(BF).astype(F4) for value in sums]
    listed = jnp.zeros((NUM_BUCKETS, width), F4)
    for at, value in enumerate(high + [sums[0] - high[0], sums[1] - high[1]]):
        listed = jnp.where(lane == at, value, listed)
    table[...] = listed
    total = None
    for j in range(n):
        shared = unfolded(both[j, 2 * HEAD_DIM :, :]).astype(F4)
        blank = jnp.zeros(shared.shape, F4)
        turn = jnp.broadcast_to((sc[0] & 1) == 0, shared.shape)
        shared = jnp.concatenate(
            [jnp.where(turn, shared, blank), jnp.where(turn, blank, shared)], axis=1
        )
        pieces = [own[j, 2 * HEAD_DIM :, :], shared.astype(BF)]
        for c in range(2):
            rows = slice(c * HEAD_DIM, (c + 1) * HEAD_DIM)
            pieces += [own[j, rows, :], both[j, rows, :]]
        part = dot(jnp.concatenate(pieces, axis=0), normed[j])
        total = part if total is None else total + part
    buf[...] = jnp.transpose(total)
    rows = buf.shape[0] // heads
    for kk in range(heads):
        to = sc[1] ^ kk
        outs[kk][...] = jnp.concatenate(
            [
                buf[pl.ds(pl.multiple_of(to * rows, 8), rows), :],
                table[pl.ds(pl.multiple_of(to * n, 8), n), :],
                jnp.zeros((8, width), F4),
            ],
            axis=0,
        ).astype(BF)


def two_parts(values, gap):
    high = values.astype(BF).astype(F4)
    lane = iota(values.shape, 1)
    low = pltpu.roll(jnp.where(lane < gap, values - high, 0.0), gap, 1)
    return jnp.where(lane < gap, high, low)


def one_part(values, gap):
    return values + pltpu.roll(values, values.shape[1] - gap, 1)


def weight_sums(n, rows, heads, sc, *refs):
    units, outer = refs[:heads], refs[heads : 2 * heads]
    outs, buf = refs[2 * heads : -1], refs[-1]
    total = (units[0][...].astype(F4) + units[1][...].astype(F4)) + (
        units[2][...].astype(F4) + units[3][...].astype(F4)
    )
    base = n * rows
    entries = two_parts(one_part(total[base : base + n], 2), 2)
    wide = (outer[0][...].astype(F4) + outer[1][...].astype(F4)) + (
        outer[2][...].astype(F4) + outer[3][...].astype(F4)
    )
    width = wide.shape[1] - LANES
    extra = two_parts(one_part(wide[:, width:], 16), 16)
    for to in range(n):
        at = slice(to * rows, (to + 1) * rows)
        entry = pltpu.roll(entries[to : to + 1, 0:LANES], 64, 1)
        entry = jnp.where(iota((rows, LANES), 0) == 0, entry, 0.0)
        buf[to] = jnp.concatenate([total[at], wide[at, 0:width], extra[at] + entry], axis=1)
    for k in range(n):
        outs[k][...] = buf[sc[0] ^ k].astype(BF)


def as_row(values):
    size = values.shape[0]
    square = jnp.where(iota((size, size), 0) == iota((size, size), 1), values, 0.0)
    return jnp.sum(square, axis=0, keepdims=True)


def weight_final(n, experts, sc, *refs):
    parts, (wq, wk, wv, gain_a) = refs[:n], refs[n : n + 4]
    grads = refs[n + 4 : n + 7]
    gain, table, grad_out, gain_out, router, buf, tables = refs[n + 7 :]
    rows = wq.shape[0]
    units = 3 * LANES
    small = slice(parts[0].shape[1] - LANES, parts[0].shape[1])
    total = None
    for j in range(n):
        part = parts[j][...].astype(F4)
        buf[sc[0] ^ j] = part[:, 0:units]
        tables[sc[0] ^ j] = part[0:1, small]
        total = part[:, units:] if total is None else total + part[:, units:]
    lane = iota((rows, LANES), 1)
    inner = jnp.zeros((rows, 1), F4)
    for c, weight in enumerate((wq, wk, wv)):
        lo = LANES * c

        def piece(head, place):
            pair, turn = head // 3, head % 3
            if turn < 2:
                tile, half = buf[2 * pair + turn, 0:rows, lo : lo + LANES], 0
            else:
                tile = (
                    buf[2 * pair, 0:rows, lo : lo + LANES]
                    + buf[2 * pair + 1, 0:rows, lo : lo + LANES]
                )
                half = 1
            return tile if half == place else pltpu.roll(tile, HEAD_DIM, 1)

        for m in range(weight.shape[1] // LANES):
            tile = jnp.where(lane < HEAD_DIM, piece(2 * m, 0), piece(2 * m + 1, 1))
            cols = slice(LANES * m, LANES * m + LANES)
            grads[c][:, cols] = tile
            inner = inner + jnp.sum(weight[:, cols].astype(F4) * tile, axis=-1, keepdims=True)
    gain[...] = as_row(inner / column(gain_a[...], rows))
    lane = iota((1, HEADS), 1)
    listed = jnp.zeros((1, HEADS), F4)
    for j in range(n):
        entry = one_part(pltpu.roll(tables[j], 64, 1), 2)
        listed = listed + jnp.where(lane == 3 * (j // 2) + j % 2, entry[:, 0:1], 0.0)
        listed = listed + jnp.where(lane == 3 * (j // 2) + 2, entry[:, 1:2], 0.0)
    table[...] = listed
    width = grad_out.shape[1]
    grad_out[...] = total[:, 0:width]
    extra = total[0:rows, width:]
    extra = one_part(jnp.where(iota(extra.shape, 1) < 32, extra, 0.0), 16)
    gain_out[...] = as_row(extra[:, 1:2])
    router[...] = jnp.transpose(pltpu.roll(extra, LANES - 2, 1))[0:experts]


def out_weight_grads(heads, sc, low, attn, rows, logs, gain, *rest):
    outs, buf = rest[:heads], rest[heads]
    width = attn.shape[1]
    buf[:, 0:width] = dot(low[...], attn[...], 0, 0)
    router = dot(flat_rows(rows), logs[...], 0, 0)
    wide = jnp.where(iota((LANES, gain.shape[1]), 0) == 1, gain[0:1, :], 0.0)
    buf[:, width : width + LANES] = two_parts(router + jnp.transpose(wide), 16)
    rows = buf.shape[0] // heads
    for kk in range(heads):
        first = pl.multiple_of((sc[1] ^ kk) * rows, 8)
        outs[kk][...] = buf[pl.ds(first, rows), :].astype(BF)


def last_grads(n, experts, sc, *refs):
    parts, own, rest = refs[: n + 4], refs[n + 4 : n + 9], refs[n + 9 :]
    weight_final(n, experts, sc, *parts, *rest[:8], *rest[9:11])
    token_grads(n, sc, *own, rest[8], rest[11])


def swap(values, axis, flip):
    if flip == 0:
        return values
    size = lax.axis_size(axis)
    return lax.ppermute(values, axis, [(i, i ^ flip) for i in range(size)])


def exchange(messages, axis):
    return [swap(message, axis, k) for k, message in enumerate(messages)]


def hold(values, *earlier):
    return lax.optimization_barrier((values, earlier))[0]


def over_heads(stack):
    across = swap(stack, HEAD, 2)
    return (stack, swap(stack, HEAD, 1), across, swap(across, HEAD, 1))


def on_plane(
    tokens,
    attn_gain,
    w_query,
    w_key,
    w_value,
    w_out,
    bias_table,
    moe_gain,
    w_router,
    expert_in,
    expert_out,
    seq_lengths,
    rel_buckets,
    routes,
    cotangent,
):
    heads = lax.axis_size(HEAD)
    n = lax.axis_size(BLK)
    tok, width = tokens.shape[0], tokens.shape[2]
    rows = w_query.shape[0]
    total_rows = n * tok
    experts = w_router.shape[1]
    cap = 3 * tok // (2 * experts)
    slots = n * cap
    scope = jax.named_scope
    x = tokens.reshape(tok, width)
    cot = cotangent.reshape(tok, width)
    gain_a = attn_gain.reshape(1, rows)
    gain_m = moe_gain.reshape(1, rows)
    in_own, out_own = expert_in.reshape(expert_in.shape[1:]), expert_out.reshape(expert_out.shape[1:])

    def call(body, args, outs, scratch=(), ties=(), loose=(), away=()):
        return vmem_call(body, seq_lengths, args, outs, scratch, ties, loose, away)

    def all_to_all(stack, axis=BLK):
        return lax.all_to_all(stack, axis, split_axis=0, concat_axis=0, tiled=True)

    order = [ring_of(i, n) for i in range(n)]
    ahead = [(order[i], order[(i + 1) % n]) for i in range(n)]
    astern = [(b, a) for a, b in ahead]
    unit_cols = 4 * LANES

    def hop(front, back):
        with scope("rin"):
            front = lax.ppermute(front, BLK, ahead)
            back = lax.ppermute(back, BLK, astern)
            return lax.optimization_barrier((front, back))

    first = hop(x, x)
    with scope("uw"):
        packed, packed_token = call(
            functools.partial(pack_units, n),
            (w_query, w_key, w_value)
            + (gain_a, gain_m, jnp.transpose(w_router), bias_table.reshape(1, -1)),
            [shaped((n, rows, unit_cols), BF)],
        )
        unit_in = all_to_all(hold(packed, first[0]))
    with scope("cr"):
        cot_out, target, w_stack, cot_token = call(
            functools.partial(dispatch_rows, n, cap),
            (routes.reshape(1, tok), cot, jnp.transpose(w_out), w_query, w_key, w_value),
            [
                shaped((n, cap + rows, width), BF),
                shaped((8, tok), jnp.int32),
                shaped((n, 3 * rows, width), BF),
            ],
            ties=(packed_token,),
        )
    with scope("es"):
        in_other = swap(in_own, HEAD, 2)
    second = hop(*hold(first, packed_token))
    with scope("uw"):
        unit_parts = over_heads(hold(unit_in, second[0]))
    third = hop(*hold(second, unit_in, cot_token))
    half = tok // 2
    with scope("rin"):
        front_half, back_half = hold((third[0][:half], third[1][half:]), in_other)
        front, back = lax.ppermute(front_half, BLK, ahead), lax.ppermute(back_half, BLK, astern)
    with scope("uw"):
        unit_w, misc, misc_t, table, unused = call(
            functools.partial(unpack_units, n, rows),
            unit_parts,
            [
                shaped((width, 3 * LANES), BF),
                shaped((width, LANES), BF),
                shaped((LANES, width), F4),
                shaped((NUM_BUCKETS, LANES), F4),
            ],
            [pltpu.VMEM((width, unit_cols), F4)],
        )
    with scope("es"):
        out_other = swap(hold(out_own, unit_parts[2], unit_parts[3]), HEAD, 2)

    buckets = rel_buckets.reshape(1, -1)

    with scope("cr"):
        cot_in = all_to_all(hold(cot_out, front, back, table))
        cot_rows, wo_rows = cot_in[:, :cap], cot_in[:, cap:]

    kept = [
        shaped((n, tok, width), BF),
        shaped((total_rows, LANES), BF),
        shaped((total_rows, LANES), BF),
        shaped((LANES, total_rows), BF),
        shaped((LANES, total_rows), BF),
        shaped((total_rows, LANES), BF),
        shaped((2, n + 1, QB, QB), F4),
    ]
    with scope("att"):
        (
            head_out,
            logs_own,
            logs_both,
            normed,
            key_own,
            key_both,
            query_t,
            key_t,
            value_r,
            strips,
            attend_token,
        ) = call(
            functools.partial(attend_units, n),
            (x,) + first + second + third + (front, back, misc_t, unit_w, table, buckets),
            [
                shaped((n, HEAD_DIM, QB + LANES), BF),
                shaped((n, 1, QB), F4),
                shaped((n, 1, LANES), F4),
            ]
            + kept,
            [pltpu.VMEM(k.shape, k.dtype) for k in kept]
            + [
                pltpu.VMEM((LANES, total_rows), BF),
                pltpu.VMEM((1, QB + total_rows), F4),
                pltpu.SemaphoreType.DMA((len(kept),)),
            ],
            ties=(cot_token,),
            away=range(3, 3 + len(kept)),
        )
        head_in = all_to_all(head_out)
    with scope("ow"):
        wo_parts = over_heads(hold(wo_rows, logs_both))
    with scope("cp"):
        all_cot = over_heads(hold(cot_rows, wo_parts[2]))
        cot_pair = all_cot[1]
    with scope("hid"):
        attn, hidden, moe_out, out_t, hidden_token = call(
            functools.partial(hidden_rows, n, cap),
            (head_in,) + wo_parts + (x, misc_t, target),
            [
                shaped((tok, width), BF),
                shaped((tok, width), F4),
                shaped((n, cap, width), BF),
                shaped((width, width), BF),
            ],
            [pltpu.VMEM((width, tok), F4), pltpu.VMEM((width, width), F4)],
            ties=(hold(attend_token, out_other),),

        )

    with scope("mr"):
        moe_rows = all_to_all(moe_out)
        moe_pair = swap(hold(moe_rows, all_cot[2], cot_pair), HEAD, 1)
    with scope("ec"):
        ins = (in_own, in_other, swap(in_own, HEAD, 1), swap(in_other, HEAD, 1))
        outs = (out_own, out_other, swap(out_own, HEAD, 1), swap(out_other, HEAD, 1))
    def backward_rows(rows_in, cots_in, kind, ties=()):
        return call(
            functools.partial(expert_back, experts),
            (rows_in, cots_in, in_own, out_own, in_other, out_other, misc),
            [
                shaped((slots, width), kind),
                shaped((slots, width), BF),
                shaped((slots, LANES), BF),
            ],
            ties=ties,
        )

    with scope("fw"):
        w_in = all_to_all(hold(w_stack, moe_rows, ins[2:], outs[2:], all_cot[2]))
    with scope("mf"):
        moe_far = swap(moe_rows, HEAD, 2)
        far_pair = swap(moe_far, HEAD, 1)

    with scope("eb"):
        back_out, res_out, logs, back_token = call(
            functools.partial(expert_back, experts),
            (moe_rows, cot_rows) + ins + outs + (misc,),
            [
                shaped((n, cap, width), BF),
                shaped((n, cap, width), BF),
                shaped((slots, LANES), BF),
            ],
        )
        back_in = all_to_all(hold(back_out, w_in))
    with scope("fw"):
        w_parts = over_heads(hold(w_in, back_token))
    with scope("ewg"):
        expert_ends = (in_own, out_own, misc)
        *begun, expert_token = expert_weights_call(
            experts,
            seq_lengths,
            (moe_rows, moe_pair),
            all_cot[:2],
            *expert_ends,
            (back_token,),
        )
    with scope("hg"):
        grad_hidden, grad_low, gain_moe_part, grad_heads_out, unused = call(
            functools.partial(hidden_grads, n, cap),
            (back_in, target, hidden, misc_t, cot, out_t),
            [
                shaped((tok, width), F4),
                shaped((tok, width), BF),
                shaped((8, width), F4),
                shaped((n, HEAD_DIM, QB + LANES), BF),
            ],
            [pltpu.VMEM((width, tok), BF)],
            ties=(hold(expert_token, far_pair, all_cot[3]),),
        )
        grad_heads = all_to_all(grad_heads_out)
    wide = width + LANES
    with scope("owg"):
        *out_parts, out_token = call(
            functools.partial(out_weight_grads, heads),
            (grad_low, attn, moe_rows, logs, gain_moe_part),
            [shaped((width // heads, wide), BF)] * heads,
            [pltpu.VMEM((width, wide), F4)],
        )
        out_parts_in = exchange(out_parts, HEAD)
    with scope("rr"):
        res_in = all_to_all(hold(res_out, grad_heads, out_token))

    with scope("ag"):
        stacked, lines, unused = call(
            functools.partial(unit_grads, n),
            (
                key_own,
                key_both,
                query_t,
                key_t,
                value_r,
                strips,
                head_out,
                grad_heads,
                logs_own,
                logs_both,
            ),
            [shaped((n, 5 * HEAD_DIM + HEAD_DIM // 2, tok), BF), shaped((2 * n, 1, TILE), F4)],
            [
                pltpu.VMEM((HEAD_DIM, total_rows), BF),
                pltpu.VMEM((HEAD_DIM, total_rows // 2), BF),
                pltpu.VMEM((n, 1, QB), F4),
                pltpu.VMEM((n, 1, LANES), F4),
                pltpu.VMEM((total_rows, LANES), F4),
                pltpu.VMEM((total_rows, LANES), F4),
                pltpu.VMEM((n + 1, QB, QB), F4),
                pltpu.VMEM((2, n + 1, QB, QB), F4),
                pltpu.SemaphoreType.DMA((2,)),
            ],
            loose=(5,),
            ties=(hold(out_token, w_parts),),
        )
        unit_in = all_to_all(hold(stacked, res_in, out_parts_in))

    with scope("wg"):
        *unit_grad_parts, parts_token = call(
            functools.partial(unit_weight_grads, n, heads),
            (normed, stacked, lines, buckets),
            [shaped((width // heads + n + 8, 3 * LANES), BF)] * heads,
            [pltpu.VMEM((width, 3 * LANES), F4), pltpu.VMEM((NUM_BUCKETS, 3 * LANES), F4)],
        )
        unit_parts_in = exchange(unit_grad_parts, HEAD)
    with scope("res"):
        result, result_token = call(
            functools.partial(result_rows, n, cap),
            (res_in, target, hidden),
            [shaped((tok, width), BF)],
            ties=(parts_token,),
        )
    with scope("fw"):
        full_w, full_token = call(
            functools.partial(unpack_full, n, rows),
            w_parts,
            [shaped((width, 3 * width), BF)],
            [pltpu.VMEM((width, 3 * width), F4)],
            ties=(parts_token,),
        )
    with scope("wg"):
        *sums, sums_token = call(
            functools.partial(weight_sums, n, rows, heads),
            unit_parts_in + out_parts_in,
            [shaped((rows, 3 * LANES + wide), BF)] * n,
            [pltpu.VMEM((n, rows, 3 * LANES + wide), F4)],
            ties=(full_token, result_token),
        )
        sums_in = exchange(sums, BLK)
    with scope("ewg"):
        grad_in, grad_out, expert_token = expert_weights_call(
            experts,
            seq_lengths,
            (moe_far, far_pair),
            all_cot[2:],
            *expert_ends,
            (sums_token,),
            begun,
        )
    with scope("fin"):
        (
            grad_q,
            grad_k,
            grad_v,
            grad_gain_attn,
            grad_table,
            grad_out_w,
            grad_gain_moe,
            grad_router,
            grad_tokens,
            unused,
        ) = call(
            functools.partial(last_grads, n, experts),
            sums_in
            + [w_query, w_key, w_value, gain_a]
            + [unit_in, full_w, x, grad_hidden, misc_t],
            [shaped((rows, width), F4)] * 3
            + [
                shaped((1, rows), F4),
                shaped((1, HEADS), F4),
                shaped((rows, width), F4),
                shaped((1, rows), F4),
                shaped((experts, rows), F4),
                shaped(tokens.shape, F4),
            ],
            [
                pltpu.VMEM((n, rows, 3 * LANES), F4),
                pltpu.VMEM((n, 1, LANES), F4),
                pltpu.VMEM((3 * width, tok), BF),
            ],
            ties=(expert_token,),
        )
    return (
        result.reshape(tokens.shape),
        grad_tokens,
        grad_gain_attn.reshape(-1),
        grad_q,
        grad_k,
        grad_v,
        jnp.transpose(grad_out_w),
        grad_table.reshape(-1),
        grad_gain_moe.reshape(-1),
        jnp.transpose(grad_router),
        grad_in.reshape(expert_in.shape),
        grad_out.reshape(expert_out.shape),
    )


def ring_of(place, ring_len):
    return 2 * place if place < ring_len // 2 else 2 * ring_len - 1 - 2 * place


def solution(mesh):
    in_specs = (
        P(BLK, HEAD, None),
        P((HEAD, BLK)),
        P((HEAD, BLK), None),
        P((HEAD, BLK), None),
        P((HEAD, BLK), None),
        P(None, (HEAD, BLK)),
        P((HEAD, BLK)),
        P((HEAD, BLK)),
        P((HEAD, BLK), None),
        P(BLK, None, HEAD),
        P(BLK, HEAD, None),
        P(),
        P(),
        P(HEAD, BLK, None, None),
        P(BLK, HEAD, None),
    )
    out_specs = (
        P(BLK, HEAD, None),
        P(BLK, HEAD, None),
        P((HEAD, BLK)),
        P((HEAD, BLK), None),
        P((HEAD, BLK), None),
        P((HEAD, BLK), None),
        P(None, (HEAD, BLK)),
        P((HEAD, BLK)),
        P((HEAD, BLK)),
        P((HEAD, BLK), None),
        P(BLK, None, HEAD),
        P(BLK, HEAD, None),
    )
    one_each = mesh.shape[HEAD] == 4 and mesh.shape[BLK] == 8
    return jax.shard_map(
        on_plane if one_each else on_device, mesh=mesh, in_specs=in_specs, out_specs=out_specs, check_vma=False
    )
```

```python
import functools
import math

import jax
import jax.numpy as jnp
from jax import lax
from jax.experimental import pallas as pl
from jax.experimental.pallas import tpu as pltpu
from jax.sharding import PartitionSpec as P

HEADS = 12
HEAD_DIM = 64
NUM_BUCKETS = 32
HEAD, BLK = "head", "blk"


norm_eps = 1e-06
masked_score = -1e30


def inverse_rms(values):
    return lax.rsqrt(jnp.mean(values * values, axis=-1, keepdims=True) + norm_eps)


def norm_backward(grad_normed, source, inv_scale, gain):
    weighted = grad_normed * gain
    inner_mean = jnp.mean(weighted * source, axis=-1, keepdims=True)
    grad_source = inv_scale * weighted - source * (inv_scale * inv_scale * inv_scale) * inner_mean
    grad_gain = jnp.sum(grad_normed * source * inv_scale, axis=0)
    return (grad_source, grad_gain)


def same_state(running):
    return running


def bucket_bounds(rel_buckets):
    bucket_count = NUM_BUCKETS
    labels = jnp.arange(bucket_count, dtype=jnp.int32)
    starts = jnp.sum((rel_buckets[:, None] < labels[None, :]).astype(jnp.int32), axis=0)
    ends = jnp.concatenate([starts[1:], jnp.full((1,), rel_buckets.shape[0] + 1, jnp.int32)])
    return (starts, ends)


def bias_terms(query_positions, key_positions, bounds, table32):
    starts, ends = bounds
    distance = jnp.maximum(query_positions[:, None] - key_positions[None, :], 0)[:, :, None]
    inside = (distance >= starts[None, None, :]) & (distance < ends[None, None, :])
    onehot = inside.astype(jnp.bfloat16)
    bias = jnp.einsum(
        "qkb,bh->hqk", onehot, table32.astype(jnp.bfloat16), preferred_element_type=jnp.float32
    )
    return (onehot, bias)


def block_scores(queries, keys, query_positions, key_positions, seq_lengths, bounds, table32):
    onehot, bias = bias_terms(query_positions, key_positions, bounds, table32)
    raw = jnp.einsum("qshd,kshd->hsqk", queries, keys, preferred_element_type=jnp.float32)
    causal = key_positions[None, :] <= query_positions[:, None]
    present = key_positions[None, :] < seq_lengths[:, None]
    valid = causal[None, :, :] & present[:, None, :]
    return (raw + bias[:, None, :, :], valid[None], onehot)


def attend_step(
    running, queries, keys, values, query_positions, key_positions, seq_lengths, bounds, table32
):
    row_top, row_total, weighted = running
    scores, valid, unused = block_scores(
        queries, keys, query_positions, key_positions, seq_lengths, bounds, table32
    )
    scores = jnp.where(valid, scores, masked_score)
    new_top = jnp.maximum(row_top, jnp.max(scores, axis=-1))
    weights = jnp.where(valid, jnp.exp(scores - new_top[..., None]), 0.0)
    decay = jnp.exp(row_top - new_top)
    row_total = row_total * decay + jnp.sum(weights, axis=-1)
    mixed = jnp.einsum(
        "hsqk,kshd->qshd", weights.astype(jnp.bfloat16), values, preferred_element_type=jnp.float32
    )
    weighted = weighted * jnp.transpose(decay, (2, 1, 0))[..., None] + mixed
    return (new_top, row_total, weighted)


def grad_step(
    queries,
    grad_heads,
    log_total,
    delta,
    query_positions,
    keys,
    values,
    key_positions,
    seq_lengths,
    bounds,
    table32,
):
    scores, valid, onehot = block_scores(
        queries, keys, query_positions, key_positions, seq_lengths, bounds, table32
    )
    probs = jnp.where(valid, jnp.exp(scores - jnp.transpose(log_total, (2, 1, 0))[..., None]), 0.0)
    grad_probs = jnp.einsum(
        "qshd,kshd->hsqk", grad_heads, values, preferred_element_type=jnp.float32
    )
    grad_scores = probs * (grad_probs - jnp.transpose(delta, (2, 1, 0))[..., None])
    grad_table = jnp.einsum(
        "hqk,qkb->bh",
        jnp.sum(grad_scores, axis=1),
        onehot.astype(jnp.float32),
        precision=lax.Precision.HIGHEST,
    )
    low_scores = grad_scores.astype(jnp.bfloat16)
    grad_queries = jnp.einsum(
        "hsqk,kshd->qshd", low_scores, keys, preferred_element_type=jnp.float32
    )
    grad_keys = jnp.einsum(
        "hsqk,qshd->kshd", low_scores, queries, preferred_element_type=jnp.float32
    )
    grad_values = jnp.einsum(
        "hsqk,qshd->kshd",
        probs.astype(jnp.bfloat16),
        grad_heads,
        preferred_element_type=jnp.float32,
    )
    return (grad_queries, grad_keys, grad_values, grad_table)


def on_device(
    tokens,
    attn_gain,
    w_query,
    w_key,
    w_value,
    w_out,
    bias_table,
    moe_gain,
    w_router,
    expert_in,
    expert_out,
    seq_lengths,
    rel_buckets,
    routes,
    cotangent,
):
    head_count = lax.axis_size(HEAD)
    blk_count = lax.axis_size(BLK)
    head_index = lax.axis_index(HEAD)
    blk_index = lax.axis_index(BLK)
    block_rows, group_seqs, width = tokens.shape
    seq_count = group_seqs * head_count
    tok_rows = block_rows * group_seqs
    local_heads = HEADS // head_count
    head_width = local_heads * HEAD_DIM
    group_rows = block_rows * max(1, blk_count // 8)
    longest = jnp.max(seq_lengths)
    query_first = blk_index * block_rows
    query_last = query_first + block_rows - 1
    query_positions = query_first + jnp.arange(block_rows, dtype=jnp.int32)
    bounds = bucket_bounds(rel_buckets)
    fetched = (
        lax.all_gather(w_query, (HEAD, BLK), axis=0, tiled=True),
        lax.all_gather(w_key, (HEAD, BLK), axis=0, tiled=True),
        lax.all_gather(w_value, (HEAD, BLK), axis=0, tiled=True),
        lax.all_gather(w_out, (HEAD, BLK), axis=1, tiled=True),
        lax.all_gather(attn_gain, (HEAD, BLK), axis=0, tiled=True),
        lax.all_gather(bias_table, (HEAD, BLK), axis=0, tiled=True),
        lax.all_gather(moe_gain, (HEAD, BLK), axis=0, tiled=True),
        lax.all_gather(w_router, (HEAD, BLK), axis=0, tiled=True),
    )
    full_query, full_key, full_value, full_out, gain_attn, table_flat, gain_moe, full_router = (
        fetched
    )
    inner_width = full_query.shape[1]
    table_all = table_flat.astype(jnp.float32).reshape(NUM_BUCKETS, HEADS)
    table32 = lax.dynamic_slice_in_dim(table_all, head_index * local_heads, local_heads, 1)
    gain_attn32 = gain_attn.astype(jnp.float32)
    gain_moe32 = gain_moe.astype(jnp.float32)

    def to_heads(values):
        parts = values.shape[1]
        shaped = values.reshape(block_rows, group_seqs, parts, head_count, head_width)
        moved = lax.all_to_all(shaped, HEAD, split_axis=3, concat_axis=1, tiled=True)
        return moved.reshape(block_rows, seq_count, parts, local_heads, HEAD_DIM)

    def to_tokens(values):
        parts = values.shape[2]
        shaped = values.reshape(block_rows, seq_count, parts, 1, head_width)
        moved = lax.all_to_all(shaped, HEAD, split_axis=1, concat_axis=3, tiled=True)
        return moved.reshape(tok_rows, parts, inner_width)

    source = tokens.astype(jnp.float32).reshape(tok_rows, width)
    inv_attn = inverse_rms(source)
    attn_in = (source * inv_attn * gain_attn32).astype(jnp.bfloat16)
    stacked_weights = jnp.stack((full_query, full_key, full_value))
    projected = jnp.einsum(
        "td,cde->tce", attn_in, stacked_weights, preferred_element_type=jnp.float32
    ).astype(jnp.bfloat16)
    heads_in = to_heads(projected)
    queries = heads_in[:, :, 0]
    keys = heads_in[:, :, 1]
    values = heads_in[:, :, 2]
    start_state = (
        jnp.full((local_heads, seq_count, block_rows), masked_score, jnp.float32),
        jnp.zeros((local_heads, seq_count, block_rows), jnp.float32),
        jnp.zeros((block_rows, seq_count, local_heads, HEAD_DIM), jnp.float32),
    )
    key_piece = lax.all_gather(keys, BLK, axis=0, tiled=True)
    value_piece = lax.all_gather(values, BLK, axis=0, tiled=True)
    piece_rows = key_piece.shape[0]
    part_rows = math.gcd(piece_rows, group_rows)

    def forward_one_part(step_index, inner_state):
        offset = step_index * part_rows
        key_part = lax.dynamic_slice_in_dim(key_piece, offset, part_rows, 0)
        value_part = lax.dynamic_slice_in_dim(value_piece, offset, part_rows, 0)
        key_positions = offset + jnp.arange(part_rows, dtype=jnp.int32)

        def attend_now(current):
            return attend_step(
                current,
                queries,
                key_part,
                value_part,
                query_positions,
                key_positions,
                seq_lengths,
                bounds,
                table32,
            )

        skipped = (offset > query_last) | (offset >= longest)
        return lax.cond(skipped, same_state, attend_now, inner_state)

    row_top, row_total, weighted = lax.fori_loop(
        0, piece_rows // part_rows, forward_one_part, start_state
    )
    attn_heads = (weighted / jnp.transpose(row_total, (2, 1, 0))[..., None]).astype(jnp.bfloat16)
    log_total = jnp.transpose(row_top + jnp.log(row_total), (2, 1, 0))
    attn_tok = to_tokens(attn_heads[:, :, None])[:, 0]
    branch = jnp.dot(attn_tok, full_out, preferred_element_type=jnp.float32)
    hidden = source + branch
    expert_count = full_router.shape[1]
    local_experts = expert_in.shape[0]
    capacity = max(2, 3 * tok_rows // (2 * expert_count))
    inv_moe = inverse_rms(hidden)
    moe_in = (hidden * inv_moe * gain_moe32).astype(jnp.bfloat16)
    logits = jnp.dot(moe_in, full_router, preferred_element_type=jnp.float32)
    router_probs = jax.nn.softmax(logits, axis=-1)
    route_flat = routes.reshape(tok_rows)
    chosen = route_flat[:, None] == jnp.arange(expert_count, dtype=jnp.int32)[None, :]
    gate = jnp.sum(jnp.where(chosen, router_probs, 0.0), axis=-1)
    filled = jnp.cumsum(chosen.astype(jnp.int32), axis=0)
    slot = jnp.sum(jnp.where(chosen, filled - 1, 0), axis=-1)
    target = route_flat * capacity + slot
    dispatch = (
        target[:, None] == jnp.arange(expert_count * capacity, dtype=jnp.int32)[None, :]
    ).astype(jnp.bfloat16)

    def to_buffer(token_rows):
        packed = jnp.einsum(
            "tj,td->jd", dispatch, token_rows, preferred_element_type=jnp.float32
        ).astype(jnp.bfloat16)
        return packed.reshape(blk_count, local_experts, capacity, width)

    def from_buffer(buffer):
        return jnp.dot(
            dispatch,
            buffer.reshape(expert_count * capacity, width),
            preferred_element_type=jnp.float32,
        )

    def to_experts(buffer):
        return lax.all_to_all(buffer, BLK, split_axis=0, concat_axis=0, tiled=True)

    def all_rows(buffer):
        return lax.all_gather(buffer, HEAD, axis=0, tiled=True)

    def summed_rows(partial_terms):
        return lax.psum_scatter(
            partial_terms.astype(jnp.bfloat16), HEAD, scatter_dimension=0, tiled=True
        ).astype(jnp.float32)

    def to_owners(buffer):
        return lax.all_to_all(buffer, BLK, split_axis=0, concat_axis=0, tiled=True)

    expert_rows_in = all_rows(to_experts(to_buffer(moe_in)))
    expert_pre = jnp.einsum(
        "necd,edf->necf", expert_rows_in, expert_in, preferred_element_type=jnp.float32
    )
    expert_act, gelu_pull = jax.vjp(jax.nn.gelu, expert_pre)
    expert_low = expert_act.astype(jnp.bfloat16)
    expert_terms = jnp.einsum(
        "necf,efd->necd", expert_low, expert_out, preferred_element_type=jnp.float32
    )
    expert_tok = from_buffer(to_owners(summed_rows(expert_terms).astype(jnp.bfloat16)))
    result = hidden + gate[:, None] * expert_tok
    grad_result = cotangent.astype(jnp.float32).reshape(tok_rows, width)
    grad_expert_tok = (gate[:, None] * grad_result).astype(jnp.bfloat16)
    grad_gate = jnp.sum(grad_result * expert_tok, axis=-1)
    grad_logits = (
        router_probs * (jnp.where(chosen, grad_gate[:, None], 0.0) - (gate * grad_gate)[:, None])
    ).astype(jnp.bfloat16)
    grad_router = jnp.einsum("td,te->de", moe_in, grad_logits, preferred_element_type=jnp.float32)
    grad_rows = all_rows(to_experts(to_buffer(grad_expert_tok)))
    grad_act = jnp.einsum(
        "necd,efd->necf", grad_rows, expert_out, preferred_element_type=jnp.float32
    )
    grad_pre = gelu_pull(grad_act)[0].astype(jnp.bfloat16)
    grad_expert_out = jnp.einsum(
        "necf,necd->efd", expert_low, grad_rows, preferred_element_type=jnp.float32
    )
    grad_expert_in = jnp.einsum(
        "necd,necf->edf", expert_rows_in, grad_pre, preferred_element_type=jnp.float32
    )
    grad_back = jnp.einsum(
        "necf,edf->necd", grad_pre, expert_in, preferred_element_type=jnp.float32
    )
    grad_moe_in = from_buffer(to_owners(summed_rows(grad_back).astype(jnp.bfloat16)))
    grad_moe_in = grad_moe_in + jnp.einsum(
        "te,de->td", grad_logits, full_router, preferred_element_type=jnp.float32
    )
    grad_norm_moe, grad_gain_moe = norm_backward(grad_moe_in, hidden, inv_moe, gain_moe32)
    grad_hidden = grad_result + grad_norm_moe
    grad_branch = grad_hidden.astype(jnp.bfloat16)
    grad_out_w = jnp.einsum("te,td->ed", attn_tok, grad_branch, preferred_element_type=jnp.float32)
    grad_attn_tok = jnp.einsum(
        "td,ed->te", grad_branch, full_out, preferred_element_type=jnp.float32
    ).astype(jnp.bfloat16)
    grad_heads = to_heads(grad_attn_tok[:, None])[:, :, 0]
    delta = jnp.sum(grad_heads.astype(jnp.float32) * attn_heads.astype(jnp.float32), axis=-1)
    all_keys = lax.all_gather(keys, BLK, axis=0, tiled=True)
    all_values = lax.all_gather(values, BLK, axis=0, tiled=True)
    total_rows = all_keys.shape[0]
    step_rows = math.gcd(total_rows, group_rows)
    zero_heads = jnp.zeros((block_rows, seq_count, local_heads, HEAD_DIM), jnp.float32)
    zero_table = jnp.zeros(table32.shape, jnp.float32)

    def query_side(step_index, running):
        offset = step_index * step_rows
        key_block = lax.dynamic_slice_in_dim(all_keys, offset, step_rows, 0)
        value_block = lax.dynamic_slice_in_dim(all_values, offset, step_rows, 0)
        key_positions = offset + jnp.arange(step_rows, dtype=jnp.int32)

        def query_compute(current):
            grads = grad_step(
                queries,
                grad_heads,
                log_total,
                delta,
                query_positions,
                key_block,
                value_block,
                key_positions,
                seq_lengths,
                bounds,
                table32,
            )
            return (current[0] + grads[0], current[1] + grads[3])

        skipped = (offset > query_last) | (offset >= longest)
        return lax.cond(skipped, same_state, query_compute, running)

    grad_queries, grad_table = lax.fori_loop(
        0, total_rows // step_rows, query_side, (zero_heads, zero_table)
    )
    all_totals, all_deltas = (
        lax.all_gather(log_total, BLK, axis=0, tiled=True),
        lax.all_gather(delta, BLK, axis=0, tiled=True),
    )
    query_piece = lax.all_gather(queries, BLK, axis=0, tiled=True)
    grad_piece = lax.all_gather(grad_heads, BLK, axis=0, tiled=True)
    piece_rows = query_piece.shape[0]
    key_part_rows = math.gcd(piece_rows, group_rows)

    def key_one_part(step_index, inner_state):
        offset = step_index * key_part_rows
        query_part = lax.dynamic_slice_in_dim(query_piece, offset, key_part_rows, 0)
        grad_part = lax.dynamic_slice_in_dim(grad_piece, offset, key_part_rows, 0)
        total_part = lax.dynamic_slice_in_dim(all_totals, offset, key_part_rows, 0)
        delta_part = lax.dynamic_slice_in_dim(all_deltas, offset, key_part_rows, 0)
        part_positions = offset + jnp.arange(key_part_rows, dtype=jnp.int32)

        def key_compute(current):
            grads = grad_step(
                query_part,
                grad_part,
                total_part,
                delta_part,
                part_positions,
                keys,
                values,
                query_positions,
                seq_lengths,
                bounds,
                table32,
            )
            return (current[0] + grads[1], current[1] + grads[2])

        skipped = (offset + key_part_rows - 1 < query_first) | (query_first >= longest)
        return lax.cond(skipped, same_state, key_compute, inner_state)

    grad_keys, grad_values = lax.fori_loop(
        0, piece_rows // key_part_rows, key_one_part, (zero_heads, zero_heads)
    )
    grad_stack = jnp.stack((grad_queries, grad_keys, grad_values), axis=2).astype(jnp.bfloat16)
    grad_projected = to_tokens(grad_stack)
    grad_weights = jnp.einsum(
        "td,tce->cde", attn_in, grad_projected, preferred_element_type=jnp.float32
    )
    grad_attn_in = jnp.einsum(
        "tce,cde->td", grad_projected, stacked_weights, preferred_element_type=jnp.float32
    )
    grad_norm_attn, grad_gain_attn = norm_backward(grad_attn_in, source, inv_attn, gain_attn32)
    grad_tokens = grad_hidden + grad_norm_attn
    table_terms = lax.dynamic_update_slice_in_dim(
        jnp.zeros((NUM_BUCKETS, HEADS), jnp.float32), grad_table, head_index * local_heads, 1
    ).reshape(NUM_BUCKETS * HEADS)
    reduced = (
        lax.psum_scatter(grad_weights[0], (HEAD, BLK), scatter_dimension=0, tiled=True),
        lax.psum_scatter(grad_weights[1], (HEAD, BLK), scatter_dimension=0, tiled=True),
        lax.psum_scatter(grad_weights[2], (HEAD, BLK), scatter_dimension=0, tiled=True),
        lax.psum_scatter(grad_out_w, (HEAD, BLK), scatter_dimension=1, tiled=True),
        lax.psum_scatter(grad_gain_attn, (HEAD, BLK), scatter_dimension=0, tiled=True),
        lax.psum_scatter(table_terms, (HEAD, BLK), scatter_dimension=0, tiled=True),
        lax.psum_scatter(grad_gain_moe, (HEAD, BLK), scatter_dimension=0, tiled=True),
        lax.psum_scatter(grad_router, (HEAD, BLK), scatter_dimension=0, tiled=True),
    )
    return (
        result.astype(jnp.bfloat16).reshape(tokens.shape),
        grad_tokens.reshape(tokens.shape),
        reduced[4],
        reduced[0],
        reduced[1],
        reduced[2],
        reduced[3],
        reduced[5],
        reduced[6],
        reduced[7],
        grad_expert_in,
        grad_expert_out,
    )


BF = jnp.bfloat16
F4 = jnp.float32
NEG = -1e30
QB = 256
TILE = 512
LANES = 128


def dot(left, right, left_dim=1, right_dim=0):
    dims = (((left_dim,), (right_dim,)), ((), ()))
    return lax.dot_general(left, right, dims, preferred_element_type=F4)


def iota(shape, dim):
    return lax.broadcasted_iota(jnp.int32, shape, dim)


class Place:
    def __init__(self, lengths):
        self.lengths = lengths

    def __getitem__(self, item):
        if item == 0:
            return lax.axis_index(BLK)
        if item == 1:
            return lax.axis_index(HEAD)
        return self.lengths[lax.axis_index(HEAD)]


class Made(tuple):
    @property
    def token(self):
        return self[-1]


def vmem_call(body, lengths, args, outs, scratch=(), ties=(), loose=(), away=()):
    count, tied, made = len(args), len(ties), len(outs)

    def kernel(length_ref, *refs):
        inputs, rest = refs[:count], refs[count + tied :]
        body(Place(length_ref), *inputs, *rest[:made], *rest[made + 1 :])
        rest[made][...] = jnp.zeros((8, LANES), F4)

    vmem = pl.BlockSpec(memory_space=pltpu.VMEM)
    place = pl.BlockSpec(memory_space=pl.ANY)
    return Made(
        pl.pallas_call(
            kernel,
            out_shape=tuple(outs) + (shaped((8, LANES), F4),),
            in_specs=[pl.BlockSpec(memory_space=pltpu.SMEM)]
            + [place if i in loose else vmem for i in range(count)]
            + [vmem] * tied,
            out_specs=tuple(place if i in away else vmem for i in range(made)) + (vmem,),
            scratch_shapes=list(scratch),
            compiler_params=pltpu.CompilerParams(vmem_limit_bytes=60 * 1024 * 1024),
            cost_estimate=pl.CostEstimate(flops=1, bytes_accessed=1, transcendentals=0),
        )(lengths, *args, *ties)
    )


def shaped(shape, dtype):
    return jax.ShapeDtypeStruct(shape, dtype)


def ring_block(step, own_blk, ring_len):
    half = ring_len // 2
    place = jnp.where((own_blk & 1) == 0, own_blk >> 1, ring_len - 1 - (own_blk >> 1))
    place = (place + step) & (ring_len - 1)
    return jnp.where(place < half, 2 * place, 2 * ring_len - 1 - 2 * place)


def ring_steps(ring_len):
    steps = [0]
    for hop in range(1, ring_len // 2):
        steps += [-hop, hop]
    return steps + [ring_len // 2]


def norm_scale(values):
    return lax.rsqrt(jnp.mean(values * values, axis=-1, keepdims=True) + norm_eps)


def head_tile(block, head, place):
    tile = block[:, LANES * (head // 2) : LANES * (head // 2) + LANES].astype(F4)
    return tile if head % 2 == place else pltpu.roll(tile, HEAD_DIM, 1)


def column(row, size):
    square = jnp.where(iota((size, size), 0) == iota((size, size), 1), row.astype(F4), 0.0)
    return jnp.sum(square, axis=1, keepdims=True)


def pack_units(n, sc, wq, wk, wv, gain_a, gain_m, router, table, out):
    rows = wq.shape[0]
    lane = iota((rows, LANES), 1)
    row = iota((rows, LANES), 0)

    def widen(values, at):
        blank = jnp.zeros((values.shape[0], LANES - values.shape[1]), F4)
        return pltpu.roll(jnp.concatenate([values.astype(F4), blank], axis=1), at, 1)

    misc = widen(jnp.transpose(router[...].astype(F4)), 2)
    misc = jnp.where(lane == 0, column(gain_a[...], rows), misc)
    misc = jnp.where(lane == 1, column(gain_m[...], rows), misc)
    listed = jnp.broadcast_to(widen(table[...], 16), (rows, LANES))
    misc = (misc + jnp.where(row == 0, listed, 0.0)).astype(BF)
    for j in range(n):
        pair, turn = j // 2, j % 2
        for c, weight in enumerate((wq, wk, wv)):
            own = head_tile(weight, 3 * pair + turn, 0)
            both = head_tile(weight, 3 * pair + 2, 1)
            out[j, :, LANES * c : LANES * c + LANES] = jnp.where(
                lane < HEAD_DIM, own, both
            ).astype(BF)
        out[j, :, 3 * LANES : 4 * LANES] = misc


def place_rows(sc, n, rows, parts, dest):
    for kk, part in enumerate(parts):
        for j in range(n):
            first = pl.multiple_of(((sc[1] ^ kk) * n + j) * rows, 8)
            dest[pl.ds(first, rows), :] = part[j].astype(F4)


def unpack_units(n, rows, sc, p0, p1, p2, p3, unit_w, misc, misc_t, table, buf):
    place_rows(sc, n, rows, (p0, p1, p2, p3), buf)
    unit_w[...] = buf[:, 0 : 3 * LANES].astype(BF)
    for b in range(NUM_BUCKETS):
        table[b : b + 1, :] = buf[rows * b : rows * b + 1, 3 * LANES : 4 * LANES]
    tail = buf[:, 3 * LANES : 4 * LANES]
    misc[...] = tail.astype(BF)
    misc_t[...] = jnp.transpose(tail)


def bias_strips(n, sc, table, buckets, out, line):
    row = iota((8, TILE), 0)
    pair, turn = sc[0] >> 1, sc[0] & 1
    listed = table[...]
    lane = iota(listed.shape, 1)
    reach = buckets.shape[1]
    inside = iota((NUM_BUCKETS, reach), 0) == buckets[...]
    for unit, head in enumerate((3 * pair + turn, 3 * pair + 2)):
        entry = jnp.sum(jnp.where(lane == 16 + head, listed, 0.0), axis=1, keepdims=True)
        line[:, 0:QB] = jnp.zeros((1, QB), F4)
        line[:, QB:] = jnp.sum(jnp.where(inside, entry, 0.0), axis=0, keepdims=True)
        out[unit, 0] = jnp.full((QB, QB), NEG, F4)
        for far in range(n):
            flat = jnp.broadcast_to(line[:, far * QB : far * QB + TILE], (8, TILE))
            turned = flat
            for c in range(1, 8):
                turned = jnp.where(row == c, pltpu.roll(flat, c, 1), turned)
            for group in range(QB // 8):
                moved = turned if group == 0 else pltpu.roll(turned, 8 * group, 1)
                strip = moved[:, QB:]
                if far == 0:
                    after = iota((8, QB), 1) >= iota((8, QB), 0) + 8 * group
                    strip = jnp.where(after, strip, NEG)
                out[unit, far + 1, 8 * group : 8 * group + 8, :] = strip


def ones_row(cols):
    return jnp.where(iota((HEAD_DIM, cols), 0) == 0, 1.0, 0.0).astype(BF)


def unit_operands(n, sc, blocks, misc_t, unit_w, normed, outs):
    key_own, key_both, query_t, key_t, value_t, value_r = outs
    lane = iota((QB, LANES), 1)
    row = iota((QB, LANES), 0)
    gain = misc_t[0:1, :]
    for i, step in enumerate(ring_steps(n)):
        place = ring_block(step, sc[0], n)
        first = pl.multiple_of(place * QB, QB)
        block = jnp.concatenate([part[...].astype(F4) for part in blocks[i]], axis=0)
        rows = (block * norm_scale(block) * gain).astype(BF)
        normed[place] = rows
        made = dot(rows, unit_w[...])
        low = made.astype(BF)
        turned = jnp.transpose(made).astype(BF)
        keys = made[:, LANES : 2 * LANES]
        hidden_key = jnp.where(first + row < sc[2], 0.0, NEG)
        own = jnp.where(lane < HEAD_DIM, keys, jnp.where(lane == HEAD_DIM, hidden_key, 0.0))
        both = jnp.where(lane >= HEAD_DIM, keys, jnp.where(lane == 0, hidden_key, 0.0))
        key_own[pl.ds(first, QB), :] = own.astype(BF)
        key_both[pl.ds(first, QB), :] = both.astype(BF)
        query_t[:, pl.ds(first, QB)] = turned[0:LANES]
        key_t[:, pl.ds(first, QB)] = turned[LANES : 2 * LANES]
        value_t[:, pl.ds(first, QB)] = turned[2 * LANES :]
        value_r[pl.ds(first, QB), :] = low[:, 2 * LANES :]


class Unit:
    def __init__(self, shared, sc):
        self.shared = shared
        self.lo = HEAD_DIM if shared else 0
        self.part = LANES if shared else QB
        self.shift = pl.multiple_of((sc[0] & 1) * LANES, LANES) if shared else 0

    def lanes(self, block):
        start = block * QB if isinstance(block, int) else pl.multiple_of(block * QB, QB)
        return pl.ds(start + self.shift, self.part)

    def columns(self, ref, pair):
        rows = pl.ds(self.lo, HEAD_DIM)
        return jnp.concatenate([ref[rows, self.lanes(2 * pair + q)] for q in range(2)], axis=1)

    def padded(self, half, other):
        return jnp.concatenate([other, half] if self.shared else [half, other], axis=0)

    def strip(self, bias, far):
        def piece(key_half, query_half):
            at = max(far + query_half - key_half, -1) + 1 if isinstance(far, int) else (
                jnp.maximum(far + query_half - key_half, -1) + 1
            )
            return bias[at, :, pl.ds(self.shift, self.part)]

        return jnp.concatenate(
            [jnp.concatenate([piece(k, 0), piece(k, 1)], axis=1) for k in range(2)], axis=0
        )


def attend_tiles(n, unit, key_ref, query_t, value_t, bias, heads, log_ref):
    cols = 2 * unit.part
    for pair in range(n // 2):
        queries = unit.padded(unit.columns(query_t, pair), ones_row(cols))
        top = jnp.zeros((1, cols), F4) + NEG
        total = jnp.zeros((1, cols), F4)
        mixed = jnp.zeros((HEAD_DIM, cols), F4)
        for part in range(pair + 1):
            tile = dot(key_ref[part * TILE : (part + 1) * TILE, :], queries)
            tile = tile + unit.strip(bias, 2 * (pair - part))
            new_top = jnp.maximum(top, jnp.max(tile, axis=0, keepdims=True))
            weights = jnp.exp(tile - new_top)
            decay = jnp.exp(top - new_top)
            top = new_top
            total = total * decay + jnp.sum(weights, axis=0, keepdims=True)
            values = value_t[unit.lo : unit.lo + HEAD_DIM, part * TILE : (part + 1) * TILE]
            mixed = mixed * decay + dot(values, weights.astype(BF))
        made = (mixed / total).astype(BF)
        log_total = top + jnp.log(total)
        at = slice(QB, QB + LANES) if unit.shared else slice(0, QB)
        for q in range(2):
            cut = slice(q * unit.part, (q + 1) * unit.part)
            heads[2 * pair + q, :, at] = made[:, cut]
            log_ref[2 * pair + q] = log_total[:, cut]


def copies_of(pairs, sems):
    return [
        pltpu.make_async_copy(source, dest, sems.at[i]) for i, (source, dest) in enumerate(pairs)
    ]


def attend_units(n, sc, *refs):
    blocks = [(ref,) for ref in refs[: n - 1]] + [refs[n - 1 : n + 1]]
    misc_t, unit_w, table, buckets, heads, logs_own, logs_both = refs[n + 1 : n + 8]
    outs = refs[n + 8 : n + 15]
    kept, (value_t, line, sems) = refs[n + 15 : n + 22], refs[n + 22 :]
    normed, key_own, key_both, query_t, key_t, value_r, bias = kept
    copies = copies_of(list(zip(kept, outs)), sems)
    placed = (key_own, key_both, query_t, key_t, value_t, value_r)
    unit_operands(n, sc, blocks, misc_t, unit_w, normed, placed)
    for copy in copies[:-1]:
        copy.start()
    bias_strips(n, sc, table, buckets, bias, line)
    copies[-1].start()
    for shared, key_ref, log_ref in ((False, key_own, logs_own), (True, key_both, logs_both)):
        strips = bias.at[int(shared)]
        attend_tiles(n, Unit(shared, sc), key_ref, query_t, value_t, strips, heads, log_ref)
    for copy in copies:
        copy.wait()


def split_units(ref):
    return (ref.at[:, 0 : 3 * HEAD_DIM, :], ref.at[:, 3 * HEAD_DIM :, :])


def unit_grads(n, sc, *refs):
    key_own, key_both, query_t, key_t, value_r, strips_in, heads, grads_in = refs[:8]
    logs_own, logs_both, stacked, table = refs[8:12]
    grads_own, grads_both, delta_own, delta_both, grad_k, grad_v, strips, bias, sems = refs[12:]
    leave = copies_of([(strips.at[i], table.at[i]) for i in (1, 0)], sems.at[2:4])
    copies = copies_of([(strips_in.at[i], bias.at[i]) for i in (1, 0)], sems)
    for copy in copies:
        copy.start()
    own, both = split_units(stacked)
    common = (query_t, key_t, value_r, heads, grads_in)
    shared_only = (logs_both, both, leave[0], grads_both, delta_both)
    own_only = (logs_own, own, leave[1], grads_own, delta_own)
    sums = (grad_k, grad_v)
    grads_of_unit(n, True, sc, copies[0], bias.at[1], key_both, *common, *shared_only, *sums, strips.at[1])
    grads_of_unit(n, False, sc, copies[1], bias.at[0], key_own, *common, *own_only, *sums, strips.at[0])
    for copy in leave:
        copy.wait()


def grads_of_unit(
    n,
    shared,
    sc,
    copy,
    bias,
    key_ref,
    query_t,
    key_t,
    value_r,
    heads,
    grads_in,
    logs,
    stacked,
    leave,
    grad_t,
    delta,
    grad_k,
    grad_v,
    strips,
):
    unit = Unit(shared, sc)
    cols = 2 * unit.part
    at = slice(QB, QB + LANES) if shared else slice(0, QB)
    rows = slice(unit.lo, unit.lo + HEAD_DIM)
    for j in range(n):
        grads = grads_in[j, :, at]
        grad_t[:, j * unit.part : (j + 1) * unit.part] = grads
        product = grads.astype(F4) * heads[j, :, at].astype(F4)
        delta[j] = jnp.sum(product, axis=0, keepdims=True)
    grad_k[...] = jnp.zeros(grad_k.shape, F4)
    grad_v[...] = jnp.zeros(grad_v.shape, F4)
    strips[...] = jnp.zeros(strips.shape, F4)
    copy.wait()

    def one_tile(pair, carry):
        nothing = jnp.zeros((HEAD_DIM, cols), BF)
        raw_queries = unit.columns(query_t, pair)
        queries = unit.padded(raw_queries, ones_row(cols))
        plain = unit.padded(raw_queries, nothing)
        start = pair * cols
        grads = unit.padded(grad_t[:, pl.ds(start, cols)], nothing)
        log_total = jnp.concatenate([logs[2 * pair + q] for q in range(2)], axis=1)
        inner = jnp.concatenate([delta[2 * pair + q] for q in range(2)], axis=1)

        def step(part, made):
            key_at = part * TILE
            far = 2 * (pair - part)
            scores = dot(key_ref[pl.ds(key_at, TILE), :], queries)
            scores = scores + unit.strip(bias, far)
            probs = jnp.exp(scores - log_total)
            grad_probs = dot(value_r[pl.ds(key_at, TILE), :], grads)
            grad_scores = probs * (grad_probs - inner)
            for key_half in range(2):
                for q in range(2):
                    place = max(far + q - key_half, -1) + 1
                    strips[place, :, pl.ds(unit.shift, unit.part)] += grad_scores[
                        key_half * QB : (key_half + 1) * QB, q * unit.part : (q + 1) * unit.part
                    ]
            low = grad_scores.astype(BF)
            grad_v[pl.ds(key_at, TILE), :] += dot(probs.astype(BF), grads, 1, 1)
            grad_k[pl.ds(key_at, TILE), :] += dot(low, plain, 1, 1)
            return made + dot(key_t[pl.ds(unit.lo, HEAD_DIM), pl.ds(key_at, TILE)], low)

        made = jnp.zeros((HEAD_DIM, cols), F4)
        for part in range(pair + 1):
            made = step(part, made)
        for q in range(2):
            cut = made[:, q * unit.part : (q + 1) * unit.part]
            if shared:
                half = HEAD_DIM // 2
                cut = jnp.concatenate([cut[0:half], cut[half:]], axis=1)
            stacked[2 * pair + q, 2 * HEAD_DIM :, :] = cut.astype(BF)
        return carry

    for pair in range(n // 2):
        one_tile(pair, 0)
    leave.start()
    for j in range(n):
        block = slice(QB * j, QB * (j + 1))
        stacked[j, 0:HEAD_DIM, :] = jnp.transpose(grad_k[block, :])[rows].astype(BF)
        stacked[j, HEAD_DIM : 2 * HEAD_DIM, :] = jnp.transpose(grad_v[block, :])[rows].astype(BF)


def distance_sums(n, strips, table):
    row = iota((8, TILE), 0)
    empty = jnp.zeros((8, QB), F4)
    for far in range(n):
        total = jnp.zeros((8, TILE), F4)
        for group in range(QB // 8):
            rows8 = strips[far + 1, 8 * group : 8 * group + 8, :]
            wide = jnp.concatenate([empty, rows8], axis=1)
            total = total + (wide if group == 0 else pltpu.roll(wide, TILE - 8 * group, 1))
        lined = jnp.where(row == 0, total, 0.0)
        for c in range(1, 8):
            lined = lined + jnp.where(row == c, pltpu.roll(total, TILE - c, 1), 0.0)
        table[far] = jnp.sum(lined, axis=0, keepdims=True)


def dispatch_rows(n, cap, sc, route_ref, cot, wo_t, wq, wk, wv, out, target, w_out):
    tok = cot.shape[0]
    route = route_ref[...]
    chosen = iota((n, tok), 0) == route
    upto = jnp.where(iota((tok, tok), 0) <= iota((tok, tok), 1), 1.0, 0.0).astype(BF)
    filled = dot(jnp.where(chosen, 1.0, 0.0).astype(BF), upto)
    slot = jnp.sum(jnp.where(chosen, filled - 1.0, 0.0), axis=0, keepdims=True)
    slot = slot.astype(jnp.int32)
    place = route * cap + slot
    target[...] = jnp.broadcast_to(place, target.shape)
    spread = jnp.where(iota((n * cap, tok), 0) == place, 1.0, 0.0).astype(BF)
    packed = dot(spread, cot[...]).astype(BF)
    weights = jnp.concatenate([w[...].astype(F4) for w in (wq, wk, wv)], axis=0).astype(BF)
    for j in range(n):
        out[j, 0:cap, :] = packed[j * cap : (j + 1) * cap]
        out[j, cap:, :] = wo_t[...]
        w_out[j] = weights


def spread_matrix(target, rows):
    place = target[0:1, :]
    return jnp.where(iota((rows, place.shape[1]), 0) == place, 1.0, 0.0)


def hidden_rows(
    n, cap, sc, heads, p0, p1, p2, p3, tokens, misc_t, target, attn, hidden_out, out, wo_t, buf, wide
):
    place_rows(sc, n, p0.shape[1], (p0, p1, p2, p3), wide)
    wo_t[...] = wide[...].astype(BF)
    for pair in range(n // 2):
        at = 3 * pair * HEAD_DIM
        for turn in range(2):
            made = heads[2 * pair + turn].astype(F4)
            buf[at + turn * HEAD_DIM : at + (turn + 1) * HEAD_DIM, :] = made[:, 0:QB]
            both = slice(turn * LANES, (turn + 1) * LANES)
            buf[at + 2 * HEAD_DIM : at + 3 * HEAD_DIM, both] = made[:, QB:]
    rows = jnp.transpose(buf[...]).astype(BF)
    attn[...] = rows
    hidden = tokens[...].astype(F4) + dot(rows, wo_t[...], 1, 1)
    hidden_out[...] = hidden
    moe_in = (hidden * norm_scale(hidden) * misc_t[1:2, :]).astype(BF)
    packed = dot(spread_matrix(target, n * cap).astype(BF), moe_in).astype(BF)
    for j in range(n):
        out[j] = packed[j * cap : (j + 1) * cap]


def gelu_pair(values):
    scale = math.sqrt(2.0 / math.pi)
    square = values * values
    bend = jnp.tanh(scale * (values + 0.044715 * values * square))
    act = 0.5 * values * (1.0 + bend)
    slope = 0.5 * (1.0 + bend) + 0.5 * values * (1.0 - bend * bend) * scale * (
        1.0 + 3.0 * 0.044715 * square
    )
    return (act, slope)


def route_probs(experts, sc, rows, misc):
    logits = dot(rows, misc[...])
    lane = iota(logits.shape, 1)
    real = (lane >= 2) & (lane < 2 + experts)
    logits = jnp.where(real, logits, NEG)
    powers = jnp.where(real, jnp.exp(logits - jnp.max(logits, axis=-1, keepdims=True)), 0.0)
    probs = powers / jnp.sum(powers, axis=-1, keepdims=True)
    chosen = lane == sc[0] + 2
    gate = jnp.sum(jnp.where(chosen, probs, 0.0), axis=-1, keepdims=True)
    return (probs, chosen, gate)


def flat_rows(ref, cap=None):
    return jnp.concatenate([ref[j][0:cap] for j in range(ref.shape[0])], axis=0)


def expert_back(experts, sc, rows_ref, cot_ref, *refs):
    ins, outs, (misc, back, made, log_out) = refs[0:4], refs[4:8], refs[8:12]
    rows, cots = flat_rows(rows_ref), flat_rows(cot_ref, rows_ref.shape[1])
    probs, chosen, gate = route_probs(experts, sc, rows, misc)
    inner = jnp.zeros(gate.shape, F4)
    total = jnp.zeros(rows.shape, F4)
    result = jnp.zeros(rows.shape, F4)
    for w_in, w_out in zip(ins, outs):
        act, slope = gelu_pair(dot(rows, w_in[...]))
        low = act.astype(BF)
        result = result + dot(low, w_out[...])
        grad_act = dot(cots, w_out[...], 1, 1)
        inner = inner + jnp.sum(low.astype(F4) * grad_act, axis=-1, keepdims=True)
        total = total + dot((gate * grad_act * slope).astype(BF), w_in[...], 1, 1)
    grad_logits = (inner * probs * (jnp.where(chosen, 1.0, 0.0) - gate)).astype(BF)
    log_out[...] = grad_logits
    total = (total + dot(grad_logits, misc[...], 1, 1)).astype(BF)
    result = (gate * result).astype(BF)
    cap = made.shape[1]
    for j in range(made.shape[0]):
        back[j] = total[j * cap : (j + 1) * cap]
        made[j] = result[j * cap : (j + 1) * cap]


def expert_weights(experts, count, more, sc, *refs):
    rows_refs, cot_refs = refs[:count], refs[count : 2 * count]
    w_in, w_out, misc = refs[2 * count : 2 * count + 3]
    begun = refs[2 * count + 3 : 2 * count + 5] if more else None
    grad_in, grad_out, token, all_rows, all_grads, turned = refs[2 * count + (5 if more else 3) :]
    token[...] = jnp.zeros(token.shape, F4)
    size = rows_refs[0].shape[0] * rows_refs[0].shape[1]

    @pl.when(pl.program_id(0) == 0)
    def _():
        for i in range(count):
            at = slice(i * size, (i + 1) * size)
            rows, cots = flat_rows(rows_refs[i]), flat_rows(cot_refs[i], rows_refs[i].shape[1])
            gate = route_probs(experts, sc, rows, misc)[2]
            all_rows[at, :] = rows
            turned[:, at] = jnp.transpose(rows.astype(F4)).astype(BF)
            all_grads[at, :] = (gate * cots.astype(F4)).astype(BF)

    rows, grads = all_rows[...], all_grads[...]
    act, slope = gelu_pair(dot(rows, w_in[...]))
    grad_pre = (dot(grads, w_out[...], 1, 1) * slope).astype(BF)
    in_part = dot(turned[...], grad_pre)
    out_part = dot(act.astype(BF), grads, 0, 0)
    grad_in[...] = begun[0][...] + in_part if more else in_part
    grad_out[...] = begun[1][...] + out_part if more else out_part


def chunked_specs(w_in):
    depth, hidden = w_in.shape
    chunk = 2 * LANES
    columns = pl.BlockSpec((depth, chunk), lambda i: (0, i))
    lines = pl.BlockSpec((chunk, depth), lambda i: (i, 0))
    return hidden // chunk, columns, lines


def expert_weights_call(experts, lengths, rows_in, cots_in, w_in, w_out, misc, ties, begun=()):
    count, (depth, hidden) = len(rows_in), w_in.shape
    size = rows_in[0].shape[0] * rows_in[0].shape[1]
    body = functools.partial(expert_weights, experts, count, bool(begun))
    args = tuple(rows_in) + tuple(cots_in) + (w_in, w_out, misc) + tuple(begun)

    def kernel(length_ref, *refs):
        body(Place(length_ref), *refs[: len(args)], *refs[len(args) + len(ties) :])

    whole = pl.BlockSpec(memory_space=pltpu.VMEM)
    steps, columns, lines = chunked_specs(w_in)
    return pl.pallas_call(
        kernel,
        grid=(steps,),
        out_shape=(
            shaped((depth, hidden), F4),
            shaped((hidden, depth), F4),
            shaped((8, LANES), F4),
        ),
        in_specs=[pl.BlockSpec(memory_space=pltpu.SMEM)]
        + [whole] * (2 * count)
        + [columns, lines, whole]
        + ([columns, lines] if begun else [])
        + [whole] * len(ties),
        out_specs=(columns, lines, whole),
        scratch_shapes=[
            pltpu.VMEM((count * size, depth), BF),
            pltpu.VMEM((count * size, depth), BF),
            pltpu.VMEM((depth, count * size), BF),
        ],
        compiler_params=pltpu.CompilerParams(vmem_limit_bytes=60 * 1024 * 1024),
        cost_estimate=pl.CostEstimate(flops=1, bytes_accessed=1, transcendentals=0),
    )(lengths, *args, *ties)


def result_rows(n, cap, sc, made, target, hidden, out):
    rows = flat_rows(made)
    spread = jnp.transpose(spread_matrix(target, n * cap)).astype(BF)
    out[...] = (hidden[...] + dot(spread, rows)).astype(BF)


def norm_back(grads, source, gain):
    scale = norm_scale(source)
    weighted = grads * gain
    inner = jnp.mean(weighted * source, axis=-1, keepdims=True)
    return (scale * weighted - source * (scale * scale * scale) * inner, scale)


def hidden_grads(
    n, cap, sc, back, target, hidden_ref, misc_t, cot, wo_t, grad_out, low_out, gain_out, out, buf
):
    spread = jnp.transpose(spread_matrix(target, n * cap)).astype(BF)
    grads = dot(spread, flat_rows(back))
    hidden = hidden_ref[...]
    normed, scale = norm_back(grads, hidden, misc_t[1:2, :])
    gain_out[...] = jnp.broadcast_to(
        jnp.sum(grads * hidden * scale, axis=0, keepdims=True), gain_out.shape
    )
    total = cot[...].astype(F4) + normed
    grad_out[...] = total
    low = total.astype(BF)
    low_out[...] = low
    buf[...] = jnp.transpose(dot(low, wo_t[...])).astype(BF)
    for pair in range(n // 2):
        at = 3 * pair * HEAD_DIM
        for turn in range(2):
            out[2 * pair + turn, :, 0:QB] = buf[at + turn * HEAD_DIM : at + (turn + 1) * HEAD_DIM, :]
            both = slice(turn * LANES, (turn + 1) * LANES)
            out[2 * pair + turn, :, QB:] = buf[at + 2 * HEAD_DIM : at + 3 * HEAD_DIM, both]


def unfolded(piece):
    return jnp.concatenate([piece[:, 0:LANES], piece[:, LANES:]], axis=0)


def unpack_full(n, rows, sc, p0, p1, p2, p3, out, wide):
    inner = wide.shape[1] // 3
    for kk, part in enumerate((p0, p1, p2, p3)):
        for j in range(n):
            first = pl.multiple_of(((sc[1] ^ kk) * n + j) * rows, 8)
            block = part[j].astype(F4)
            for c in range(3):
                wide[pl.ds(first, rows), c * inner : (c + 1) * inner] = block[
                    c * rows : (c + 1) * rows
                ]
    out[...] = wide[...].astype(BF)


def token_grads(n, sc, stacked, weights, tokens, hidden_grad, misc_t, out, buf):
    own, both = split_units(stacked)
    inner = weights.shape[1] // 3
    for pair in range(n // 2):
        at = 3 * pair * HEAD_DIM
        last = at + 2 * HEAD_DIM
        for turn in range(2):
            j = 2 * pair + turn
            for c, piece in enumerate((2, 0, 1)):
                lo = c * inner + at + turn * HEAD_DIM
                buf[lo : lo + HEAD_DIM, :] = own[j, piece * HEAD_DIM : (piece + 1) * HEAD_DIM, :]
            half = slice(turn * LANES, (turn + 1) * LANES)
            buf[last : last + HEAD_DIM, half] = unfolded(both[j, 2 * HEAD_DIM :, :])
        for c in (1, 2):
            rows = slice((c - 1) * HEAD_DIM, c * HEAD_DIM)
            total = both[2 * pair, rows, :].astype(F4) + both[2 * pair + 1, rows, :].astype(F4)
            buf[c * inner + last : c * inner + last + HEAD_DIM, :] = total.astype(BF)
    made = jnp.transpose(dot(weights[...], buf[...]))
    normed, unused = norm_back(made, tokens[...].astype(F4), misc_t[0:1, :])
    out[...] = (hidden_grad[...] + normed).reshape(out.shape)


def unit_weight_grads(n, heads, sc, normed, stacked, strips, buckets, *rest):
    own, both = split_units(stacked)
    outs, (buf, table, lines_ref) = rest[:heads], rest[heads:]
    for unit in range(2):
        distance_sums(n, strips.at[unit], lines_ref.at[unit * n : (unit + 1) * n])
    width = buf.shape[1]
    sums = []
    for unit in range(2):
        made = jnp.zeros((NUM_BUCKETS, 1), F4)
        for far in range(n):
            lines = lines_ref.at[unit * n : (unit + 1) * n]
            line = lines[far][:, QB:]
            if far + 1 < n:
                line = line + lines[far + 1][:, :QB]
            inside = iota((NUM_BUCKETS, QB), 0) == buckets[:, far * QB : (far + 1) * QB]
            made = made + jnp.sum(jnp.where(inside, line, 0.0), axis=1, keepdims=True)
        sums.append(made)
    lane = iota((NUM_BUCKETS, width), 1)
    high = [value.astype(BF).astype(F4) for value in sums]
    listed = jnp.zeros((NUM_BUCKETS, width), F4)
    for at, value in enumerate(high + [sums[0] - high[0], sums[1] - high[1]]):
        listed = jnp.where(lane == at, value, listed)
    table[...] = listed
    total = None
    for j in range(n):
        shared = unfolded(both[j, 2 * HEAD_DIM :, :]).astype(F4)
        blank = jnp.zeros(shared.shape, F4)
        turn = jnp.broadcast_to((sc[0] & 1) == 0, shared.shape)
        shared = jnp.concatenate(
            [jnp.where(turn, shared, blank), jnp.where(turn, blank, shared)], axis=1
        )
        pieces = [own[j, 2 * HEAD_DIM :, :], shared.astype(BF)]
        for c in range(2):
            rows = slice(c * HEAD_DIM, (c + 1) * HEAD_DIM)
            pieces += [own[j, rows, :], both[j, rows, :]]
        part = dot(jnp.concatenate(pieces, axis=0), normed[j])
        total = part if total is None else total + part
    buf[...] = jnp.transpose(total)
    rows = buf.shape[0] // heads
    for kk in range(heads):
        to = sc[1] ^ kk
        outs[kk][...] = jnp.concatenate(
            [
                buf[pl.ds(pl.multiple_of(to * rows, 8), rows), :],
                table[pl.ds(pl.multiple_of(to * n, 8), n), :],
                jnp.zeros((8, width), F4),
            ],
            axis=0,
        ).astype(BF)


def two_parts(values, gap):
    high = values.astype(BF).astype(F4)
    lane = iota(values.shape, 1)
    low = pltpu.roll(jnp.where(lane < gap, values - high, 0.0), gap, 1)
    return jnp.where(lane < gap, high, low)


def one_part(values, gap):
    return values + pltpu.roll(values, values.shape[1] - gap, 1)


def weight_sums(n, rows, heads, sc, *refs):
    units, outer = refs[:heads], refs[heads : 2 * heads]
    outs, buf = refs[2 * heads : -1], refs[-1]
    total = (units[0][...].astype(F4) + units[1][...].astype(F4)) + (
        units[2][...].astype(F4) + units[3][...].astype(F4)
    )
    base = n * rows
    entries = two_parts(one_part(total[base : base + n], 2), 2)
    wide = (outer[0][...].astype(F4) + outer[1][...].astype(F4)) + (
        outer[2][...].astype(F4) + outer[3][...].astype(F4)
    )
    width = wide.shape[1] - LANES
    extra = two_parts(one_part(wide[:, width:], 16), 16)
    for to in range(n):
        at = slice(to * rows, (to + 1) * rows)
        entry = pltpu.roll(entries[to : to + 1, 0:LANES], 64, 1)
        entry = jnp.where(iota((rows, LANES), 0) == 0, entry, 0.0)
        buf[to] = jnp.concatenate([total[at], wide[at, 0:width], extra[at] + entry], axis=1)
    for k in range(n):
        outs[k][...] = buf[sc[0] ^ k].astype(BF)


def as_row(values):
    size = values.shape[0]
    square = jnp.where(iota((size, size), 0) == iota((size, size), 1), values, 0.0)
    return jnp.sum(square, axis=0, keepdims=True)


def weight_final(n, experts, sc, *refs):
    parts, (wq, wk, wv, gain_a) = refs[:n], refs[n : n + 4]
    grads = refs[n + 4 : n + 7]
    gain, table, grad_out, gain_out, router, buf, tables = refs[n + 7 :]
    rows = wq.shape[0]
    units = 3 * LANES
    small = slice(parts[0].shape[1] - LANES, parts[0].shape[1])
    total = None
    for j in range(n):
        part = parts[j][...].astype(F4)
        buf[sc[0] ^ j] = part[:, 0:units]
        tables[sc[0] ^ j] = part[0:1, small]
        total = part[:, units:] if total is None else total + part[:, units:]
    lane = iota((rows, LANES), 1)
    inner = jnp.zeros((rows, 1), F4)
    for c, weight in enumerate((wq, wk, wv)):
        lo = LANES * c

        def piece(head, place):
            pair, turn = head // 3, head % 3
            if turn < 2:
                tile, half = buf[2 * pair + turn, 0:rows, lo : lo + LANES], 0
            else:
                tile = (
                    buf[2 * pair, 0:rows, lo : lo + LANES]
                    + buf[2 * pair + 1, 0:rows, lo : lo + LANES]
                )
                half = 1
            return tile if half == place else pltpu.roll(tile, HEAD_DIM, 1)

        for m in range(weight.shape[1] // LANES):
            tile = jnp.where(lane < HEAD_DIM, piece(2 * m, 0), piece(2 * m + 1, 1))
            cols = slice(LANES * m, LANES * m + LANES)
            grads[c][:, cols] = tile
            inner = inner + jnp.sum(weight[:, cols].astype(F4) * tile, axis=-1, keepdims=True)
    gain[...] = as_row(inner / column(gain_a[...], rows))
    lane = iota((1, HEADS), 1)
    listed = jnp.zeros((1, HEADS), F4)
    for j in range(n):
        entry = one_part(pltpu.roll(tables[j], 64, 1), 2)
        listed = listed + jnp.where(lane == 3 * (j // 2) + j % 2, entry[:, 0:1], 0.0)
        listed = listed + jnp.where(lane == 3 * (j // 2) + 2, entry[:, 1:2], 0.0)
    table[...] = listed
    width = grad_out.shape[1]
    grad_out[...] = total[:, 0:width]
    extra = total[0:rows, width:]
    extra = one_part(jnp.where(iota(extra.shape, 1) < 32, extra, 0.0), 16)
    gain_out[...] = as_row(extra[:, 1:2])
    router[...] = jnp.transpose(pltpu.roll(extra, LANES - 2, 1))[0:experts]


def out_weight_grads(heads, sc, low, attn, rows, logs, gain, *rest):
    outs, buf = rest[:heads], rest[heads]
    width = attn.shape[1]
    buf[:, 0:width] = dot(low[...], attn[...], 0, 0)
    router = dot(flat_rows(rows), logs[...], 0, 0)
    wide = jnp.where(iota((LANES, gain.shape[1]), 0) == 1, gain[0:1, :], 0.0)
    buf[:, width : width + LANES] = two_parts(router + jnp.transpose(wide), 16)
    rows = buf.shape[0] // heads
    for kk in range(heads):
        first = pl.multiple_of((sc[1] ^ kk) * rows, 8)
        outs[kk][...] = buf[pl.ds(first, rows), :].astype(BF)


def last_grads(n, experts, sc, *refs):
    parts, own, rest = refs[: n + 4], refs[n + 4 : n + 9], refs[n + 9 :]
    weight_final(n, experts, sc, *parts, *rest[:8], *rest[9:11])
    token_grads(n, sc, *own, rest[8], rest[11])


def swap(values, axis, flip):
    if flip == 0:
        return values
    size = lax.axis_size(axis)
    return lax.ppermute(values, axis, [(i, i ^ flip) for i in range(size)])


def exchange(messages, axis):
    return [swap(message, axis, k) for k, message in enumerate(messages)]


def hold(values, *earlier):
    return lax.optimization_barrier((values, earlier))[0]


def over_heads(stack):
    across = swap(stack, HEAD, 2)
    return (stack, swap(stack, HEAD, 1), across, swap(across, HEAD, 1))


def on_plane(
    tokens,
    attn_gain,
    w_query,
    w_key,
    w_value,
    w_out,
    bias_table,
    moe_gain,
    w_router,
    expert_in,
    expert_out,
    seq_lengths,
    rel_buckets,
    routes,
    cotangent,
):
    heads = lax.axis_size(HEAD)
    n = lax.axis_size(BLK)
    tok, width = tokens.shape[0], tokens.shape[2]
    rows = w_query.shape[0]
    total_rows = n * tok
    experts = w_router.shape[1]
    cap = 3 * tok // (2 * experts)
    slots = n * cap
    scope = jax.named_scope
    x = tokens.reshape(tok, width)
    cot = cotangent.reshape(tok, width)
    gain_a = attn_gain.reshape(1, rows)
    gain_m = moe_gain.reshape(1, rows)
    in_own, out_own = expert_in.reshape(expert_in.shape[1:]), expert_out.reshape(expert_out.shape[1:])

    def call(body, args, outs, scratch=(), ties=(), loose=(), away=()):
        return vmem_call(body, seq_lengths, args, outs, scratch, ties, loose, away)

    def all_to_all(stack, axis=BLK):
        return lax.all_to_all(stack, axis, split_axis=0, concat_axis=0, tiled=True)

    order = [ring_of(i, n) for i in range(n)]
    ahead = [(order[i], order[(i + 1) % n]) for i in range(n)]
    astern = [(b, a) for a, b in ahead]
    unit_cols = 4 * LANES

    def hop(front, back):
        with scope("rin"):
            front = lax.ppermute(front, BLK, ahead)
            back = lax.ppermute(back, BLK, astern)
            return lax.optimization_barrier((front, back))

    first = hop(x, x)
    with scope("uw"):
        packed, packed_token = call(
            functools.partial(pack_units, n),
            (w_query, w_key, w_value)
            + (gain_a, gain_m, jnp.transpose(w_router), bias_table.reshape(1, -1)),
            [shaped((n, rows, unit_cols), BF)],
        )
        unit_in = all_to_all(hold(packed, first[0]))
    with scope("cr"):
        cot_out, target, w_stack, cot_token = call(
            functools.partial(dispatch_rows, n, cap),
            (routes.reshape(1, tok), cot, jnp.transpose(w_out), w_query, w_key, w_value),
            [
                shaped((n, cap + rows, width), BF),
                shaped((8, tok), jnp.int32),
                shaped((n, 3 * rows, width), BF),
            ],
            ties=(packed_token,),
        )
    with scope("es"):
        in_other = swap(in_own, HEAD, 2)
    second = hop(*hold(first, packed_token))
    with scope("uw"):
        unit_parts = over_heads(hold(unit_in, second[0]))
    third = hop(*hold(second, unit_in, cot_token))
    half = tok // 2
    with scope("rin"):
        front_half, back_half = hold((third[0][:half], third[1][half:]), in_other)
        front, back = lax.ppermute(front_half, BLK, ahead), lax.ppermute(back_half, BLK, astern)
    with scope("uw"):
        unit_w, misc, misc_t, table, unused = call(
            functools.partial(unpack_units, n, rows),
            unit_parts,
            [
                shaped((width, 3 * LANES), BF),
                shaped((width, LANES), BF),
                shaped((LANES, width), F4),
                shaped((NUM_BUCKETS, LANES), F4),
            ],
            [pltpu.VMEM((width, unit_cols), F4)],
        )
    with scope("es"):
        out_other = swap(hold(out_own, unit_parts[2], unit_parts[3]), HEAD, 2)

    buckets = rel_buckets.reshape(1, -1)

    with scope("cr"):
        cot_in = all_to_all(hold(cot_out, front, back, table))
        cot_rows, wo_rows = cot_in[:, :cap], cot_in[:, cap:]

    kept = [
        shaped((n, tok, width), BF),
        shaped((total_rows, LANES), BF),
        shaped((total_rows, LANES), BF),
        shaped((LANES, total_rows), BF),
        shaped((LANES, total_rows), BF),
        shaped((total_rows, LANES), BF),
        shaped((2, n + 1, QB, QB), F4),
    ]
    with scope("att"):
        (
            head_out,
            logs_own,
            logs_both,
            normed,
            key_own,
            key_both,
            query_t,
            key_t,
            value_r,
            strips,
            attend_token,
        ) = call(
            functools.partial(attend_units, n),
            (x,) + first + second + third + (front, back, misc_t, unit_w, table, buckets),
            [
                shaped((n, HEAD_DIM, QB + LANES), BF),
                shaped((n, 1, QB), F4),
                shaped((n, 1, LANES), F4),
            ]
            + kept,
            [pltpu.VMEM(k.shape, k.dtype) for k in kept]
            + [
                pltpu.VMEM((LANES, total_rows), BF),
                pltpu.VMEM((1, QB + total_rows), F4),
                pltpu.SemaphoreType.DMA((len(kept),)),
            ],
            ties=(cot_token,),
            away=range(3, 3 + len(kept)),
        )
        head_in = all_to_all(head_out)
    with scope("ow"):
        wo_parts = over_heads(hold(wo_rows, logs_both))
    with scope("cp"):
        all_cot = over_heads(hold(cot_rows, wo_parts[2]))
        cot_pair = all_cot[1]
    with scope("hid"):
        attn, hidden, moe_out, out_t, hidden_token = call(
            functools.partial(hidden_rows, n, cap),
            (head_in,) + wo_parts + (x, misc_t, target),
            [
                shaped((tok, width), BF),
                shaped((tok, width), F4),
                shaped((n, cap, width), BF),
                shaped((width, width), BF),
            ],
            [pltpu.VMEM((width, tok), F4), pltpu.VMEM((width, width), F4)],
            ties=(hold(attend_token, out_other),),

        )

    with scope("mr"):
        moe_rows = all_to_all(moe_out)
        moe_pair = swap(moe_rows, HEAD, 1)
    with scope("ec"):
        ins = (in_own, in_other, swap(in_own, HEAD, 1), swap(in_other, HEAD, 1))
        outs = (out_own, out_other, swap(out_own, HEAD, 1), swap(out_other, HEAD, 1))
    def backward_rows(rows_in, cots_in, kind, ties=()):
        return call(
            functools.partial(expert_back, experts),
            (rows_in, cots_in, in_own, out_own, in_other, out_other, misc),
            [
                shaped((slots, width), kind),
                shaped((slots, width), BF),
                shaped((slots, LANES), BF),
            ],
            ties=ties,
        )

    with scope("fw"):
        w_in = all_to_all(hold(w_stack, moe_rows, ins[2:], outs[2:]))
    with scope("mf"):
        moe_far = swap(moe_rows, HEAD, 2)
        far_pair = swap(moe_far, HEAD, 1)

    with scope("eb"):
        back_out, res_out, logs, back_token = call(
            functools.partial(expert_back, experts),
            (moe_rows, cot_rows) + ins + outs + (misc,),
            [
                shaped((n, cap, width), BF),
                shaped((n, cap, width), BF),
                shaped((slots, LANES), BF),
            ],
        )
        back_in = all_to_all(hold(back_out, w_in))
    with scope("fw"):
        w_parts = over_heads(hold(w_in, back_token))
    with scope("ewg"):
        expert_ends = (in_own, out_own, misc)
        *begun, expert_token = expert_weights_call(
            experts,
            seq_lengths,
            (moe_rows, moe_pair),
            all_cot[:2],
            *expert_ends,
            (back_token,),
        )
    with scope("hg"):
        grad_hidden, grad_low, gain_moe_part, grad_heads_out, unused = call(
            functools.partial(hidden_grads, n, cap),
            (back_in, target, hidden, misc_t, cot, out_t),
            [
                shaped((tok, width), F4),
                shaped((tok, width), BF),
                shaped((8, width), F4),
                shaped((n, HEAD_DIM, QB + LANES), BF),
            ],
            [pltpu.VMEM((width, tok), BF)],
            ties=(hold(expert_token, far_pair, all_cot[3]),),
        )
        grad_heads = all_to_all(grad_heads_out)
    wide = width + LANES
    with scope("owg"):
        *out_parts, out_token = call(
            functools.partial(out_weight_grads, heads),
            (grad_low, attn, moe_rows, logs, gain_moe_part),
            [shaped((width // heads, wide), BF)] * heads,
            [pltpu.VMEM((width, wide), F4)],
        )
        out_parts_in = exchange(out_parts, HEAD)
    with scope("rr"):
        res_in = all_to_all(hold(res_out, grad_heads, out_token))

    with scope("ag"):
        stacked, lines, unused = call(
            functools.partial(unit_grads, n),
            (
                key_own,
                key_both,
                query_t,
                key_t,
                value_r,
                strips,
                head_out,
                grad_heads,
                logs_own,
                logs_both,
            ),
            [shaped((n, 5 * HEAD_DIM + HEAD_DIM // 2, tok), BF), shaped((2, n + 1, QB, QB), F4)],
            [
                pltpu.VMEM((HEAD_DIM, total_rows), BF),
                pltpu.VMEM((HEAD_DIM, total_rows // 2), BF),
                pltpu.VMEM((n, 1, QB), F4),
                pltpu.VMEM((n, 1, LANES), F4),
                pltpu.VMEM((total_rows, LANES), F4),
                pltpu.VMEM((total_rows, LANES), F4),
                pltpu.VMEM((2, n + 1, QB, QB), F4),
                pltpu.VMEM((2, n + 1, QB, QB), F4),
                pltpu.SemaphoreType.DMA((4,)),
            ],
            loose=(5,),
            away=(1,),
            ties=(hold(out_token, w_parts),),
        )
        unit_in = all_to_all(hold(stacked, res_in, out_parts_in))

    with scope("wg"):
        *unit_grad_parts, parts_token = call(
            functools.partial(unit_weight_grads, n, heads),
            (normed, stacked, lines, buckets),
            [shaped((width // heads + n + 8, 3 * LANES), BF)] * heads,
            [
                pltpu.VMEM((width, 3 * LANES), F4),
                pltpu.VMEM((NUM_BUCKETS, 3 * LANES), F4),
                pltpu.VMEM((2 * n, 1, TILE), F4),
            ],
        )
        unit_parts_in = exchange(unit_grad_parts, HEAD)
    with scope("res"):
        result, result_token = call(
            functools.partial(result_rows, n, cap),
            (res_in, target, hidden),
            [shaped((tok, width), BF)],
            ties=(parts_token,),
        )
    with scope("fw"):
        full_w, full_token = call(
            functools.partial(unpack_full, n, rows),
            w_parts,
            [shaped((width, 3 * width), BF)],
            [pltpu.VMEM((width, 3 * width), F4)],
            ties=(parts_token,),
        )
    with scope("wg"):
        *sums, sums_token = call(
            functools.partial(weight_sums, n, rows, heads),
            unit_parts_in + out_parts_in,
            [shaped((rows, 3 * LANES + wide), BF)] * n,
            [pltpu.VMEM((n, rows, 3 * LANES + wide), F4)],
            ties=(full_token, result_token),
        )
        sums_in = exchange(sums, BLK)
    with scope("ewg"):
        grad_in, grad_out, expert_token = expert_weights_call(
            experts,
            seq_lengths,
            (moe_far, far_pair),
            all_cot[2:],
            *expert_ends,
            (sums_token,),
            begun,
        )
    with scope("fin"):
        (
            grad_q,
            grad_k,
            grad_v,
            grad_gain_attn,
            grad_table,
            grad_out_w,
            grad_gain_moe,
            grad_router,
            grad_tokens,
            unused,
        ) = call(
            functools.partial(last_grads, n, experts),
            sums_in
            + [w_query, w_key, w_value, gain_a]
            + [unit_in, full_w, x, grad_hidden, misc_t],
            [shaped((rows, width), F4)] * 3
            + [
                shaped((1, rows), F4),
                shaped((1, HEADS), F4),
                shaped((rows, width), F4),
                shaped((1, rows), F4),
                shaped((experts, rows), F4),
                shaped(tokens.shape, F4),
            ],
            [
                pltpu.VMEM((n, rows, 3 * LANES), F4),
                pltpu.VMEM((n, 1, LANES), F4),
                pltpu.VMEM((3 * width, tok), BF),
            ],
            ties=(expert_token,),
        )
    return (
        result.reshape(tokens.shape),
        grad_tokens,
        grad_gain_attn.reshape(-1),
        grad_q,
        grad_k,
        grad_v,
        jnp.transpose(grad_out_w),
        grad_table.reshape(-1),
        grad_gain_moe.reshape(-1),
        jnp.transpose(grad_router),
        grad_in.reshape(expert_in.shape),
        grad_out.reshape(expert_out.shape),
    )


def ring_of(place, ring_len):
    return 2 * place if place < ring_len // 2 else 2 * ring_len - 1 - 2 * place


def solution(mesh):
    in_specs = (
        P(BLK, HEAD, None),
        P((HEAD, BLK)),
        P((HEAD, BLK), None),
        P((HEAD, BLK), None),
        P((HEAD, BLK), None),
        P(None, (HEAD, BLK)),
        P((HEAD, BLK)),
        P((HEAD, BLK)),
        P((HEAD, BLK), None),
        P(BLK, None, HEAD),
        P(BLK, HEAD, None),
        P(),
        P(),
        P(HEAD, BLK, None, None),
        P(BLK, HEAD, None),
    )
    out_specs = (
        P(BLK, HEAD, None),
        P(BLK, HEAD, None),
        P((HEAD, BLK)),
        P((HEAD, BLK), None),
        P((HEAD, BLK), None),
        P((HEAD, BLK), None),
        P(None, (HEAD, BLK)),
        P((HEAD, BLK)),
        P((HEAD, BLK)),
        P((HEAD, BLK), None),
        P(BLK, None, HEAD),
        P(BLK, HEAD, None),
    )
    one_each = mesh.shape[HEAD] == 4 and mesh.shape[BLK] == 8
    return jax.shard_map(
        on_plane if one_each else on_device, mesh=mesh, in_specs=in_specs, out_specs=out_specs, check_vma=False
    )
```
